32 devices in a mesh: group: 4 (over y, core), seq: 4 (over z), tensor: 2 (over x).
Axes of the slice: x: 2, y: 2, z: 4, core: 2. Of those that a mesh axis runs over, the one named last changes fastest.
Arguments:
- span_tokens: bfloat16 [4, 1024, 2048], P('group', 'seq', 'tensor'), may hold values from -6 to 6
- q_weight: bfloat16 [2048, 2048], P(None, 'tensor'), may hold values from -0.125 to 0.125
- kv_weight: bfloat16 [2048, 512], P(None, 'tensor'), may hold values from -0.125 to 0.125
- out_weight: bfloat16 [2048, 2048], P('tensor'), may hold values from -0.1875 to 0.1875
- kv_pool: bfloat16 [64, 128, 512], P('group', None, 'tensor'), may hold values from -55 to 55, as said below
- cache_lengths: int32 [4], replicated, may hold values from 128 to 8192, as said below
- slot_requests: int32 [4], replicated, may hold values from 0 to 3, as said below
- page_table: int32 [4, 16], replicated, may hold values from 0 to 63, as said below
Outputs:
- attended: bfloat16 [4, 1024, 2048], P('group', 'seq', 'tensor')
The draws below stay inside these ranges and needn't reach their ends.
Inputs may be any that keep to these rules, and one draw needn't show every extreme that they name: `slot_requests`: A permutation; slot j is processed by group j. `page_table`: no pool page is named twice. The window pages of the requests dealt to one group lie 4 in each group's pool. `cache_lengths`: multiples of 128. `kv_pool`: cached keys and values.
All inputs are finite; a program needn't handle non-finite values.
Results may differ from the reference program's by a relative error of at most 0.015.
Values may be sent and summed in bfloat16 or wider, within the bound.
No kernel may reach another device: no remote copies, remote signals or barrier semaphores. Data moves between devices by JAX's collectives and lax.ppermute only.
A program may use at most 64 MiB of HBM per device.

```python
import jax
import jax.numpy as jnp
from jax import lax

D = 2048
H = 32
HD = 64
KVH = 4
WINDOW = 2048
PAGE = 128
SPAN = 1024
REQ_G = 1
REQUESTS = 4
KV_PER = 4
WP = 16
POOL_G = 16
CAP = 4
PAGES = 64
MAXP = 64
N_TENSOR = 2


def dealing(key):
    dealt_key = jax.random.fold_in(key, 11)
    slot_key, rotate_key, pool_key = jax.random.split(dealt_key, 3)
    group_count = REQUESTS // REQ_G
    slot_requests = jax.random.permutation(slot_key, REQUESTS).astype(jnp.int32)
    rotations = jax.random.randint(rotate_key, (group_count,), 0, group_count)
    pool_orders = jax.vmap(lambda sub_key: jax.random.permutation(sub_key, POOL_G))(jax.random.split(pool_key, group_count))
    slots = jnp.arange(REQUESTS, dtype=jnp.int32)
    target_group = slots // REQ_G
    within = slots % REQ_G
    entry_index = within[:, None] * WP + jnp.arange(WP, dtype=jnp.int32)[None, :]
    owner_group = (entry_index + rotations[target_group][:, None]) % group_count
    pool_place = pool_orders[owner_group, target_group[:, None] * CAP + entry_index // group_count]
    by_slot = (owner_group * POOL_G + pool_place).astype(jnp.int32)
    page_rows = jnp.zeros((REQUESTS, WP), jnp.int32).at[slot_requests].set(by_slot)
    return (slot_requests, page_rows)


def draw_slot_requests(key, part):
    return dealing(key)[0]


def draw_page_table(key, part):
    return dealing(key)[1]


def draw_cache_lengths(key, part):
    count_key, order_key = jax.random.split(jax.random.fold_in(key, 23))
    page_counts = jax.random.randint(count_key, (REQUESTS,), 1, MAXP + 1)
    order = jax.random.permutation(order_key, REQUESTS)
    page_counts = page_counts.at[order[0]].set(MAXP).at[order[1]].set(1)
    return (page_counts * PAGE).astype(jnp.int32)


def draw_kv_pool(key, part):
    value_key = jax.random.fold_in(jax.random.fold_in(key, 37), 0)
    shape_all = (PAGES, PAGE, 2 * KVH * HD)
    values = jnp.clip(jax.random.normal(value_key, shape_all, jnp.float32), -6.0, 6.0)
    return values.astype(jnp.bfloat16)


def spiked(entries, stream_key, source, target, blocks, factor):
    owner, partner = [(jnp.arange(entries.shape[position]) // (entries.shape[position] // blocks)).reshape([-1 if axis == position else 1 for axis in range(entries.ndim)]) for position in (source, target)]
    chosen = jax.random.permutation(stream_key, blocks)[partner]
    strong = (owner == chosen) | (owner == (partner + blocks // 2) % blocks)
    return jnp.where(strong, factor * entries, entries)


def levels(key, shape, shards, least, top_value):
    factor_of = 1.0
    for dim, blocks in shards:
        draws = jax.random.uniform(jax.random.fold_in(jax.random.fold_in(key, 6), dim), (blocks,), jnp.float32, least / len(shards), top_value / len(shards))
        factor_of = factor_of * jnp.repeat(jnp.exp(draws), shape[dim] // blocks).reshape((-1,) + (1,) * (len(shape) - 1 - dim))
    return factor_of


def bell_draw(stream_key, dims, deviation, limit, cuts=(), kind=jnp.bfloat16):
    loudness = levels(stream_key, dims, cuts, -0.22, 0.18) if cuts else 1.0
    values = jax.random.normal(stream_key, dims, jnp.float32) * deviation * loudness
    return jnp.minimum(jnp.maximum(values, -limit), limit).astype(kind)


def noise_with(rng, extent, spread, reach, pieces, heavy, kind=jnp.bfloat16):
    drawn = spread * jax.random.normal(rng, extent, jnp.float32)
    if pieces:
        drawn = drawn * levels(rng, extent, pieces, -0.22, 0.18)
    return jnp.clip(spiked(drawn, jax.random.fold_in(rng, 3), *heavy), -reach, reach).astype(kind)


def setup_inputs(seed: int = 0) -> dict:
    key_list = jax.random.split(jax.random.key(seed), 9)
    span_tokens = bell_draw(key_list[0], (REQUESTS, SPAN, D), 1.0, 6.0, ((0, 4), (1, 4), (2, 2)))
    q_weight = bell_draw(key_list[1], (D, H * HD), D ** -0.5, 0.125, ((1, 2),))
    kv_weight = bell_draw(key_list[2], (D, 2 * KVH * HD), D ** -0.5, 0.125, ((1, 2),))
    out_weight = noise_with(key_list[3], (H * HD, D), (H * HD) ** -0.5, 0.1875, ((0, 2),), (0, 1, 2, 2.0))
    kv_pool = draw_kv_pool(jax.random.fold_in(key_list[8], 71), 0)
    cache_lengths = draw_cache_lengths(jax.random.fold_in(key_list[8], 71), 0)
    slot_requests = draw_slot_requests(jax.random.fold_in(key_list[8], 71), 0)
    page_table = draw_page_table(jax.random.fold_in(key_list[8], 71), 0)
    return dict(span_tokens=span_tokens, q_weight=q_weight, kv_weight=kv_weight, out_weight=out_weight, kv_pool=kv_pool, cache_lengths=cache_lengths, slot_requests=slot_requests, page_table=page_table)


def rotate(values, positions):
    half_dim = HD // 2
    frequency = jnp.power(jnp.float32(10000.0), -jnp.arange(half_dim, dtype=jnp.float32) / half_dim)
    angles = positions.astype(jnp.float32)[:, None] * frequency[None, :]
    cosine = jnp.cos(angles)[:, None, :]
    sine_part = jnp.sin(angles)[:, None, :]
    front_half = values[..., :half_dim]
    back_half = values[..., half_dim:]
    return jnp.concatenate([front_half * cosine - back_half * sine_part, back_half * cosine + front_half * sine_part], axis=-1)


def attend(block_q, block_k, block_v, base_pos):
    query_count = block_q.shape[0]
    key_count = block_k.shape[0]
    scores = jnp.einsum("tkgd,nkd->kgtn", block_q.astype(jnp.float32), block_k.astype(jnp.float32)) * (HD ** -0.5)
    query_at = jnp.arange(query_count, dtype=jnp.int32)[:, None]
    key_at = jnp.arange(key_count, dtype=jnp.int32)[None, :]
    allowed = (key_at > query_at) & (key_at <= query_at + WINDOW) & (base_pos + key_at >= 0)
    masked = jnp.where(allowed, scores, jnp.float32(-1e30))
    row_top = jnp.max(masked, axis=-1, keepdims=True)
    weights = jnp.where(allowed, jnp.exp(masked - row_top), jnp.float32(0.0))
    row_total = jnp.sum(weights, axis=-1)
    rounded = weights.astype(jnp.bfloat16)
    mixed_rows = jnp.einsum("kgtn,nkd->tkgd", rounded.astype(jnp.float32), block_v.astype(jnp.float32))
    mixed_rows = mixed_rows / jnp.transpose(row_total, (2, 0, 1))[..., None]
    return mixed_rows.astype(jnp.bfloat16).reshape(query_count, -1)


def reference(span_tokens, q_weight, kv_weight, out_weight, kv_pool, cache_lengths, slot_requests, page_table):
    block_len = min(128, SPAN)
    per_kv = H // KVH
    head_groups = N_TENSOR // 2

    def one_slot(slot_index):
        request = slot_requests[slot_index]
        length = cache_lengths[request]
        tokens = span_tokens[slot_index]
        positions = length + jnp.arange(SPAN, dtype=jnp.int32)
        queries = jnp.dot(tokens, q_weight, preferred_element_type=jnp.float32).reshape(SPAN, H, HD)
        queries = rotate(queries, positions).astype(jnp.bfloat16).reshape(SPAN, KVH, per_kv, HD)
        fresh_rows = jnp.dot(tokens, kv_weight, preferred_element_type=jnp.float32).reshape(SPAN, head_groups, 2, KV_PER, HD)
        new_keys = rotate(fresh_rows[:, :, 0].reshape(SPAN, KVH, HD), positions).astype(jnp.bfloat16)
        new_values = fresh_rows[:, :, 1].reshape(SPAN, KVH, HD).astype(jnp.bfloat16)
        page_rows = kv_pool[page_table[request]].reshape(WINDOW, head_groups, 2, KV_PER, HD)
        key_rows = jnp.concatenate([page_rows[:, :, 0].reshape(WINDOW, KVH, HD), new_keys], axis=0)
        value_rows = jnp.concatenate([page_rows[:, :, 1].reshape(WINDOW, KVH, HD), new_values], axis=0)

        def one_block(block_index):
            first_row = block_index * block_len
            block_q = lax.dynamic_slice_in_dim(queries, first_row, block_len, 0)
            block_k = lax.dynamic_slice_in_dim(key_rows, first_row, WINDOW + block_len, 0)
            block_v = lax.dynamic_slice_in_dim(value_rows, first_row, WINDOW + block_len, 0)
            return attend(block_q, block_k, block_v, length - WINDOW + first_row)

        blocks = lax.map(one_block, jnp.arange(SPAN // block_len, dtype=jnp.int32))
        heads_out = blocks.reshape(SPAN, N_TENSOR, H * HD // N_TENSOR)
        out_groups = out_weight.reshape(N_TENSOR, H * HD // N_TENSOR, D)
        partial_value = jnp.einsum("tgk,gkd->gtd", heads_out.astype(jnp.float32), out_groups.astype(jnp.float32)).astype(jnp.bfloat16)
        return jnp.sum(partial_value.astype(jnp.float32), axis=0).astype(jnp.bfloat16)

    return lax.map(one_slot, jnp.arange(REQUESTS, dtype=jnp.int32))
```

```python
import jax
import jax.numpy as jnp
from jax import lax
from jax.experimental import pallas as pl
from jax.experimental.pallas import tpu as pltpu
from jax.sharding import PartitionSpec as P

HD = 64
KVH = 4
WINDOW = 2048
PAGE = 128


def shifted(block, axis, distance):
    devices = range(lax.axis_size(axis))
    route = [(i - distance, i) for i in devices if i - distance in devices]
    return lax.ppermute(block, axis, route)


def swapped(value, axis, stride):
    return lax.ppermute(value, axis, [(i, i ^ 1 << stride) for i in range(lax.axis_size(axis))])


def rotate(values, positions):
    half_dim = HD // 2
    frequency = jnp.power(jnp.float32(10000.0), -jnp.arange(half_dim, dtype=jnp.float32) / half_dim)
    angles = positions.astype(jnp.float32)[:, None] * frequency[None, :]
    cosine = jnp.cos(angles)[:, None, :]
    sine_part = jnp.sin(angles)[:, None, :]
    front_half = values[..., :half_dim]
    back_half = values[..., half_dim:]
    return jnp.concatenate(
        [front_half * cosine - back_half * sine_part, back_half * cosine + front_half * sine_part],
        axis=-1,
    )


def attend(block_q, block_k, block_v, base_pos):
    query_count = block_q.shape[0]
    key_count = block_k.shape[0]
    scores = jnp.einsum(
        "tkgd,nkd->kgtn", block_q, block_k, preferred_element_type=jnp.float32
    ) * HD ** (-0.5)
    query_at = jnp.arange(query_count, dtype=jnp.int32)[:, None]
    key_at = jnp.arange(key_count, dtype=jnp.int32)[None, :]
    allowed = (key_at > query_at) & (key_at <= query_at + WINDOW) & (base_pos + key_at >= 0)
    masked = jnp.where(allowed, scores, jnp.float32(-1e30))
    row_top = jnp.max(masked, axis=-1, keepdims=True)
    weights = jnp.where(allowed, jnp.exp(masked - row_top), jnp.float32(0.0))
    row_total = jnp.sum(weights, axis=-1)
    rounded = weights.astype(jnp.bfloat16)
    mixed_rows = jnp.einsum("kgtn,nkd->tkgd", rounded, block_v, preferred_element_type=jnp.float32)
    mixed_rows = mixed_rows / jnp.transpose(row_total, (2, 0, 1))[..., None]
    return mixed_rows.astype(jnp.bfloat16).reshape(query_count, -1)


def shards(
    span_tokens, q_weight, kv_weight, out_weight, kv_pool, cache_lengths, slot_requests, page_table
):
    groups = lax.axis_size("group")
    seq_count = lax.axis_size("seq")
    tensor_count = lax.axis_size("tensor")
    group_id = lax.axis_index("group")
    seq_id = lax.axis_index("seq")
    tensor_id = lax.axis_index("tensor")
    local_reqs, seg_len, feat_local = span_tokens.shape
    head_cols = q_weight.shape[1]
    kv_cols = kv_weight.shape[1]
    local_heads = head_cols // HD
    group_heads = kv_cols // HD
    kv_local = max(1, KVH // tensor_count)
    per_kv = local_heads // kv_local
    head_first = tensor_id * KVH // tensor_count % group_heads
    holds_keys = tensor_id % 2 == 0
    pool_rows = kv_pool.shape[0]
    capacity = pool_rows // groups
    row_count = local_reqs * seg_len
    my_slots = group_id * local_reqs + jnp.arange(local_reqs, dtype=jnp.int32)
    my_requests = slot_requests[my_slots]
    my_lengths = cache_lengths[my_requests]
    project_piece_rows = lax.all_gather(span_tokens, "tensor", axis=2, tiled=True)
    feat_width = project_piece_rows.shape[2]
    flat_rows = project_piece_rows.reshape(row_count, feat_width)
    query_lin = jnp.dot(flat_rows, q_weight, preferred_element_type=jnp.float32)
    fresh_lin = jnp.dot(flat_rows, kv_weight, preferred_element_type=jnp.float32)
    positions = (
        my_lengths[:, None] + seq_id * seg_len + jnp.arange(seg_len, dtype=jnp.int32)[None, :]
    )
    queries = jax.vmap(rotate)(query_lin.reshape(local_reqs, seg_len, local_heads, HD), positions)
    queries = queries.astype(jnp.bfloat16).reshape(local_reqs, seg_len, kv_local, per_kv, HD)
    fresh_heads = fresh_lin.reshape(local_reqs, seg_len, group_heads, HD)
    rotated = jax.vmap(rotate)(fresh_heads, positions)
    span_kv = (
        jnp.where(holds_keys, rotated, fresh_heads)
        .astype(jnp.bfloat16)
        .reshape(local_reqs, seg_len, kv_cols)
    )
    all_ids = page_table[slot_requests]
    owned_here = all_ids // pool_rows == group_id
    slot_rank = jnp.cumsum(owned_here.astype(jnp.int32), axis=1) - 1
    local_rows = all_ids - group_id * pool_rows
    chosen = owned_here[:, :, None] & (
        slot_rank[:, :, None] == jnp.arange(capacity, dtype=jnp.int32)[None, None, :]
    )
    wanted = jnp.sum(jnp.where(chosen, local_rows[:, :, None], 0), axis=1)
    my_ids = page_table[my_requests].reshape(-1)
    my_owner = my_ids // pool_rows
    onehot = (my_owner[:, None] == jnp.arange(groups, dtype=jnp.int32)[None, :]).astype(jnp.int32)
    arrival = jnp.sum((jnp.cumsum(onehot, axis=0) - 1) * onehot, axis=1)
    arrived_row = my_owner * capacity + arrival
    outgoing = kv_pool[wanted]
    arrived = lax.all_to_all(outgoing, "group", split_axis=0, concat_axis=0, tiled=True)
    cached = arrived.reshape(groups * capacity, PAGE, kv_cols)[arrived_row]
    cached = cached.reshape(local_reqs, WINDOW, kv_cols)
    span_all = jnp.zeros((local_reqs, seg_len * seq_count, kv_cols), jnp.bfloat16)
    for back_step in range(seq_count - 1, -1, -1):
        piece_rows = span_kv if back_step == 0 else shifted(span_kv, "seq", back_step)
        span_all = lax.dynamic_update_slice_in_dim(
            span_all, piece_rows, (seq_id - back_step) * seg_len, 1
        )
    joined = jnp.concatenate([cached, span_all], axis=1)
    visible = lax.dynamic_slice_in_dim(joined, seq_id * seg_len, WINDOW + seg_len, 1)
    partner_rows = swapped(visible, "tensor", 0)
    key_all = jnp.where(holds_keys, visible, partner_rows).reshape(
        local_reqs, WINDOW + seg_len, group_heads, HD
    )
    value_all = jnp.where(holds_keys, partner_rows, visible).reshape(
        local_reqs, WINDOW + seg_len, group_heads, HD
    )
    key_rows = lax.dynamic_slice_in_dim(key_all, head_first, kv_local, 2)
    value_rows = lax.dynamic_slice_in_dim(value_all, head_first, kv_local, 2)
    block_len = min(128, seg_len)
    block_count = seg_len // block_len

    def per_request(request_items):
        request_q, request_k, request_v, length = request_items

        def per_block(block_index):
            first_row = block_index * block_len
            block_q = lax.dynamic_slice_in_dim(request_q, first_row, block_len, 0)
            block_k = lax.dynamic_slice_in_dim(request_k, first_row, WINDOW + block_len, 0)
            block_v = lax.dynamic_slice_in_dim(request_v, first_row, WINDOW + block_len, 0)
            return attend(block_q, block_k, block_v, length - WINDOW + seq_id * seg_len + first_row)

        return lax.map(per_block, jnp.arange(block_count, dtype=jnp.int32)).reshape(
            seg_len, head_cols
        )

    attended_heads = lax.map(per_request, (queries, key_rows, value_rows, my_lengths))
    flat_heads = attended_heads.reshape(row_count, head_cols)
    out_cols = out_weight.shape[1] // tensor_count
    summed = lax.psum_scatter(
        lax.dot_general(
            out_weight, flat_heads, (((0,), (1,)), ((), ())), preferred_element_type=jnp.float32
        ).astype(jnp.bfloat16),
        "tensor",
        scatter_dimension=0,
        tiled=True,
    ).astype(jnp.float32)
    result = summed.T
    return result.astype(jnp.bfloat16).reshape(local_reqs, seg_len, out_cols)


LOG2E = 1.4426950408889634
MASKED = -1e30
F32 = jnp.float32
BF16 = jnp.bfloat16
HBM = pl.BlockSpec(memory_space=pl.ANY)
VMEM = pl.BlockSpec(memory_space=pltpu.VMEM)
SMEM = pl.BlockSpec(memory_space=pltpu.SMEM)
VMEM_BYTES = 60 * 2**20


def params():
    return pltpu.CompilerParams(vmem_limit_bytes=VMEM_BYTES)


def cost(flops, moved):
    return pl.CostEstimate(flops=flops, bytes_accessed=moved, transcendentals=0)


def stage_kernel(where, slots, table, pool, *refs):
    outs, sems = refs[:7], refs[7]
    group, tensor = where[0], where[2]
    pages = pool.shape[0]
    half = pool.shape[2] // 2
    mine = pl.ds(pl.multiple_of(tensor * half, half), half)
    theirs = pl.ds(pl.multiple_of((1 - tensor) * half, half), half)
    for flip in range(4):
        request = slots[group ^ flip]

        def take(w, rank, flip=flip, request=request):
            page = table[request, w]
            here = page // pages == group

            @pl.when(here)
            def _():
                row = page % pages
                pltpu.make_async_copy(
                    pool.at[row, :, theirs], outs[flip].at[rank], sems.at[flip]
                ).start()
                if flip:
                    pltpu.make_async_copy(
                        pool.at[row, :, mine], outs[3 + flip].at[rank], sems.at[3 + flip]
                    ).start()

            return rank + here.astype(jnp.int32)

        lax.fori_loop(0, table.shape[1], take, jnp.int32(0))
    for i in range(7):
        pltpu.make_async_copy(outs[i], outs[i], sems.at[i]).wait()


def stage(where, slots, table, pool):
    piece = jax.ShapeDtypeStruct((pool.shape[0] // 4, pool.shape[1], pool.shape[2] // 2), BF16)
    return pl.pallas_call(
        stage_kernel,
        out_shape=[piece] * 7,
        in_specs=[SMEM, SMEM, SMEM, HBM],
        out_specs=[HBM] * 7,
        scratch_shapes=[pltpu.SemaphoreType.DMA((7,))],
        compiler_params=params(),
        cost_estimate=cost(0, 2 * 7 * 4 * 128 * 128 * 2),
    )(where, slots, table, pool)


def first_kernel(where, x, wq, wkv, acc_q, acc_kv):
    acc_q[...] = jnp.dot(x[...], wq[...], preferred_element_type=F32)
    acc_kv[...] = jnp.dot(x[...], wkv[...], preferred_element_type=F32)


def first_project(where, x, wq, wkv):
    rows, feats = x.shape
    q_cols, kv_cols = wq.shape[1] // 2, wkv.shape[1] // 2
    return pl.pallas_call(
        first_kernel,
        out_shape=[
            jax.ShapeDtypeStruct((rows, 2 * q_cols), F32),
            jax.ShapeDtypeStruct((rows, 2 * kv_cols), F32),
        ],
        grid_spec=pltpu.PrefetchScalarGridSpec(
            num_scalar_prefetch=1,
            grid=(2,),
            in_specs=[
                pl.BlockSpec((rows, feats), lambda i, w: (0, 0)),
                pl.BlockSpec((feats, q_cols), lambda i, w: (w[2], i)),
                pl.BlockSpec((feats, kv_cols), lambda i, w: (w[2], i)),
            ],
            out_specs=[
                pl.BlockSpec((rows, q_cols), lambda i, w: (0, i)),
                pl.BlockSpec((rows, kv_cols), lambda i, w: (0, i)),
            ],
        ),
        compiler_params=params(),
        cost_estimate=cost(2 * rows * feats * 1280, feats * 1280 * 2),
    )(where, x, wq, wkv)


def turned(x, cosine, sine):
    lane = lax.broadcasted_iota(jnp.int32, x.shape, 1)
    other = jnp.where(lane % HD < HD // 2, pltpu.roll(x, 128 - HD // 2, 1), pltpu.roll(x, HD // 2, 1))
    return x * cosine + other * sine


def second_kernel(where, x, wq, wkv, acc_q, acc_kv, cosine, sine, q, kept, sent):
    tensor = where[2]
    cos_all, sin_all = cosine[...], sine[...]

    @pl.when(pl.program_id(0) == 0)
    def _():
        fresh = acc_kv[...] + jnp.dot(x[...], wkv[...], preferred_element_type=F32)
        keys = tensor == 0
        cos_kv = jnp.where(keys, cos_all, 1.0)
        sin_kv = jnp.where(keys, sin_all, 0.0)
        low = turned(fresh[:, :128], cos_kv, sin_kv).astype(BF16)
        high = turned(fresh[:, 128:], cos_kv, sin_kv).astype(BF16)
        kept[...] = jnp.where(keys, low, high)
        sent[...] = jnp.where(keys, high, low)

    lin = acc_q[...] + jnp.dot(x[...], wq[...], preferred_element_type=F32)
    scale = HD**-0.5 * LOG2E
    for c in range(0, lin.shape[1], 128):
        q[:, c : c + 128] = (turned(lin[:, c : c + 128], cos_all, sin_all) * scale).astype(BF16)


def second_project(where, x, wq, wkv, acc_q, acc_kv, cosine, sine):
    rows, feats = x.shape
    q_cols, kv_cols = wq.shape[1] // 2, wkv.shape[1]
    piece = jax.ShapeDtypeStruct((rows, kv_cols // 2), BF16)
    return pl.pallas_call(
        second_kernel,
        out_shape=[jax.ShapeDtypeStruct((rows, 2 * q_cols), BF16), piece, piece],
        grid_spec=pltpu.PrefetchScalarGridSpec(
            num_scalar_prefetch=1,
            grid=(2,),
            in_specs=[
                pl.BlockSpec((rows, feats), lambda i, w: (0, 0)),
                pl.BlockSpec((feats, q_cols), lambda i, w: (1 - w[2], i)),
                pl.BlockSpec((feats, kv_cols), lambda i, w: (1 - w[2], 0)),
                pl.BlockSpec((rows, q_cols), lambda i, w: (0, i)),
                pl.BlockSpec((rows, kv_cols), lambda i, w: (0, 0)),
                pl.BlockSpec((rows, 128), lambda i, w: (0, 0)),
                pl.BlockSpec((rows, 128), lambda i, w: (0, 0)),
            ],
            out_specs=[
                pl.BlockSpec((rows, q_cols), lambda i, w: (0, i)),
                pl.BlockSpec((rows, kv_cols // 2), lambda i, w: (0, 0)),
                pl.BlockSpec((rows, kv_cols // 2), lambda i, w: (0, 0)),
            ],
        ),
        compiler_params=params(),
        cost_estimate=cost(2 * rows * feats * 1280, feats * 1280 * 2),
    )(where, x, wq, wkv, acc_q, acc_kv, cosine, sine)


def attend_kernel(
    where, slots, table, lengths, q, pool, own1, own2, own3, oth0, oth1, oth2, oth3,
    kept, got, z1, z2, z3, out, flow, rank, kv, keys, values, sem
):
    group, seq, tensor = where[0], where[1], where[2]
    pages = pool.shape[0]
    window_pages = table.shape[1]
    request = slots[group]
    rows = q.shape[0]
    per = rows // PAGE
    blocks = kv.shape[1] // PAGE
    half = pool.shape[2] // 2
    mine = pl.ds(pl.multiple_of(tensor * half, half), half)
    owns = (None, own1, own2, own3)
    others = (oth0, oth1, oth2, oth3)

    def note(w, counts):
        came = table[request, w] // pages ^ group
        place = jnp.int32(0)
        for d in range(4):
            place = jnp.where(came == d, counts[d], place)
        flow[w] = came
        rank[w] = place
        return tuple(counts[d] + (came == d).astype(jnp.int32) for d in range(4))

    lax.fori_loop(0, window_pages, note, (jnp.int32(0),) * 4)

    def fetch(n, _):
        block = seq * per + n
        here = pl.ds(pl.multiple_of(n * PAGE, PAGE), PAGE)

        def bring(own, other):
            pltpu.make_async_copy(own, kv.at[tensor, here], sem).start()
            pltpu.make_async_copy(other, kv.at[1 - tensor, here], sem).start()

        @pl.when(block < window_pages)
        def _():
            for d in range(4):

                @pl.when(flow[block] == d)
                def _(d=d):
                    at = rank[block]
                    if d:
                        bring(owns[d].at[at], others[d].at[at])
                    else:
                        bring(pool.at[table[request, block] % pages, :, mine], others[0].at[at])

        @pl.when(block >= window_pages)
        def _():
            fresh = block - window_pages
            away = fresh // per ^ seq
            part = pl.ds(pl.multiple_of(fresh % per * PAGE, PAGE), PAGE)

            @pl.when(away == 0)
            def _():
                bring(kept.at[part], got.at[part])

            for d, z in ((1, z1), (2, z2), (3, z3)):

                @pl.when(away == d)
                def _(z=z):
                    bring(z.at[0, part], z.at[1, part])

        return 0

    lax.fori_loop(0, blocks, fetch, 0)
    pltpu.make_async_copy(kv, kv, sem).wait()

    lane = lax.broadcasted_iota(jnp.int32, (PAGE, 2 * HD), 1)
    low = lane < HD
    first = lengths[request] - WINDOW + seq * rows

    def prepare(n, _):
        here = pl.ds(pl.multiple_of(n * PAGE, PAGE), PAGE)
        bias = jnp.where(first + n * PAGE >= 0, 0.0, MASKED)
        k = kv[0, here].astype(F32)
        v = kv[1, here].astype(F32)
        kr = pltpu.roll(k, HD, 1)
        vr = pltpu.roll(v, HD, 1)
        even = jnp.where(lane == HD, bias, 0.0)
        odd = jnp.where(lane == 0, bias, 0.0)
        keys[0, 0, here] = jnp.where(low, k, even).astype(BF16)
        keys[0, 1, here] = jnp.where(low, odd, kr).astype(BF16)
        keys[1, 0, here] = jnp.where(low, kr, even).astype(BF16)
        keys[1, 1, here] = jnp.where(low, odd, k).astype(BF16)
        values[0, 0, here] = jnp.where(low, v, 1.0).astype(BF16)
        values[0, 1, here] = jnp.where(low, 1.0, vr).astype(BF16)
        values[1, 0, here] = jnp.where(low, vr, 1.0).astype(BF16)
        values[1, 1, here] = jnp.where(low, 1.0, v).astype(BF16)
        return 0

    lax.fori_loop(0, blocks, prepare, 0)

    qlane = lax.broadcasted_iota(jnp.int32, (rows, 2 * HD), 1)
    qlow = qlane < HD
    mark_even = jnp.where(qlane == HD, 1.0, 0.0).astype(BF16)
    mark_odd = jnp.where(qlane == 0, 1.0, 0.0).astype(BF16)
    stack = 2
    query_at = lax.broadcasted_iota(jnp.int32, (stack * rows, rows), 0) % rows
    key_at = lax.broadcasted_iota(jnp.int32, (stack * rows, rows), 1)

    def scores(qs, ks):
        s = lax.dot_general(qs, ks, (((1,), (1,)), ((), ())), preferred_element_type=F32)
        return jnp.concatenate(
            [
                jnp.where(key_at > query_at, s[:, :rows], MASKED),
                s[:, rows:-rows],
                jnp.where(key_at <= query_at, s[:, -rows:], MASKED),
            ],
            axis=1,
        )

    def weigh(s):
        return jnp.exp2(s - jnp.max(s, axis=1, keepdims=True)).astype(BF16)

    def heads(i, _):
        kv_head = i // (4 // stack)
        tiles = [
            q[:, pl.ds(pl.multiple_of((i * stack + j) * 128, 128), 128)] for j in range(stack)
        ]
        q_even = jnp.concatenate([jnp.where(qlow, x, mark_even) for x in tiles], axis=0)
        q_odd = jnp.concatenate([jnp.where(qlow, mark_odd, x) for x in tiles], axis=0)
        s_even = scores(q_even, keys[kv_head, 0])
        s_odd = scores(q_odd, keys[kv_head, 1])
        p_even = weigh(s_even)
        p_odd = weigh(s_odd)
        o_even = jnp.dot(p_even, values[kv_head, 0], preferred_element_type=F32)
        o_odd = jnp.dot(p_odd, values[kv_head, 1], preferred_element_type=F32)
        for j in range(stack):
            a = o_even[j * rows : (j + 1) * rows]
            b = o_odd[j * rows : (j + 1) * rows]
            done = jnp.where(qlow, a / pltpu.roll(a, HD, 1), b / pltpu.roll(b, HD, 1))
            out[:, pl.ds(pl.multiple_of((i * stack + j) * 128, 128), 128)] = done.astype(BF16)
        return 0

    lax.fori_loop(0, q.shape[1] // 128 // stack, heads, 0)


def attend_all(where, slots, table, lengths, q, pool, owns, others, kept, got, zs):
    rows = q.shape[0]
    span = WINDOW + rows
    return pl.pallas_call(
        attend_kernel,
        out_shape=jax.ShapeDtypeStruct(q.shape, BF16),
        in_specs=[SMEM] * 4 + [VMEM] + [HBM] * 13,
        out_specs=VMEM,
        scratch_shapes=[
            pltpu.SMEM((table.shape[1],), jnp.int32),
            pltpu.SMEM((table.shape[1],), jnp.int32),
            pltpu.VMEM((2, span, 2 * HD), BF16),
            pltpu.VMEM((2, 2, span, 2 * HD), BF16),
            pltpu.VMEM((2, 2, span, 2 * HD), BF16),
            pltpu.SemaphoreType.DMA,
        ],
        compiler_params=params(),
        cost_estimate=cost(4 * rows * span * 2048, 4 * span * 128),
    )(where, slots, table, lengths, q, pool, *owns, *others, kept, got, *zs)


def out_kernel(where, x, w, o):
    o[...] = jnp.dot(x[...], w[...], preferred_element_type=F32).astype(BF16)


def out_project(where, x, w, mine):
    rows, depth = x.shape
    cols = w.shape[1] // 4

    def weight_at(i, where_ref):
        side = where_ref[2] if mine else 1 - where_ref[2]
        return (0, 2 * side + i)

    return pl.pallas_call(
        out_kernel,
        out_shape=jax.ShapeDtypeStruct((rows, 2 * cols), BF16),
        grid_spec=pltpu.PrefetchScalarGridSpec(
            num_scalar_prefetch=1,
            grid=(2,),
            in_specs=[
                pl.BlockSpec((rows, depth), lambda i, s: (0, 0)),
                pl.BlockSpec((depth, cols), weight_at),
            ],
            out_specs=pl.BlockSpec((rows, cols), lambda i, s: (0, i)),
        ),
        compiler_params=params(),
        cost_estimate=cost(4 * rows * depth * cols, 4 * depth * cols),
    )(where, x, w)


def flipped(value, axes, count, bits):
    return lax.ppermute(value, axes, [(i, i ^ bits) for i in range(count)])


def shards_fast(
    span_tokens, q_weight, kv_weight, out_weight, kv_pool, cache_lengths, slot_requests, page_table
):
    group_id = lax.axis_index("group")
    seq_id = lax.axis_index("seq")
    tensor_id = lax.axis_index("tensor")
    where = jnp.stack([group_id, seq_id, tensor_id]).astype(jnp.int32)
    mine = span_tokens[0]
    rows = mine.shape[0]
    theirs = flipped(mine, "tensor", 2, 1)
    pieces = stage(where, slot_requests, page_table, kv_pool)
    others = [flipped(pieces[d], ("group", "tensor"), 8, 2 * d + 1) for d in range(4)]
    owns = [flipped(pieces[3 + d], "group", 4, d) for d in range(1, 4)]
    length = cache_lengths[slot_requests[group_id]]
    positions = length + seq_id * rows + jnp.arange(rows, dtype=jnp.int32)
    half_dim = HD // 2
    lane = jnp.arange(128, dtype=jnp.int32)
    frequency = jnp.power(jnp.float32(10000.0), -(lane % half_dim).astype(F32) / half_dim)
    angles = positions.astype(F32)[:, None] * frequency[None, :]
    cosine = jnp.cos(angles)
    sine = jnp.where(lane % HD < half_dim, -1.0, 1.0)[None, :] * jnp.sin(angles)
    acc_q, acc_kv = first_project(where, mine, q_weight, kv_weight)
    q, kept, sent = second_project(
        where, theirs, q_weight, kv_weight, acc_q, acc_kv, cosine, sine
    )
    got = flipped(sent, "tensor", 2, 1)
    fresh = jnp.stack([kept, got])
    zs = [flipped(fresh, "seq", 4, d) for d in range(1, 4)]
    heads = attend_all(
        where, slot_requests, page_table, cache_lengths, q, kv_pool, owns, others, kept, got, zs
    )
    away = flipped(out_project(where, heads, out_weight, False), "tensor", 2, 1)
    home = out_project(where, heads, out_weight, True)
    return (home.astype(F32) + away.astype(F32)).astype(BF16)[None]


def solution(mesh):
    sizes = tuple(mesh.shape[a] for a in ("group", "seq", "tensor"))
    body = shards_fast if sizes == (4, 4, 2) else shards
    placed = (
        P("group", "seq", "tensor"),
        P(None, "tensor"),
        P(None, "tensor"),
        P("tensor", None),
        P("group", None, "tensor"),
        P(),
        P(),
        P(),
    )
    return jax.shard_map(
        body, mesh=mesh, in_specs=placed, out_specs=P("group", "seq", "tensor"), check_vma=False
    )
```

```python
import functools

import jax
import jax.numpy as jnp
from jax import lax
from jax.experimental import pallas as pl
from jax.experimental.pallas import tpu as pltpu
from jax.sharding import PartitionSpec as P

HD = 64
KVH = 4
WINDOW = 2048
PAGE = 128


def shifted(block, axis, distance):
    devices = range(lax.axis_size(axis))
    route = [(i - distance, i) for i in devices if i - distance in devices]
    return lax.ppermute(block, axis, route)


def swapped(value, axis, stride):
    return lax.ppermute(value, axis, [(i, i ^ 1 << stride) for i in range(lax.axis_size(axis))])


def rotate(values, positions):
    half_dim = HD // 2
    frequency = jnp.power(jnp.float32(10000.0), -jnp.arange(half_dim, dtype=jnp.float32) / half_dim)
    angles = positions.astype(jnp.float32)[:, None] * frequency[None, :]
    cosine = jnp.cos(angles)[:, None, :]
    sine_part = jnp.sin(angles)[:, None, :]
    front_half = values[..., :half_dim]
    back_half = values[..., half_dim:]
    return jnp.concatenate(
        [front_half * cosine - back_half * sine_part, back_half * cosine + front_half * sine_part],
        axis=-1,
    )


def attend(block_q, block_k, block_v, base_pos):
    query_count = block_q.shape[0]
    key_count = block_k.shape[0]
    scores = jnp.einsum(
        "tkgd,nkd->kgtn", block_q, block_k, preferred_element_type=jnp.float32
    ) * HD ** (-0.5)
    query_at = jnp.arange(query_count, dtype=jnp.int32)[:, None]
    key_at = jnp.arange(key_count, dtype=jnp.int32)[None, :]
    allowed = (key_at > query_at) & (key_at <= query_at + WINDOW) & (base_pos + key_at >= 0)
    masked = jnp.where(allowed, scores, jnp.float32(-1e30))
    row_top = jnp.max(masked, axis=-1, keepdims=True)
    weights = jnp.where(allowed, jnp.exp(masked - row_top), jnp.float32(0.0))
    row_total = jnp.sum(weights, axis=-1)
    rounded = weights.astype(jnp.bfloat16)
    mixed_rows = jnp.einsum("kgtn,nkd->tkgd", rounded, block_v, preferred_element_type=jnp.float32)
    mixed_rows = mixed_rows / jnp.transpose(row_total, (2, 0, 1))[..., None]
    return mixed_rows.astype(jnp.bfloat16).reshape(query_count, -1)


def shards(
    span_tokens, q_weight, kv_weight, out_weight, kv_pool, cache_lengths, slot_requests, page_table
):
    groups = lax.axis_size("group")
    seq_count = lax.axis_size("seq")
    tensor_count = lax.axis_size("tensor")
    group_id = lax.axis_index("group")
    seq_id = lax.axis_index("seq")
    tensor_id = lax.axis_index("tensor")
    local_reqs, seg_len, feat_local = span_tokens.shape
    head_cols = q_weight.shape[1]
    kv_cols = kv_weight.shape[1]
    local_heads = head_cols // HD
    group_heads = kv_cols // HD
    kv_local = max(1, KVH // tensor_count)
    per_kv = local_heads // kv_local
    head_first = tensor_id * KVH // tensor_count % group_heads
    holds_keys = tensor_id % 2 == 0
    pool_rows = kv_pool.shape[0]
    capacity = pool_rows // groups
    row_count = local_reqs * seg_len
    my_slots = group_id * local_reqs + jnp.arange(local_reqs, dtype=jnp.int32)
    my_requests = slot_requests[my_slots]
    my_lengths = cache_lengths[my_requests]
    project_piece_rows = lax.all_gather(span_tokens, "tensor", axis=2, tiled=True)
    feat_width = project_piece_rows.shape[2]
    flat_rows = project_piece_rows.reshape(row_count, feat_width)
    query_lin = jnp.dot(flat_rows, q_weight, preferred_element_type=jnp.float32)
    fresh_lin = jnp.dot(flat_rows, kv_weight, preferred_element_type=jnp.float32)
    positions = (
        my_lengths[:, None] + seq_id * seg_len + jnp.arange(seg_len, dtype=jnp.int32)[None, :]
    )
    queries = jax.vmap(rotate)(query_lin.reshape(local_reqs, seg_len, local_heads, HD), positions)
    queries = queries.astype(jnp.bfloat16).reshape(local_reqs, seg_len, kv_local, per_kv, HD)
    fresh_heads = fresh_lin.reshape(local_reqs, seg_len, group_heads, HD)
    rotated = jax.vmap(rotate)(fresh_heads, positions)
    span_kv = (
        jnp.where(holds_keys, rotated, fresh_heads)
        .astype(jnp.bfloat16)
        .reshape(local_reqs, seg_len, kv_cols)
    )
    all_ids = page_table[slot_requests]
    owned_here = all_ids // pool_rows == group_id
    slot_rank = jnp.cumsum(owned_here.astype(jnp.int32), axis=1) - 1
    local_rows = all_ids - group_id * pool_rows
    chosen = owned_here[:, :, None] & (
        slot_rank[:, :, None] == jnp.arange(capacity, dtype=jnp.int32)[None, None, :]
    )
    wanted = jnp.sum(jnp.where(chosen, local_rows[:, :, None], 0), axis=1)
    my_ids = page_table[my_requests].reshape(-1)
    my_owner = my_ids // pool_rows
    onehot = (my_owner[:, None] == jnp.arange(groups, dtype=jnp.int32)[None, :]).astype(jnp.int32)
    arrival = jnp.sum((jnp.cumsum(onehot, axis=0) - 1) * onehot, axis=1)
    arrived_row = my_owner * capacity + arrival
    outgoing = kv_pool[wanted]
    arrived = lax.all_to_all(outgoing, "group", split_axis=0, concat_axis=0, tiled=True)
    cached = arrived.reshape(groups * capacity, PAGE, kv_cols)[arrived_row]
    cached = cached.reshape(local_reqs, WINDOW, kv_cols)
    span_all = jnp.zeros((local_reqs, seg_len * seq_count, kv_cols), jnp.bfloat16)
    for back_step in range(seq_count - 1, -1, -1):
        piece_rows = span_kv if back_step == 0 else shifted(span_kv, "seq", back_step)
        span_all = lax.dynamic_update_slice_in_dim(
            span_all, piece_rows, (seq_id - back_step) * seg_len, 1
        )
    joined = jnp.concatenate([cached, span_all], axis=1)
    visible = lax.dynamic_slice_in_dim(joined, seq_id * seg_len, WINDOW + seg_len, 1)
    partner_rows = swapped(visible, "tensor", 0)
    key_all = jnp.where(holds_keys, visible, partner_rows).reshape(
        local_reqs, WINDOW + seg_len, group_heads, HD
    )
    value_all = jnp.where(holds_keys, partner_rows, visible).reshape(
        local_reqs, WINDOW + seg_len, group_heads, HD
    )
    key_rows = lax.dynamic_slice_in_dim(key_all, head_first, kv_local, 2)
    value_rows = lax.dynamic_slice_in_dim(value_all, head_first, kv_local, 2)
    block_len = min(128, seg_len)
    block_count = seg_len // block_len

    def per_request(request_items):
        request_q, request_k, request_v, length = request_items

        def per_block(block_index):
            first_row = block_index * block_len
            block_q = lax.dynamic_slice_in_dim(request_q, first_row, block_len, 0)
            block_k = lax.dynamic_slice_in_dim(request_k, first_row, WINDOW + block_len, 0)
            block_v = lax.dynamic_slice_in_dim(request_v, first_row, WINDOW + block_len, 0)
            return attend(block_q, block_k, block_v, length - WINDOW + seq_id * seg_len + first_row)

        return lax.map(per_block, jnp.arange(block_count, dtype=jnp.int32)).reshape(
            seg_len, head_cols
        )

    attended_heads = lax.map(per_request, (queries, key_rows, value_rows, my_lengths))
    flat_heads = attended_heads.reshape(row_count, head_cols)
    out_cols = out_weight.shape[1] // tensor_count
    summed = lax.psum_scatter(
        lax.dot_general(
            out_weight, flat_heads, (((0,), (1,)), ((), ())), preferred_element_type=jnp.float32
        ).astype(jnp.bfloat16),
        "tensor",
        scatter_dimension=0,
        tiled=True,
    ).astype(jnp.float32)
    result = summed.T
    return result.astype(jnp.bfloat16).reshape(local_reqs, seg_len, out_cols)


LOG2E = 1.4426950408889634
MASKED = -1e30
F32 = jnp.float32
BF16 = jnp.bfloat16
HBM = pl.BlockSpec(memory_space=pl.ANY)
VMEM = pl.BlockSpec(memory_space=pltpu.VMEM)
SMEM = pl.BlockSpec(memory_space=pltpu.SMEM)


def params(mebibytes):
    return pltpu.CompilerParams(vmem_limit_bytes=mebibytes * 2**20)


def cost(flops, moved):
    return pl.CostEstimate(flops=flops, bytes_accessed=moved, transcendentals=0)


def stage_kernel(where, slots, table, pool, *refs):
    outs, sems = refs[:7], refs[7]
    group, tensor = where[0], where[2]
    pages = pool.shape[0]
    half = pool.shape[2] // 2
    mine = pl.ds(pl.multiple_of(tensor * half, half), half)
    theirs = pl.ds(pl.multiple_of((1 - tensor) * half, half), half)
    for flip in range(4):
        request = slots[group ^ flip]

        def take(w, rank, flip=flip, request=request):
            page = table[request, w]
            here = page // pages == group

            @pl.when(here)
            def _():
                row = page % pages
                pltpu.make_async_copy(
                    pool.at[row, :, theirs], outs[flip].at[rank], sems.at[flip]
                ).start()
                if flip:
                    pltpu.make_async_copy(
                        pool.at[row, :, mine], outs[3 + flip].at[rank], sems.at[3 + flip]
                    ).start()

            return rank + here.astype(jnp.int32)

        lax.fori_loop(0, table.shape[1], take, jnp.int32(0))
    for i in range(7):
        pltpu.make_async_copy(outs[i], outs[i], sems.at[i]).wait()


def stage(where, slots, table, pool):
    piece = jax.ShapeDtypeStruct((pool.shape[0] // 4, pool.shape[1], pool.shape[2] // 2), BF16)
    return pl.pallas_call(
        stage_kernel,
        out_shape=[piece] * 7,
        in_specs=[SMEM, SMEM, SMEM, HBM],
        out_specs=[VMEM] * 7,
        scratch_shapes=[pltpu.SemaphoreType.DMA((7,))],
        compiler_params=params(8),
        cost_estimate=cost(0, 2 * 7 * 4 * 128 * 128 * 2),
    )(where, slots, table, pool)


def turned(x, cosine, sine):
    lane = lax.broadcasted_iota(jnp.int32, x.shape, 1)
    other = jnp.where(lane % HD < HD // 2, pltpu.roll(x, 128 - HD // 2, 1), pltpu.roll(x, HD // 2, 1))
    return x * cosine + other * sine


def first_kernel(where, slots, lengths, frequency, x, wq, wkv, acc_q, acc_kv, cosine, sine):
    rows, feats = x.shape
    here = pl.ds(pl.multiple_of(where[2] * feats, feats), feats)
    acc_q[...] = jnp.dot(x[...], wq[here], preferred_element_type=F32)
    acc_kv[...] = jnp.dot(x[...], wkv[here], preferred_element_type=F32)
    start = lengths[slots[where[0]]] + where[1] * rows
    position = (start + lax.broadcasted_iota(jnp.int32, (rows, 128), 0)).astype(F32)
    angles = position * frequency[0:1, :]
    lane = lax.broadcasted_iota(jnp.int32, (rows, 128), 1)
    cosine[...] = jnp.cos(angles)
    sine[...] = jnp.where(lane % HD < HD // 2, -1.0, 1.0) * jnp.sin(angles)


def first_project(where, slots, lengths, frequency, x, wq, wkv):
    rows, feats = x.shape
    table = jax.ShapeDtypeStruct((rows, 128), F32)
    return pl.pallas_call(
        first_kernel,
        out_shape=[
            jax.ShapeDtypeStruct((rows, wq.shape[1]), F32),
            jax.ShapeDtypeStruct((rows, wkv.shape[1]), F32),
            table,
            table,
        ],
        in_specs=[SMEM] * 3 + [VMEM] * 4,
        out_specs=[VMEM] * 4,
        compiler_params=params(20),
        cost_estimate=cost(2 * rows * feats * 1280, feats * 1280 * 2),
    )(where, slots, lengths, frequency, x, wq, wkv)


def second_kernel(where, x, wq, wkv, acc_q, acc_kv, cosine, sine, q, kept, sent):
    feats = x.shape[1]
    here = pl.ds(pl.multiple_of((1 - where[2]) * feats, feats), feats)
    keys = where[2] == 0
    cos_all, sin_all = cosine[...], sine[...]
    fresh = acc_kv[...] + jnp.dot(x[...], wkv[here], preferred_element_type=F32)
    cos_kv = jnp.where(keys, cos_all, 1.0)
    sin_kv = jnp.where(keys, sin_all, 0.0)
    low = turned(fresh[:, :128], cos_kv, sin_kv).astype(BF16)
    high = turned(fresh[:, 128:], cos_kv, sin_kv).astype(BF16)
    kept[...] = jnp.where(keys, low, high)
    sent[...] = jnp.where(keys, high, low)
    scale = HD**-0.5 * LOG2E
    tile = 256
    for c in range(0, q.shape[1], tile):
        lin = acc_q[:, c : c + tile] + jnp.dot(
            x[...], wq[here, c : c + tile], preferred_element_type=F32
        )
        for e in range(0, tile, 128):
            q[:, c + e : c + e + 128] = (
                turned(lin[:, e : e + 128], cos_all, sin_all) * scale
            ).astype(BF16)


def second_project(where, x, wq, wkv, acc_q, acc_kv, cosine, sine):
    rows, feats = x.shape
    piece = jax.ShapeDtypeStruct((rows, wkv.shape[1] // 2), BF16)
    return pl.pallas_call(
        second_kernel,
        out_shape=[jax.ShapeDtypeStruct((rows, wq.shape[1]), BF16), piece, piece],
        in_specs=[SMEM] + [VMEM] * 7,
        out_specs=[VMEM] * 3,
        compiler_params=params(20),
        cost_estimate=cost(2 * rows * feats * 1280, feats * 1280 * 2),
    )(where, x, wq, wkv, acc_q, acc_kv, cosine, sine)


def attend_kernel(
    where, slots, table, lengths, q, pool, own1, own2, own3, oth0, oth1, oth2, oth3,
    kept, got, z1, z2, z3, out, flow, rank, kv, keys, values, sem
):
    group, seq, tensor = where[0], where[1], where[2]
    pages = pool.shape[0]
    window_pages = table.shape[1]
    request = slots[group]
    rows = q.shape[0]
    per = rows // PAGE
    blocks = kv.shape[1] // PAGE
    half = pool.shape[2] // 2
    mine = pl.ds(pl.multiple_of(tensor * half, half), half)
    owns = (None, own1, own2, own3)
    others = (oth0, oth1, oth2, oth3)

    def note(w, counts):
        came = table[request, w] // pages ^ group
        place = jnp.int32(0)
        for d in range(4):
            place = jnp.where(came == d, counts[d], place)
        flow[w] = came
        rank[w] = place
        return tuple(counts[d] + (came == d).astype(jnp.int32) for d in range(4))

    lax.fori_loop(0, window_pages, note, (jnp.int32(0),) * 4)

    def fetch(n, _):
        block = seq * per + n
        here = pl.ds(pl.multiple_of(n * PAGE, PAGE), PAGE)

        def bring(own, other):
            pltpu.make_async_copy(own, kv.at[tensor, here], sem).start()
            pltpu.make_async_copy(other, kv.at[1 - tensor, here], sem).start()

        @pl.when(block < window_pages)
        def _():
            for d in range(4):

                @pl.when(flow[block] == d)
                def _(d=d):
                    at = rank[block]
                    if d:
                        bring(owns[d].at[at], others[d].at[at])
                    else:
                        bring(pool.at[table[request, block] % pages, :, mine], others[0].at[at])

        @pl.when(block >= window_pages)
        def _():
            fresh = block - window_pages
            away = fresh // per ^ seq
            part = pl.ds(pl.multiple_of(fresh % per * PAGE, PAGE), PAGE)

            @pl.when(away == 0)
            def _():
                bring(kept.at[part], got.at[part])

            for d, z in ((1, z1), (2, z2), (3, z3)):

                @pl.when(away == d)
                def _(z=z):
                    bring(z.at[0, part], z.at[1, part])

        return 0

    lax.fori_loop(0, blocks, fetch, 0)
    pltpu.make_async_copy(kv, kv, sem).wait()

    lane = lax.broadcasted_iota(jnp.int32, (PAGE, 2 * HD), 1)
    low = lane < HD
    first = lengths[request] - WINDOW + seq * rows

    def prepare(n, _):
        here = pl.ds(pl.multiple_of(n * PAGE, PAGE), PAGE)
        bias = jnp.where(first + n * PAGE >= 0, 0.0, MASKED)
        k = kv[0, here].astype(F32)
        v = kv[1, here].astype(F32)
        kr = pltpu.roll(k, HD, 1)
        vr = pltpu.roll(v, HD, 1)
        even = jnp.where(lane == HD, bias, 0.0)
        odd = jnp.where(lane == 0, bias, 0.0)
        keys[0, 0, here] = jnp.where(low, k, even).astype(BF16)
        keys[0, 1, here] = jnp.where(low, odd, kr).astype(BF16)
        keys[1, 0, here] = jnp.where(low, kr, even).astype(BF16)
        keys[1, 1, here] = jnp.where(low, odd, k).astype(BF16)
        values[0, 0, here] = jnp.where(low, v, 1.0).astype(BF16)
        values[0, 1, here] = jnp.where(low, 1.0, vr).astype(BF16)
        values[1, 0, here] = jnp.where(low, vr, 1.0).astype(BF16)
        values[1, 1, here] = jnp.where(low, 1.0, v).astype(BF16)
        return 0

    lax.fori_loop(0, blocks, prepare, 0)

    qlane = lax.broadcasted_iota(jnp.int32, (rows, 2 * HD), 1)
    qlow = qlane < HD
    mark_even = jnp.where(qlane == HD, 1.0, 0.0).astype(BF16)
    mark_odd = jnp.where(qlane == 0, 1.0, 0.0).astype(BF16)
    stack = 2
    query_at = lax.broadcasted_iota(jnp.int32, (stack * rows, rows), 0) % rows
    key_at = lax.broadcasted_iota(jnp.int32, (stack * rows, rows), 1)

    def scores(qs, ks):
        s = lax.dot_general(qs, ks, (((1,), (1,)), ((), ())), preferred_element_type=F32)
        return jnp.concatenate(
            [
                jnp.where(key_at > query_at, s[:, :rows], MASKED),
                s[:, rows:-rows],
                jnp.where(key_at <= query_at, s[:, -rows:], MASKED),
            ],
            axis=1,
        )

    def weigh(s):
        return jnp.exp2(s - jnp.max(s, axis=1, keepdims=True)).astype(BF16)

    def heads(i, _):
        kv_head = i // (4 // stack)
        tiles = [
            q[:, pl.ds(pl.multiple_of((i * stack + j) * 128, 128), 128)] for j in range(stack)
        ]
        q_even = jnp.concatenate([jnp.where(qlow, x, mark_even) for x in tiles], axis=0)
        q_odd = jnp.concatenate([jnp.where(qlow, mark_odd, x) for x in tiles], axis=0)
        s_even = scores(q_even, keys[kv_head, 0])
        s_odd = scores(q_odd, keys[kv_head, 1])
        p_even = weigh(s_even)
        p_odd = weigh(s_odd)
        o_even = jnp.dot(p_even, values[kv_head, 0], preferred_element_type=F32)
        o_odd = jnp.dot(p_odd, values[kv_head, 1], preferred_element_type=F32)
        for j in range(stack):
            a = o_even[j * rows : (j + 1) * rows]
            b = o_odd[j * rows : (j + 1) * rows]
            done = jnp.where(qlow, a / pltpu.roll(a, HD, 1), b / pltpu.roll(b, HD, 1))
            out[:, pl.ds(pl.multiple_of((i * stack + j) * 128, 128), 128)] = done.astype(BF16)
        return 0

    lax.fori_loop(0, q.shape[1] // 128 // stack, heads, 0)


def attend_all(where, slots, table, lengths, q, pool, owns, others, kept, got, zs):
    rows = q.shape[0]
    span = WINDOW + rows
    return pl.pallas_call(
        attend_kernel,
        out_shape=jax.ShapeDtypeStruct(q.shape, BF16),
        in_specs=[SMEM] * 4 + [VMEM] + [HBM] * 13,
        out_specs=VMEM,
        scratch_shapes=[
            pltpu.SMEM((table.shape[1],), jnp.int32),
            pltpu.SMEM((table.shape[1],), jnp.int32),
            pltpu.VMEM((2, span, 2 * HD), BF16),
            pltpu.VMEM((2, 2, span, 2 * HD), BF16),
            pltpu.VMEM((2, 2, span, 2 * HD), BF16),
            pltpu.SemaphoreType.DMA,
        ],
        compiler_params=params(36),
        cost_estimate=cost(4 * rows * span * 2048, 4 * span * 128),
    )(where, slots, table, lengths, q, pool, *owns, *others, kept, got, *zs)


def out_kernel(where, x, w, o, *, mine):
    cols = o.shape[1]
    side = where[2] if mine else 1 - where[2]
    here = pl.ds(pl.multiple_of(side * cols, cols), cols)
    o[...] = jnp.dot(x[...], w[:, here], preferred_element_type=F32).astype(BF16)


def out_project(where, x, w, mine):
    rows, depth = x.shape
    cols = w.shape[1] // 2
    return pl.pallas_call(
        functools.partial(out_kernel, mine=mine),
        out_shape=jax.ShapeDtypeStruct((rows, cols), BF16),
        in_specs=[SMEM, VMEM, VMEM],
        out_specs=VMEM,
        compiler_params=params(16),
        cost_estimate=cost(2 * rows * depth * cols, 2 * depth * cols),
    )(where, x, w)


def add_kernel(a, b, o):
    o[...] = (a[...].astype(F32) + b[...].astype(F32)).astype(BF16)


def added(a, b):
    return pl.pallas_call(
        add_kernel,
        out_shape=jax.ShapeDtypeStruct(a.shape, BF16),
        in_specs=[VMEM, VMEM],
        out_specs=VMEM,
        compiler_params=params(8),
    )(a, b)


def flipped(value, axes, count, bits):
    return lax.ppermute(value, axes, [(i, i ^ bits) for i in range(count)])


def shards_fast(
    span_tokens, q_weight, kv_weight, out_weight, kv_pool, cache_lengths, slot_requests, page_table
):
    group_id = lax.axis_index("group")
    seq_id = lax.axis_index("seq")
    tensor_id = lax.axis_index("tensor")
    where = jnp.stack([group_id, seq_id, tensor_id]).astype(jnp.int32)
    mine = span_tokens[0]
    rows = mine.shape[0]
    theirs = flipped(mine, "tensor", 2, 1)
    pieces = stage(where, slot_requests, page_table, kv_pool)
    others = [flipped(pieces[d], ("group", "tensor"), 8, 2 * d + 1) for d in range(4)]
    owns = [flipped(pieces[3 + d], "group", 4, d) for d in range(1, 4)]
    half_dim = HD // 2
    lane = jnp.arange(128, dtype=jnp.int32) % half_dim
    frequency = jnp.power(jnp.float32(10000.0), -lane.astype(F32) / half_dim)
    frequency = jnp.broadcast_to(frequency[None, :], (8, 128))
    acc_q, acc_kv, cosine, sine = first_project(
        where, slot_requests, cache_lengths, frequency, mine, q_weight, kv_weight
    )
    q, kept, sent = second_project(
        where, theirs, q_weight, kv_weight, acc_q, acc_kv, cosine, sine
    )
    got = flipped(sent, "tensor", 2, 1)
    fresh = jnp.stack([kept, got])
    zs = [flipped(fresh, "seq", 4, d) for d in range(1, 4)]
    heads = attend_all(
        where, slot_requests, page_table, cache_lengths, q, kv_pool, owns, others, kept, got, zs
    )
    away = flipped(out_project(where, heads, out_weight, False), "tensor", 2, 1)
    home = out_project(where, heads, out_weight, True)
    return added(home, away)[None]


def solution(mesh):
    sizes = tuple(mesh.shape[a] for a in ("group", "seq", "tensor"))
    body = shards_fast if sizes == (4, 4, 2) else shards
    placed = (
        P("group", "seq", "tensor"),
        P(None, "tensor"),
        P(None, "tensor"),
        P("tensor", None),
        P("group", None, "tensor"),
        P(),
        P(),
        P(),
    )
    return jax.shard_map(
        body, mesh=mesh, in_specs=placed, out_specs=P("group", "seq", "tensor"), check_vma=False
    )
```

```python
import functools

import jax
import jax.numpy as jnp
from jax import lax
from jax.experimental import pallas as pl
from jax.experimental.pallas import tpu as pltpu
from jax.sharding import PartitionSpec as P

HD = 64
KVH = 4
WINDOW = 2048
PAGE = 128


def shifted(block, axis, distance):
    devices = range(lax.axis_size(axis))
    route = [(i - distance, i) for i in devices if i - distance in devices]
    return lax.ppermute(block, axis, route)


def swapped(value, axis, stride):
    return lax.ppermute(value, axis, [(i, i ^ 1 << stride) for i in range(lax.axis_size(axis))])


def rotate(values, positions):
    half_dim = HD // 2
    frequency = jnp.power(jnp.float32(10000.0), -jnp.arange(half_dim, dtype=jnp.float32) / half_dim)
    angles = positions.astype(jnp.float32)[:, None] * frequency[None, :]
    cosine = jnp.cos(angles)[:, None, :]
    sine_part = jnp.sin(angles)[:, None, :]
    front_half = values[..., :half_dim]
    back_half = values[..., half_dim:]
    return jnp.concatenate(
        [front_half * cosine - back_half * sine_part, back_half * cosine + front_half * sine_part],
        axis=-1,
    )


def attend(block_q, block_k, block_v, base_pos):
    query_count = block_q.shape[0]
    key_count = block_k.shape[0]
    scores = jnp.einsum(
        "tkgd,nkd->kgtn", block_q, block_k, preferred_element_type=jnp.float32
    ) * HD ** (-0.5)
    query_at = jnp.arange(query_count, dtype=jnp.int32)[:, None]
    key_at = jnp.arange(key_count, dtype=jnp.int32)[None, :]
    allowed = (key_at > query_at) & (key_at <= query_at + WINDOW) & (base_pos + key_at >= 0)
    masked = jnp.where(allowed, scores, jnp.float32(-1e30))
    row_top = jnp.max(masked, axis=-1, keepdims=True)
    weights = jnp.where(allowed, jnp.exp(masked - row_top), jnp.float32(0.0))
    row_total = jnp.sum(weights, axis=-1)
    rounded = weights.astype(jnp.bfloat16)
    mixed_rows = jnp.einsum("kgtn,nkd->tkgd", rounded, block_v, preferred_element_type=jnp.float32)
    mixed_rows = mixed_rows / jnp.transpose(row_total, (2, 0, 1))[..., None]
    return mixed_rows.astype(jnp.bfloat16).reshape(query_count, -1)


def shards(
    span_tokens, q_weight, kv_weight, out_weight, kv_pool, cache_lengths, slot_requests, page_table
):
    groups = lax.axis_size("group")
    seq_count = lax.axis_size("seq")
    tensor_count = lax.axis_size("tensor")
    group_id = lax.axis_index("group")
    seq_id = lax.axis_index("seq")
    tensor_id = lax.axis_index("tensor")
    local_reqs, seg_len, feat_local = span_tokens.shape
    head_cols = q_weight.shape[1]
    kv_cols = kv_weight.shape[1]
    local_heads = head_cols // HD
    group_heads = kv_cols // HD
    kv_local = max(1, KVH // tensor_count)
    per_kv = local_heads // kv_local
    head_first = tensor_id * KVH // tensor_count % group_heads
    holds_keys = tensor_id % 2 == 0
    pool_rows = kv_pool.shape[0]
    capacity = pool_rows // groups
    row_count = local_reqs * seg_len
    my_slots = group_id * local_reqs + jnp.arange(local_reqs, dtype=jnp.int32)
    my_requests = slot_requests[my_slots]
    my_lengths = cache_lengths[my_requests]
    project_piece_rows = lax.all_gather(span_tokens, "tensor", axis=2, tiled=True)
    feat_width = project_piece_rows.shape[2]
    flat_rows = project_piece_rows.reshape(row_count, feat_width)
    query_lin = jnp.dot(flat_rows, q_weight, preferred_element_type=jnp.float32)
    fresh_lin = jnp.dot(flat_rows, kv_weight, preferred_element_type=jnp.float32)
    positions = (
        my_lengths[:, None] + seq_id * seg_len + jnp.arange(seg_len, dtype=jnp.int32)[None, :]
    )
    queries = jax.vmap(rotate)(query_lin.reshape(local_reqs, seg_len, local_heads, HD), positions)
    queries = queries.astype(jnp.bfloat16).reshape(local_reqs, seg_len, kv_local, per_kv, HD)
    fresh_heads = fresh_lin.reshape(local_reqs, seg_len, group_heads, HD)
    rotated = jax.vmap(rotate)(fresh_heads, positions)
    span_kv = (
        jnp.where(holds_keys, rotated, fresh_heads)
        .astype(jnp.bfloat16)
        .reshape(local_reqs, seg_len, kv_cols)
    )
    all_ids = page_table[slot_requests]
    owned_here = all_ids // pool_rows == group_id
    slot_rank = jnp.cumsum(owned_here.astype(jnp.int32), axis=1) - 1
    local_rows = all_ids - group_id * pool_rows
    chosen = owned_here[:, :, None] & (
        slot_rank[:, :, None] == jnp.arange(capacity, dtype=jnp.int32)[None, None, :]
    )
    wanted = jnp.sum(jnp.where(chosen, local_rows[:, :, None], 0), axis=1)
    my_ids = page_table[my_requests].reshape(-1)
    my_owner = my_ids // pool_rows
    onehot = (my_owner[:, None] == jnp.arange(groups, dtype=jnp.int32)[None, :]).astype(jnp.int32)
    arrival = jnp.sum((jnp.cumsum(onehot, axis=0) - 1) * onehot, axis=1)
    arrived_row = my_owner * capacity + arrival
    outgoing = kv_pool[wanted]
    arrived = lax.all_to_all(outgoing, "group", split_axis=0, concat_axis=0, tiled=True)
    cached = arrived.reshape(groups * capacity, PAGE, kv_cols)[arrived_row]
    cached = cached.reshape(local_reqs, WINDOW, kv_cols)
    span_all = jnp.zeros((local_reqs, seg_len * seq_count, kv_cols), jnp.bfloat16)
    for back_step in range(seq_count - 1, -1, -1):
        piece_rows = span_kv if back_step == 0 else shifted(span_kv, "seq", back_step)
        span_all = lax.dynamic_update_slice_in_dim(
            span_all, piece_rows, (seq_id - back_step) * seg_len, 1
        )
    joined = jnp.concatenate([cached, span_all], axis=1)
    visible = lax.dynamic_slice_in_dim(joined, seq_id * seg_len, WINDOW + seg_len, 1)
    partner_rows = swapped(visible, "tensor", 0)
    key_all = jnp.where(holds_keys, visible, partner_rows).reshape(
        local_reqs, WINDOW + seg_len, group_heads, HD
    )
    value_all = jnp.where(holds_keys, partner_rows, visible).reshape(
        local_reqs, WINDOW + seg_len, group_heads, HD
    )
    key_rows = lax.dynamic_slice_in_dim(key_all, head_first, kv_local, 2)
    value_rows = lax.dynamic_slice_in_dim(value_all, head_first, kv_local, 2)
    block_len = min(128, seg_len)
    block_count = seg_len // block_len

    def per_request(request_items):
        request_q, request_k, request_v, length = request_items

        def per_block(block_index):
            first_row = block_index * block_len
            block_q = lax.dynamic_slice_in_dim(request_q, first_row, block_len, 0)
            block_k = lax.dynamic_slice_in_dim(request_k, first_row, WINDOW + block_len, 0)
            block_v = lax.dynamic_slice_in_dim(request_v, first_row, WINDOW + block_len, 0)
            return attend(block_q, block_k, block_v, length - WINDOW + seq_id * seg_len + first_row)

        return lax.map(per_block, jnp.arange(block_count, dtype=jnp.int32)).reshape(
            seg_len, head_cols
        )

    attended_heads = lax.map(per_request, (queries, key_rows, value_rows, my_lengths))
    flat_heads = attended_heads.reshape(row_count, head_cols)
    out_cols = out_weight.shape[1] // tensor_count
    summed = lax.psum_scatter(
        lax.dot_general(
            out_weight, flat_heads, (((0,), (1,)), ((), ())), preferred_element_type=jnp.float32
        ).astype(jnp.bfloat16),
        "tensor",
        scatter_dimension=0,
        tiled=True,
    ).astype(jnp.float32)
    result = summed.T
    return result.astype(jnp.bfloat16).reshape(local_reqs, seg_len, out_cols)


LOG2E = 1.4426950408889634
MASKED = -1e30
F32 = jnp.float32
BF16 = jnp.bfloat16
HBM = pl.BlockSpec(memory_space=pl.ANY)
VMEM = pl.BlockSpec(memory_space=pltpu.VMEM)
SMEM = pl.BlockSpec(memory_space=pltpu.SMEM)
GROUPS, SEQS, TENSORS = 4, 4, 2


def params(mebibytes):
    return pltpu.CompilerParams(vmem_limit_bytes=mebibytes * 2**20)


def cost(flops, moved):
    return pl.CostEstimate(flops=flops, bytes_accessed=moved, transcendentals=0)


class Info:
    def __init__(self, ref):
        self.ref = ref
        self.group, self.seq, self.tensor = ref[0], ref[1], ref[2]
        self.window_pages = (ref.shape[0] - 3 - 2 * GROUPS) // GROUPS

    def request(self, slot):
        return self.ref[3 + slot]

    def length(self, request):
        return self.ref[3 + GROUPS + request]

    def page(self, request, w):
        return self.ref[3 + 2 * GROUPS + request * self.window_pages + w]


def stage_kernel(info_ref, pool, *refs):
    outs, sems = refs[:7], refs[7]
    info = Info(info_ref)
    pages = pool.shape[0]
    half = pool.shape[2] // 2
    mine = pl.ds(pl.multiple_of(info.tensor * half, half), half)
    theirs = pl.ds(pl.multiple_of((1 - info.tensor) * half, half), half)
    for flip in (1, 2, 3, 0):
        request = info.request(info.group ^ flip)

        def take(w, rank, flip=flip, request=request):
            page = info.page(request, w)
            here = page // pages == info.group

            @pl.when(here)
            def _():
                row = page % pages
                pltpu.make_async_copy(
                    pool.at[row, :, theirs], outs[flip].at[rank], sems.at[flip]
                ).start()
                if flip:
                    pltpu.make_async_copy(
                        pool.at[row, :, mine], outs[3 + flip].at[rank], sems.at[3 + flip]
                    ).start()

            return rank + here.astype(jnp.int32)

        lax.fori_loop(0, info.window_pages, take, jnp.int32(0))
    for i in range(7):
        pltpu.make_async_copy(outs[i], outs[i], sems.at[i]).wait()


def stage(info, pool):
    piece = jax.ShapeDtypeStruct((pool.shape[0] // GROUPS, pool.shape[1], pool.shape[2] // 2), BF16)
    return pl.pallas_call(
        stage_kernel,
        out_shape=[piece] * 7,
        in_specs=[SMEM, HBM],
        out_specs=[VMEM] * 7,
        scratch_shapes=[pltpu.SemaphoreType.DMA((7,))],
        compiler_params=params(8),
        cost_estimate=cost(0, 2 * pool.size),
    )(info, pool)


def turned(x, cosine, sine):
    lane = lax.broadcasted_iota(jnp.int32, x.shape, 1)
    other = jnp.where(lane % HD < HD // 2, pltpu.roll(x, 128 - HD // 2, 1), pltpu.roll(x, HD // 2, 1))
    return x * cosine + other * sine


def first_kernel(info_ref, frequency, x, wq, wkv, acc_q, acc_kv, cosine, sine):
    info = Info(info_ref)
    rows, feats = x.shape
    here = pl.ds(pl.multiple_of(info.tensor * feats, feats), feats)
    acc_q[...] = jnp.dot(x[...], wq[here], preferred_element_type=F32)
    acc_kv[...] = jnp.dot(x[...], wkv[here], preferred_element_type=F32)
    start = info.length(info.request(info.group)) + info.seq * rows
    position = (start + lax.broadcasted_iota(jnp.int32, (rows, 128), 0)).astype(F32)
    angles = position * frequency[0:1, :]
    lane = lax.broadcasted_iota(jnp.int32, (rows, 128), 1)
    cosine[...] = jnp.cos(angles)
    sine[...] = jnp.where(lane % HD < HD // 2, -1.0, 1.0) * jnp.sin(angles)


def first_project(info, frequency, x, wq, wkv):
    rows, feats = x.shape
    table = jax.ShapeDtypeStruct((rows, 128), F32)
    return pl.pallas_call(
        first_kernel,
        out_shape=[
            jax.ShapeDtypeStruct((rows, wq.shape[1]), F32),
            jax.ShapeDtypeStruct((rows, wkv.shape[1]), F32),
            table,
            table,
        ],
        in_specs=[SMEM] + [VMEM] * 4,
        out_specs=[VMEM] * 4,
        compiler_params=params(20),
        cost_estimate=cost(2 * rows * feats * 1280, feats * 1280 * 2),
    )(info, frequency, x, wq, wkv)


def second_kernel(info_ref, x, wq, wkv, acc_q, acc_kv, cosine, sine, q, kept, sent):
    info = Info(info_ref)
    feats = x.shape[1]
    here = pl.ds(pl.multiple_of((1 - info.tensor) * feats, feats), feats)
    keys = info.tensor == 0
    cos_all, sin_all = cosine[...], sine[...]
    fresh = acc_kv[...] + jnp.dot(x[...], wkv[here], preferred_element_type=F32)
    cos_kv = jnp.where(keys, cos_all, 1.0)
    sin_kv = jnp.where(keys, sin_all, 0.0)
    low = turned(fresh[:, :128], cos_kv, sin_kv).astype(BF16)
    high = turned(fresh[:, 128:], cos_kv, sin_kv).astype(BF16)
    kept[...] = jnp.where(keys, low, high)
    sent[...] = jnp.where(keys, high, low)
    scale = HD**-0.5 * LOG2E
    tile = 256
    for c in range(0, q.shape[1], tile):
        lin = acc_q[:, c : c + tile] + jnp.dot(
            x[...], wq[here, c : c + tile], preferred_element_type=F32
        )
        for e in range(0, tile, 128):
            q[:, c + e : c + e + 128] = (
                turned(lin[:, e : e + 128], cos_all, sin_all) * scale
            ).astype(BF16)


def second_project(info, x, wq, wkv, acc_q, acc_kv, cosine, sine):
    rows, feats = x.shape
    piece = jax.ShapeDtypeStruct((rows, wkv.shape[1] // 2), BF16)
    return pl.pallas_call(
        second_kernel,
        out_shape=[jax.ShapeDtypeStruct((rows, wq.shape[1]), BF16), piece, piece],
        in_specs=[SMEM] + [VMEM] * 7,
        out_specs=[VMEM] * 3,
        compiler_params=params(20),
        cost_estimate=cost(2 * rows * feats * 1280, feats * 1280 * 2),
    )(info, x, wq, wkv, acc_q, acc_kv, cosine, sine)


def lane_low(rows):
    return lax.broadcasted_iota(jnp.int32, (rows, 2 * HD), 1) < HD


def widen(k, v, bias, keys, values, here):
    lane = lax.broadcasted_iota(jnp.int32, k.shape, 1)
    low = lane < HD
    kr = pltpu.roll(k, HD, 1)
    vr = pltpu.roll(v, HD, 1)
    even = jnp.where(lane == HD, bias, 0.0)
    odd = jnp.where(lane == 0, bias, 0.0)
    keys[0, 0, here] = jnp.where(low, k, even).astype(BF16)
    keys[0, 1, here] = jnp.where(low, odd, kr).astype(BF16)
    keys[1, 0, here] = jnp.where(low, kr, even).astype(BF16)
    keys[1, 1, here] = jnp.where(low, odd, k).astype(BF16)
    values[0, 0, here] = jnp.where(low, v, 1.0).astype(BF16)
    values[0, 1, here] = jnp.where(low, 1.0, vr).astype(BF16)
    values[1, 0, here] = jnp.where(low, vr, 1.0).astype(BF16)
    values[1, 1, here] = jnp.where(low, 1.0, v).astype(BF16)


def soft_heads(q, keys, values, count, masked, emit):
    rows = q.shape[0]
    stack = 2
    lane = lax.broadcasted_iota(jnp.int32, (rows, 2 * HD), 1)
    low = lane < HD
    mark_even = jnp.where(lane == HD, 1.0, 0.0).astype(BF16)
    mark_odd = jnp.where(lane == 0, 1.0, 0.0).astype(BF16)
    query_at = lax.broadcasted_iota(jnp.int32, (stack * rows, rows), 0) % rows
    key_at = lax.broadcasted_iota(jnp.int32, (stack * rows, rows), 1)

    def scores(qs, ks):
        s = lax.dot_general(qs, ks, (((1,), (1,)), ((), ())), preferred_element_type=F32)
        if not masked:
            return s
        return jnp.concatenate(
            [
                jnp.where(key_at <= query_at, s[:, :rows], MASKED),
                jnp.where(key_at > query_at, s[:, rows : 2 * rows], MASKED),
                s[:, 2 * rows :],
            ],
            axis=1,
        )

    def heads(i, _):
        kv_head = i // (4 // stack)
        spots = [pl.ds(pl.multiple_of((i * stack + j) * 128, 128), 128) for j in range(stack)]
        tiles = [q[:, spot] for spot in spots]
        q_even = jnp.concatenate([jnp.where(low, x, mark_even) for x in tiles], axis=0)
        q_odd = jnp.concatenate([jnp.where(low, mark_odd, x) for x in tiles], axis=0)
        s_even = scores(q_even, keys[kv_head, 0, :count])
        s_odd = scores(q_odd, keys[kv_head, 1, :count])
        m_even = jnp.max(s_even, axis=1, keepdims=True)
        m_odd = jnp.max(s_odd, axis=1, keepdims=True)
        p_even = jnp.exp2(s_even - m_even).astype(BF16)
        p_odd = jnp.exp2(s_odd - m_odd).astype(BF16)
        o_even = jnp.dot(p_even, values[kv_head, 0, :count], preferred_element_type=F32)
        o_odd = jnp.dot(p_odd, values[kv_head, 1, :count], preferred_element_type=F32)
        for j in range(stack):
            part = slice(j * rows, (j + 1) * rows)
            a, b = o_even[part], o_odd[part]
            total = jnp.where(low, a, b)
            weight = jnp.where(low, pltpu.roll(a, HD, 1), pltpu.roll(b, HD, 1))
            top = jnp.where(low, m_even[part], m_odd[part])
            emit(spots[j], total, weight, top)
        return 0

    lax.fori_loop(0, q.shape[1] // 128 // stack, heads, 0)


def near_kernel(
    info_ref, q, pool, own1, own2, own3, oth0, oth1, oth2, oth3, kept, got,
    total, weight, top, flow, rank, kv, keys, values, sem
):
    info = Info(info_ref)
    group, seq, tensor = info.group, info.seq, info.tensor
    pages = pool.shape[0]
    request = info.request(group)
    rows = q.shape[0]
    per = rows // PAGE
    blocks = kv.shape[1] // PAGE
    seen = blocks - seq * per
    half = pool.shape[2] // 2
    mine = pl.ds(pl.multiple_of(tensor * half, half), half)
    owns = (None, own1, own2, own3)
    others = (oth0, oth1, oth2, oth3)

    def note(w, counts):
        came = info.page(request, w) // pages ^ group
        place = jnp.int32(0)
        for d in range(4):
            place = jnp.where(came == d, counts[d], place)
        flow[w] = came
        rank[w] = place
        return tuple(counts[d] + (came == d).astype(jnp.int32) for d in range(4))

    lax.fori_loop(0, info.window_pages, note, (jnp.int32(0),) * 4)

    def bring(own, other, here):
        pltpu.make_async_copy(own, kv.at[tensor, here], sem).start()
        pltpu.make_async_copy(other, kv.at[1 - tensor, here], sem).start()

    bring(kept, got, pl.ds(0, rows))

    def fetch(n, _):
        here = pl.ds(pl.multiple_of(n * PAGE, PAGE), PAGE)
        w = n - per + seq * per
        for d in range(4):

            @pl.when(flow[w] == d)
            def _(d=d):
                at = rank[w]
                if d:
                    bring(owns[d].at[at], others[d].at[at], here)
                else:
                    bring(pool.at[info.page(request, w) % pages, :, mine], others[0].at[at], here)

        return 0

    lax.fori_loop(per, seen, fetch, 0)

    def settle(n, _):
        here = kv.at[:, pl.ds(pl.multiple_of(n * PAGE, PAGE), PAGE)]
        pltpu.make_async_copy(here, here, sem).wait()
        return 0

    lax.fori_loop(0, seen, settle, 0)
    first = info.length(request) - WINDOW + seq * rows

    def prepare(n, _):
        here = pl.ds(pl.multiple_of(n * PAGE, PAGE), PAGE)
        hidden = (n >= per) & (first + (n - per) * PAGE < 0)
        bias = jnp.where(hidden, MASKED, 0.0)
        widen(kv[0, here].astype(F32), kv[1, here].astype(F32), bias, keys, values, here)
        return 0

    lax.fori_loop(0, seen, prepare, 0)

    def emit(spot, o, l, m):
        total[:, spot] = o
        weight[:, spot] = l
        top[:, spot] = m

    for k in range(SEQS):

        @pl.when(seq == k)
        def _(k=k):
            soft_heads(q, keys, values, (blocks - k * per) * PAGE, True, emit)


def attend_near(info, q, pool, owns, others, kept, got):
    rows = q.shape[0]
    span = WINDOW + rows
    pages = pool.shape[0]
    state = jax.ShapeDtypeStruct(q.shape, F32)
    return pl.pallas_call(
        near_kernel,
        out_shape=[state] * 3,
        in_specs=[SMEM, VMEM] + [HBM] * 10,
        out_specs=[VMEM] * 3,
        scratch_shapes=[
            pltpu.SMEM((pages,), jnp.int32),
            pltpu.SMEM((pages,), jnp.int32),
            pltpu.VMEM((2, span, 2 * HD), BF16),
            pltpu.VMEM((2, 2, span, 2 * HD), BF16),
            pltpu.VMEM((2, 2, span, 2 * HD), BF16),
            pltpu.SemaphoreType.DMA,
        ],
        compiler_params=params(36),
        cost_estimate=cost(4 * rows * span * 2048, 4 * span * 128),
    )(info, q, pool, *owns, *others, kept, got)


def far_kernel(
    info_ref, q, total, weight, top, z1, z2, z3, w, heads_out, partial, keys, values
):
    info = Info(info_ref)
    rows = q.shape[0]
    seq = info.seq
    zs = (None, z1, z2, z3)

    for k in range(SEQS):

        @pl.when(seq == k)
        def _(k=k):
            if k == 0:
                heads_out[...] = (total[...] / weight[...]).astype(BF16)
                return
            for n in range(k):
                z = zs[n ^ k]
                here = slice(n * rows, (n + 1) * rows)
                a = z[0].astype(F32)
                b = z[1].astype(F32)
                is_key = info.tensor == 0
                widen(jnp.where(is_key, a, b), jnp.where(is_key, b, a), 0.0, keys, values, here)

            def emit(spot, o, l, m):
                before = top[:, spot]
                peak = jnp.maximum(before, m)
                a = jnp.exp2(before - peak)
                b = jnp.exp2(m - peak)
                done = (total[:, spot] * a + o * b) / (weight[:, spot] * a + l * b)
                heads_out[:, spot] = done.astype(BF16)

            soft_heads(q, keys, values, k * rows, False, emit)

    cols = partial.shape[1]
    here = pl.ds(pl.multiple_of((1 - info.tensor) * cols, cols), cols)
    partial[...] = jnp.dot(heads_out[...], w[:, here], preferred_element_type=F32).astype(BF16)


def attend_far(info, q, total, weight, top, zs, w):
    rows = q.shape[0]
    span = (SEQS - 1) * rows
    return pl.pallas_call(
        far_kernel,
        out_shape=[
            jax.ShapeDtypeStruct(q.shape, BF16),
            jax.ShapeDtypeStruct((rows, w.shape[1] // TENSORS), BF16),
        ],
        in_specs=[SMEM] + [VMEM] * 8,
        out_specs=[VMEM] * 2,
        scratch_shapes=[
            pltpu.VMEM((2, 2, span, 2 * HD), BF16),
            pltpu.VMEM((2, 2, span, 2 * HD), BF16),
        ],
        compiler_params=params(32),
        cost_estimate=cost(4 * rows * span * 1024 + 2 * rows * 1024 * 1024, 4 * span * 128),
    )(info, q, total, weight, top, *zs, w)


def home_kernel(info_ref, x, w, o):
    cols = o.shape[1]
    here = pl.ds(pl.multiple_of(Info(info_ref).tensor * cols, cols), cols)
    o[...] = jnp.dot(x[...], w[:, here], preferred_element_type=F32).astype(BF16)


def home_project(info, x, w):
    rows, depth = x.shape
    cols = w.shape[1] // TENSORS
    return pl.pallas_call(
        home_kernel,
        out_shape=jax.ShapeDtypeStruct((rows, cols), BF16),
        in_specs=[SMEM, VMEM, VMEM],
        out_specs=VMEM,
        compiler_params=params(16),
        cost_estimate=cost(2 * rows * depth * cols, 2 * depth * cols),
    )(info, x, w)


def add_kernel(a, b, o):
    o[...] = (a[...].astype(F32) + b[...].astype(F32)).astype(BF16)


def added(a, b):
    return pl.pallas_call(
        add_kernel,
        out_shape=jax.ShapeDtypeStruct(a.shape, BF16),
        in_specs=[VMEM, VMEM],
        out_specs=VMEM,
        compiler_params=params(8),
    )(a, b)


def flipped(value, axes, count, bits):
    return lax.ppermute(value, axes, [(i, i ^ bits) for i in range(count)])


def after(value, *others):
    return lax.optimization_barrier((value, *others))[0]


def shards_fast(
    span_tokens, q_weight, kv_weight, out_weight, kv_pool, cache_lengths, slot_requests, page_table
):
    group_id = lax.axis_index("group")
    seq_id = lax.axis_index("seq")
    tensor_id = lax.axis_index("tensor")
    info = jnp.concatenate(
        [
            jnp.stack([group_id, seq_id, tensor_id]).astype(jnp.int32),
            slot_requests,
            cache_lengths,
            page_table.reshape(-1),
        ]
    )
    mine = span_tokens[0]
    theirs = flipped(mine, "tensor", 2, 1)
    pieces = stage(info, kv_pool)
    own = [flipped(pieces[3 + d], "group", 4, d) for d in range(1, 4)]
    other = [flipped(pieces[d], ("group", "tensor"), 8, 2 * d + 1) for d in range(4)]
    half_dim = HD // 2
    lane = jnp.arange(128, dtype=jnp.int32) % half_dim
    frequency = jnp.power(jnp.float32(10000.0), -lane.astype(F32) / half_dim)
    frequency = jnp.broadcast_to(frequency[None, :], (8, 128))
    acc_q, acc_kv, cosine, sine = first_project(
        after(info, pieces[0]), frequency, mine, q_weight, kv_weight
    )
    q, kept, sent = second_project(
        info, theirs, q_weight, kv_weight, acc_q, acc_kv, cosine, sine
    )
    got = flipped(sent, "tensor", 2, 1)
    fresh = jnp.stack([kept, got])
    zs = [flipped(fresh, "seq", 4, d) for d in range(1, 4)]
    total, weight, top = attend_near(info, q, kv_pool, own, other, kept, got)
    heads, partial = attend_far(info, q, total, weight, top, zs, out_weight)
    away = flipped(partial, "tensor", 2, 1)
    home = home_project(info, heads, out_weight)
    return added(home, away)[None]


def solution(mesh):
    sizes = tuple(mesh.shape[a] for a in ("group", "seq", "tensor"))
    body = shards_fast if sizes == (GROUPS, SEQS, TENSORS) else shards
    placed = (
        P("group", "seq", "tensor"),
        P(None, "tensor"),
        P(None, "tensor"),
        P("tensor", None),
        P("group", None, "tensor"),
        P(),
        P(),
        P(),
    )
    return jax.shard_map(
        body, mesh=mesh, in_specs=placed, out_specs=P("group", "seq", "tensor"), check_vma=False
    )
```

```python
import functools

import jax
import jax.numpy as jnp
from jax import lax
from jax.experimental import pallas as pl
from jax.experimental.pallas import tpu as pltpu
from jax.sharding import PartitionSpec as P

HD = 64
KVH = 4
WINDOW = 2048
PAGE = 128


def shifted(block, axis, distance):
    devices = range(lax.axis_size(axis))
    route = [(i - distance, i) for i in devices if i - distance in devices]
    return lax.ppermute(block, axis, route)


def swapped(value, axis, stride):
    return lax.ppermute(value, axis, [(i, i ^ 1 << stride) for i in range(lax.axis_size(axis))])


def rotate(values, positions):
    half_dim = HD // 2
    frequency = jnp.power(jnp.float32(10000.0), -jnp.arange(half_dim, dtype=jnp.float32) / half_dim)
    angles = positions.astype(jnp.float32)[:, None] * frequency[None, :]
    cosine = jnp.cos(angles)[:, None, :]
    sine_part = jnp.sin(angles)[:, None, :]
    front_half = values[..., :half_dim]
    back_half = values[..., half_dim:]
    return jnp.concatenate(
        [front_half * cosine - back_half * sine_part, back_half * cosine + front_half * sine_part],
        axis=-1,
    )


def attend(block_q, block_k, block_v, base_pos):
    query_count = block_q.shape[0]
    key_count = block_k.shape[0]
    scores = jnp.einsum(
        "tkgd,nkd->kgtn", block_q, block_k, preferred_element_type=jnp.float32
    ) * HD ** (-0.5)
    query_at = jnp.arange(query_count, dtype=jnp.int32)[:, None]
    key_at = jnp.arange(key_count, dtype=jnp.int32)[None, :]
    allowed = (key_at > query_at) & (key_at <= query_at + WINDOW) & (base_pos + key_at >= 0)
    masked = jnp.where(allowed, scores, jnp.float32(-1e30))
    row_top = jnp.max(masked, axis=-1, keepdims=True)
    weights = jnp.where(allowed, jnp.exp(masked - row_top), jnp.float32(0.0))
    row_total = jnp.sum(weights, axis=-1)
    rounded = weights.astype(jnp.bfloat16)
    mixed_rows = jnp.einsum("kgtn,nkd->tkgd", rounded, block_v, preferred_element_type=jnp.float32)
    mixed_rows = mixed_rows / jnp.transpose(row_total, (2, 0, 1))[..., None]
    return mixed_rows.astype(jnp.bfloat16).reshape(query_count, -1)


def shards(
    span_tokens, q_weight, kv_weight, out_weight, kv_pool, cache_lengths, slot_requests, page_table
):
    groups = lax.axis_size("group")
    seq_count = lax.axis_size("seq")
    tensor_count = lax.axis_size("tensor")
    group_id = lax.axis_index("group")
    seq_id = lax.axis_index("seq")
    tensor_id = lax.axis_index("tensor")
    local_reqs, seg_len, feat_local = span_tokens.shape
    head_cols = q_weight.shape[1]
    kv_cols = kv_weight.shape[1]
    local_heads = head_cols // HD
    group_heads = kv_cols // HD
    kv_local = max(1, KVH // tensor_count)
    per_kv = local_heads // kv_local
    head_first = tensor_id * KVH // tensor_count % group_heads
    holds_keys = tensor_id % 2 == 0
    pool_rows = kv_pool.shape[0]
    capacity = pool_rows // groups
    row_count = local_reqs * seg_len
    my_slots = group_id * local_reqs + jnp.arange(local_reqs, dtype=jnp.int32)
    my_requests = slot_requests[my_slots]
    my_lengths = cache_lengths[my_requests]
    project_piece_rows = lax.all_gather(span_tokens, "tensor", axis=2, tiled=True)
    feat_width = project_piece_rows.shape[2]
    flat_rows = project_piece_rows.reshape(row_count, feat_width)
    query_lin = jnp.dot(flat_rows, q_weight, preferred_element_type=jnp.float32)
    fresh_lin = jnp.dot(flat_rows, kv_weight, preferred_element_type=jnp.float32)
    positions = (
        my_lengths[:, None] + seq_id * seg_len + jnp.arange(seg_len, dtype=jnp.int32)[None, :]
    )
    queries = jax.vmap(rotate)(query_lin.reshape(local_reqs, seg_len, local_heads, HD), positions)
    queries = queries.astype(jnp.bfloat16).reshape(local_reqs, seg_len, kv_local, per_kv, HD)
    fresh_heads = fresh_lin.reshape(local_reqs, seg_len, group_heads, HD)
    rotated = jax.vmap(rotate)(fresh_heads, positions)
    span_kv = (
        jnp.where(holds_keys, rotated, fresh_heads)
        .astype(jnp.bfloat16)
        .reshape(local_reqs, seg_len, kv_cols)
    )
    all_ids = page_table[slot_requests]
    owned_here = all_ids // pool_rows == group_id
    slot_rank = jnp.cumsum(owned_here.astype(jnp.int32), axis=1) - 1
    local_rows = all_ids - group_id * pool_rows
    chosen = owned_here[:, :, None] & (
        slot_rank[:, :, None] == jnp.arange(capacity, dtype=jnp.int32)[None, None, :]
    )
    wanted = jnp.sum(jnp.where(chosen, local_rows[:, :, None], 0), axis=1)
    my_ids = page_table[my_requests].reshape(-1)
    my_owner = my_ids // pool_rows
    onehot = (my_owner[:, None] == jnp.arange(groups, dtype=jnp.int32)[None, :]).astype(jnp.int32)
    arrival = jnp.sum((jnp.cumsum(onehot, axis=0) - 1) * onehot, axis=1)
    arrived_row = my_owner * capacity + arrival
    outgoing = kv_pool[wanted]
    arrived = lax.all_to_all(outgoing, "group", split_axis=0, concat_axis=0, tiled=True)
    cached = arrived.reshape(groups * capacity, PAGE, kv_cols)[arrived_row]
    cached = cached.reshape(local_reqs, WINDOW, kv_cols)
    span_all = jnp.zeros((local_reqs, seg_len * seq_count, kv_cols), jnp.bfloat16)
    for back_step in range(seq_count - 1, -1, -1):
        piece_rows = span_kv if back_step == 0 else shifted(span_kv, "seq", back_step)
        span_all = lax.dynamic_update_slice_in_dim(
            span_all, piece_rows, (seq_id - back_step) * seg_len, 1
        )
    joined = jnp.concatenate([cached, span_all], axis=1)
    visible = lax.dynamic_slice_in_dim(joined, seq_id * seg_len, WINDOW + seg_len, 1)
    partner_rows = swapped(visible, "tensor", 0)
    key_all = jnp.where(holds_keys, visible, partner_rows).reshape(
        local_reqs, WINDOW + seg_len, group_heads, HD
    )
    value_all = jnp.where(holds_keys, partner_rows, visible).reshape(
        local_reqs, WINDOW + seg_len, group_heads, HD
    )
    key_rows = lax.dynamic_slice_in_dim(key_all, head_first, kv_local, 2)
    value_rows = lax.dynamic_slice_in_dim(value_all, head_first, kv_local, 2)
    block_len = min(128, seg_len)
    block_count = seg_len // block_len

    def per_request(request_items):
        request_q, request_k, request_v, length = request_items

        def per_block(block_index):
            first_row = block_index * block_len
            block_q = lax.dynamic_slice_in_dim(request_q, first_row, block_len, 0)
            block_k = lax.dynamic_slice_in_dim(request_k, first_row, WINDOW + block_len, 0)
            block_v = lax.dynamic_slice_in_dim(request_v, first_row, WINDOW + block_len, 0)
            return attend(block_q, block_k, block_v, length - WINDOW + seq_id * seg_len + first_row)

        return lax.map(per_block, jnp.arange(block_count, dtype=jnp.int32)).reshape(
            seg_len, head_cols
        )

    attended_heads = lax.map(per_request, (queries, key_rows, value_rows, my_lengths))
    flat_heads = attended_heads.reshape(row_count, head_cols)
    out_cols = out_weight.shape[1] // tensor_count
    summed = lax.psum_scatter(
        lax.dot_general(
            out_weight, flat_heads, (((0,), (1,)), ((), ())), preferred_element_type=jnp.float32
        ).astype(jnp.bfloat16),
        "tensor",
        scatter_dimension=0,
        tiled=True,
    ).astype(jnp.float32)
    result = summed.T
    return result.astype(jnp.bfloat16).reshape(local_reqs, seg_len, out_cols)


LOG2E = 1.4426950408889634
MASKED = -1e30
F32 = jnp.float32
BF16 = jnp.bfloat16
HBM = pl.BlockSpec(memory_space=pl.ANY)
VMEM = pl.BlockSpec(memory_space=pltpu.VMEM)
SMEM = pl.BlockSpec(memory_space=pltpu.SMEM)
GROUPS, SEQS, TENSORS = 4, 4, 2


def params(mebibytes):
    return pltpu.CompilerParams(vmem_limit_bytes=mebibytes * 2**20)


def cost(flops, moved):
    return pl.CostEstimate(flops=flops, bytes_accessed=moved, transcendentals=0)


class Info:
    def __init__(self, ref):
        self.ref = ref
        self.group, self.seq, self.tensor = ref[0, 0], ref[0, 1], ref[0, 2]
        self.window_pages = ref.shape[1]

    def request(self, slot):
        return self.ref[0, 3 + slot]

    def length(self, request):
        return self.ref[0, 3 + GROUPS + request]

    def page(self, request, w):
        return self.ref[1 + request, w]


def stage_kernel(info_ref, pool, same, across, beyond, mate, sems):
    info = Info(info_ref)
    pages = pool.shape[0]
    capacity = pages // GROUPS
    half = pool.shape[2] // 2
    mine = pl.ds(pl.multiple_of(info.tensor * half, half), half)
    theirs = pl.ds(pl.multiple_of((1 - info.tensor) * half, half), half)
    spots = {
        1: ((mate, 0, 3), (mate, 3 * capacity, 3)),
        3: ((mate, capacity, 3), (mate, 2 * capacity, 3)),
        2: ((across, 0, 1), (beyond, 0, 2)),
        0: ((same, 0, 0), None),
    }
    for flip, (other, own) in spots.items():
        request = info.request(info.group ^ flip)

        def take(w, rank):
            page = info.page(request, w)
            here = page // pages == info.group

            @pl.when(here)
            def _():
                row = page % pages
                for target, cols in ((other, theirs), (own, mine)):
                    if target is not None:
                        out, base, sem = target
                        pltpu.make_async_copy(
                            pool.at[row, :, cols], out.at[base + rank], sems.at[sem]
                        ).start()

            return rank + here.astype(jnp.int32)

        lax.fori_loop(0, info.window_pages, take, jnp.int32(0))
    for i, out in enumerate((same, across, beyond, mate)):
        pltpu.make_async_copy(out, out, sems.at[i]).wait()


def stage(info, pool):
    pages, page, cols = pool.shape
    single = jax.ShapeDtypeStruct((pages // GROUPS, page, cols // 2), BF16)
    whole = jax.ShapeDtypeStruct((pages, page, cols // 2), BF16)
    return pl.pallas_call(
        stage_kernel,
        out_shape=[single, single, single, whole],
        in_specs=[SMEM, HBM],
        out_specs=[VMEM] * 4,
        scratch_shapes=[pltpu.SemaphoreType.DMA((4,))],
        compiler_params=params(8),
        cost_estimate=cost(0, pool.shape[1]),
    )(info, pool)


def turned(x, cosine, sine):
    lane = lax.broadcasted_iota(jnp.int32, x.shape, 1)
    other = jnp.where(lane % HD < HD // 2, pltpu.roll(x, 128 - HD // 2, 1), pltpu.roll(x, HD // 2, 1))
    return x * cosine + other * sine


def first_kernel(info_ref, frequency, x, wq, wkv, acc_q, acc_kv, cosine, sine):
    info = Info(info_ref)
    rows, feats = x.shape
    here = pl.ds(pl.multiple_of(info.tensor * feats, feats), feats)
    acc_q[...] = jnp.dot(x[...], wq[here], preferred_element_type=F32)
    acc_kv[...] = jnp.dot(x[...], wkv[here], preferred_element_type=F32)
    start = info.length(info.request(info.group)) + info.seq * rows
    position = (start + lax.broadcasted_iota(jnp.int32, (rows, 128), 0)).astype(F32)
    angles = position * frequency[0:1, :]
    lane = lax.broadcasted_iota(jnp.int32, (rows, 128), 1)
    cosine[...] = jnp.cos(angles)
    sine[...] = jnp.where(lane % HD < HD // 2, -1.0, 1.0) * jnp.sin(angles)


def first_project(info, frequency, x, wq, wkv):
    rows, feats = x.shape
    table = jax.ShapeDtypeStruct((rows, 128), F32)
    return pl.pallas_call(
        first_kernel,
        out_shape=[
            jax.ShapeDtypeStruct((rows, wq.shape[1]), F32),
            jax.ShapeDtypeStruct((rows, wkv.shape[1]), F32),
            table,
            table,
        ],
        in_specs=[SMEM] + [VMEM] * 4,
        out_specs=[VMEM] * 4,
        compiler_params=params(20),
        cost_estimate=cost(rows * feats, rows * feats),
    )(info, frequency, x, wq, wkv)


def fresh_kernel(info_ref, x, wkv, acc_kv, cosine, sine, kept, sent):
    info = Info(info_ref)
    feats = x.shape[1]
    here = pl.ds(pl.multiple_of((1 - info.tensor) * feats, feats), feats)
    keys = info.tensor == 0
    fresh = acc_kv[...] + jnp.dot(x[...], wkv[here], preferred_element_type=F32)
    cos_kv = jnp.where(keys, cosine[...], 1.0)
    sin_kv = jnp.where(keys, sine[...], 0.0)
    low = turned(fresh[:, :128], cos_kv, sin_kv).astype(BF16)
    high = turned(fresh[:, 128:], cos_kv, sin_kv).astype(BF16)
    kept[...] = jnp.where(keys, low, high)
    sent[...] = jnp.where(keys, high, low)


def fresh_rows(info, x, wkv, acc_kv, cosine, sine):
    rows, feats = x.shape
    piece = jax.ShapeDtypeStruct((rows, wkv.shape[1] // 2), BF16)
    return pl.pallas_call(
        fresh_kernel,
        out_shape=[piece, piece],
        in_specs=[SMEM] + [VMEM] * 5,
        out_specs=[VMEM] * 2,
        compiler_params=params(12),
        cost_estimate=cost(rows * feats, rows * feats),
    )(info, x, wkv, acc_kv, cosine, sine)


def query_kernel(info_ref, x, wq, acc_q, cosine, sine, q):
    feats = x.shape[1]
    here = pl.ds(pl.multiple_of((1 - Info(info_ref).tensor) * feats, feats), feats)
    cos_all, sin_all = cosine[...], sine[...]
    scale = HD**-0.5 * LOG2E
    tile = 256
    for c in range(0, q.shape[1], tile):
        lin = acc_q[:, c : c + tile] + jnp.dot(
            x[...], wq[here, c : c + tile], preferred_element_type=F32
        )
        for e in range(0, tile, 128):
            q[:, c + e : c + e + 128] = (
                turned(lin[:, e : e + 128], cos_all, sin_all) * scale
            ).astype(BF16)


def query_rows(info, x, wq, acc_q, cosine, sine):
    rows, feats = x.shape
    return pl.pallas_call(
        query_kernel,
        out_shape=jax.ShapeDtypeStruct((rows, wq.shape[1]), BF16),
        in_specs=[SMEM] + [VMEM] * 5,
        out_specs=VMEM,
        compiler_params=params(16),
        cost_estimate=cost(rows * feats, rows * feats),
    )(info, x, wq, acc_q, cosine, sine)


def lane_low(rows):
    return lax.broadcasted_iota(jnp.int32, (rows, 2 * HD), 1) < HD


def widen(k, v, bias, keys, values, here):
    lane = lax.broadcasted_iota(jnp.int32, k.shape, 1)
    low = lane < HD
    kr = pltpu.roll(k, HD, 1)
    vr = pltpu.roll(v, HD, 1)
    even = jnp.where(lane == HD, bias, 0.0)
    odd = jnp.where(lane == 0, bias, 0.0)
    keys[0, 0, here] = jnp.where(low, k, even).astype(BF16)
    keys[0, 1, here] = jnp.where(low, odd, kr).astype(BF16)
    keys[1, 0, here] = jnp.where(low, kr, even).astype(BF16)
    keys[1, 1, here] = jnp.where(low, odd, k).astype(BF16)
    values[0, 0, here] = jnp.where(low, v, 1.0).astype(BF16)
    values[0, 1, here] = jnp.where(low, 1.0, vr).astype(BF16)
    values[1, 0, here] = jnp.where(low, vr, 1.0).astype(BF16)
    values[1, 1, here] = jnp.where(low, 1.0, v).astype(BF16)


def soft_heads(q, keys, values, count, masked, emit):
    rows = q.shape[0]
    stack = 2
    lane = lax.broadcasted_iota(jnp.int32, (rows, 2 * HD), 1)
    low = lane < HD
    mark_even = jnp.where(lane == HD, 1.0, 0.0).astype(BF16)
    mark_odd = jnp.where(lane == 0, 1.0, 0.0).astype(BF16)
    query_at = lax.broadcasted_iota(jnp.int32, (stack * rows, rows), 0) % rows
    key_at = lax.broadcasted_iota(jnp.int32, (stack * rows, rows), 1)

    def scores(qs, ks):
        s = lax.dot_general(qs, ks, (((1,), (1,)), ((), ())), preferred_element_type=F32)
        if not masked:
            return s
        return jnp.concatenate(
            [
                jnp.where(key_at <= query_at, s[:, :rows], MASKED),
                jnp.where(key_at > query_at, s[:, rows : 2 * rows], MASKED),
                s[:, 2 * rows :],
            ],
            axis=1,
        )

    def heads(i, _):
        kv_head = i // (4 // stack)
        spots = [pl.ds(pl.multiple_of((i * stack + j) * 128, 128), 128) for j in range(stack)]
        tiles = [q[:, spot] for spot in spots]
        q_even = jnp.concatenate([jnp.where(low, x, mark_even) for x in tiles], axis=0)
        q_odd = jnp.concatenate([jnp.where(low, mark_odd, x) for x in tiles], axis=0)
        s_even = scores(q_even, keys[kv_head, 0, :count])
        s_odd = scores(q_odd, keys[kv_head, 1, :count])
        m_even = jnp.max(s_even, axis=1, keepdims=True)
        m_odd = jnp.max(s_odd, axis=1, keepdims=True)
        p_even = jnp.exp2(s_even - m_even).astype(BF16)
        p_odd = jnp.exp2(s_odd - m_odd).astype(BF16)
        o_even = jnp.dot(p_even, values[kv_head, 0, :count], preferred_element_type=F32)
        o_odd = jnp.dot(p_odd, values[kv_head, 1, :count], preferred_element_type=F32)
        for j in range(stack):
            part = slice(j * rows, (j + 1) * rows)
            a, b = o_even[part], o_odd[part]
            total = jnp.where(low, a, b)
            weight = jnp.where(low, pltpu.roll(a, HD, 1), pltpu.roll(b, HD, 1))
            top = jnp.where(low, m_even[part], m_odd[part])
            emit(spots[j], total, weight, top)
        return 0

    lax.fori_loop(0, q.shape[1] // 128 // stack, heads, 0)


def near_kernel(
    info_ref, q, pool, same, across, beyond, mate, kept, got,
    total, weight, top, flow, rank, kv, keys, values, sem
):
    info = Info(info_ref)
    group, seq, tensor = info.group, info.seq, info.tensor
    pages = pool.shape[0]
    request = info.request(group)
    rows = q.shape[0]
    per = rows // PAGE
    blocks = kv.shape[1] // PAGE
    seen = blocks - seq * per
    half = pool.shape[2] // 2
    mine = pl.ds(pl.multiple_of(tensor * half, half), half)
    capacity = pages // GROUPS
    owns = (None, mate, beyond, beyond)
    own_bases = (0, 3 * capacity, 0, capacity)
    others = (same, same, across, across)
    other_bases = (0, capacity, 0, capacity)

    def note(w, counts):
        came = info.page(request, w) // pages ^ group
        place = jnp.int32(0)
        for d in range(4):
            place = jnp.where(came == d, counts[d], place)
        flow[w] = came
        rank[w] = place
        return tuple(counts[d] + (came == d).astype(jnp.int32) for d in range(4))

    lax.fori_loop(0, info.window_pages, note, (jnp.int32(0),) * 4)

    def bring(own, other, here):
        pltpu.make_async_copy(own, kv.at[tensor, here], sem).start()
        pltpu.make_async_copy(other, kv.at[1 - tensor, here], sem).start()

    bring(kept, got, pl.ds(0, rows))

    def fetch(n, _):
        here = pl.ds(pl.multiple_of(n * PAGE, PAGE), PAGE)
        w = n - per + seq * per
        for d in range(4):

            @pl.when(flow[w] == d)
            def _(d=d):
                other = others[d].at[other_bases[d] + rank[w]]
                if d:
                    bring(owns[d].at[own_bases[d] + rank[w]], other, here)
                else:
                    bring(pool.at[info.page(request, w) % pages, :, mine], other, here)

        return 0

    lax.fori_loop(per, seen, fetch, 0)

    def settle(n, _):
        here = kv.at[:, pl.ds(pl.multiple_of(n * PAGE, PAGE), PAGE)]
        pltpu.make_async_copy(here, here, sem).wait()
        return 0

    lax.fori_loop(0, seen, settle, 0)
    first = info.length(request) - WINDOW + seq * rows

    def prepare(n, _):
        here = pl.ds(pl.multiple_of(n * PAGE, PAGE), PAGE)
        hidden = (n >= per) & (first + (n - per) * PAGE < 0)
        bias = jnp.where(hidden, MASKED, 0.0)
        widen(kv[0, here].astype(F32), kv[1, here].astype(F32), bias, keys, values, here)
        return 0

    lax.fori_loop(0, seen, prepare, 0)

    def emit(spot, o, l, m):
        total[:, spot] = o
        weight[:, spot] = l
        top[:, spot] = m

    for k in range(SEQS):

        @pl.when(seq == k)
        def _(k=k):
            soft_heads(q, keys, values, (blocks - k * per) * PAGE, True, emit)


def attend_near(info, q, pool, pieces, kept, got):
    rows = q.shape[0]
    span = WINDOW + rows
    pages = pool.shape[0]
    state = jax.ShapeDtypeStruct(q.shape, F32)
    return pl.pallas_call(
        near_kernel,
        out_shape=[state] * 3,
        in_specs=[SMEM, VMEM] + [HBM] * 7,
        out_specs=[VMEM] * 3,
        scratch_shapes=[
            pltpu.SMEM((pages,), jnp.int32),
            pltpu.SMEM((pages,), jnp.int32),
            pltpu.VMEM((2, span, 2 * HD), BF16),
            pltpu.VMEM((2, 2, span, 2 * HD), BF16),
            pltpu.VMEM((2, 2, span, 2 * HD), BF16),
            pltpu.SemaphoreType.DMA,
        ],
        compiler_params=params(36),
        cost_estimate=cost(rows * span, 4 * span),
    )(info, q, pool, *pieces, kept, got)


def far_kernel(
    info_ref, q, total, weight, top, z1, z2, z3, w, heads_out, partial, keys, values
):
    info = Info(info_ref)
    rows = q.shape[0]
    seq = info.seq
    zs = (None, z1, z2, z3)

    for k in range(SEQS):

        @pl.when(seq == k)
        def _(k=k):
            if k == 0:
                heads_out[...] = (total[...] / weight[...]).astype(BF16)
                return
            for n in range(k):
                z = zs[n ^ k]
                here = slice(n * rows, (n + 1) * rows)
                a = z[0].astype(F32)
                b = z[1].astype(F32)
                is_key = info.tensor == 0
                widen(jnp.where(is_key, a, b), jnp.where(is_key, b, a), 0.0, keys, values, here)

            def emit(spot, o, l, m):
                before = top[:, spot]
                peak = jnp.maximum(before, m)
                a = jnp.exp2(before - peak)
                b = jnp.exp2(m - peak)
                done = (total[:, spot] * a + o * b) / (weight[:, spot] * a + l * b)
                heads_out[:, spot] = done.astype(BF16)

            soft_heads(q, keys, values, k * rows, False, emit)

    cols = partial.shape[1]
    here = pl.ds(pl.multiple_of((1 - info.tensor) * cols, cols), cols)
    partial[...] = jnp.dot(heads_out[...], w[:, here], preferred_element_type=F32).astype(BF16)


def attend_far(info, q, total, weight, top, zs, w):
    rows = q.shape[0]
    span = (SEQS - 1) * rows
    return pl.pallas_call(
        far_kernel,
        out_shape=[
            jax.ShapeDtypeStruct(q.shape, BF16),
            jax.ShapeDtypeStruct((rows, w.shape[1] // TENSORS), BF16),
        ],
        in_specs=[SMEM] + [VMEM] * 8,
        out_specs=[VMEM] * 2,
        scratch_shapes=[
            pltpu.VMEM((2, 2, span, 2 * HD), BF16),
            pltpu.VMEM((2, 2, span, 2 * HD), BF16),
        ],
        compiler_params=params(32),
        cost_estimate=cost(4 * rows * span * 1024 + 2 * rows * 1024 * 1024, 4 * span * 128),
    )(info, q, total, weight, top, *zs, w)


def home_kernel(info_ref, x, w, o):
    cols = o.shape[1]
    here = pl.ds(pl.multiple_of(Info(info_ref).tensor * cols, cols), cols)
    o[...] = jnp.dot(x[...], w[:, here], preferred_element_type=F32).astype(BF16)


def home_project(info, x, w):
    rows, depth = x.shape
    cols = w.shape[1] // TENSORS
    return pl.pallas_call(
        home_kernel,
        out_shape=jax.ShapeDtypeStruct((rows, cols), BF16),
        in_specs=[SMEM, VMEM, VMEM],
        out_specs=VMEM,
        compiler_params=params(16),
        cost_estimate=cost(2 * rows * depth * cols, 2 * depth * cols),
    )(info, x, w)


def add_kernel(a, b, o):
    o[...] = (a[...].astype(F32) + b[...].astype(F32)).astype(BF16)


def added(a, b):
    return pl.pallas_call(
        add_kernel,
        out_shape=jax.ShapeDtypeStruct(a.shape, BF16),
        in_specs=[VMEM, VMEM],
        out_specs=VMEM,
        compiler_params=params(8),
    )(a, b)


def flipped(value, axes, count, bits):
    return lax.ppermute(value, axes, [(i, i ^ bits) for i in range(count)])


def after(value, *others):
    return lax.optimization_barrier((value, *others))[0]


def shards_fast(
    span_tokens, q_weight, kv_weight, out_weight, kv_pool, cache_lengths, slot_requests, page_table
):
    group_id = lax.axis_index("group")
    seq_id = lax.axis_index("seq")
    tensor_id = lax.axis_index("tensor")
    place = jnp.stack([group_id, seq_id, tensor_id]).astype(jnp.int32)
    row = jnp.concatenate([place, slot_requests, cache_lengths])
    row = jnp.pad(row, (0, page_table.shape[1] - row.shape[0]))
    info = jnp.concatenate([row[None], page_table])
    mine = span_tokens[0]
    theirs = flipped(mine, "tensor", 2, 1)
    same, across, beyond, mate = stage(info, kv_pool)
    capacity = same.shape[0]
    mate = flipped(mate, "group", 4, 1)
    half_dim = HD // 2
    lane = jnp.arange(128, dtype=jnp.int32) % half_dim
    frequency = jnp.power(jnp.float32(10000.0), -lane.astype(F32) / half_dim)
    frequency = jnp.broadcast_to(frequency[None, :], (8, 128))
    acc_q, acc_kv, cosine, sine = first_project(
        after(info, same), frequency, mine, q_weight, kv_weight
    )
    kept, sent = fresh_rows(info, theirs, kv_weight, acc_kv, cosine, sine)
    got = flipped(sent, "tensor", 2, 1)
    mate, _ = lax.optimization_barrier((mate, sent))
    same = jnp.concatenate([same, mate[:capacity]])
    across = jnp.concatenate([across, mate[capacity : 2 * capacity]])
    beyond = jnp.concatenate([beyond, mate[2 * capacity : 3 * capacity]])
    info, same, across, beyond = lax.optimization_barrier((info, same, across, beyond))
    same = flipped(same, "tensor", 2, 1)
    across = flipped(across, ("group", "tensor"), 8, 5)
    beyond = flipped(beyond, "group", 4, 2)
    q = query_rows(info, theirs, q_weight, acc_q, cosine, sine)
    fresh = jnp.stack([kept, got])
    zs = [flipped(fresh, "seq", 4, d) for d in range(1, 4)]
    total, weight, top = attend_near(
        info, q, kv_pool, (same, across, beyond, mate), kept, got
    )
    heads, partial = attend_far(info, q, total, weight, top, zs, out_weight)
    away = flipped(partial, "tensor", 2, 1)
    home = home_project(info, heads, out_weight)
    return added(home, away)[None]


def solution(mesh):
    sizes = tuple(mesh.shape[a] for a in ("group", "seq", "tensor"))
    body = shards_fast if sizes == (GROUPS, SEQS, TENSORS) else shards
    placed = (
        P("group", "seq", "tensor"),
        P(None, "tensor"),
        P(None, "tensor"),
        P("tensor", None),
        P("group", None, "tensor"),
        P(),
        P(),
        P(),
    )
    return jax.shard_map(
        body, mesh=mesh, in_specs=placed, out_specs=P("group", "seq", "tensor"), check_vma=False
    )
```

```python
import functools

import jax
import jax.numpy as jnp
from jax import lax
from jax.experimental import pallas as pl
from jax.experimental.pallas import tpu as pltpu
from jax.sharding import PartitionSpec as P

HD = 64
KVH = 4
WINDOW = 2048
PAGE = 128


def shifted(block, axis, distance):
    devices = range(lax.axis_size(axis))
    route = [(i - distance, i) for i in devices if i - distance in devices]
    return lax.ppermute(block, axis, route)


def swapped(value, axis, stride):
    return lax.ppermute(value, axis, [(i, i ^ 1 << stride) for i in range(lax.axis_size(axis))])


def rotate(values, positions):
    half_dim = HD // 2
    frequency = jnp.power(jnp.float32(10000.0), -jnp.arange(half_dim, dtype=jnp.float32) / half_dim)
    angles = positions.astype(jnp.float32)[:, None] * frequency[None, :]
    cosine = jnp.cos(angles)[:, None, :]
    sine_part = jnp.sin(angles)[:, None, :]
    front_half = values[..., :half_dim]
    back_half = values[..., half_dim:]
    return jnp.concatenate(
        [front_half * cosine - back_half * sine_part, back_half * cosine + front_half * sine_part],
        axis=-1,
    )


def attend(block_q, block_k, block_v, base_pos):
    query_count = block_q.shape[0]
    key_count = block_k.shape[0]
    scores = jnp.einsum(
        "tkgd,nkd->kgtn", block_q, block_k, preferred_element_type=jnp.float32
    ) * HD ** (-0.5)
    query_at = jnp.arange(query_count, dtype=jnp.int32)[:, None]
    key_at = jnp.arange(key_count, dtype=jnp.int32)[None, :]
    allowed = (key_at > query_at) & (key_at <= query_at + WINDOW) & (base_pos + key_at >= 0)
    masked = jnp.where(allowed, scores, jnp.float32(-1e30))
    row_top = jnp.max(masked, axis=-1, keepdims=True)
    weights = jnp.where(allowed, jnp.exp(masked - row_top), jnp.float32(0.0))
    row_total = jnp.sum(weights, axis=-1)
    rounded = weights.astype(jnp.bfloat16)
    mixed_rows = jnp.einsum("kgtn,nkd->tkgd", rounded, block_v, preferred_element_type=jnp.float32)
    mixed_rows = mixed_rows / jnp.transpose(row_total, (2, 0, 1))[..., None]
    return mixed_rows.astype(jnp.bfloat16).reshape(query_count, -1)


def shards(
    span_tokens, q_weight, kv_weight, out_weight, kv_pool, cache_lengths, slot_requests, page_table
):
    groups = lax.axis_size("group")
    seq_count = lax.axis_size("seq")
    tensor_count = lax.axis_size("tensor")
    group_id = lax.axis_index("group")
    seq_id = lax.axis_index("seq")
    tensor_id = lax.axis_index("tensor")
    local_reqs, seg_len, feat_local = span_tokens.shape
    head_cols = q_weight.shape[1]
    kv_cols = kv_weight.shape[1]
    local_heads = head_cols // HD
    group_heads = kv_cols // HD
    kv_local = max(1, KVH // tensor_count)
    per_kv = local_heads // kv_local
    head_first = tensor_id * KVH // tensor_count % group_heads
    holds_keys = tensor_id % 2 == 0
    pool_rows = kv_pool.shape[0]
    capacity = pool_rows // groups
    row_count = local_reqs * seg_len
    my_slots = group_id * local_reqs + jnp.arange(local_reqs, dtype=jnp.int32)
    my_requests = slot_requests[my_slots]
    my_lengths = cache_lengths[my_requests]
    project_piece_rows = lax.all_gather(span_tokens, "tensor", axis=2, tiled=True)
    feat_width = project_piece_rows.shape[2]
    flat_rows = project_piece_rows.reshape(row_count, feat_width)
    query_lin = jnp.dot(flat_rows, q_weight, preferred_element_type=jnp.float32)
    fresh_lin = jnp.dot(flat_rows, kv_weight, preferred_element_type=jnp.float32)
    positions = (
        my_lengths[:, None] + seq_id * seg_len + jnp.arange(seg_len, dtype=jnp.int32)[None, :]
    )
    queries = jax.vmap(rotate)(query_lin.reshape(local_reqs, seg_len, local_heads, HD), positions)
    queries = queries.astype(jnp.bfloat16).reshape(local_reqs, seg_len, kv_local, per_kv, HD)
    fresh_heads = fresh_lin.reshape(local_reqs, seg_len, group_heads, HD)
    rotated = jax.vmap(rotate)(fresh_heads, positions)
    span_kv = (
        jnp.where(holds_keys, rotated, fresh_heads)
        .astype(jnp.bfloat16)
        .reshape(local_reqs, seg_len, kv_cols)
    )
    all_ids = page_table[slot_requests]
    owned_here = all_ids // pool_rows == group_id
    slot_rank = jnp.cumsum(owned_here.astype(jnp.int32), axis=1) - 1
    local_rows = all_ids - group_id * pool_rows
    chosen = owned_here[:, :, None] & (
        slot_rank[:, :, None] == jnp.arange(capacity, dtype=jnp.int32)[None, None, :]
    )
    wanted = jnp.sum(jnp.where(chosen, local_rows[:, :, None], 0), axis=1)
    my_ids = page_table[my_requests].reshape(-1)
    my_owner = my_ids // pool_rows
    onehot = (my_owner[:, None] == jnp.arange(groups, dtype=jnp.int32)[None, :]).astype(jnp.int32)
    arrival = jnp.sum((jnp.cumsum(onehot, axis=0) - 1) * onehot, axis=1)
    arrived_row = my_owner * capacity + arrival
    outgoing = kv_pool[wanted]
    arrived = lax.all_to_all(outgoing, "group", split_axis=0, concat_axis=0, tiled=True)
    cached = arrived.reshape(groups * capacity, PAGE, kv_cols)[arrived_row]
    cached = cached.reshape(local_reqs, WINDOW, kv_cols)
    span_all = jnp.zeros((local_reqs, seg_len * seq_count, kv_cols), jnp.bfloat16)
    for back_step in range(seq_count - 1, -1, -1):
        piece_rows = span_kv if back_step == 0 else shifted(span_kv, "seq", back_step)
        span_all = lax.dynamic_update_slice_in_dim(
            span_all, piece_rows, (seq_id - back_step) * seg_len, 1
        )
    joined = jnp.concatenate([cached, span_all], axis=1)
    visible = lax.dynamic_slice_in_dim(joined, seq_id * seg_len, WINDOW + seg_len, 1)
    partner_rows = swapped(visible, "tensor", 0)
    key_all = jnp.where(holds_keys, visible, partner_rows).reshape(
        local_reqs, WINDOW + seg_len, group_heads, HD
    )
    value_all = jnp.where(holds_keys, partner_rows, visible).reshape(
        local_reqs, WINDOW + seg_len, group_heads, HD
    )
    key_rows = lax.dynamic_slice_in_dim(key_all, head_first, kv_local, 2)
    value_rows = lax.dynamic_slice_in_dim(value_all, head_first, kv_local, 2)
    block_len = min(128, seg_len)
    block_count = seg_len // block_len

    def per_request(request_items):
        request_q, request_k, request_v, length = request_items

        def per_block(block_index):
            first_row = block_index * block_len
            block_q = lax.dynamic_slice_in_dim(request_q, first_row, block_len, 0)
            block_k = lax.dynamic_slice_in_dim(request_k, first_row, WINDOW + block_len, 0)
            block_v = lax.dynamic_slice_in_dim(request_v, first_row, WINDOW + block_len, 0)
            return attend(block_q, block_k, block_v, length - WINDOW + seq_id * seg_len + first_row)

        return lax.map(per_block, jnp.arange(block_count, dtype=jnp.int32)).reshape(
            seg_len, head_cols
        )

    attended_heads = lax.map(per_request, (queries, key_rows, value_rows, my_lengths))
    flat_heads = attended_heads.reshape(row_count, head_cols)
    out_cols = out_weight.shape[1] // tensor_count
    summed = lax.psum_scatter(
        lax.dot_general(
            out_weight, flat_heads, (((0,), (1,)), ((), ())), preferred_element_type=jnp.float32
        ).astype(jnp.bfloat16),
        "tensor",
        scatter_dimension=0,
        tiled=True,
    ).astype(jnp.float32)
    result = summed.T
    return result.astype(jnp.bfloat16).reshape(local_reqs, seg_len, out_cols)


LOG2E = 1.4426950408889634
MASKED = -1e30
F32 = jnp.float32
BF16 = jnp.bfloat16
HBM = pl.BlockSpec(memory_space=pl.ANY)
VMEM = pl.BlockSpec(memory_space=pltpu.VMEM)
SMEM = pl.BlockSpec(memory_space=pltpu.SMEM)
GROUPS, SEQS, TENSORS = 4, 4, 2


def params(mebibytes):
    return pltpu.CompilerParams(vmem_limit_bytes=mebibytes * 2**20)


def cost(flops, moved):
    return pl.CostEstimate(flops=flops, bytes_accessed=moved, transcendentals=0)


class Info:
    def __init__(self, ref):
        self.ref = ref
        self.group, self.seq, self.tensor = ref[0, 0], ref[0, 1], ref[0, 2]
        self.window_pages = ref.shape[1]

    def request(self, slot):
        return self.ref[0, 3 + slot]

    def length(self, request):
        return self.ref[0, 3 + GROUPS + request]

    def page(self, request, w):
        return self.ref[1 + request, w]


def stage_kernel(info_ref, pool, same, beyond, beside, across, diagonal, sems):
    info = Info(info_ref)
    pages = pool.shape[0]
    capacity = pages // GROUPS
    half = pool.shape[2] // 2
    mine = pl.ds(pl.multiple_of(info.tensor * half, half), half)
    theirs = pl.ds(pl.multiple_of((1 - info.tensor) * half, half), half)
    spots = {
        0: ((same, 0, 0), None),
        1: ((same, capacity, 0), (beside, 0, 2)),
        2: ((across, 0, 3), (beyond, 0, 1)),
        3: ((diagonal, 0, 4), (beyond, capacity, 1)),
    }
    for flip, (other, own) in spots.items():
        request = info.request(info.group ^ flip)

        def take(w, rank):
            page = info.page(request, w)
            here = page // pages == info.group

            @pl.when(here)
            def _():
                row = page % pages
                for target, cols in ((other, theirs), (own, mine)):
                    if target is not None:
                        out, base, sem = target
                        pltpu.make_async_copy(
                            pool.at[row, :, cols], out.at[base + rank], sems.at[sem]
                        ).start()

            return rank + here.astype(jnp.int32)

        lax.fori_loop(0, info.window_pages, take, jnp.int32(0))
    for i, out in enumerate((same, beyond, beside, across, diagonal)):
        pltpu.make_async_copy(out, out, sems.at[i]).wait()


def stage(info, pool):
    pages, page, cols = pool.shape
    single = jax.ShapeDtypeStruct((pages // GROUPS, page, cols // 2), BF16)
    double = jax.ShapeDtypeStruct((2 * pages // GROUPS, page, cols // 2), BF16)
    return pl.pallas_call(
        stage_kernel,
        out_shape=[double, double, single, single, single],
        in_specs=[SMEM, HBM],
        out_specs=[VMEM] * 5,
        scratch_shapes=[pltpu.SemaphoreType.DMA((5,))],
        compiler_params=params(8),
        cost_estimate=cost(0, page),
    )(info, pool)


def turned(x, cosine, sine):
    lane = lax.broadcasted_iota(jnp.int32, x.shape, 1)
    other = jnp.where(lane % HD < HD // 2, pltpu.roll(x, 128 - HD // 2, 1), pltpu.roll(x, HD // 2, 1))
    return x * cosine + other * sine


def first_kernel(info_ref, frequency, x, wq, wkv, acc_q, acc_kv, cosine, sine):
    info = Info(info_ref)
    rows, feats = x.shape
    here = pl.ds(pl.multiple_of(info.tensor * feats, feats), feats)
    acc_q[...] = jnp.dot(x[...], wq[here], preferred_element_type=F32)
    acc_kv[...] = jnp.dot(x[...], wkv[here], preferred_element_type=F32)
    start = info.length(info.request(info.group)) + info.seq * rows
    position = (start + lax.broadcasted_iota(jnp.int32, (rows, 128), 0)).astype(F32)
    angles = position * frequency[0:1, :]
    lane = lax.broadcasted_iota(jnp.int32, (rows, 128), 1)
    cosine[...] = jnp.cos(angles)
    sine[...] = jnp.where(lane % HD < HD // 2, -1.0, 1.0) * jnp.sin(angles)


def first_project(info, frequency, x, wq, wkv):
    rows, feats = x.shape
    table = jax.ShapeDtypeStruct((rows, 128), F32)
    return pl.pallas_call(
        first_kernel,
        out_shape=[
            jax.ShapeDtypeStruct((rows, wq.shape[1]), F32),
            jax.ShapeDtypeStruct((rows, wkv.shape[1]), F32),
            table,
            table,
        ],
        in_specs=[SMEM] + [VMEM] * 4,
        out_specs=[VMEM] * 4,
        compiler_params=params(20),
        cost_estimate=cost(rows * feats, rows * feats),
    )(info, frequency, x, wq, wkv)


def fresh_kernel(info_ref, x, wkv, acc_kv, cosine, sine, kept, sent):
    info = Info(info_ref)
    feats = x.shape[1]
    here = pl.ds(pl.multiple_of((1 - info.tensor) * feats, feats), feats)
    keys = info.tensor == 0
    fresh = acc_kv[...] + jnp.dot(x[...], wkv[here], preferred_element_type=F32)
    cos_kv = jnp.where(keys, cosine[...], 1.0)
    sin_kv = jnp.where(keys, sine[...], 0.0)
    low = turned(fresh[:, :128], cos_kv, sin_kv).astype(BF16)
    high = turned(fresh[:, 128:], cos_kv, sin_kv).astype(BF16)
    kept[...] = jnp.where(keys, low, high)
    sent[...] = jnp.where(keys, high, low)


def fresh_rows(info, x, wkv, acc_kv, cosine, sine):
    rows, feats = x.shape
    piece = jax.ShapeDtypeStruct((rows, wkv.shape[1] // 2), BF16)
    return pl.pallas_call(
        fresh_kernel,
        out_shape=[piece, piece],
        in_specs=[SMEM] + [VMEM] * 5,
        out_specs=[VMEM] * 2,
        compiler_params=params(12),
        cost_estimate=cost(2 * rows * feats * 2560, rows * feats),
    )(info, x, wkv, acc_kv, cosine, sine)


def query_kernel(info_ref, x, wq, acc_q, cosine, sine, q):
    feats = x.shape[1]
    here = pl.ds(pl.multiple_of((1 - Info(info_ref).tensor) * feats, feats), feats)
    cos_all, sin_all = cosine[...], sine[...]
    scale = HD**-0.5 * LOG2E
    tile = 256
    for c in range(0, q.shape[1], tile):
        lin = acc_q[:, c : c + tile] + jnp.dot(
            x[...], wq[here, c : c + tile], preferred_element_type=F32
        )
        for e in range(0, tile, 128):
            q[:, c + e : c + e + 128] = (
                turned(lin[:, e : e + 128], cos_all, sin_all) * scale
            ).astype(BF16)


def query_rows(info, x, wq, acc_q, cosine, sine):
    rows, feats = x.shape
    return pl.pallas_call(
        query_kernel,
        out_shape=jax.ShapeDtypeStruct((rows, wq.shape[1]), BF16),
        in_specs=[SMEM] + [VMEM] * 5,
        out_specs=VMEM,
        compiler_params=params(16),
        cost_estimate=cost(rows * feats, rows * feats),
    )(info, x, wq, acc_q, cosine, sine)


def lane_low(rows):
    return lax.broadcasted_iota(jnp.int32, (rows, 2 * HD), 1) < HD


def widen(k, v, bias, keys, values, here):
    lane = lax.broadcasted_iota(jnp.int32, k.shape, 1)
    low = lane < HD
    kr = pltpu.roll(k, HD, 1)
    vr = pltpu.roll(v, HD, 1)
    even = jnp.where(lane == HD, bias, 0.0)
    odd = jnp.where(lane == 0, bias, 0.0)
    keys[0, 0, here] = jnp.where(low, k, even).astype(BF16)
    keys[0, 1, here] = jnp.where(low, odd, kr).astype(BF16)
    keys[1, 0, here] = jnp.where(low, kr, even).astype(BF16)
    keys[1, 1, here] = jnp.where(low, odd, k).astype(BF16)
    values[0, 0, here] = jnp.where(low, v, 1.0).astype(BF16)
    values[0, 1, here] = jnp.where(low, 1.0, vr).astype(BF16)
    values[1, 0, here] = jnp.where(low, vr, 1.0).astype(BF16)
    values[1, 1, here] = jnp.where(low, 1.0, v).astype(BF16)


def soft_heads(q, keys, values, count, masked, emit):
    rows = q.shape[0]
    stack = 2
    lane = lax.broadcasted_iota(jnp.int32, (rows, 2 * HD), 1)
    low = lane < HD
    mark_even = jnp.where(lane == HD, 1.0, 0.0).astype(BF16)
    mark_odd = jnp.where(lane == 0, 1.0, 0.0).astype(BF16)
    query_at = lax.broadcasted_iota(jnp.int32, (stack * rows, rows), 0) % rows
    key_at = lax.broadcasted_iota(jnp.int32, (stack * rows, rows), 1)

    def scores(qs, ks):
        s = lax.dot_general(qs, ks, (((1,), (1,)), ((), ())), preferred_element_type=F32)
        if not masked:
            return s
        return jnp.concatenate(
            [
                jnp.where(key_at <= query_at, s[:, :rows], MASKED),
                jnp.where(key_at > query_at, s[:, rows : 2 * rows], MASKED),
                s[:, 2 * rows :],
            ],
            axis=1,
        )

    def heads(i, _):
        kv_head = i // (4 // stack)
        spots = [pl.ds(pl.multiple_of((i * stack + j) * 128, 128), 128) for j in range(stack)]
        tiles = [q[:, spot] for spot in spots]
        q_even = jnp.concatenate([jnp.where(low, x, mark_even) for x in tiles], axis=0)
        q_odd = jnp.concatenate([jnp.where(low, mark_odd, x) for x in tiles], axis=0)
        s_even = scores(q_even, keys[kv_head, 0, :count])
        s_odd = scores(q_odd, keys[kv_head, 1, :count])
        m_even = jnp.max(s_even, axis=1, keepdims=True)
        m_odd = jnp.max(s_odd, axis=1, keepdims=True)
        p_even = jnp.exp2(s_even - m_even).astype(BF16)
        p_odd = jnp.exp2(s_odd - m_odd).astype(BF16)
        o_even = jnp.dot(p_even, values[kv_head, 0, :count], preferred_element_type=F32)
        o_odd = jnp.dot(p_odd, values[kv_head, 1, :count], preferred_element_type=F32)
        for j in range(stack):
            part = slice(j * rows, (j + 1) * rows)
            a, b = o_even[part], o_odd[part]
            total = jnp.where(low, a, b)
            weight = jnp.where(low, pltpu.roll(a, HD, 1), pltpu.roll(b, HD, 1))
            top = jnp.where(low, m_even[part], m_odd[part])
            emit(spots[j], total, weight, top)
        return 0

    lax.fori_loop(0, q.shape[1] // 128 // stack, heads, 0)


def near_kernel(
    info_ref, q, pool, same, beyond, mate, across, diagonal, kept, got,
    total, weight, top, flow, rank, kv, keys, values, sem
):
    info = Info(info_ref)
    group, seq, tensor = info.group, info.seq, info.tensor
    pages = pool.shape[0]
    request = info.request(group)
    rows = q.shape[0]
    per = rows // PAGE
    blocks = kv.shape[1] // PAGE
    seen = blocks - seq * per
    half = pool.shape[2] // 2
    mine = pl.ds(pl.multiple_of(tensor * half, half), half)
    capacity = pages // GROUPS
    owns = (None, mate, beyond, mate)
    own_bases = (0, 0, 0, capacity)
    others = (same, mate, across, diagonal)
    other_bases = (0, 2 * capacity, 0, 0)

    def note(w, counts):
        came = info.page(request, w) // pages ^ group
        place = jnp.int32(0)
        for d in range(4):
            place = jnp.where(came == d, counts[d], place)
        flow[w] = came
        rank[w] = place
        return tuple(counts[d] + (came == d).astype(jnp.int32) for d in range(4))

    lax.fori_loop(0, info.window_pages, note, (jnp.int32(0),) * 4)

    def bring(own, other, here):
        pltpu.make_async_copy(own, kv.at[tensor, here], sem).start()
        pltpu.make_async_copy(other, kv.at[1 - tensor, here], sem).start()

    bring(kept, got, pl.ds(0, rows))

    def fetch(n, _):
        here = pl.ds(pl.multiple_of(n * PAGE, PAGE), PAGE)
        w = n - per + seq * per
        for d in range(4):

            @pl.when(flow[w] == d)
            def _(d=d):
                other = others[d].at[other_bases[d] + rank[w]]
                if d:
                    bring(owns[d].at[own_bases[d] + rank[w]], other, here)
                else:
                    bring(pool.at[info.page(request, w) % pages, :, mine], other, here)

        return 0

    lax.fori_loop(per, seen, fetch, 0)

    def settle(n, _):
        here = kv.at[:, pl.ds(pl.multiple_of(n * PAGE, PAGE), PAGE)]
        pltpu.make_async_copy(here, here, sem).wait()
        return 0

    lax.fori_loop(0, seen, settle, 0)
    first = info.length(request) - WINDOW + seq * rows

    def prepare(n, _):
        here = pl.ds(pl.multiple_of(n * PAGE, PAGE), PAGE)
        hidden = (n >= per) & (first + (n - per) * PAGE < 0)
        bias = jnp.where(hidden, MASKED, 0.0)
        widen(kv[0, here].astype(F32), kv[1, here].astype(F32), bias, keys, values, here)
        return 0

    lax.fori_loop(0, seen, prepare, 0)

    def emit(spot, o, l, m):
        total[:, spot] = o
        weight[:, spot] = l
        top[:, spot] = m

    for k in range(SEQS):

        @pl.when(seq == k)
        def _(k=k):
            soft_heads(q, keys, values, (blocks - k * per) * PAGE, True, emit)


def attend_near(info, q, pool, pieces, kept, got):
    rows = q.shape[0]
    span = WINDOW + rows
    pages = pool.shape[0]
    state = jax.ShapeDtypeStruct(q.shape, F32)
    return pl.pallas_call(
        near_kernel,
        out_shape=[state] * 3,
        in_specs=[SMEM, VMEM] + [HBM] * 8,
        out_specs=[VMEM] * 3,
        scratch_shapes=[
            pltpu.SMEM((pages,), jnp.int32),
            pltpu.SMEM((pages,), jnp.int32),
            pltpu.VMEM((2, span, 2 * HD), BF16),
            pltpu.VMEM((2, 2, span, 2 * HD), BF16),
            pltpu.VMEM((2, 2, span, 2 * HD), BF16),
            pltpu.SemaphoreType.DMA,
        ],
        compiler_params=params(36),
        cost_estimate=cost(rows * span, 4 * span),
    )(info, q, pool, *pieces, kept, got)


def far_kernel(
    info_ref, q, total, weight, top, z1, z2, z3, w, heads_out, partial, keys, values
):
    info = Info(info_ref)
    rows = q.shape[0]
    seq = info.seq
    zs = (None, z1, z2, z3)

    for k in range(SEQS):

        @pl.when(seq == k)
        def _(k=k):
            if k == 0:
                heads_out[...] = (total[...] / weight[...]).astype(BF16)
                return
            for n in range(k):
                z = zs[n ^ k]
                here = slice(n * rows, (n + 1) * rows)
                a = z[0].astype(F32)
                b = z[1].astype(F32)
                is_key = info.tensor == 0
                widen(jnp.where(is_key, a, b), jnp.where(is_key, b, a), 0.0, keys, values, here)

            def emit(spot, o, l, m):
                before = top[:, spot]
                peak = jnp.maximum(before, m)
                a = jnp.exp2(before - peak)
                b = jnp.exp2(m - peak)
                done = (total[:, spot] * a + o * b) / (weight[:, spot] * a + l * b)
                heads_out[:, spot] = done.astype(BF16)

            soft_heads(q, keys, values, k * rows, False, emit)

    cols = partial.shape[1]
    here = pl.ds(pl.multiple_of((1 - info.tensor) * cols, cols), cols)
    partial[...] = jnp.dot(heads_out[...], w[:, here], preferred_element_type=F32).astype(BF16)


def attend_far(info, q, total, weight, top, zs, w):
    rows = q.shape[0]
    span = (SEQS - 1) * rows
    return pl.pallas_call(
        far_kernel,
        out_shape=[
            jax.ShapeDtypeStruct(q.shape, BF16),
            jax.ShapeDtypeStruct((rows, w.shape[1] // TENSORS), BF16),
        ],
        in_specs=[SMEM] + [VMEM] * 8,
        out_specs=[VMEM] * 2,
        scratch_shapes=[
            pltpu.VMEM((2, 2, span, 2 * HD), BF16),
            pltpu.VMEM((2, 2, span, 2 * HD), BF16),
        ],
        compiler_params=params(32),
        cost_estimate=cost(4 * rows * span * 1024 + 2 * rows * 1024 * 1024, 4 * span * 128),
    )(info, q, total, weight, top, *zs, w)


def home_kernel(info_ref, x, w, o):
    cols = o.shape[1]
    here = pl.ds(pl.multiple_of(Info(info_ref).tensor * cols, cols), cols)
    o[...] = jnp.dot(x[...], w[:, here], preferred_element_type=F32).astype(BF16)


def home_project(info, x, w):
    rows, depth = x.shape
    cols = w.shape[1] // TENSORS
    return pl.pallas_call(
        home_kernel,
        out_shape=jax.ShapeDtypeStruct((rows, cols), BF16),
        in_specs=[SMEM, VMEM, VMEM],
        out_specs=VMEM,
        compiler_params=params(16),
        cost_estimate=cost(2 * rows * depth * cols, 2 * depth * cols),
    )(info, x, w)


def add_kernel(a, b, o):
    o[...] = (a[...].astype(F32) + b[...].astype(F32)).astype(BF16)


def added(a, b):
    return pl.pallas_call(
        add_kernel,
        out_shape=jax.ShapeDtypeStruct(a.shape, BF16),
        in_specs=[VMEM, VMEM],
        out_specs=VMEM,
        compiler_params=params(8),
    )(a, b)


def flipped(value, axes, count, bits):
    return lax.ppermute(value, axes, [(i, i ^ bits) for i in range(count)])


def after(value, *others):
    return lax.optimization_barrier((value, *others))[0]


def shards_fast(
    span_tokens, q_weight, kv_weight, out_weight, kv_pool, cache_lengths, slot_requests, page_table
):
    group_id = lax.axis_index("group")
    seq_id = lax.axis_index("seq")
    tensor_id = lax.axis_index("tensor")
    place = jnp.stack([group_id, seq_id, tensor_id]).astype(jnp.int32)
    row = jnp.concatenate([place, slot_requests, cache_lengths])
    row = jnp.pad(row, (0, page_table.shape[1] - row.shape[0]))
    info = jnp.concatenate([row[None], page_table])
    mine = span_tokens[0]
    theirs = flipped(mine, "tensor", 2, 1)
    same, beyond, beside, across, diagonal = stage(info, kv_pool)
    capacity = beside.shape[0]
    same = flipped(same, "tensor", 2, 1)
    beyond = flipped(beyond, "group", 4, 2)
    half_dim = HD // 2
    lane = jnp.arange(128, dtype=jnp.int32) % half_dim
    frequency = jnp.power(jnp.float32(10000.0), -lane.astype(F32) / half_dim)
    frequency = jnp.broadcast_to(frequency[None, :], (8, 128))
    acc_q, acc_kv, cosine, sine = first_project(
        after(info, beside), frequency, mine, q_weight, kv_weight
    )
    kept, sent = fresh_rows(info, theirs, kv_weight, acc_kv, cosine, sine)
    got = flipped(sent, "tensor", 2, 1)
    across, diagonal, _ = lax.optimization_barrier((across, diagonal, sent))
    across = flipped(across, ("group", "tensor"), 8, 5)
    diagonal = flipped(diagonal, ("group", "tensor"), 8, 7)
    q = query_rows(info, theirs, q_weight, acc_q, cosine, sine)
    fresh = jnp.stack([kept, got])
    same, beyond, _ = lax.optimization_barrier((same, beyond, fresh))
    mate = jnp.concatenate([beside, beyond[capacity:], same[capacity:]])
    mate = flipped(mate, "group", 4, 1)
    zs = [flipped(fresh, "seq", 4, d) for d in range(1, 4)]
    total, weight, top = attend_near(
        info, q, kv_pool, (same, beyond, mate, across, diagonal), kept, got
    )
    heads, partial = attend_far(info, q, total, weight, top, zs, out_weight)
    away = flipped(partial, "tensor", 2, 1)
    home = home_project(info, heads, out_weight)
    return added(home, away)[None]


def solution(mesh):
    sizes = tuple(mesh.shape[a] for a in ("group", "seq", "tensor"))
    body = shards_fast if sizes == (GROUPS, SEQS, TENSORS) else shards
    placed = (
        P("group", "seq", "tensor"),
        P(None, "tensor"),
        P(None, "tensor"),
        P("tensor", None),
        P("group", None, "tensor"),
        P(),
        P(),
        P(),
    )
    return jax.shard_map(
        body, mesh=mesh, in_specs=placed, out_specs=P("group", "seq", "tensor"), check_vma=False
    )
```

```python
import functools

import jax
import jax.numpy as jnp
from jax import lax
from jax.experimental import pallas as pl
from jax.experimental.pallas import tpu as pltpu
from jax.sharding import PartitionSpec as P

HD = 64
KVH = 4
WINDOW = 2048
PAGE = 128


def shifted(block, axis, distance):
    devices = range(lax.axis_size(axis))
    route = [(i - distance, i) for i in devices if i - distance in devices]
    return lax.ppermute(block, axis, route)


def swapped(value, axis, stride):
    return lax.ppermute(value, axis, [(i, i ^ 1 << stride) for i in range(lax.axis_size(axis))])


def rotate(values, positions):
    half_dim = HD // 2
    frequency = jnp.power(jnp.float32(10000.0), -jnp.arange(half_dim, dtype=jnp.float32) / half_dim)
    angles = positions.astype(jnp.float32)[:, None] * frequency[None, :]
    cosine = jnp.cos(angles)[:, None, :]
    sine_part = jnp.sin(angles)[:, None, :]
    front_half = values[..., :half_dim]
    back_half = values[..., half_dim:]
    return jnp.concatenate(
        [front_half * cosine - back_half * sine_part, back_half * cosine + front_half * sine_part],
        axis=-1,
    )


def attend(block_q, block_k, block_v, base_pos):
    query_count = block_q.shape[0]
    key_count = block_k.shape[0]
    scores = jnp.einsum(
        "tkgd,nkd->kgtn", block_q, block_k, preferred_element_type=jnp.float32
    ) * HD ** (-0.5)
    query_at = jnp.arange(query_count, dtype=jnp.int32)[:, None]
    key_at = jnp.arange(key_count, dtype=jnp.int32)[None, :]
    allowed = (key_at > query_at) & (key_at <= query_at + WINDOW) & (base_pos + key_at >= 0)
    masked = jnp.where(allowed, scores, jnp.float32(-1e30))
    row_top = jnp.max(masked, axis=-1, keepdims=True)
    weights = jnp.where(allowed, jnp.exp(masked - row_top), jnp.float32(0.0))
    row_total = jnp.sum(weights, axis=-1)
    rounded = weights.astype(jnp.bfloat16)
    mixed_rows = jnp.einsum("kgtn,nkd->tkgd", rounded, block_v, preferred_element_type=jnp.float32)
    mixed_rows = mixed_rows / jnp.transpose(row_total, (2, 0, 1))[..., None]
    return mixed_rows.astype(jnp.bfloat16).reshape(query_count, -1)


def shards(
    span_tokens, q_weight, kv_weight, out_weight, kv_pool, cache_lengths, slot_requests, page_table
):
    groups = lax.axis_size("group")
    seq_count = lax.axis_size("seq")
    tensor_count = lax.axis_size("tensor")
    group_id = lax.axis_index("group")
    seq_id = lax.axis_index("seq")
    tensor_id = lax.axis_index("tensor")
    local_reqs, seg_len, feat_local = span_tokens.shape
    head_cols = q_weight.shape[1]
    kv_cols = kv_weight.shape[1]
    local_heads = head_cols // HD
    group_heads = kv_cols // HD
    kv_local = max(1, KVH // tensor_count)
    per_kv = local_heads // kv_local
    head_first = tensor_id * KVH // tensor_count % group_heads
    holds_keys = tensor_id % 2 == 0
    pool_rows = kv_pool.shape[0]
    capacity = pool_rows // groups
    row_count = local_reqs * seg_len
    my_slots = group_id * local_reqs + jnp.arange(local_reqs, dtype=jnp.int32)
    my_requests = slot_requests[my_slots]
    my_lengths = cache_lengths[my_requests]
    project_piece_rows = lax.all_gather(span_tokens, "tensor", axis=2, tiled=True)
    feat_width = project_piece_rows.shape[2]
    flat_rows = project_piece_rows.reshape(row_count, feat_width)
    query_lin = jnp.dot(flat_rows, q_weight, preferred_element_type=jnp.float32)
    fresh_lin = jnp.dot(flat_rows, kv_weight, preferred_element_type=jnp.float32)
    positions = (
        my_lengths[:, None] + seq_id * seg_len + jnp.arange(seg_len, dtype=jnp.int32)[None, :]
    )
    queries = jax.vmap(rotate)(query_lin.reshape(local_reqs, seg_len, local_heads, HD), positions)
    queries = queries.astype(jnp.bfloat16).reshape(local_reqs, seg_len, kv_local, per_kv, HD)
    fresh_heads = fresh_lin.reshape(local_reqs, seg_len, group_heads, HD)
    rotated = jax.vmap(rotate)(fresh_heads, positions)
    span_kv = (
        jnp.where(holds_keys, rotated, fresh_heads)
        .astype(jnp.bfloat16)
        .reshape(local_reqs, seg_len, kv_cols)
    )
    all_ids = page_table[slot_requests]
    owned_here = all_ids // pool_rows == group_id
    slot_rank = jnp.cumsum(owned_here.astype(jnp.int32), axis=1) - 1
    local_rows = all_ids - group_id * pool_rows
    chosen = owned_here[:, :, None] & (
        slot_rank[:, :, None] == jnp.arange(capacity, dtype=jnp.int32)[None, None, :]
    )
    wanted = jnp.sum(jnp.where(chosen, local_rows[:, :, None], 0), axis=1)
    my_ids = page_table[my_requests].reshape(-1)
    my_owner = my_ids // pool_rows
    onehot = (my_owner[:, None] == jnp.arange(groups, dtype=jnp.int32)[None, :]).astype(jnp.int32)
    arrival = jnp.sum((jnp.cumsum(onehot, axis=0) - 1) * onehot, axis=1)
    arrived_row = my_owner * capacity + arrival
    outgoing = kv_pool[wanted]
    arrived = lax.all_to_all(outgoing, "group", split_axis=0, concat_axis=0, tiled=True)
    cached = arrived.reshape(groups * capacity, PAGE, kv_cols)[arrived_row]
    cached = cached.reshape(local_reqs, WINDOW, kv_cols)
    span_all = jnp.zeros((local_reqs, seg_len * seq_count, kv_cols), jnp.bfloat16)
    for back_step in range(seq_count - 1, -1, -1):
        piece_rows = span_kv if back_step == 0 else shifted(span_kv, "seq", back_step)
        span_all = lax.dynamic_update_slice_in_dim(
            span_all, piece_rows, (seq_id - back_step) * seg_len, 1
        )
    joined = jnp.concatenate([cached, span_all], axis=1)
    visible = lax.dynamic_slice_in_dim(joined, seq_id * seg_len, WINDOW + seg_len, 1)
    partner_rows = swapped(visible, "tensor", 0)
    key_all = jnp.where(holds_keys, visible, partner_rows).reshape(
        local_reqs, WINDOW + seg_len, group_heads, HD
    )
    value_all = jnp.where(holds_keys, partner_rows, visible).reshape(
        local_reqs, WINDOW + seg_len, group_heads, HD
    )
    key_rows = lax.dynamic_slice_in_dim(key_all, head_first, kv_local, 2)
    value_rows = lax.dynamic_slice_in_dim(value_all, head_first, kv_local, 2)
    block_len = min(128, seg_len)
    block_count = seg_len // block_len

    def per_request(request_items):
        request_q, request_k, request_v, length = request_items

        def per_block(block_index):
            first_row = block_index * block_len
            block_q = lax.dynamic_slice_in_dim(request_q, first_row, block_len, 0)
            block_k = lax.dynamic_slice_in_dim(request_k, first_row, WINDOW + block_len, 0)
            block_v = lax.dynamic_slice_in_dim(request_v, first_row, WINDOW + block_len, 0)
            return attend(block_q, block_k, block_v, length - WINDOW + seq_id * seg_len + first_row)

        return lax.map(per_block, jnp.arange(block_count, dtype=jnp.int32)).reshape(
            seg_len, head_cols
        )

    attended_heads = lax.map(per_request, (queries, key_rows, value_rows, my_lengths))
    flat_heads = attended_heads.reshape(row_count, head_cols)
    out_cols = out_weight.shape[1] // tensor_count
    summed = lax.psum_scatter(
        lax.dot_general(
            out_weight, flat_heads, (((0,), (1,)), ((), ())), preferred_element_type=jnp.float32
        ).astype(jnp.bfloat16),
        "tensor",
        scatter_dimension=0,
        tiled=True,
    ).astype(jnp.float32)
    result = summed.T
    return result.astype(jnp.bfloat16).reshape(local_reqs, seg_len, out_cols)


LOG2E = 1.4426950408889634
MASKED = -1e30
F32 = jnp.float32
BF16 = jnp.bfloat16
HBM = pl.BlockSpec(memory_space=pl.ANY)
VMEM = pl.BlockSpec(memory_space=pltpu.VMEM)
SMEM = pl.BlockSpec(memory_space=pltpu.SMEM)
STAYS = pl.BlockSpec(memory_space=pltpu.HBM)
GROUPS, SEQS, TENSORS = 4, 4, 2


def params(mebibytes):
    return pltpu.CompilerParams(vmem_limit_bytes=mebibytes * 2**20)


def cost(flops, moved):
    return pl.CostEstimate(flops=flops, bytes_accessed=moved, transcendentals=0)


class Info:
    def __init__(self, ref):
        self.ref = ref
        self.group, self.seq, self.tensor = ref[0, 0], ref[0, 1], ref[0, 2]
        self.window_pages = ref.shape[1]

    def request(self, slot):
        return self.ref[0, 3 + slot]

    def length(self, request):
        return self.ref[0, 3 + GROUPS + request]

    def page(self, request, w):
        return self.ref[1 + request, w]


def stage_kernel(info_ref, pool, same, beyond, beside, across, diagonal, sems):
    info = Info(info_ref)
    pages = pool.shape[0]
    capacity = pages // GROUPS
    half = pool.shape[2] // 2
    mine = pl.ds(pl.multiple_of(info.tensor * half, half), half)
    theirs = pl.ds(pl.multiple_of((1 - info.tensor) * half, half), half)
    spots = {
        0: ((same, 0, 0), None),
        1: ((same, capacity, 0), (beside, 0, 2)),
        2: ((across, 0, 3), (beyond, 0, 1)),
        3: ((diagonal, 0, 4), (beyond, capacity, 1)),
    }
    for flip, (other, own) in spots.items():
        request = info.request(info.group ^ flip)

        def take(w, rank):
            page = info.page(request, w)
            here = page // pages == info.group

            @pl.when(here)
            def _():
                row = page % pages
                for target, cols in ((other, theirs), (own, mine)):
                    if target is not None:
                        out, base, sem = target
                        pltpu.make_async_copy(
                            pool.at[row, :, cols], out.at[base + rank], sems.at[sem]
                        ).start()

            return rank + here.astype(jnp.int32)

        lax.fori_loop(0, info.window_pages, take, jnp.int32(0))
    for i, out in enumerate((same, beyond, beside, across, diagonal)):
        pltpu.make_async_copy(out, out, sems.at[i]).wait()


def stage(info, pool):
    pages, page, cols = pool.shape
    single = jax.ShapeDtypeStruct((pages // GROUPS, page, cols // 2), BF16)
    double = jax.ShapeDtypeStruct((2 * pages // GROUPS, page, cols // 2), BF16)
    return pl.pallas_call(
        stage_kernel,
        out_shape=[double, double, single, single, single],
        in_specs=[SMEM, STAYS],
        out_specs=[VMEM] * 5,
        scratch_shapes=[pltpu.SemaphoreType.DMA((5,))],
        compiler_params=params(8),
        cost_estimate=cost(0, page),
    )(info, pool)


def turned(x, cosine, sine):
    lane = lax.broadcasted_iota(jnp.int32, x.shape, 1)
    other = jnp.where(lane % HD < HD // 2, pltpu.roll(x, 128 - HD // 2, 1), pltpu.roll(x, HD // 2, 1))
    return x * cosine + other * sine


def first_kernel(
    info_ref, frequency, x_hbm, wq_hbm, wkv_hbm, acc_q, acc_kv, cosine, sine, x, wq, wkv, sems
):
    info = Info(info_ref)
    rows, feats = x.shape
    here = pl.ds(pl.multiple_of(info.tensor * feats, feats), feats)
    copies = [
        pltpu.make_async_copy(x_hbm, x, sems.at[0]),
        pltpu.make_async_copy(wkv_hbm.at[here], wkv, sems.at[1]),
        pltpu.make_async_copy(wq_hbm.at[here], wq, sems.at[2]),
    ]
    for copy in copies:
        copy.start()
    start = info.length(info.request(info.group)) + info.seq * rows
    position = (start + lax.broadcasted_iota(jnp.int32, (rows, 128), 0)).astype(F32)
    angles = position * frequency[0:1, :]
    lane = lax.broadcasted_iota(jnp.int32, (rows, 128), 1)
    cosine[...] = jnp.cos(angles)
    sine[...] = jnp.where(lane % HD < HD // 2, -1.0, 1.0) * jnp.sin(angles)
    copies[0].wait()
    copies[1].wait()
    acc_kv[...] = jnp.dot(x[...], wkv[...], preferred_element_type=F32)
    copies[2].wait()
    acc_q[...] = jnp.dot(x[...], wq[...], preferred_element_type=F32)


def first_project(info, frequency, x, wq, wkv):
    rows, feats = x.shape
    table = jax.ShapeDtypeStruct((rows, 128), F32)
    return pl.pallas_call(
        first_kernel,
        out_shape=[
            jax.ShapeDtypeStruct((rows, wq.shape[1]), F32),
            jax.ShapeDtypeStruct((rows, wkv.shape[1]), F32),
            table,
            table,
        ],
        in_specs=[SMEM, VMEM] + [STAYS] * 3,
        out_specs=[VMEM] * 4,
        scratch_shapes=[
            pltpu.VMEM((rows, feats), BF16),
            pltpu.VMEM((feats, wq.shape[1]), BF16),
            pltpu.VMEM((feats, wkv.shape[1]), BF16),
            pltpu.SemaphoreType.DMA((3,)),
        ],
        compiler_params=params(52),
        cost_estimate=cost(rows * feats, rows * feats),
    )(info, frequency, x, wq, wkv)


def fresh_kernel(info_ref, x, wkv, acc_kv, cosine, sine, kept, sent):
    info = Info(info_ref)
    feats = x.shape[1]
    here = pl.ds(pl.multiple_of((1 - info.tensor) * feats, feats), feats)
    keys = info.tensor == 0
    fresh = acc_kv[...] + jnp.dot(x[...], wkv[here], preferred_element_type=F32)
    cos_kv = jnp.where(keys, cosine[...], 1.0)
    sin_kv = jnp.where(keys, sine[...], 0.0)
    low = turned(fresh[:, :128], cos_kv, sin_kv).astype(BF16)
    high = turned(fresh[:, 128:], cos_kv, sin_kv).astype(BF16)
    kept[...] = jnp.where(keys, low, high)
    sent[...] = jnp.where(keys, high, low)


def fresh_rows(info, x, wkv, acc_kv, cosine, sine):
    rows, feats = x.shape
    piece = jax.ShapeDtypeStruct((rows, wkv.shape[1] // 2), BF16)
    return pl.pallas_call(
        fresh_kernel,
        out_shape=[piece, piece],
        in_specs=[SMEM] + [VMEM] * 5,
        out_specs=[VMEM] * 2,
        compiler_params=params(12),
        cost_estimate=cost(2 * rows * feats * 2560, rows * feats),
    )(info, x, wkv, acc_kv, cosine, sine)


def query_kernel(info_ref, x, wq, acc_q, cosine, sine, q):
    feats = x.shape[1]
    here = pl.ds(pl.multiple_of((1 - Info(info_ref).tensor) * feats, feats), feats)
    cos_all, sin_all = cosine[...], sine[...]
    scale = HD**-0.5 * LOG2E
    tile = 256
    for c in range(0, q.shape[1], tile):
        lin = acc_q[:, c : c + tile] + jnp.dot(
            x[...], wq[here, c : c + tile], preferred_element_type=F32
        )
        for e in range(0, tile, 128):
            q[:, c + e : c + e + 128] = (
                turned(lin[:, e : e + 128], cos_all, sin_all) * scale
            ).astype(BF16)


def query_rows(info, x, wq, acc_q, cosine, sine):
    rows, feats = x.shape
    return pl.pallas_call(
        query_kernel,
        out_shape=jax.ShapeDtypeStruct((rows, wq.shape[1]), BF16),
        in_specs=[SMEM] + [VMEM] * 5,
        out_specs=VMEM,
        compiler_params=params(16),
        cost_estimate=cost(rows * feats, rows * feats),
    )(info, x, wq, acc_q, cosine, sine)


def lane_low(rows):
    return lax.broadcasted_iota(jnp.int32, (rows, 2 * HD), 1) < HD


def widen(k, v, bias, keys, values, here):
    lane = lax.broadcasted_iota(jnp.int32, k.shape, 1)
    low = lane < HD
    kr = pltpu.roll(k, HD, 1)
    vr = pltpu.roll(v, HD, 1)
    even = jnp.where(lane == HD, bias, 0.0)
    odd = jnp.where(lane == 0, bias, 0.0)
    keys[0, 0, here] = jnp.where(low, k, even).astype(BF16)
    keys[0, 1, here] = jnp.where(low, odd, kr).astype(BF16)
    keys[1, 0, here] = jnp.where(low, kr, even).astype(BF16)
    keys[1, 1, here] = jnp.where(low, odd, k).astype(BF16)
    values[0, 0, here] = jnp.where(low, v, 1.0).astype(BF16)
    values[0, 1, here] = jnp.where(low, 1.0, vr).astype(BF16)
    values[1, 0, here] = jnp.where(low, vr, 1.0).astype(BF16)
    values[1, 1, here] = jnp.where(low, 1.0, v).astype(BF16)


def soft_heads(q, keys, values, count, masked, emit):
    rows = q.shape[0]
    stack = 2
    lane = lax.broadcasted_iota(jnp.int32, (rows, 2 * HD), 1)
    low = lane < HD
    mark_even = jnp.where(lane == HD, 1.0, 0.0).astype(BF16)
    mark_odd = jnp.where(lane == 0, 1.0, 0.0).astype(BF16)
    query_at = lax.broadcasted_iota(jnp.int32, (stack * rows, rows), 0) % rows
    key_at = lax.broadcasted_iota(jnp.int32, (stack * rows, rows), 1)

    def scores(qs, ks):
        s = lax.dot_general(qs, ks, (((1,), (1,)), ((), ())), preferred_element_type=F32)
        if not masked:
            return s
        return jnp.concatenate(
            [
                jnp.where(key_at <= query_at, s[:, :rows], MASKED),
                jnp.where(key_at > query_at, s[:, rows : 2 * rows], MASKED),
                s[:, 2 * rows :],
            ],
            axis=1,
        )

    def heads(i, _):
        kv_head = i // (4 // stack)
        spots = [pl.ds(pl.multiple_of((i * stack + j) * 128, 128), 128) for j in range(stack)]
        tiles = [q[:, spot] for spot in spots]
        q_even = jnp.concatenate([jnp.where(low, x, mark_even) for x in tiles], axis=0)
        q_odd = jnp.concatenate([jnp.where(low, mark_odd, x) for x in tiles], axis=0)
        s_even = scores(q_even, keys[kv_head, 0, :count])
        s_odd = scores(q_odd, keys[kv_head, 1, :count])
        m_even = jnp.max(s_even, axis=1, keepdims=True)
        m_odd = jnp.max(s_odd, axis=1, keepdims=True)
        p_even = jnp.exp2(s_even - m_even).astype(BF16)
        p_odd = jnp.exp2(s_odd - m_odd).astype(BF16)
        o_even = jnp.dot(p_even, values[kv_head, 0, :count], preferred_element_type=F32)
        o_odd = jnp.dot(p_odd, values[kv_head, 1, :count], preferred_element_type=F32)
        for j in range(stack):
            part = slice(j * rows, (j + 1) * rows)
            a, b = o_even[part], o_odd[part]
            total = jnp.where(low, a, b)
            weight = jnp.where(low, pltpu.roll(a, HD, 1), pltpu.roll(b, HD, 1))
            top = jnp.where(low, m_even[part], m_odd[part])
            emit(spots[j], total, weight, top)
        return 0

    lax.fori_loop(0, q.shape[1] // 128 // stack, heads, 0)


def gather_kernel(
    info_ref, pool, same, beyond, mate, across, diagonal, kept, got,
    keys, values, flow, rank, kv, sem
):
    info = Info(info_ref)
    group, seq, tensor = info.group, info.seq, info.tensor
    pages = pool.shape[0]
    request = info.request(group)
    rows = kept.shape[0]
    per = rows // PAGE
    blocks = kv.shape[1] // PAGE
    seen = blocks - seq * per
    half = pool.shape[2] // 2
    mine = pl.ds(pl.multiple_of(tensor * half, half), half)
    capacity = pages // GROUPS
    owns = (None, mate, beyond, mate)
    own_bases = (0, 0, 0, capacity)
    others = (same, mate, across, diagonal)
    other_bases = (0, 2 * capacity, 0, 0)

    def note(w, counts):
        came = info.page(request, w) // pages ^ group
        place = jnp.int32(0)
        for d in range(4):
            place = jnp.where(came == d, counts[d], place)
        flow[w] = came
        rank[w] = place
        return tuple(counts[d] + (came == d).astype(jnp.int32) for d in range(4))

    lax.fori_loop(0, info.window_pages, note, (jnp.int32(0),) * 4)

    def bring(own, other, here):
        pltpu.make_async_copy(own, kv.at[tensor, here], sem).start()
        pltpu.make_async_copy(other, kv.at[1 - tensor, here], sem).start()

    bring(kept, got, pl.ds(0, rows))

    def fetch(n, _):
        here = pl.ds(pl.multiple_of(n * PAGE, PAGE), PAGE)
        w = n - per + seq * per
        for d in range(4):

            @pl.when(flow[w] == d)
            def _(d=d):
                other = others[d].at[other_bases[d] + rank[w]]
                if d:
                    bring(owns[d].at[own_bases[d] + rank[w]], other, here)
                else:
                    bring(pool.at[info.page(request, w) % pages, :, mine], other, here)

        return 0

    lax.fori_loop(per, seen, fetch, 0)

    def settle(n, _):
        here = kv.at[:, pl.ds(pl.multiple_of(n * PAGE, PAGE), PAGE)]
        pltpu.make_async_copy(here, here, sem).wait()
        return 0

    lax.fori_loop(0, seen, settle, 0)
    first = info.length(request) - WINDOW + seq * rows

    def prepare(n, _):
        here = pl.ds(pl.multiple_of(n * PAGE, PAGE), PAGE)
        hidden = (n >= per) & (first + (n - per) * PAGE < 0)
        bias = jnp.where(hidden, MASKED, 0.0)
        widen(kv[0, here].astype(F32), kv[1, here].astype(F32), bias, keys, values, here)
        return 0

    lax.fori_loop(0, seen, prepare, 0)


def gather_rows(info, pool, pieces, kept, got):
    span = WINDOW + kept.shape[0]
    pages = pool.shape[0]
    wide = jax.ShapeDtypeStruct((2, 2, span, 2 * HD), BF16)
    return pl.pallas_call(
        gather_kernel,
        out_shape=[wide, wide],
        in_specs=[SMEM, STAYS] + [HBM] * 7,
        out_specs=[VMEM] * 2,
        scratch_shapes=[
            pltpu.SMEM((pages,), jnp.int32),
            pltpu.SMEM((pages,), jnp.int32),
            pltpu.VMEM((2, span, 2 * HD), BF16),
            pltpu.SemaphoreType.DMA,
        ],
        compiler_params=params(16),
        cost_estimate=cost(20 * 10**9, 4 * span),
    )(info, pool, *pieces, kept, got)


def near_kernel(info_ref, q, keys, values, total, weight, top):
    seq = Info(info_ref).seq
    rows = q.shape[0]

    def emit(spot, o, l, m):
        total[:, spot] = o
        weight[:, spot] = l
        top[:, spot] = m

    for k in range(SEQS):

        @pl.when(seq == k)
        def _(k=k):
            soft_heads(q, keys, values, WINDOW + rows - k * rows, True, emit)


def attend_near(info, q, keys, values):
    rows = q.shape[0]
    state = jax.ShapeDtypeStruct(q.shape, F32)
    return pl.pallas_call(
        near_kernel,
        out_shape=[state] * 3,
        in_specs=[SMEM] + [VMEM] * 3,
        out_specs=[VMEM] * 3,
        compiler_params=params(32),
        cost_estimate=cost(rows * WINDOW, 4 * WINDOW),
    )(info, q, keys, values)


def far_kernel(
    info_ref, q, total, weight, top, z1, z2, z3, w, heads_out, partial, keys, values
):
    info = Info(info_ref)
    rows = q.shape[0]
    seq = info.seq
    zs = (None, z1, z2, z3)

    for k in range(SEQS):

        @pl.when(seq == k)
        def _(k=k):
            if k == 0:
                heads_out[...] = (total[...] / weight[...]).astype(BF16)
                return
            for n in range(k):
                z = zs[n ^ k]
                here = slice(n * rows, (n + 1) * rows)
                a = z[0].astype(F32)
                b = z[1].astype(F32)
                is_key = info.tensor == 0
                widen(jnp.where(is_key, a, b), jnp.where(is_key, b, a), 0.0, keys, values, here)

            def emit(spot, o, l, m):
                before = top[:, spot]
                peak = jnp.maximum(before, m)
                a = jnp.exp2(before - peak)
                b = jnp.exp2(m - peak)
                done = (total[:, spot] * a + o * b) / (weight[:, spot] * a + l * b)
                heads_out[:, spot] = done.astype(BF16)

            soft_heads(q, keys, values, k * rows, False, emit)

    cols = partial.shape[1]
    here = pl.ds(pl.multiple_of((1 - info.tensor) * cols, cols), cols)
    partial[...] = jnp.dot(heads_out[...], w[:, here], preferred_element_type=F32).astype(BF16)


def attend_far(info, q, total, weight, top, zs, w):
    rows = q.shape[0]
    span = (SEQS - 1) * rows
    return pl.pallas_call(
        far_kernel,
        out_shape=[
            jax.ShapeDtypeStruct(q.shape, BF16),
            jax.ShapeDtypeStruct((rows, w.shape[1] // TENSORS), BF16),
        ],
        in_specs=[SMEM] + [VMEM] * 8,
        out_specs=[VMEM] * 2,
        scratch_shapes=[
            pltpu.VMEM((2, 2, span, 2 * HD), BF16),
            pltpu.VMEM((2, 2, span, 2 * HD), BF16),
        ],
        compiler_params=params(32),
        cost_estimate=cost(4 * rows * span * 1024 + 2 * rows * 1024 * 1024, 4 * span * 128),
    )(info, q, total, weight, top, *zs, w)


def home_kernel(info_ref, x, w, o):
    cols = o.shape[1]
    here = pl.ds(pl.multiple_of(Info(info_ref).tensor * cols, cols), cols)
    o[...] = jnp.dot(x[...], w[:, here], preferred_element_type=F32).astype(BF16)


def home_project(info, x, w):
    rows, depth = x.shape
    cols = w.shape[1] // TENSORS
    return pl.pallas_call(
        home_kernel,
        out_shape=jax.ShapeDtypeStruct((rows, cols), BF16),
        in_specs=[SMEM, VMEM, VMEM],
        out_specs=VMEM,
        compiler_params=params(16),
        cost_estimate=cost(2 * rows * depth * cols, 2 * depth * cols),
    )(info, x, w)


def add_kernel(a, b, o):
    o[...] = (a[...].astype(F32) + b[...].astype(F32)).astype(BF16)


def added(a, b):
    return pl.pallas_call(
        add_kernel,
        out_shape=jax.ShapeDtypeStruct(a.shape, BF16),
        in_specs=[VMEM, VMEM],
        out_specs=VMEM,
        compiler_params=params(8),
    )(a, b)


def flipped(value, axes, count, bits):
    return lax.ppermute(value, axes, [(i, i ^ bits) for i in range(count)])


def after(value, *others):
    return lax.optimization_barrier((value, *others))[0]


def shards_fast(
    span_tokens, q_weight, kv_weight, out_weight, kv_pool, cache_lengths, slot_requests, page_table
):
    group_id = lax.axis_index("group")
    seq_id = lax.axis_index("seq")
    tensor_id = lax.axis_index("tensor")
    place = jnp.stack([group_id, seq_id, tensor_id]).astype(jnp.int32)
    row = jnp.concatenate([place, slot_requests, cache_lengths])
    row = jnp.pad(row, (0, page_table.shape[1] - row.shape[0]))
    info = jnp.concatenate([row[None], page_table])
    mine = span_tokens[0]
    theirs = flipped(mine, "tensor", 2, 1)
    same, beyond, beside, across, diagonal = stage(info, kv_pool)
    capacity = beside.shape[0]
    same = flipped(same, "tensor", 2, 1)
    beyond = flipped(beyond, "group", 4, 2)
    half_dim = HD // 2
    lane = jnp.arange(128, dtype=jnp.int32) % half_dim
    frequency = jnp.power(jnp.float32(10000.0), -lane.astype(F32) / half_dim)
    frequency = jnp.broadcast_to(frequency[None, :], (8, 128))
    acc_q, acc_kv, cosine, sine = first_project(
        after(info, beside), frequency, mine, q_weight, kv_weight
    )
    kept, sent = fresh_rows(info, theirs, kv_weight, acc_kv, cosine, sine)
    got = flipped(sent, "tensor", 2, 1)
    across, diagonal, _ = lax.optimization_barrier((across, diagonal, sent))
    across = flipped(across, ("group", "tensor"), 8, 5)
    diagonal = flipped(diagonal, ("group", "tensor"), 8, 7)
    q = query_rows(info, theirs, q_weight, acc_q, cosine, sine)
    fresh = jnp.stack([kept, got])
    same, beyond, _ = lax.optimization_barrier((same, beyond, sent))
    mate = jnp.concatenate([beside, beyond[capacity:], same[capacity:]])
    mate = flipped(mate, "group", 4, 1)
    zs = [flipped(fresh, "seq", 4, d) for d in range(1, 4)]
    keys, values = gather_rows(
        info, kv_pool, (same, beyond, mate, across, diagonal), kept, got
    )
    total, weight, top = attend_near(info, q, keys, values)
    heads, partial = attend_far(info, q, total, weight, top, zs, out_weight)
    away = flipped(partial, "tensor", 2, 1)
    home = home_project(info, heads, out_weight)
    return added(home, away)[None]


def solution(mesh):
    sizes = tuple(mesh.shape[a] for a in ("group", "seq", "tensor"))
    body = shards_fast if sizes == (GROUPS, SEQS, TENSORS) else shards
    placed = (
        P("group", "seq", "tensor"),
        P(None, "tensor"),
        P(None, "tensor"),
        P("tensor", None),
        P("group", None, "tensor"),
        P(),
        P(),
        P(),
    )
    return jax.shard_map(
        body, mesh=mesh, in_specs=placed, out_specs=P("group", "seq", "tensor"), check_vma=False
    )
```

```python
import functools

import jax
import jax.numpy as jnp
from jax import lax
from jax.experimental import pallas as pl
from jax.experimental.pallas import tpu as pltpu
from jax.sharding import PartitionSpec as P

HD = 64
KVH = 4
WINDOW = 2048
PAGE = 128


def shifted(block, axis, distance):
    devices = range(lax.axis_size(axis))
    route = [(i - distance, i) for i in devices if i - distance in devices]
    return lax.ppermute(block, axis, route)


def swapped(value, axis, stride):
    return lax.ppermute(value, axis, [(i, i ^ 1 << stride) for i in range(lax.axis_size(axis))])


def rotate(values, positions):
    half_dim = HD // 2
    frequency = jnp.power(jnp.float32(10000.0), -jnp.arange(half_dim, dtype=jnp.float32) / half_dim)
    angles = positions.astype(jnp.float32)[:, None] * frequency[None, :]
    cosine = jnp.cos(angles)[:, None, :]
    sine_part = jnp.sin(angles)[:, None, :]
    front_half = values[..., :half_dim]
    back_half = values[..., half_dim:]
    return jnp.concatenate(
        [front_half * cosine - back_half * sine_part, back_half * cosine + front_half * sine_part],
        axis=-1,
    )


def attend(block_q, block_k, block_v, base_pos):
    query_count = block_q.shape[0]
    key_count = block_k.shape[0]
    scores = jnp.einsum(
        "tkgd,nkd->kgtn", block_q, block_k, preferred_element_type=jnp.float32
    ) * HD ** (-0.5)
    query_at = jnp.arange(query_count, dtype=jnp.int32)[:, None]
    key_at = jnp.arange(key_count, dtype=jnp.int32)[None, :]
    allowed = (key_at > query_at) & (key_at <= query_at + WINDOW) & (base_pos + key_at >= 0)
    masked = jnp.where(allowed, scores, jnp.float32(-1e30))
    row_top = jnp.max(masked, axis=-1, keepdims=True)
    weights = jnp.where(allowed, jnp.exp(masked - row_top), jnp.float32(0.0))
    row_total = jnp.sum(weights, axis=-1)
    rounded = weights.astype(jnp.bfloat16)
    mixed_rows = jnp.einsum("kgtn,nkd->tkgd", rounded, block_v, preferred_element_type=jnp.float32)
    mixed_rows = mixed_rows / jnp.transpose(row_total, (2, 0, 1))[..., None]
    return mixed_rows.astype(jnp.bfloat16).reshape(query_count, -1)


def shards(
    span_tokens, q_weight, kv_weight, out_weight, kv_pool, cache_lengths, slot_requests, page_table
):
    groups = lax.axis_size("group")
    seq_count = lax.axis_size("seq")
    tensor_count = lax.axis_size("tensor")
    group_id = lax.axis_index("group")
    seq_id = lax.axis_index("seq")
    tensor_id = lax.axis_index("tensor")
    local_reqs, seg_len, feat_local = span_tokens.shape
    head_cols = q_weight.shape[1]
    kv_cols = kv_weight.shape[1]
    local_heads = head_cols // HD
    group_heads = kv_cols // HD
    kv_local = max(1, KVH // tensor_count)
    per_kv = local_heads // kv_local
    head_first = tensor_id * KVH // tensor_count % group_heads
    holds_keys = tensor_id % 2 == 0
    pool_rows = kv_pool.shape[0]
    capacity = pool_rows // groups
    row_count = local_reqs * seg_len
    my_slots = group_id * local_reqs + jnp.arange(local_reqs, dtype=jnp.int32)
    my_requests = slot_requests[my_slots]
    my_lengths = cache_lengths[my_requests]
    project_piece_rows = lax.all_gather(span_tokens, "tensor", axis=2, tiled=True)
    feat_width = project_piece_rows.shape[2]
    flat_rows = project_piece_rows.reshape(row_count, feat_width)
    query_lin = jnp.dot(flat_rows, q_weight, preferred_element_type=jnp.float32)
    fresh_lin = jnp.dot(flat_rows, kv_weight, preferred_element_type=jnp.float32)
    positions = (
        my_lengths[:, None] + seq_id * seg_len + jnp.arange(seg_len, dtype=jnp.int32)[None, :]
    )
    queries = jax.vmap(rotate)(query_lin.reshape(local_reqs, seg_len, local_heads, HD), positions)
    queries = queries.astype(jnp.bfloat16).reshape(local_reqs, seg_len, kv_local, per_kv, HD)
    fresh_heads = fresh_lin.reshape(local_reqs, seg_len, group_heads, HD)
    rotated = jax.vmap(rotate)(fresh_heads, positions)
    span_kv = (
        jnp.where(holds_keys, rotated, fresh_heads)
        .astype(jnp.bfloat16)
        .reshape(local_reqs, seg_len, kv_cols)
    )
    all_ids = page_table[slot_requests]
    owned_here = all_ids // pool_rows == group_id
    slot_rank = jnp.cumsum(owned_here.astype(jnp.int32), axis=1) - 1
    local_rows = all_ids - group_id * pool_rows
    chosen = owned_here[:, :, None] & (
        slot_rank[:, :, None] == jnp.arange(capacity, dtype=jnp.int32)[None, None, :]
    )
    wanted = jnp.sum(jnp.where(chosen, local_rows[:, :, None], 0), axis=1)
    my_ids = page_table[my_requests].reshape(-1)
    my_owner = my_ids // pool_rows
    onehot = (my_owner[:, None] == jnp.arange(groups, dtype=jnp.int32)[None, :]).astype(jnp.int32)
    arrival = jnp.sum((jnp.cumsum(onehot, axis=0) - 1) * onehot, axis=1)
    arrived_row = my_owner * capacity + arrival
    outgoing = kv_pool[wanted]
    arrived = lax.all_to_all(outgoing, "group", split_axis=0, concat_axis=0, tiled=True)
    cached = arrived.reshape(groups * capacity, PAGE, kv_cols)[arrived_row]
    cached = cached.reshape(local_reqs, WINDOW, kv_cols)
    span_all = jnp.zeros((local_reqs, seg_len * seq_count, kv_cols), jnp.bfloat16)
    for back_step in range(seq_count - 1, -1, -1):
        piece_rows = span_kv if back_step == 0 else shifted(span_kv, "seq", back_step)
        span_all = lax.dynamic_update_slice_in_dim(
            span_all, piece_rows, (seq_id - back_step) * seg_len, 1
        )
    joined = jnp.concatenate([cached, span_all], axis=1)
    visible = lax.dynamic_slice_in_dim(joined, seq_id * seg_len, WINDOW + seg_len, 1)
    partner_rows = swapped(visible, "tensor", 0)
    key_all = jnp.where(holds_keys, visible, partner_rows).reshape(
        local_reqs, WINDOW + seg_len, group_heads, HD
    )
    value_all = jnp.where(holds_keys, partner_rows, visible).reshape(
        local_reqs, WINDOW + seg_len, group_heads, HD
    )
    key_rows = lax.dynamic_slice_in_dim(key_all, head_first, kv_local, 2)
    value_rows = lax.dynamic_slice_in_dim(value_all, head_first, kv_local, 2)
    block_len = min(128, seg_len)
    block_count = seg_len // block_len

    def per_request(request_items):
        request_q, request_k, request_v, length = request_items

        def per_block(block_index):
            first_row = block_index * block_len
            block_q = lax.dynamic_slice_in_dim(request_q, first_row, block_len, 0)
            block_k = lax.dynamic_slice_in_dim(request_k, first_row, WINDOW + block_len, 0)
            block_v = lax.dynamic_slice_in_dim(request_v, first_row, WINDOW + block_len, 0)
            return attend(block_q, block_k, block_v, length - WINDOW + seq_id * seg_len + first_row)

        return lax.map(per_block, jnp.arange(block_count, dtype=jnp.int32)).reshape(
            seg_len, head_cols
        )

    attended_heads = lax.map(per_request, (queries, key_rows, value_rows, my_lengths))
    flat_heads = attended_heads.reshape(row_count, head_cols)
    out_cols = out_weight.shape[1] // tensor_count
    summed = lax.psum_scatter(
        lax.dot_general(
            out_weight, flat_heads, (((0,), (1,)), ((), ())), preferred_element_type=jnp.float32
        ).astype(jnp.bfloat16),
        "tensor",
        scatter_dimension=0,
        tiled=True,
    ).astype(jnp.float32)
    result = summed.T
    return result.astype(jnp.bfloat16).reshape(local_reqs, seg_len, out_cols)


LOG2E = 1.4426950408889634
MASKED = -1e30
F32 = jnp.float32
BF16 = jnp.bfloat16
HBM = pl.BlockSpec(memory_space=pl.ANY)
VMEM = pl.BlockSpec(memory_space=pltpu.VMEM)
SMEM = pl.BlockSpec(memory_space=pltpu.SMEM)
STAYS = pl.BlockSpec(memory_space=pltpu.HBM)
GROUPS, SEQS, TENSORS = 4, 4, 2


def params(mebibytes):
    return pltpu.CompilerParams(vmem_limit_bytes=mebibytes * 2**20)


def cost(flops, moved):
    return pl.CostEstimate(flops=flops, bytes_accessed=moved, transcendentals=0)


class Info:
    def __init__(self, ref):
        self.ref = ref
        self.group, self.seq, self.tensor = ref[0, 0], ref[0, 1], ref[0, 2]
        self.window_pages = ref.shape[1]

    def request(self, slot):
        return self.ref[0, 3 + slot]

    def length(self, request):
        return self.ref[0, 3 + GROUPS + request]

    def page(self, request, w):
        return self.ref[1 + request, w]


def turned(x, cosine, sine):
    lane = lax.broadcasted_iota(jnp.int32, x.shape, 1)
    other = jnp.where(lane % HD < HD // 2, pltpu.roll(x, 128 - HD // 2, 1), pltpu.roll(x, HD // 2, 1))
    return x * cosine + other * sine


def open_kernel(
    info_ref, frequency, pool, x_hbm, wq_hbm, wkv_hbm,
    home, same, cross, beyond, beside, across, diagonal, acc_q, acc_kv, cosine, sine,
    x, wq, wkv, sems, page_sems,
):
    info = Info(info_ref)
    rows, feats = x.shape
    here = pl.ds(pl.multiple_of(info.tensor * feats, feats), feats)
    copies = [
        pltpu.make_async_copy(x_hbm, x, sems.at[0]),
        pltpu.make_async_copy(wkv_hbm.at[here], wkv, sems.at[1]),
        pltpu.make_async_copy(wq_hbm.at[here], wq, sems.at[2]),
    ]
    for copy in copies:
        copy.start()
    pages = pool.shape[0]
    capacity = pages // GROUPS
    half = pool.shape[2] // 2
    mine = pl.ds(pl.multiple_of(info.tensor * half, half), half)
    theirs = pl.ds(pl.multiple_of((1 - info.tensor) * half, half), half)
    outs = (home, same, cross, beyond, beside, across, diagonal)
    spots = (((0, 0), 1), ((4, 0), 2), ((3, 0), 5), ((3, capacity), 6))
    for flip, ((own, base), other) in enumerate(spots):
        request = info.request(info.group ^ flip)

        def take(w, rank):
            page = info.page(request, w)
            near = page // pages == info.group

            @pl.when(near)
            def _():
                row = page % pages
                pltpu.make_async_copy(
                    pool.at[row, :, mine], outs[own].at[base + rank], page_sems.at[own]
                ).start()
                pltpu.make_async_copy(
                    pool.at[row, :, theirs], outs[other].at[rank], page_sems.at[other]
                ).start()

            return rank + near.astype(jnp.int32)

        lax.fori_loop(0, info.window_pages, take, jnp.int32(0))
    start = info.length(info.request(info.group)) + info.seq * rows
    position = (start + lax.broadcasted_iota(jnp.int32, (rows, 128), 0)).astype(F32)
    angles = position * frequency[0:1, :]
    lane = lax.broadcasted_iota(jnp.int32, (rows, 128), 1)
    cosine[...] = jnp.cos(angles)
    sine[...] = jnp.where(lane % HD < HD // 2, -1.0, 1.0) * jnp.sin(angles)
    copies[0].wait()
    copies[1].wait()
    acc_kv[...] = jnp.dot(x[...], wkv[...], preferred_element_type=F32)
    copies[2].wait()
    acc_q[...] = jnp.dot(x[...], wq[...], preferred_element_type=F32)
    for i, out in enumerate(outs):
        pltpu.make_async_copy(out, out, page_sems.at[i]).wait()


def open_rows(info, frequency, pool, x, wq, wkv):
    rows, feats = x.shape
    pages, page, cols = pool.shape
    single = jax.ShapeDtypeStruct((pages // GROUPS, page, cols // 2), BF16)
    double = jax.ShapeDtypeStruct((2 * pages // GROUPS, page, cols // 2), BF16)
    table = jax.ShapeDtypeStruct((rows, 128), F32)
    return pl.pallas_call(
        open_kernel,
        out_shape=[
            single,
            single,
            single,
            double,
            single,
            single,
            single,
            jax.ShapeDtypeStruct((rows, wq.shape[1]), F32),
            jax.ShapeDtypeStruct((rows, wkv.shape[1]), F32),
            table,
            table,
        ],
        in_specs=[SMEM, VMEM] + [STAYS] * 4,
        out_specs=[VMEM] * 11,
        scratch_shapes=[
            pltpu.VMEM((rows, feats), BF16),
            pltpu.VMEM((feats, wq.shape[1]), BF16),
            pltpu.VMEM((feats, wkv.shape[1]), BF16),
            pltpu.SemaphoreType.DMA((3,)),
            pltpu.SemaphoreType.DMA((7,)),
        ],
        compiler_params=params(52),
        cost_estimate=cost(rows * feats, rows * feats),
    )(info, frequency, pool, x, wq, wkv)


def fresh_kernel(info_ref, x, wkv, acc_kv, cosine, sine, kept, sent):
    info = Info(info_ref)
    feats = x.shape[1]
    here = pl.ds(pl.multiple_of((1 - info.tensor) * feats, feats), feats)
    keys = info.tensor == 0
    fresh = acc_kv[...] + jnp.dot(x[...], wkv[here], preferred_element_type=F32)
    cos_kv = jnp.where(keys, cosine[...], 1.0)
    sin_kv = jnp.where(keys, sine[...], 0.0)
    low = turned(fresh[:, :128], cos_kv, sin_kv).astype(BF16)
    high = turned(fresh[:, 128:], cos_kv, sin_kv).astype(BF16)
    kept[...] = jnp.where(keys, low, high)
    sent[...] = jnp.where(keys, high, low)


def fresh_rows(info, x, wkv, acc_kv, cosine, sine):
    rows, feats = x.shape
    piece = jax.ShapeDtypeStruct((rows, wkv.shape[1] // 2), BF16)
    return pl.pallas_call(
        fresh_kernel,
        out_shape=[piece, piece],
        in_specs=[SMEM] + [VMEM] * 5,
        out_specs=[VMEM] * 2,
        compiler_params=params(12),
        cost_estimate=cost(2 * rows * feats * 2560, rows * feats),
    )(info, x, wkv, acc_kv, cosine, sine)


def query_kernel(info_ref, x, wq, acc_q, cosine, sine, q):
    feats = x.shape[1]
    here = pl.ds(pl.multiple_of((1 - Info(info_ref).tensor) * feats, feats), feats)
    cos_all, sin_all = cosine[...], sine[...]
    scale = HD**-0.5 * LOG2E
    tile = 256
    for c in range(0, q.shape[1], tile):
        lin = acc_q[:, c : c + tile] + jnp.dot(
            x[...], wq[here, c : c + tile], preferred_element_type=F32
        )
        for e in range(0, tile, 128):
            q[:, c + e : c + e + 128] = (
                turned(lin[:, e : e + 128], cos_all, sin_all) * scale
            ).astype(BF16)


def query_rows(info, x, wq, acc_q, cosine, sine):
    rows, feats = x.shape
    return pl.pallas_call(
        query_kernel,
        out_shape=jax.ShapeDtypeStruct((rows, wq.shape[1]), BF16),
        in_specs=[SMEM] + [VMEM] * 5,
        out_specs=VMEM,
        compiler_params=params(16),
        cost_estimate=cost(rows * feats, rows * feats),
    )(info, x, wq, acc_q, cosine, sine)


def soft_heads(q, tokens, keys, values, span, mask, emit):
    rows = tokens.stop - tokens.start
    stack = 4
    lane = lax.broadcasted_iota(jnp.int32, (rows, 2 * HD), 1)
    low = lane < HD

    def swap(x):
        return pltpu.roll(x, HD, 1)

    def heads(i, _):
        first = i == 0
        spots = [pl.ds(pl.multiple_of((i * stack + j) * 128, 128), 128) for j in range(stack)]
        tiles = [q[tokens, spot] for spot in spots]
        turns = [swap(x.astype(F32)).astype(BF16) for x in tiles]
        keep = low == first

        def stacked(a, b):
            zero = jnp.zeros_like(a[0])
            return jnp.concatenate(
                [jnp.where(keep, jnp.where(first, x, y), zero) for x, y in zip(a, b)], axis=0
            )

        def scores(qs):
            s = lax.dot_general(
                qs, keys[span], (((1,), (1,)), ((), ())), preferred_element_type=F32
            )
            return mask(s)

        s_even = scores(stacked(tiles, turns))
        s_odd = scores(stacked(turns, tiles))
        m_even = jnp.max(s_even, axis=1, keepdims=True)
        m_odd = jnp.max(s_odd, axis=1, keepdims=True)
        p_even = jnp.exp2(s_even - m_even).astype(BF16)
        p_odd = jnp.exp2(s_odd - m_odd).astype(BF16)
        o_even = jnp.dot(p_even, values[span], preferred_element_type=F32)
        o_odd = jnp.dot(p_odd, values[span], preferred_element_type=F32)
        for j in range(stack):
            part = slice(j * rows, (j + 1) * rows)
            a, b = o_even[part, : 2 * HD], o_odd[part, : 2 * HD]
            a = jnp.where(first, a, swap(a))
            b = jnp.where(first, swap(b), b)
            total = jnp.where(low, a, b)
            weight = jnp.where(low, o_even[part, 2 * HD :], o_odd[part, 2 * HD :])
            top = jnp.where(low, m_even[part], m_odd[part])
            emit(spots[j], total, weight, top)
        return 0

    lax.fori_loop(0, q.shape[1] // 128 // stack, heads, 0)


def bundle_kernel(*refs):
    out = refs[-1]
    at = 0
    for ref in refs[:-1]:
        out[at : at + ref.shape[0]] = ref[...]
        at += ref.shape[0]


def bundled(*parts):
    count = sum(part.shape[0] for part in parts)
    return pl.pallas_call(
        bundle_kernel,
        out_shape=jax.ShapeDtypeStruct((count, *parts[0].shape[1:]), BF16),
        in_specs=[VMEM] * len(parts),
        out_specs=VMEM,
        compiler_params=params(8),
        cost_estimate=cost(20 * 10**9, 4 * count),
    )(*parts)


def gather_kernel(info_ref, chip, beyond, kept, got, keys, values, bias, source):
    info = Info(info_ref)
    group, seq = info.group, info.seq
    request = info.request(group)
    rows = kept.shape[0]
    per = rows // PAGE
    count = chip.shape[0]
    capacity = count // GROUPS
    seen = keys.shape[0] // PAGE - seq * per
    is_key = info.tensor == 0
    key_base = info.tensor * (count // 2)
    value_base = count // 2 - key_base

    def note(w, counts):
        came = info.page(request, w) // count ^ group
        place = came * capacity
        for d in range(GROUPS):
            place = place + jnp.where(came == d, counts[d], 0)
        source[w] = place
        return tuple(counts[d] + (came == d).astype(jnp.int32) for d in range(GROUPS))

    lax.fori_loop(0, info.window_pages, note, (jnp.int32(0),) * GROUPS)
    values[:, 2 * HD :] = jnp.ones((values.shape[0], 2 * HD), BF16)
    bias[...] = jnp.zeros_like(bias)

    def fresh(block, part):
        here = pl.ds(pl.multiple_of(block * PAGE, PAGE), PAGE)
        a = kept[part]
        b = got[part]
        keys[here] = jnp.where(is_key, a, b)
        values[here, : 2 * HD] = jnp.where(is_key, b, a)

    fresh(1, slice(0, PAGE))
    fresh(seen - 1, slice(PAGE, 2 * PAGE))
    first = info.length(request) - WINDOW + seq * rows

    def bring(n, _):
        block = jnp.where(n == 0, 0, n + 1)
        here = pl.ds(pl.multiple_of(block * PAGE, PAGE), PAGE)
        at = source[seq * per + n]

        for base, pages in ((0, chip), (count // 2, beyond)):

            @pl.when((at >= base) & (at < base + count // 2))
            def _(base=base, pages=pages):
                keys[here] = pages[key_base + at - base]
                values[here, : 2 * HD] = pages[value_base + at - base]

        hidden = jnp.where(first + n * PAGE >= 0, 0.0, MASKED)
        bias[:, here] = jnp.full((bias.shape[0], PAGE), hidden, F32)
        return 0

    lax.fori_loop(0, seen - per, bring, 0)


def gather_rows(info, chip, beyond, kept, got):
    span = WINDOW + kept.shape[0]
    return pl.pallas_call(
        gather_kernel,
        out_shape=[
            jax.ShapeDtypeStruct((span, 2 * HD), BF16),
            jax.ShapeDtypeStruct((span, 4 * HD), BF16),
            jax.ShapeDtypeStruct((8, span), F32),
        ],
        in_specs=[SMEM] + [VMEM] * 4,
        out_specs=[VMEM] * 3,
        scratch_shapes=[pltpu.SMEM((chip.shape[0],), jnp.int32)],
        compiler_params=params(12),
        cost_estimate=cost(20 * 10**9, 4 * span),
    )(info, chip, beyond, kept, got)


def near_kernel(info_ref, q, keys, values, bias, total, weight, top, *, half):
    seq = Info(info_ref).seq
    rows = q.shape[0]
    blocks = keys.shape[0] // PAGE
    per = rows // PAGE
    tokens = slice(half * PAGE, (half + 1) * PAGE)
    stack = 4
    query_at = lax.broadcasted_iota(jnp.int32, (stack * PAGE, PAGE), 0) % PAGE
    key_at = lax.broadcasted_iota(jnp.int32, (stack * PAGE, PAGE), 1)
    newer = key_at > query_at

    def emit(spot, o, l, m):
        total[:, spot] = o
        weight[:, spot] = l
        top[:, spot] = m

    for k in range(SEQS):
        span = slice(half * PAGE, (blocks - k * per - 1 + half) * PAGE)

        def mask(s, span=span):
            s = s + bias[0:1, span]
            if half == 0:
                parts = [
                    jnp.where(newer, s[:, :PAGE], MASKED),
                    jnp.where(newer, MASKED, s[:, PAGE : 2 * PAGE]),
                    s[:, 2 * PAGE :],
                ]
            else:
                parts = [
                    s[:, :PAGE],
                    jnp.where(newer, s[:, PAGE : 2 * PAGE], MASKED),
                    s[:, 2 * PAGE : -PAGE],
                    jnp.where(newer, MASKED, s[:, -PAGE:]),
                ]
            return jnp.concatenate(parts, axis=1)

        @pl.when(seq == k)
        def _(span=span, mask=mask):
            soft_heads(q, tokens, keys, values, span, mask, emit)


def attend_near(info, q, keys, values, bias, half):
    state = jax.ShapeDtypeStruct((PAGE, q.shape[1]), F32)
    return pl.pallas_call(
        functools.partial(near_kernel, half=half),
        out_shape=[state] * 3,
        in_specs=[SMEM] + [VMEM] * 4,
        out_specs=[VMEM] * 3,
        compiler_params=params(32),
        cost_estimate=cost(PAGE * WINDOW, 4 * WINDOW),
    )(info, q, keys, values, bias)


def far_kernel(
    info_ref, q, total, weight, top, z1, z2, z3, w, heads_out, partial, keys, values, *, half
):
    info = Info(info_ref)
    rows = q.shape[0]
    seq = info.seq
    zs = (None, z1, z2, z3)
    is_key = info.tensor == 0
    tokens = slice(half * PAGE, (half + 1) * PAGE)

    for k in range(SEQS):

        @pl.when(seq == k)
        def _(k=k):
            if k == 0:
                heads_out[...] = (total[...] / weight[...]).astype(BF16)
                return
            for n in range(k):
                z = zs[n ^ k]
                here = slice(n * rows, (n + 1) * rows)
                a, b = z[0], z[1]
                keys[here] = jnp.where(is_key, a, b)
                values[here, : 2 * HD] = jnp.where(is_key, b, a)
                values[here, 2 * HD :] = jnp.ones((rows, 2 * HD), BF16)

            def emit(spot, o, l, m):
                before = top[:, spot]
                peak = jnp.maximum(before, m)
                a = jnp.exp2(before - peak)
                b = jnp.exp2(m - peak)
                done = (total[:, spot] * a + o * b) / (weight[:, spot] * a + l * b)
                heads_out[:, spot] = done.astype(BF16)

            soft_heads(q, tokens, keys, values, slice(0, k * rows), lambda s: s, emit)

    cols = partial.shape[1]
    here = pl.ds(pl.multiple_of((1 - info.tensor) * cols, cols), cols)
    partial[...] = jnp.dot(heads_out[...], w[:, here], preferred_element_type=F32).astype(BF16)


def attend_far(info, q, state, zs, w, half):
    rows = q.shape[0]
    span = (SEQS - 1) * rows
    return pl.pallas_call(
        functools.partial(far_kernel, half=half),
        out_shape=[
            jax.ShapeDtypeStruct((PAGE, q.shape[1]), BF16),
            jax.ShapeDtypeStruct((PAGE, w.shape[1] // TENSORS), BF16),
        ],
        in_specs=[SMEM] + [VMEM] * 8,
        out_specs=[VMEM] * 2,
        scratch_shapes=[
            pltpu.VMEM((span, 2 * HD), BF16),
            pltpu.VMEM((span, 4 * HD), BF16),
        ],
        compiler_params=params(24),
        cost_estimate=cost(rows * span, 4 * span),
    )(info, q, *state, *zs, w)


def home_kernel(info_ref, x1, x2, away, w, out, home, first, sem):
    rows, cols = home.shape
    here = pl.ds(pl.multiple_of(Info(info_ref).tensor * cols, cols), cols)
    x = jnp.concatenate([x1[...], x2[...]], axis=0)
    o = jnp.dot(x, w[:, here], preferred_element_type=F32).astype(BF16)
    home[...] = o[rows:]
    first[...] = (o[:rows].astype(F32) + away[...].astype(F32)).astype(BF16)
    copy = pltpu.make_async_copy(first, out.at[pl.ds(0, rows)], sem)
    copy.start()
    copy.wait()


def home_project(info, x1, x2, away, w):
    rows, depth = x1.shape
    cols = w.shape[1] // TENSORS
    return pl.pallas_call(
        home_kernel,
        out_shape=[
            jax.ShapeDtypeStruct((2 * rows, cols), BF16),
            jax.ShapeDtypeStruct((rows, cols), BF16),
        ],
        in_specs=[SMEM] + [VMEM] * 4,
        out_specs=[STAYS, VMEM],
        scratch_shapes=[pltpu.VMEM((rows, cols), BF16), pltpu.SemaphoreType.DMA],
        compiler_params=params(16),
        cost_estimate=cost(20 * 10**9, 2 * depth * cols),
    )(info, x1, x2, away, w)


def add_kernel(before, a, b, out, last, sem):
    rows = a.shape[0]
    last[...] = (a[...].astype(F32) + b[...].astype(F32)).astype(BF16)
    copy = pltpu.make_async_copy(last, out.at[pl.ds(rows, rows)], sem)
    copy.start()
    copy.wait()


def added(before, a, b):
    return pl.pallas_call(
        add_kernel,
        out_shape=jax.ShapeDtypeStruct(before.shape, BF16),
        in_specs=[STAYS, VMEM, VMEM],
        out_specs=STAYS,
        scratch_shapes=[pltpu.VMEM(a.shape, BF16), pltpu.SemaphoreType.DMA],
        input_output_aliases={0: 0},
        compiler_params=params(8),
    )(before, a, b)


def flipped(value, axes, count, bits):
    return lax.ppermute(value, axes, [(i, i ^ bits) for i in range(count)])


def after(value, *others):
    return lax.optimization_barrier((value, *others))[0]


def shards_fast(
    span_tokens, q_weight, kv_weight, out_weight, kv_pool, cache_lengths, slot_requests, page_table
):
    group_id = lax.axis_index("group")
    seq_id = lax.axis_index("seq")
    tensor_id = lax.axis_index("tensor")
    place = jnp.stack([group_id, seq_id, tensor_id]).astype(jnp.int32)
    row = jnp.concatenate([place, slot_requests, cache_lengths])
    row = jnp.pad(row, (0, page_table.shape[1] - row.shape[0]))
    info = jnp.concatenate([row[None], page_table])
    mine = span_tokens[0]
    theirs = flipped(mine, "tensor", 2, 1)
    half_dim = HD // 2
    lane = jnp.arange(128, dtype=jnp.int32) % half_dim
    frequency = jnp.power(jnp.float32(10000.0), -lane.astype(F32) / half_dim)
    frequency = jnp.broadcast_to(frequency[None, :], (8, 128))
    pages = open_rows(info, frequency, kv_pool, mine, q_weight, kv_weight)
    home, same, cross, beyond, beside, across, diagonal = pages[:7]
    acc_q, acc_kv, cosine, sine = pages[7:]
    capacity = home.shape[0]
    same = flipped(same, "tensor", 2, 1)
    cross = flipped(cross, ("group", "tensor"), 8, 3)
    beyond = flipped(beyond, "group", 4, 2)
    kept, sent = fresh_rows(info, theirs, kv_weight, acc_kv, cosine, sine)
    got = flipped(sent, "tensor", 2, 1)
    across, diagonal, _ = lax.optimization_barrier((across, diagonal, sent))
    across = flipped(across, ("group", "tensor"), 8, 5)
    diagonal = flipped(diagonal, ("group", "tensor"), 8, 7)
    q = query_rows(info, theirs, q_weight, acc_q, cosine, sine)
    fresh = jnp.stack([kept, got])
    beyond, _ = lax.optimization_barrier((beyond, sent))
    mate = jnp.concatenate([beside, beyond[capacity:]])
    mate = flipped(mate, "group", 4, 1)
    chip = bundled(home, mate[:capacity], same, cross)
    across, diagonal, fresh, chip = lax.optimization_barrier((across, diagonal, fresh, chip))
    zs = [flipped(fresh, "seq", 4, d) for d in range(1, 4)]
    other_chip = jnp.concatenate([beyond[:capacity], mate[capacity:], across, diagonal])
    keys, values, bias = gather_rows(info, chip, other_chip, kept, got)
    state = attend_near(info, q, keys, values, bias, 0)
    heads_0, partial_0 = attend_far(info, q, state, zs, out_weight, 0)
    away_0 = flipped(partial_0, "tensor", 2, 1)
    state = attend_near(after(info, partial_0), q, keys, values, bias, 1)
    heads_1, partial_1 = attend_far(info, q, state, zs, out_weight, 1)
    away_1 = flipped(partial_1, "tensor", 2, 1)
    out, home_1 = home_project(info, heads_0, heads_1, away_0, out_weight)
    return added(out, home_1, away_1)[None]


def solution(mesh):
    sizes = tuple(mesh.shape[a] for a in ("group", "seq", "tensor"))
    body = shards_fast if sizes == (GROUPS, SEQS, TENSORS) else shards
    placed = (
        P("group", "seq", "tensor"),
        P(None, "tensor"),
        P(None, "tensor"),
        P("tensor", None),
        P("group", None, "tensor"),
        P(),
        P(),
        P(),
    )
    return jax.shard_map(
        body, mesh=mesh, in_specs=placed, out_specs=P("group", "seq", "tensor"), check_vma=False
    )
```

```python
import functools

import jax
import jax.numpy as jnp
from jax import lax
from jax.experimental import pallas as pl
from jax.experimental.pallas import tpu as pltpu
from jax.sharding import PartitionSpec as P

HD = 64
KVH = 4
WINDOW = 2048
PAGE = 128


def shifted(block, axis, distance):
    devices = range(lax.axis_size(axis))
    route = [(i - distance, i) for i in devices if i - distance in devices]
    return lax.ppermute(block, axis, route)


def swapped(value, axis, stride):
    return lax.ppermute(value, axis, [(i, i ^ 1 << stride) for i in range(lax.axis_size(axis))])


def rotate(values, positions):
    half_dim = HD // 2
    frequency = jnp.power(jnp.float32(10000.0), -jnp.arange(half_dim, dtype=jnp.float32) / half_dim)
    angles = positions.astype(jnp.float32)[:, None] * frequency[None, :]
    cosine = jnp.cos(angles)[:, None, :]
    sine_part = jnp.sin(angles)[:, None, :]
    front_half = values[..., :half_dim]
    back_half = values[..., half_dim:]
    return jnp.concatenate(
        [front_half * cosine - back_half * sine_part, back_half * cosine + front_half * sine_part],
        axis=-1,
    )


def attend(block_q, block_k, block_v, base_pos):
    query_count = block_q.shape[0]
    key_count = block_k.shape[0]
    scores = jnp.einsum(
        "tkgd,nkd->kgtn", block_q, block_k, preferred_element_type=jnp.float32
    ) * HD ** (-0.5)
    query_at = jnp.arange(query_count, dtype=jnp.int32)[:, None]
    key_at = jnp.arange(key_count, dtype=jnp.int32)[None, :]
    allowed = (key_at > query_at) & (key_at <= query_at + WINDOW) & (base_pos + key_at >= 0)
    masked = jnp.where(allowed, scores, jnp.float32(-1e30))
    row_top = jnp.max(masked, axis=-1, keepdims=True)
    weights = jnp.where(allowed, jnp.exp(masked - row_top), jnp.float32(0.0))
    row_total = jnp.sum(weights, axis=-1)
    rounded = weights.astype(jnp.bfloat16)
    mixed_rows = jnp.einsum("kgtn,nkd->tkgd", rounded, block_v, preferred_element_type=jnp.float32)
    mixed_rows = mixed_rows / jnp.transpose(row_total, (2, 0, 1))[..., None]
    return mixed_rows.astype(jnp.bfloat16).reshape(query_count, -1)


def shards(
    span_tokens, q_weight, kv_weight, out_weight, kv_pool, cache_lengths, slot_requests, page_table
):
    groups = lax.axis_size("group")
    seq_count = lax.axis_size("seq")
    tensor_count = lax.axis_size("tensor")
    group_id = lax.axis_index("group")
    seq_id = lax.axis_index("seq")
    tensor_id = lax.axis_index("tensor")
    local_reqs, seg_len, feat_local = span_tokens.shape
    head_cols = q_weight.shape[1]
    kv_cols = kv_weight.shape[1]
    local_heads = head_cols // HD
    group_heads = kv_cols // HD
    kv_local = max(1, KVH // tensor_count)
    per_kv = local_heads // kv_local
    head_first = tensor_id * KVH // tensor_count % group_heads
    holds_keys = tensor_id % 2 == 0
    pool_rows = kv_pool.shape[0]
    capacity = pool_rows // groups
    row_count = local_reqs * seg_len
    my_slots = group_id * local_reqs + jnp.arange(local_reqs, dtype=jnp.int32)
    my_requests = slot_requests[my_slots]
    my_lengths = cache_lengths[my_requests]
    project_piece_rows = lax.all_gather(span_tokens, "tensor", axis=2, tiled=True)
    feat_width = project_piece_rows.shape[2]
    flat_rows = project_piece_rows.reshape(row_count, feat_width)
    query_lin = jnp.dot(flat_rows, q_weight, preferred_element_type=jnp.float32)
    fresh_lin = jnp.dot(flat_rows, kv_weight, preferred_element_type=jnp.float32)
    positions = (
        my_lengths[:, None] + seq_id * seg_len + jnp.arange(seg_len, dtype=jnp.int32)[None, :]
    )
    queries = jax.vmap(rotate)(query_lin.reshape(local_reqs, seg_len, local_heads, HD), positions)
    queries = queries.astype(jnp.bfloat16).reshape(local_reqs, seg_len, kv_local, per_kv, HD)
    fresh_heads = fresh_lin.reshape(local_reqs, seg_len, group_heads, HD)
    rotated = jax.vmap(rotate)(fresh_heads, positions)
    span_kv = (
        jnp.where(holds_keys, rotated, fresh_heads)
        .astype(jnp.bfloat16)
        .reshape(local_reqs, seg_len, kv_cols)
    )
    all_ids = page_table[slot_requests]
    owned_here = all_ids // pool_rows == group_id
    slot_rank = jnp.cumsum(owned_here.astype(jnp.int32), axis=1) - 1
    local_rows = all_ids - group_id * pool_rows
    chosen = owned_here[:, :, None] & (
        slot_rank[:, :, None] == jnp.arange(capacity, dtype=jnp.int32)[None, None, :]
    )
    wanted = jnp.sum(jnp.where(chosen, local_rows[:, :, None], 0), axis=1)
    my_ids = page_table[my_requests].reshape(-1)
    my_owner = my_ids // pool_rows
    onehot = (my_owner[:, None] == jnp.arange(groups, dtype=jnp.int32)[None, :]).astype(jnp.int32)
    arrival = jnp.sum((jnp.cumsum(onehot, axis=0) - 1) * onehot, axis=1)
    arrived_row = my_owner * capacity + arrival
    outgoing = kv_pool[wanted]
    arrived = lax.all_to_all(outgoing, "group", split_axis=0, concat_axis=0, tiled=True)
    cached = arrived.reshape(groups * capacity, PAGE, kv_cols)[arrived_row]
    cached = cached.reshape(local_reqs, WINDOW, kv_cols)
    span_all = jnp.zeros((local_reqs, seg_len * seq_count, kv_cols), jnp.bfloat16)
    for back_step in range(seq_count - 1, -1, -1):
        piece_rows = span_kv if back_step == 0 else shifted(span_kv, "seq", back_step)
        span_all = lax.dynamic_update_slice_in_dim(
            span_all, piece_rows, (seq_id - back_step) * seg_len, 1
        )
    joined = jnp.concatenate([cached, span_all], axis=1)
    visible = lax.dynamic_slice_in_dim(joined, seq_id * seg_len, WINDOW + seg_len, 1)
    partner_rows = swapped(visible, "tensor", 0)
    key_all = jnp.where(holds_keys, visible, partner_rows).reshape(
        local_reqs, WINDOW + seg_len, group_heads, HD
    )
    value_all = jnp.where(holds_keys, partner_rows, visible).reshape(
        local_reqs, WINDOW + seg_len, group_heads, HD
    )
    key_rows = lax.dynamic_slice_in_dim(key_all, head_first, kv_local, 2)
    value_rows = lax.dynamic_slice_in_dim(value_all, head_first, kv_local, 2)
    block_len = min(128, seg_len)
    block_count = seg_len // block_len

    def per_request(request_items):
        request_q, request_k, request_v, length = request_items

        def per_block(block_index):
            first_row = block_index * block_len
            block_q = lax.dynamic_slice_in_dim(request_q, first_row, block_len, 0)
            block_k = lax.dynamic_slice_in_dim(request_k, first_row, WINDOW + block_len, 0)
            block_v = lax.dynamic_slice_in_dim(request_v, first_row, WINDOW + block_len, 0)
            return attend(block_q, block_k, block_v, length - WINDOW + seq_id * seg_len + first_row)

        return lax.map(per_block, jnp.arange(block_count, dtype=jnp.int32)).reshape(
            seg_len, head_cols
        )

    attended_heads = lax.map(per_request, (queries, key_rows, value_rows, my_lengths))
    flat_heads = attended_heads.reshape(row_count, head_cols)
    out_cols = out_weight.shape[1] // tensor_count
    summed = lax.psum_scatter(
        lax.dot_general(
            out_weight, flat_heads, (((0,), (1,)), ((), ())), preferred_element_type=jnp.float32
        ).astype(jnp.bfloat16),
        "tensor",
        scatter_dimension=0,
        tiled=True,
    ).astype(jnp.float32)
    result = summed.T
    return result.astype(jnp.bfloat16).reshape(local_reqs, seg_len, out_cols)


LOG2E = 1.4426950408889634
MASKED = -1e30
F32 = jnp.float32
BF16 = jnp.bfloat16
HBM = pl.BlockSpec(memory_space=pl.ANY)
VMEM = pl.BlockSpec(memory_space=pltpu.VMEM)
SMEM = pl.BlockSpec(memory_space=pltpu.SMEM)
STAYS = pl.BlockSpec(memory_space=pltpu.HBM)
GROUPS, SEQS, TENSORS = 4, 4, 2


def params(mebibytes):
    return pltpu.CompilerParams(vmem_limit_bytes=mebibytes * 2**20)


def cost(flops, moved):
    return pl.CostEstimate(flops=flops, bytes_accessed=moved, transcendentals=0)


class Info:
    def __init__(self, ref):
        self.ref = ref
        self.group, self.seq, self.tensor = ref[0, 0], ref[0, 1], ref[0, 2]
        self.window_pages = ref.shape[1]

    def request(self, slot):
        return self.ref[0, 3 + slot]

    def length(self, request):
        return self.ref[0, 3 + GROUPS + request]

    def page(self, request, w):
        return self.ref[1 + request, w]


def turned(x, cosine, sine):
    lane = lax.broadcasted_iota(jnp.int32, x.shape, 1)
    other = jnp.where(lane % HD < HD // 2, pltpu.roll(x, 128 - HD // 2, 1), pltpu.roll(x, HD // 2, 1))
    return x * cosine + other * sine


def open_kernel(
    info_ref, frequency, pool, x_hbm, wq_hbm, wkv_hbm,
    home, same, beyond, beside, across, diagonal, acc_q, acc_kv, cosine, sine,
    x, wq, wkv, sems, page_sems,
):
    info = Info(info_ref)
    rows, feats = x.shape
    here = pl.ds(pl.multiple_of(info.tensor * feats, feats), feats)
    copies = [
        pltpu.make_async_copy(x_hbm, x, sems.at[0]),
        pltpu.make_async_copy(wkv_hbm.at[here], wkv, sems.at[1]),
        pltpu.make_async_copy(wq_hbm.at[here], wq, sems.at[2]),
    ]
    for copy in copies:
        copy.start()
    pages = pool.shape[0]
    capacity = pages // GROUPS
    half = pool.shape[2] // 2
    mine = pl.ds(pl.multiple_of(info.tensor * half, half), half)
    theirs = pl.ds(pl.multiple_of((1 - info.tensor) * half, half), half)
    outs = (home, same, beyond, beside, across, diagonal)
    spots = (
        ((0, 0), (1, 0)),
        ((3, 0), (1, capacity)),
        ((2, 0), (4, 0)),
        ((2, capacity), (5, 0)),
    )
    for flip, targets in enumerate(spots):
        request = info.request(info.group ^ flip)

        def take(w, rank):
            page = info.page(request, w)
            near = page // pages == info.group

            @pl.when(near)
            def _():
                row = page % pages
                for (out, base), cols in zip(targets, (mine, theirs)):
                    pltpu.make_async_copy(
                        pool.at[row, :, cols], outs[out].at[base + rank], page_sems.at[out]
                    ).start()

            return rank + near.astype(jnp.int32)

        lax.fori_loop(0, info.window_pages, take, jnp.int32(0))
    start = info.length(info.request(info.group)) + info.seq * rows
    position = (start + lax.broadcasted_iota(jnp.int32, (rows, 128), 0)).astype(F32)
    angles = position * frequency[0:1, :]
    lane = lax.broadcasted_iota(jnp.int32, (rows, 128), 1)
    cosine[...] = jnp.cos(angles)
    sine[...] = jnp.where(lane % HD < HD // 2, -1.0, 1.0) * jnp.sin(angles)
    copies[0].wait()
    copies[1].wait()
    acc_kv[...] = jnp.dot(x[...], wkv[...], preferred_element_type=F32)
    copies[2].wait()
    acc_q[...] = jnp.dot(x[...], wq[...], preferred_element_type=F32)
    for i, out in enumerate(outs):
        pltpu.make_async_copy(out, out, page_sems.at[i]).wait()


def open_rows(info, frequency, pool, x, wq, wkv):
    rows, feats = x.shape
    pages, page, cols = pool.shape
    single = jax.ShapeDtypeStruct((pages // GROUPS, page, cols // 2), BF16)
    double = jax.ShapeDtypeStruct((2 * pages // GROUPS, page, cols // 2), BF16)
    table = jax.ShapeDtypeStruct((rows, 128), F32)
    return pl.pallas_call(
        open_kernel,
        out_shape=[
            single,
            double,
            double,
            single,
            single,
            single,
            jax.ShapeDtypeStruct((rows, wq.shape[1]), F32),
            jax.ShapeDtypeStruct((rows, wkv.shape[1]), F32),
            table,
            table,
        ],
        in_specs=[SMEM, VMEM] + [STAYS] * 4,
        out_specs=[VMEM] * 10,
        scratch_shapes=[
            pltpu.VMEM((rows, feats), BF16),
            pltpu.VMEM((feats, wq.shape[1]), BF16),
            pltpu.VMEM((feats, wkv.shape[1]), BF16),
            pltpu.SemaphoreType.DMA((3,)),
            pltpu.SemaphoreType.DMA((6,)),
        ],
        compiler_params=params(52),
        cost_estimate=cost(rows * feats, rows * feats),
    )(info, frequency, pool, x, wq, wkv)


def fresh_kernel(info_ref, x, wkv, acc_kv, cosine, sine, kept, sent):
    info = Info(info_ref)
    feats = x.shape[1]
    here = pl.ds(pl.multiple_of((1 - info.tensor) * feats, feats), feats)
    keys = info.tensor == 0
    fresh = acc_kv[...] + jnp.dot(x[...], wkv[here], preferred_element_type=F32)
    cos_kv = jnp.where(keys, cosine[...], 1.0)
    sin_kv = jnp.where(keys, sine[...], 0.0)
    low = turned(fresh[:, :128], cos_kv, sin_kv).astype(BF16)
    high = turned(fresh[:, 128:], cos_kv, sin_kv).astype(BF16)
    kept[...] = jnp.where(keys, low, high)
    sent[...] = jnp.where(keys, high, low)


def fresh_rows(info, x, wkv, acc_kv, cosine, sine):
    rows, feats = x.shape
    piece = jax.ShapeDtypeStruct((rows, wkv.shape[1] // 2), BF16)
    return pl.pallas_call(
        fresh_kernel,
        out_shape=[piece, piece],
        in_specs=[SMEM] + [VMEM] * 5,
        out_specs=[VMEM] * 2,
        compiler_params=params(12),
        cost_estimate=cost(2 * rows * feats * 2560, rows * feats),
    )(info, x, wkv, acc_kv, cosine, sine)


def query_kernel(info_ref, x, wq, acc_q, cosine, sine, q):
    feats = x.shape[1]
    here = pl.ds(pl.multiple_of((1 - Info(info_ref).tensor) * feats, feats), feats)
    cos_all, sin_all = cosine[...], sine[...]
    scale = HD**-0.5 * LOG2E
    tile = 256
    for c in range(0, q.shape[1], tile):
        lin = acc_q[:, c : c + tile] + jnp.dot(
            x[...], wq[here, c : c + tile], preferred_element_type=F32
        )
        for e in range(0, tile, 128):
            q[:, c + e : c + e + 128] = (
                turned(lin[:, e : e + 128], cos_all, sin_all) * scale
            ).astype(BF16)


def query_rows(info, x, wq, acc_q, cosine, sine):
    rows, feats = x.shape
    return pl.pallas_call(
        query_kernel,
        out_shape=jax.ShapeDtypeStruct((rows, wq.shape[1]), BF16),
        in_specs=[SMEM] + [VMEM] * 5,
        out_specs=VMEM,
        compiler_params=params(16),
        cost_estimate=cost(rows * feats, rows * feats),
    )(info, x, wq, acc_q, cosine, sine)


def soft_heads(q, tokens, keys, values, span, mask, emit):
    rows = tokens.stop - tokens.start
    stack = 4
    lane = lax.broadcasted_iota(jnp.int32, (rows, 2 * HD), 1)
    low = lane < HD

    def swap(x):
        return pltpu.roll(x, HD, 1)

    def heads(i, _):
        first = i == 0
        value = values.at[i]
        spots = [pl.ds(pl.multiple_of((i * stack + j) * 128, 128), 128) for j in range(stack)]
        tiles = [q[tokens, spot] for spot in spots]
        turns = [swap(x.astype(F32)).astype(BF16) for x in tiles]
        keep = low == first

        def stacked(a, b):
            zero = jnp.zeros_like(a[0])
            return jnp.concatenate(
                [jnp.where(keep, jnp.where(first, x, y), zero) for x, y in zip(a, b)], axis=0
            )

        def scores(qs):
            s = lax.dot_general(
                qs, keys[span], (((1,), (1,)), ((), ())), preferred_element_type=F32
            )
            return mask(s)

        s_even = scores(stacked(tiles, turns))
        s_odd = scores(stacked(turns, tiles))
        m_even = jnp.max(s_even, axis=1, keepdims=True)
        m_odd = jnp.max(s_odd, axis=1, keepdims=True)
        p_even = jnp.exp2(s_even - m_even).astype(BF16)
        p_odd = jnp.exp2(s_odd - m_odd).astype(BF16)
        o_even = jnp.dot(p_even, value[span], preferred_element_type=F32)
        o_odd = jnp.dot(p_odd, value[span], preferred_element_type=F32)
        for j in range(stack):
            part = slice(j * rows, (j + 1) * rows)
            a, b = o_even[part], o_odd[part]
            total = jnp.where(low, a, swap(b))
            weight = jnp.where(low, swap(a), b)
            top = jnp.where(low, m_even[part], m_odd[part])
            emit(spots[j], total, weight, top)
        return 0

    lax.fori_loop(0, q.shape[1] // 128 // stack, heads, 0)


def bundle_kernel(*refs):
    out = refs[-1]
    at = 0
    for ref in refs[:-1]:
        out[at : at + ref.shape[0]] = ref[...]
        at += ref.shape[0]


def bundled(*parts):
    count = sum(part.shape[0] for part in parts)
    return pl.pallas_call(
        bundle_kernel,
        out_shape=jax.ShapeDtypeStruct((count, *parts[0].shape[1:]), BF16),
        in_specs=[VMEM] * len(parts),
        out_specs=VMEM,
        compiler_params=params(8),
        cost_estimate=cost(20 * 10**9, 4 * count),
    )(*parts)


def widen(v, ones, values, here):
    low = lax.broadcasted_iota(jnp.int32, v.shape, 1) < HD
    values[0, here] = jnp.where(low, v, ones).astype(BF16)
    values[1, here] = jnp.where(low, pltpu.roll(v, HD, 1), ones).astype(BF16)


def gather_kernel(info_ref, own, other, fresh, keys, values, source):
    info = Info(info_ref)
    group, seq = info.group, info.seq
    request = info.request(group)
    rows = fresh.shape[1]
    per = rows // PAGE
    count = own.shape[0]
    capacity = count // GROUPS
    seen = keys.shape[0] // PAGE - seq * per
    is_key = info.tensor == 0

    def note(w, counts):
        came = info.page(request, w) // count ^ group
        place = came * capacity
        for d in range(GROUPS):
            place = place + jnp.where(came == d, counts[d], 0)
        source[w] = place
        return tuple(counts[d] + (came == d).astype(jnp.int32) for d in range(GROUPS))

    lax.fori_loop(0, info.window_pages, note, (jnp.int32(0),) * GROUPS)

    def place(block, a, b):
        here = pl.ds(pl.multiple_of(block * PAGE, PAGE), PAGE)
        keys[here] = jnp.where(is_key, a, b)
        widen(jnp.where(is_key, b, a).astype(F32), 1.0, values, here)

    for block, part in ((1, slice(0, PAGE)), (seen - 1, slice(PAGE, 2 * PAGE))):
        place(block, fresh[0, part], fresh[1, part])
    first = info.length(request) - WINDOW + seq * rows

    def bring(n, _):
        block = jnp.where(n == 0, 0, n + 1)
        at = source[seq * per + n]
        before = first + n * PAGE < 0

        @pl.when(before)
        def _():
            here = pl.ds(pl.multiple_of(block * PAGE, PAGE), PAGE)
            stand_in = keys[PAGE : PAGE + 16].astype(F32)[0:1]
            keys[here] = jnp.broadcast_to(stand_in, (PAGE, 2 * HD)).astype(BF16)
            widen(jnp.zeros((PAGE, 2 * HD), F32), 0.0, values, here)

        @pl.when(jnp.logical_not(before))
        def _():
            place(block, own[at], other[at])

        return 0

    lax.fori_loop(0, seen - per, bring, 0)


def gather_rows(info, own, other, fresh):
    span = WINDOW + fresh.shape[1]
    return pl.pallas_call(
        gather_kernel,
        out_shape=[
            jax.ShapeDtypeStruct((span, 2 * HD), BF16),
            jax.ShapeDtypeStruct((2, span, 2 * HD), BF16),
        ],
        in_specs=[SMEM] + [VMEM] * 3,
        out_specs=[VMEM] * 2,
        scratch_shapes=[pltpu.SMEM((own.shape[0],), jnp.int32)],
        compiler_params=params(12),
        cost_estimate=cost(20 * 10**9, 4 * span),
    )(info, own, other, fresh)


def bundle_kernel(a, b, out):
    out[: a.shape[0]] = a[...]
    out[a.shape[0] :] = b[...]


def bundled(a, b):
    return pl.pallas_call(
        bundle_kernel,
        out_shape=jax.ShapeDtypeStruct((a.shape[0] + b.shape[0], *a.shape[1:]), BF16),
        in_specs=[VMEM] * 2,
        out_specs=VMEM,
        compiler_params=params(8),
        cost_estimate=cost(6 * 10**9, 4),
    )(a, b)


def near_kernel(info_ref, q, keys, values, total, weight, top, *, half):
    seq = Info(info_ref).seq
    rows = q.shape[0]
    blocks = keys.shape[0] // PAGE
    per = rows // PAGE
    tokens = slice(half * PAGE, (half + 1) * PAGE)
    stack = 4
    query_at = lax.broadcasted_iota(jnp.int32, (stack * PAGE, PAGE), 0) % PAGE
    key_at = lax.broadcasted_iota(jnp.int32, (stack * PAGE, PAGE), 1)
    newer = key_at > query_at

    def emit(spot, o, l, m):
        total[:, spot] = o
        weight[:, spot] = l
        top[:, spot] = m

    for k in range(SEQS):
        span = slice(half * PAGE, (blocks - k * per - 1 + half) * PAGE)

        def mask(s):
            if half == 0:
                parts = [
                    jnp.where(newer, s[:, :PAGE], MASKED),
                    jnp.where(newer, MASKED, s[:, PAGE : 2 * PAGE]),
                    s[:, 2 * PAGE :],
                ]
            else:
                parts = [
                    s[:, :PAGE],
                    jnp.where(newer, s[:, PAGE : 2 * PAGE], MASKED),
                    s[:, 2 * PAGE : -PAGE],
                    jnp.where(newer, MASKED, s[:, -PAGE:]),
                ]
            return jnp.concatenate(parts, axis=1)

        @pl.when(seq == k)
        def _(span=span):
            soft_heads(q, tokens, keys, values, span, mask, emit)


def attend_near(info, q, keys, values, half):
    state = jax.ShapeDtypeStruct((PAGE, q.shape[1]), F32)
    return pl.pallas_call(
        functools.partial(near_kernel, half=half),
        out_shape=[state] * 3,
        in_specs=[SMEM] + [VMEM] * 3,
        out_specs=[VMEM] * 3,
        compiler_params=params(32),
        cost_estimate=cost(PAGE * WINDOW, 4 * WINDOW),
    )(info, q, keys, values)


def far_kernel(
    info_ref, q, total, weight, top, z1, z2, z3, w, heads_out, partial, keys, values, *, half
):
    info = Info(info_ref)
    rows = q.shape[0]
    seq = info.seq
    zs = (None, z1, z2, z3)
    is_key = info.tensor == 0
    tokens = slice(half * PAGE, (half + 1) * PAGE)

    for k in range(SEQS):

        @pl.when(seq == k)
        def _(k=k):
            if k == 0:
                heads_out[...] = (total[...] / weight[...]).astype(BF16)
                return
            for n in range(k):
                z = zs[n ^ k]
                here = slice(n * rows, (n + 1) * rows)
                a, b = z[0], z[1]
                keys[here] = jnp.where(is_key, a, b)
                widen(jnp.where(is_key, b, a).astype(F32), 1.0, values, here)

            def emit(spot, o, l, m):
                before = top[:, spot]
                peak = jnp.maximum(before, m)
                a = jnp.exp2(before - peak)
                b = jnp.exp2(m - peak)
                done = (total[:, spot] * a + o * b) / (weight[:, spot] * a + l * b)
                heads_out[:, spot] = done.astype(BF16)

            soft_heads(q, tokens, keys, values, slice(0, k * rows), lambda s: s, emit)

    cols = partial.shape[1]
    here = pl.ds(pl.multiple_of((1 - info.tensor) * cols, cols), cols)
    partial[...] = jnp.dot(heads_out[...], w[:, here], preferred_element_type=F32).astype(BF16)


def attend_far(info, q, state, zs, w, half):
    rows = q.shape[0]
    span = (SEQS - 1) * rows
    return pl.pallas_call(
        functools.partial(far_kernel, half=half),
        out_shape=[
            jax.ShapeDtypeStruct((PAGE, q.shape[1]), BF16),
            jax.ShapeDtypeStruct((PAGE, w.shape[1] // TENSORS), BF16),
        ],
        in_specs=[SMEM] + [VMEM] * 8,
        out_specs=[VMEM] * 2,
        scratch_shapes=[
            pltpu.VMEM((span, 2 * HD), BF16),
            pltpu.VMEM((2, span, 2 * HD), BF16),
        ],
        compiler_params=params(24),
        cost_estimate=cost(rows * span, 4 * span),
    )(info, q, *state, *zs, w)


def home_kernel(info_ref, x1, x2, away, w, out, home, first, sem):
    rows, cols = home.shape
    here = pl.ds(pl.multiple_of(Info(info_ref).tensor * cols, cols), cols)
    x = jnp.concatenate([x1[...], x2[...]], axis=0)
    o = jnp.dot(x, w[:, here], preferred_element_type=F32).astype(BF16)
    home[...] = o[rows:]
    first[...] = (o[:rows].astype(F32) + away[...].astype(F32)).astype(BF16)
    copy = pltpu.make_async_copy(first, out.at[pl.ds(0, rows)], sem)
    copy.start()
    copy.wait()


def home_project(info, x1, x2, away, w):
    rows, depth = x1.shape
    cols = w.shape[1] // TENSORS
    return pl.pallas_call(
        home_kernel,
        out_shape=[
            jax.ShapeDtypeStruct((2 * rows, cols), BF16),
            jax.ShapeDtypeStruct((rows, cols), BF16),
        ],
        in_specs=[SMEM] + [VMEM] * 4,
        out_specs=[STAYS, VMEM],
        scratch_shapes=[pltpu.VMEM((rows, cols), BF16), pltpu.SemaphoreType.DMA],
        compiler_params=params(16),
        cost_estimate=cost(20 * 10**9, 2 * depth * cols),
    )(info, x1, x2, away, w)


def add_kernel(before, a, b, out, last, sem):
    rows = a.shape[0]
    last[...] = (a[...].astype(F32) + b[...].astype(F32)).astype(BF16)
    copy = pltpu.make_async_copy(last, out.at[pl.ds(rows, rows)], sem)
    copy.start()
    copy.wait()


def added(before, a, b):
    return pl.pallas_call(
        add_kernel,
        out_shape=jax.ShapeDtypeStruct(before.shape, BF16),
        in_specs=[STAYS, VMEM, VMEM],
        out_specs=STAYS,
        scratch_shapes=[pltpu.VMEM(a.shape, BF16), pltpu.SemaphoreType.DMA],
        input_output_aliases={0: 0},
        compiler_params=params(8),
    )(before, a, b)


def flipped(value, axes, count, bits):
    return lax.ppermute(value, axes, [(i, i ^ bits) for i in range(count)])


def after(value, *others):
    return lax.optimization_barrier((value, *others))[0]


def shards_fast(
    span_tokens, q_weight, kv_weight, out_weight, kv_pool, cache_lengths, slot_requests, page_table
):
    group_id = lax.axis_index("group")
    seq_id = lax.axis_index("seq")
    tensor_id = lax.axis_index("tensor")
    place = jnp.stack([group_id, seq_id, tensor_id]).astype(jnp.int32)
    row = jnp.concatenate([place, slot_requests, cache_lengths])
    row = jnp.pad(row, (0, page_table.shape[1] - row.shape[0]))
    info = jnp.concatenate([row[None], page_table])
    mine = span_tokens[0]
    theirs = flipped(mine, "tensor", 2, 1)
    half_dim = HD // 2
    lane = jnp.arange(128, dtype=jnp.int32) % half_dim
    frequency = jnp.power(jnp.float32(10000.0), -lane.astype(F32) / half_dim)
    frequency = jnp.broadcast_to(frequency[None, :], (8, 128))
    pages = open_rows(info, frequency, kv_pool, mine, q_weight, kv_weight)
    home, same, beyond, beside, across, diagonal = pages[:6]
    acc_q, acc_kv, cosine, sine = pages[6:]
    capacity = home.shape[0]
    same = flipped(same, "tensor", 2, 1)
    beyond = flipped(beyond, "group", 4, 2)
    kept, sent = fresh_rows(info, theirs, kv_weight, acc_kv, cosine, sine)
    got = flipped(sent, "tensor", 2, 1)
    across, diagonal, _ = lax.optimization_barrier((across, diagonal, sent))
    across = flipped(across, ("group", "tensor"), 8, 5)
    diagonal = flipped(diagonal, ("group", "tensor"), 8, 7)
    q = query_rows(info, theirs, q_weight, acc_q, cosine, sine)
    same, beyond, _ = lax.optimization_barrier((same, beyond, sent))
    mate = jnp.concatenate([beside, beyond[capacity:], same[capacity:]])
    mate = flipped(mate, "group", 4, 1)
    fresh = bundled(kept[None], got[None])
    zs = [flipped(fresh, "seq", 4, d) for d in range(1, 4)]
    other_chip = bundled(across, diagonal)
    own = jnp.concatenate(
        [home, mate[:capacity], beyond[:capacity], mate[capacity : 2 * capacity]]
    )
    other = jnp.concatenate([same[:capacity], mate[2 * capacity :], other_chip])
    keys, values = gather_rows(info, own, other, fresh)
    state = attend_near(info, q, keys, values, 0)
    heads_0, partial_0 = attend_far(info, q, state, zs, out_weight, 0)
    away_0 = flipped(partial_0, "tensor", 2, 1)
    state = attend_near(after(info, partial_0), q, keys, values, 1)
    heads_1, partial_1 = attend_far(info, q, state, zs, out_weight, 1)
    away_1 = flipped(partial_1, "tensor", 2, 1)
    out, home_1 = home_project(info, heads_0, heads_1, away_0, out_weight)
    return added(out, home_1, away_1)[None]


def solution(mesh):
    sizes = tuple(mesh.shape[a] for a in ("group", "seq", "tensor"))
    body = shards_fast if sizes == (GROUPS, SEQS, TENSORS) else shards
    placed = (
        P("group", "seq", "tensor"),
        P(None, "tensor"),
        P(None, "tensor"),
        P("tensor", None),
        P("group", None, "tensor"),
        P(),
        P(),
        P(),
    )
    return jax.shard_map(
        body, mesh=mesh, in_specs=placed, out_specs=P("group", "seq", "tensor"), check_vma=False
    )
```

```python
import functools

import jax
import jax.numpy as jnp
from jax import lax
from jax.experimental import pallas as pl
from jax.experimental.pallas import tpu as pltpu
from jax.sharding import PartitionSpec as P

HD = 64
KVH = 4
WINDOW = 2048
PAGE = 128


def shifted(block, axis, distance):
    devices = range(lax.axis_size(axis))
    route = [(i - distance, i) for i in devices if i - distance in devices]
    return lax.ppermute(block, axis, route)


def swapped(value, axis, stride):
    return lax.ppermute(value, axis, [(i, i ^ 1 << stride) for i in range(lax.axis_size(axis))])


def rotate(values, positions):
    half_dim = HD // 2
    frequency = jnp.power(jnp.float32(10000.0), -jnp.arange(half_dim, dtype=jnp.float32) / half_dim)
    angles = positions.astype(jnp.float32)[:, None] * frequency[None, :]
    cosine = jnp.cos(angles)[:, None, :]
    sine_part = jnp.sin(angles)[:, None, :]
    front_half = values[..., :half_dim]
    back_half = values[..., half_dim:]
    return jnp.concatenate(
        [front_half * cosine - back_half * sine_part, back_half * cosine + front_half * sine_part],
        axis=-1,
    )


def attend(block_q, block_k, block_v, base_pos):
    query_count = block_q.shape[0]
    key_count = block_k.shape[0]
    scores = jnp.einsum(
        "tkgd,nkd->kgtn", block_q, block_k, preferred_element_type=jnp.float32
    ) * HD ** (-0.5)
    query_at = jnp.arange(query_count, dtype=jnp.int32)[:, None]
    key_at = jnp.arange(key_count, dtype=jnp.int32)[None, :]
    allowed = (key_at > query_at) & (key_at <= query_at + WINDOW) & (base_pos + key_at >= 0)
    masked = jnp.where(allowed, scores, jnp.float32(-1e30))
    row_top = jnp.max(masked, axis=-1, keepdims=True)
    weights = jnp.where(allowed, jnp.exp(masked - row_top), jnp.float32(0.0))
    row_total = jnp.sum(weights, axis=-1)
    rounded = weights.astype(jnp.bfloat16)
    mixed_rows = jnp.einsum("kgtn,nkd->tkgd", rounded, block_v, preferred_element_type=jnp.float32)
    mixed_rows = mixed_rows / jnp.transpose(row_total, (2, 0, 1))[..., None]
    return mixed_rows.astype(jnp.bfloat16).reshape(query_count, -1)


def shards(
    span_tokens, q_weight, kv_weight, out_weight, kv_pool, cache_lengths, slot_requests, page_table
):
    groups = lax.axis_size("group")
    seq_count = lax.axis_size("seq")
    tensor_count = lax.axis_size("tensor")
    group_id = lax.axis_index("group")
    seq_id = lax.axis_index("seq")
    tensor_id = lax.axis_index("tensor")
    local_reqs, seg_len, feat_local = span_tokens.shape
    head_cols = q_weight.shape[1]
    kv_cols = kv_weight.shape[1]
    local_heads = head_cols // HD
    group_heads = kv_cols // HD
    kv_local = max(1, KVH // tensor_count)
    per_kv = local_heads // kv_local
    head_first = tensor_id * KVH // tensor_count % group_heads
    holds_keys = tensor_id % 2 == 0
    pool_rows = kv_pool.shape[0]
    capacity = pool_rows // groups
    row_count = local_reqs * seg_len
    my_slots = group_id * local_reqs + jnp.arange(local_reqs, dtype=jnp.int32)
    my_requests = slot_requests[my_slots]
    my_lengths = cache_lengths[my_requests]
    project_piece_rows = lax.all_gather(span_tokens, "tensor", axis=2, tiled=True)
    feat_width = project_piece_rows.shape[2]
    flat_rows = project_piece_rows.reshape(row_count, feat_width)
    query_lin = jnp.dot(flat_rows, q_weight, preferred_element_type=jnp.float32)
    fresh_lin = jnp.dot(flat_rows, kv_weight, preferred_element_type=jnp.float32)
    positions = (
        my_lengths[:, None] + seq_id * seg_len + jnp.arange(seg_len, dtype=jnp.int32)[None, :]
    )
    queries = jax.vmap(rotate)(query_lin.reshape(local_reqs, seg_len, local_heads, HD), positions)
    queries = queries.astype(jnp.bfloat16).reshape(local_reqs, seg_len, kv_local, per_kv, HD)
    fresh_heads = fresh_lin.reshape(local_reqs, seg_len, group_heads, HD)
    rotated = jax.vmap(rotate)(fresh_heads, positions)
    span_kv = (
        jnp.where(holds_keys, rotated, fresh_heads)
        .astype(jnp.bfloat16)
        .reshape(local_reqs, seg_len, kv_cols)
    )
    all_ids = page_table[slot_requests]
    owned_here = all_ids // pool_rows == group_id
    slot_rank = jnp.cumsum(owned_here.astype(jnp.int32), axis=1) - 1
    local_rows = all_ids - group_id * pool_rows
    chosen = owned_here[:, :, None] & (
        slot_rank[:, :, None] == jnp.arange(capacity, dtype=jnp.int32)[None, None, :]
    )
    wanted = jnp.sum(jnp.where(chosen, local_rows[:, :, None], 0), axis=1)
    my_ids = page_table[my_requests].reshape(-1)
    my_owner = my_ids // pool_rows
    onehot = (my_owner[:, None] == jnp.arange(groups, dtype=jnp.int32)[None, :]).astype(jnp.int32)
    arrival = jnp.sum((jnp.cumsum(onehot, axis=0) - 1) * onehot, axis=1)
    arrived_row = my_owner * capacity + arrival
    outgoing = kv_pool[wanted]
    arrived = lax.all_to_all(outgoing, "group", split_axis=0, concat_axis=0, tiled=True)
    cached = arrived.reshape(groups * capacity, PAGE, kv_cols)[arrived_row]
    cached = cached.reshape(local_reqs, WINDOW, kv_cols)
    span_all = jnp.zeros((local_reqs, seg_len * seq_count, kv_cols), jnp.bfloat16)
    for back_step in range(seq_count - 1, -1, -1):
        piece_rows = span_kv if back_step == 0 else shifted(span_kv, "seq", back_step)
        span_all = lax.dynamic_update_slice_in_dim(
            span_all, piece_rows, (seq_id - back_step) * seg_len, 1
        )
    joined = jnp.concatenate([cached, span_all], axis=1)
    visible = lax.dynamic_slice_in_dim(joined, seq_id * seg_len, WINDOW + seg_len, 1)
    partner_rows = swapped(visible, "tensor", 0)
    key_all = jnp.where(holds_keys, visible, partner_rows).reshape(
        local_reqs, WINDOW + seg_len, group_heads, HD
    )
    value_all = jnp.where(holds_keys, partner_rows, visible).reshape(
        local_reqs, WINDOW + seg_len, group_heads, HD
    )
    key_rows = lax.dynamic_slice_in_dim(key_all, head_first, kv_local, 2)
    value_rows = lax.dynamic_slice_in_dim(value_all, head_first, kv_local, 2)
    block_len = min(128, seg_len)
    block_count = seg_len // block_len

    def per_request(request_items):
        request_q, request_k, request_v, length = request_items

        def per_block(block_index):
            first_row = block_index * block_len
            block_q = lax.dynamic_slice_in_dim(request_q, first_row, block_len, 0)
            block_k = lax.dynamic_slice_in_dim(request_k, first_row, WINDOW + block_len, 0)
            block_v = lax.dynamic_slice_in_dim(request_v, first_row, WINDOW + block_len, 0)
            return attend(block_q, block_k, block_v, length - WINDOW + seq_id * seg_len + first_row)

        return lax.map(per_block, jnp.arange(block_count, dtype=jnp.int32)).reshape(
            seg_len, head_cols
        )

    attended_heads = lax.map(per_request, (queries, key_rows, value_rows, my_lengths))
    flat_heads = attended_heads.reshape(row_count, head_cols)
    out_cols = out_weight.shape[1] // tensor_count
    summed = lax.psum_scatter(
        lax.dot_general(
            out_weight, flat_heads, (((0,), (1,)), ((), ())), preferred_element_type=jnp.float32
        ).astype(jnp.bfloat16),
        "tensor",
        scatter_dimension=0,
        tiled=True,
    ).astype(jnp.float32)
    result = summed.T
    return result.astype(jnp.bfloat16).reshape(local_reqs, seg_len, out_cols)


LOG2E = 1.4426950408889634
MASKED = -1e30
F32 = jnp.float32
BF16 = jnp.bfloat16
HBM = pl.BlockSpec(memory_space=pl.ANY)
VMEM = pl.BlockSpec(memory_space=pltpu.VMEM)
SMEM = pl.BlockSpec(memory_space=pltpu.SMEM)
STAYS = pl.BlockSpec(memory_space=pltpu.HBM)
GROUPS, SEQS, TENSORS = 4, 4, 2


def params(mebibytes):
    return pltpu.CompilerParams(vmem_limit_bytes=mebibytes * 2**20)


def cost(flops, moved):
    return pl.CostEstimate(flops=flops, bytes_accessed=moved, transcendentals=0)


class Info:
    def __init__(self, ref):
        self.ref = ref
        self.group, self.seq, self.tensor = ref[0, 0], ref[0, 1], ref[0, 2]
        self.window_pages = ref.shape[1]

    def request(self, slot):
        return self.ref[0, 3 + slot]

    def length(self, request):
        return self.ref[0, 3 + GROUPS + request]

    def page(self, request, w):
        return self.ref[1 + request, w]


def turned(x, cosine, sine):
    lane = lax.broadcasted_iota(jnp.int32, x.shape, 1)
    other = jnp.where(lane % HD < HD // 2, pltpu.roll(x, 128 - HD // 2, 1), pltpu.roll(x, HD // 2, 1))
    return x * cosine + other * sine


def open_kernel(
    info_ref, frequency, pool, x_hbm, wq_hbm, wkv_hbm,
    home, same, beyond, beside, across, diagonal, acc_q, acc_kv, cosine, sine,
    x, wq, wkv, sems, page_sems,
):
    info = Info(info_ref)
    rows, feats = x.shape
    here = pl.ds(pl.multiple_of(info.tensor * feats, feats), feats)
    copies = [
        pltpu.make_async_copy(x_hbm, x, sems.at[0]),
        pltpu.make_async_copy(wkv_hbm.at[here], wkv, sems.at[1]),
        pltpu.make_async_copy(wq_hbm.at[here], wq, sems.at[2]),
    ]
    for copy in copies:
        copy.start()
    pages = pool.shape[0]
    capacity = pages // GROUPS
    half = pool.shape[2] // 2
    mine = pl.ds(pl.multiple_of(info.tensor * half, half), half)
    theirs = pl.ds(pl.multiple_of((1 - info.tensor) * half, half), half)
    outs = (home, same, beyond, beside, across, diagonal)
    spots = (
        ((0, 0), (1, 0)),
        ((3, 0), (1, capacity)),
        ((2, 0), (4, 0)),
        ((2, capacity), (5, 0)),
    )
    for flip, targets in enumerate(spots):
        request = info.request(info.group ^ flip)

        def take(w, rank):
            page = info.page(request, w)
            near = page // pages == info.group

            @pl.when(near)
            def _():
                row = page % pages
                for (out, base), cols in zip(targets, (mine, theirs)):
                    pltpu.make_async_copy(
                        pool.at[row, :, cols], outs[out].at[base + rank], page_sems.at[out]
                    ).start()

            return rank + near.astype(jnp.int32)

        lax.fori_loop(0, info.window_pages, take, jnp.int32(0))
    start = info.length(info.request(info.group)) + info.seq * rows
    position = (start + lax.broadcasted_iota(jnp.int32, (rows, 128), 0)).astype(F32)
    angles = position * frequency[0:1, :]
    lane = lax.broadcasted_iota(jnp.int32, (rows, 128), 1)
    cosine[...] = jnp.cos(angles)
    sine[...] = jnp.where(lane % HD < HD // 2, -1.0, 1.0) * jnp.sin(angles)
    copies[0].wait()
    copies[1].wait()
    acc_kv[...] = jnp.dot(x[...], wkv[...], preferred_element_type=F32)
    copies[2].wait()
    acc_q[...] = jnp.dot(x[...], wq[...], preferred_element_type=F32)
    for i, out in enumerate(outs):
        pltpu.make_async_copy(out, out, page_sems.at[i]).wait()


def open_rows(info, frequency, pool, x, wq, wkv):
    rows, feats = x.shape
    pages, page, cols = pool.shape
    single = jax.ShapeDtypeStruct((pages // GROUPS, page, cols // 2), BF16)
    double = jax.ShapeDtypeStruct((2 * pages // GROUPS, page, cols // 2), BF16)
    table = jax.ShapeDtypeStruct((rows, 128), F32)
    return pl.pallas_call(
        open_kernel,
        out_shape=[
            single,
            double,
            double,
            single,
            single,
            single,
            jax.ShapeDtypeStruct((rows, wq.shape[1]), F32),
            jax.ShapeDtypeStruct((rows, wkv.shape[1]), F32),
            table,
            table,
        ],
        in_specs=[SMEM, VMEM] + [STAYS] * 4,
        out_specs=[VMEM] * 10,
        scratch_shapes=[
            pltpu.VMEM((rows, feats), BF16),
            pltpu.VMEM((feats, wq.shape[1]), BF16),
            pltpu.VMEM((feats, wkv.shape[1]), BF16),
            pltpu.SemaphoreType.DMA((3,)),
            pltpu.SemaphoreType.DMA((6,)),
        ],
        compiler_params=params(52),
        cost_estimate=cost(rows * feats, rows * feats),
    )(info, frequency, pool, x, wq, wkv)


def fresh_kernel(info_ref, x, wkv, acc_kv, cosine, sine, kept, sent):
    info = Info(info_ref)
    feats = x.shape[1]
    here = pl.ds(pl.multiple_of((1 - info.tensor) * feats, feats), feats)
    keys = info.tensor == 0
    fresh = acc_kv[...] + jnp.dot(x[...], wkv[here], preferred_element_type=F32)
    cos_kv = jnp.where(keys, cosine[...], 1.0)
    sin_kv = jnp.where(keys, sine[...], 0.0)
    low = turned(fresh[:, :128], cos_kv, sin_kv).astype(BF16)
    high = turned(fresh[:, 128:], cos_kv, sin_kv).astype(BF16)
    kept[...] = jnp.where(keys, low, high)
    sent[...] = jnp.where(keys, high, low)


def fresh_rows(info, x, wkv, acc_kv, cosine, sine):
    rows, feats = x.shape
    piece = jax.ShapeDtypeStruct((rows, wkv.shape[1] // 2), BF16)
    return pl.pallas_call(
        fresh_kernel,
        out_shape=[piece, piece],
        in_specs=[SMEM] + [VMEM] * 5,
        out_specs=[VMEM] * 2,
        compiler_params=params(12),
        cost_estimate=cost(2 * rows * feats * 2560, rows * feats),
    )(info, x, wkv, acc_kv, cosine, sine)


def query_kernel(info_ref, x, wq, acc_q, cosine, sine, q):
    feats = x.shape[1]
    here = pl.ds(pl.multiple_of((1 - Info(info_ref).tensor) * feats, feats), feats)
    cos_all, sin_all = cosine[...], sine[...]
    scale = HD**-0.5 * LOG2E
    tile = 256
    for c in range(0, q.shape[1], tile):
        lin = acc_q[:, c : c + tile] + jnp.dot(
            x[...], wq[here, c : c + tile], preferred_element_type=F32
        )
        for e in range(0, tile, 128):
            q[:, c + e : c + e + 128] = (
                turned(lin[:, e : e + 128], cos_all, sin_all) * scale
            ).astype(BF16)


def query_rows(info, x, wq, acc_q, cosine, sine):
    rows, feats = x.shape
    return pl.pallas_call(
        query_kernel,
        out_shape=jax.ShapeDtypeStruct((rows, wq.shape[1]), BF16),
        in_specs=[SMEM] + [VMEM] * 5,
        out_specs=VMEM,
        compiler_params=params(16),
        cost_estimate=cost(rows * feats, rows * feats),
    )(info, x, wq, acc_q, cosine, sine)


def soft_heads(q, tokens, segments, emit):
    rows = tokens.stop - tokens.start
    stack = 4
    low = lax.broadcasted_iota(jnp.int32, (rows, 2 * HD), 1) < HD

    def swap(x):
        return pltpu.roll(x, HD, 1)

    def heads(i, _):
        first = i == 0
        spots = [pl.ds(pl.multiple_of((i * stack + j) * 128, 128), 128) for j in range(stack)]
        tiles = [q[tokens, spot] for spot in spots]
        turns = [swap(x.astype(F32)).astype(BF16) for x in tiles]
        keep = low == first

        def stacked(a, b):
            zero = jnp.zeros_like(a[0])
            return jnp.concatenate(
                [jnp.where(keep, jnp.where(first, x, y), zero) for x, y in zip(a, b)], axis=0
            )

        def scores(qs):
            return [
                mask(
                    lax.dot_general(
                        qs, keys[span], (((1,), (1,)), ((), ())), preferred_element_type=F32
                    )
                )
                for keys, _, span, mask in segments
            ]

        def peak(parts):
            tops = [jnp.max(s, axis=1, keepdims=True) for s in parts]
            return functools.reduce(jnp.maximum, tops)

        def mixed(weights):
            return sum(
                jnp.dot(p, values[i, span], preferred_element_type=F32)
                for p, (_, values, span, _) in zip(weights, segments)
            )

        s_even = scores(stacked(tiles, turns))
        s_odd = scores(stacked(turns, tiles))
        m_even = peak(s_even)
        m_odd = peak(s_odd)
        p_even = [jnp.exp2(s - m_even).astype(BF16) for s in s_even]
        p_odd = [jnp.exp2(s - m_odd).astype(BF16) for s in s_odd]
        o_even = mixed(p_even)
        o_odd = mixed(p_odd)
        for j in range(stack):
            part = slice(j * rows, (j + 1) * rows)
            a, b = o_even[part], o_odd[part]
            total = jnp.where(low, a, swap(b))
            weight = jnp.where(low, swap(a), b)
            top = jnp.where(low, m_even[part], m_odd[part])
            emit(spots[j], total, weight, top)
        return 0

    lax.fori_loop(0, q.shape[1] // 128 // stack, heads, 0)


def widen(v, ones, values, here):
    low = lax.broadcasted_iota(jnp.int32, v.shape, 1) < HD
    values[0, here] = jnp.where(low, v, ones).astype(BF16)
    values[1, here] = jnp.where(low, pltpu.roll(v, HD, 1), ones).astype(BF16)


def gather_kernel(info_ref, own, other, fresh, keys, values, source):
    info = Info(info_ref)
    group, seq = info.group, info.seq
    request = info.request(group)
    rows = fresh.shape[1]
    per = rows // PAGE
    count = own.shape[0]
    capacity = count // GROUPS
    seen = keys.shape[0] // PAGE - seq * per
    is_key = info.tensor == 0

    def note(w, counts):
        came = info.page(request, w) // count ^ group
        place = came * capacity
        for d in range(GROUPS):
            place = place + jnp.where(came == d, counts[d], 0)
        source[w] = place
        return tuple(counts[d] + (came == d).astype(jnp.int32) for d in range(GROUPS))

    lax.fori_loop(0, info.window_pages, note, (jnp.int32(0),) * GROUPS)

    def place(block, a, b):
        here = pl.ds(pl.multiple_of(block * PAGE, PAGE), PAGE)
        keys[here] = jnp.where(is_key, a, b)
        widen(jnp.where(is_key, b, a).astype(F32), 1.0, values, here)

    for block, part in ((1, slice(0, PAGE)), (seen - 1, slice(PAGE, 2 * PAGE))):
        place(block, fresh[0, part], fresh[1, part])
    first = info.length(request) - WINDOW + seq * rows
    stand_in = jnp.where(is_key, fresh[0, :16], fresh[1, :16]).astype(F32)[0:1]
    stand_in = jnp.broadcast_to(stand_in, (PAGE, 2 * HD)).astype(BF16)

    def bring(i, _):
        for n in (2 * i, 2 * i + 1):
            block = jnp.where(n == 0, 0, n + 1)
            here = pl.ds(pl.multiple_of(block * PAGE, PAGE), PAGE)
            at = source[seq * per + n]
            hidden = first + n * PAGE < 0
            a, b = own[at], other[at]
            keys[here] = jnp.where(hidden, stand_in, jnp.where(is_key, a, b))
            v = jnp.where(is_key, b, a).astype(F32)
            widen(jnp.where(hidden, 0.0, v), jnp.where(hidden, 0.0, 1.0), values, here)
        return 0

    lax.fori_loop(0, (seen - per) // 2, bring, 0)


def gather_rows(info, own, other, fresh):
    span = WINDOW + fresh.shape[1]
    return pl.pallas_call(
        gather_kernel,
        out_shape=[
            jax.ShapeDtypeStruct((span, 2 * HD), BF16),
            jax.ShapeDtypeStruct((2, span, 2 * HD), BF16),
        ],
        in_specs=[SMEM] + [VMEM] * 3,
        out_specs=[VMEM] * 2,
        scratch_shapes=[pltpu.SMEM((own.shape[0],), jnp.int32)],
        compiler_params=params(12),
        cost_estimate=cost(20 * 10**9, 4 * span),
    )(info, own, other, fresh)


def bundle_kernel(a, b, out):
    out[: a.shape[0]] = a[...]
    out[a.shape[0] :] = b[...]


def bundled(a, b):
    return pl.pallas_call(
        bundle_kernel,
        out_shape=jax.ShapeDtypeStruct((a.shape[0] + b.shape[0], *a.shape[1:]), BF16),
        in_specs=[VMEM] * 2,
        out_specs=VMEM,
        compiler_params=params(8),
        cost_estimate=cost(6 * 10**9, 4),
    )(a, b)


def near_segment(keys, values, seq, half):
    blocks = keys.shape[0] // PAGE
    per = 2
    span = slice(half * PAGE, (blocks - seq * per - 1 + half) * PAGE)

    def mask(s):
        newer = lax.broadcasted_iota(jnp.int32, (s.shape[0], PAGE), 1) > (
            lax.broadcasted_iota(jnp.int32, (s.shape[0], PAGE), 0) % PAGE
        )
        if half == 0:
            parts = [
                jnp.where(newer, s[:, :PAGE], MASKED),
                jnp.where(newer, MASKED, s[:, PAGE : 2 * PAGE]),
                s[:, 2 * PAGE :],
            ]
        else:
            parts = [
                s[:, :PAGE],
                jnp.where(newer, s[:, PAGE : 2 * PAGE], MASKED),
                s[:, 2 * PAGE : -PAGE],
                jnp.where(newer, MASKED, s[:, -PAGE:]),
            ]
        return jnp.concatenate(parts, axis=1)

    return keys, values, span, mask


def far_segment(keys, values, seq):
    return keys, values, slice(0, seq * 2 * PAGE), lambda s: s


def near_kernel(info_ref, q, keys, values, total, weight, top):
    seq = Info(info_ref).seq

    def emit(spot, o, l, m):
        total[:, spot] = o
        weight[:, spot] = l
        top[:, spot] = m

    for k in range(SEQS):

        @pl.when(seq == k)
        def _(k=k):
            soft_heads(q, slice(0, PAGE), [near_segment(keys, values, k, 0)], emit)


def attend_near(info, q, keys, values):
    state = jax.ShapeDtypeStruct((PAGE, q.shape[1]), F32)
    return pl.pallas_call(
        near_kernel,
        out_shape=[state] * 3,
        in_specs=[SMEM] + [VMEM] * 3,
        out_specs=[VMEM] * 3,
        compiler_params=params(32),
        cost_estimate=cost(PAGE * WINDOW, 4 * WINDOW),
    )(info, q, keys, values)


def partner_product(info, heads_out, w, partial):
    cols = partial.shape[1]
    here = pl.ds(pl.multiple_of((1 - info.tensor) * cols, cols), cols)
    partial[...] = jnp.dot(heads_out[...], w[:, here], preferred_element_type=F32).astype(BF16)


def far_kernel(
    info_ref, q, total, weight, top, z1, z2, z3, w, heads_out, partial, keys, values
):
    info = Info(info_ref)
    rows = q.shape[0]
    seq = info.seq
    zs = (None, z1, z2, z3)
    is_key = info.tensor == 0

    for k in range(SEQS):

        @pl.when(seq == k)
        def _(k=k):
            if k == 0:
                heads_out[...] = (total[...] / weight[...]).astype(BF16)
                return
            for n in range(k):
                z = zs[n ^ k]
                here = slice(n * rows, (n + 1) * rows)
                a, b = z[0], z[1]
                keys[here] = jnp.where(is_key, a, b)
                widen(jnp.where(is_key, b, a).astype(F32), 1.0, values, here)

            def emit(spot, o, l, m):
                before = top[:, spot]
                peak = jnp.maximum(before, m)
                a = jnp.exp2(before - peak)
                b = jnp.exp2(m - peak)
                done = (total[:, spot] * a + o * b) / (weight[:, spot] * a + l * b)
                heads_out[:, spot] = done.astype(BF16)

            soft_heads(q, slice(0, PAGE), [far_segment(keys, values, k)], emit)

    partner_product(info, heads_out, w, partial)


def attend_far(info, q, state, zs, w):
    rows = q.shape[0]
    span = (SEQS - 1) * rows
    return pl.pallas_call(
        far_kernel,
        out_shape=[
            jax.ShapeDtypeStruct((PAGE, q.shape[1]), BF16),
            jax.ShapeDtypeStruct((PAGE, w.shape[1] // TENSORS), BF16),
            jax.ShapeDtypeStruct((span, 2 * HD), BF16),
            jax.ShapeDtypeStruct((2, span, 2 * HD), BF16),
        ],
        in_specs=[SMEM] + [VMEM] * 8,
        out_specs=[VMEM] * 4,
        compiler_params=params(24),
        cost_estimate=cost(rows * span, 4 * span),
    )(info, q, *state, *zs, w)


def last_kernel(info_ref, q, keys, values, far_keys, far_values, w, heads_out, partial):
    info = Info(info_ref)

    def emit(spot, o, l, m):
        heads_out[:, spot] = (o / l).astype(BF16)

    for k in range(SEQS):

        @pl.when(info.seq == k)
        def _(k=k):
            segments = [near_segment(keys, values, k, 1)]
            if k:
                segments.append(far_segment(far_keys, far_values, k))
            soft_heads(q, slice(PAGE, 2 * PAGE), segments, emit)

    partner_product(info, heads_out, w, partial)


def attend_last(info, q, keys, values, far_keys, far_values, w):
    return pl.pallas_call(
        last_kernel,
        out_shape=[
            jax.ShapeDtypeStruct((PAGE, q.shape[1]), BF16),
            jax.ShapeDtypeStruct((PAGE, w.shape[1] // TENSORS), BF16),
        ],
        in_specs=[SMEM] + [VMEM] * 6,
        out_specs=[VMEM] * 2,
        compiler_params=params(36),
        cost_estimate=cost(PAGE * WINDOW, 4 * WINDOW),
    )(info, q, keys, values, far_keys, far_values, w)


def home_kernel(info_ref, x1, x2, away, w, out, home, first, sem):
    rows, cols = home.shape
    here = pl.ds(pl.multiple_of(Info(info_ref).tensor * cols, cols), cols)
    x = jnp.concatenate([x1[...], x2[...]], axis=0)
    o = jnp.dot(x, w[:, here], preferred_element_type=F32).astype(BF16)
    home[...] = o[rows:]
    first[...] = (o[:rows].astype(F32) + away[...].astype(F32)).astype(BF16)
    copy = pltpu.make_async_copy(first, out.at[pl.ds(0, rows)], sem)
    copy.start()
    copy.wait()


def home_project(info, x1, x2, away, w):
    rows, depth = x1.shape
    cols = w.shape[1] // TENSORS
    return pl.pallas_call(
        home_kernel,
        out_shape=[
            jax.ShapeDtypeStruct((2 * rows, cols), BF16),
            jax.ShapeDtypeStruct((rows, cols), BF16),
        ],
        in_specs=[SMEM] + [VMEM] * 4,
        out_specs=[STAYS, VMEM],
        scratch_shapes=[pltpu.VMEM((rows, cols), BF16), pltpu.SemaphoreType.DMA],
        compiler_params=params(16),
        cost_estimate=cost(20 * 10**9, 2 * depth * cols),
    )(info, x1, x2, away, w)


def add_kernel(before, a, b, out, last, sem):
    rows = a.shape[0]
    last[...] = (a[...].astype(F32) + b[...].astype(F32)).astype(BF16)
    copy = pltpu.make_async_copy(last, out.at[pl.ds(rows, rows)], sem)
    copy.start()
    copy.wait()


def added(before, a, b):
    return pl.pallas_call(
        add_kernel,
        out_shape=jax.ShapeDtypeStruct(before.shape, BF16),
        in_specs=[STAYS, VMEM, VMEM],
        out_specs=STAYS,
        scratch_shapes=[pltpu.VMEM(a.shape, BF16), pltpu.SemaphoreType.DMA],
        input_output_aliases={0: 0},
        compiler_params=params(8),
    )(before, a, b)


def flipped(value, axes, count, bits):
    return lax.ppermute(value, axes, [(i, i ^ bits) for i in range(count)])


def after(value, *others):
    return lax.optimization_barrier((value, *others))[0]


def shards_fast(
    span_tokens, q_weight, kv_weight, out_weight, kv_pool, cache_lengths, slot_requests, page_table
):
    group_id = lax.axis_index("group")
    seq_id = lax.axis_index("seq")
    tensor_id = lax.axis_index("tensor")
    place = jnp.stack([group_id, seq_id, tensor_id]).astype(jnp.int32)
    row = jnp.concatenate([place, slot_requests, cache_lengths])
    row = jnp.pad(row, (0, page_table.shape[1] - row.shape[0]))
    info = jnp.concatenate([row[None], page_table])
    mine = span_tokens[0]
    theirs = flipped(mine, "tensor", 2, 1)
    half_dim = HD // 2
    lane = jnp.arange(128, dtype=jnp.int32) % half_dim
    frequency = jnp.power(jnp.float32(10000.0), -lane.astype(F32) / half_dim)
    frequency = jnp.broadcast_to(frequency[None, :], (8, 128))
    pages = open_rows(info, frequency, kv_pool, mine, q_weight, kv_weight)
    home, same, beyond, beside, across, diagonal = pages[:6]
    acc_q, acc_kv, cosine, sine = pages[6:]
    capacity = home.shape[0]
    same = flipped(same, "tensor", 2, 1)
    beyond = flipped(beyond, "group", 4, 2)
    kept, sent = fresh_rows(info, theirs, kv_weight, acc_kv, cosine, sine)
    got = flipped(sent, "tensor", 2, 1)
    across, diagonal, _ = lax.optimization_barrier((across, diagonal, sent))
    across = flipped(across, ("group", "tensor"), 8, 5)
    diagonal = flipped(diagonal, ("group", "tensor"), 8, 7)
    q = query_rows(info, theirs, q_weight, acc_q, cosine, sine)
    same, beyond, _ = lax.optimization_barrier((same, beyond, sent))
    mate = jnp.concatenate([beside, beyond[capacity:], same[capacity:]])
    mate = flipped(mate, "group", 4, 1)
    fresh = bundled(kept[None], got[None])
    zs = [flipped(fresh, "seq", 4, d) for d in range(1, 4)]
    other_chip = bundled(across, diagonal)
    own = jnp.concatenate(
        [home, mate[:capacity], beyond[:capacity], mate[capacity : 2 * capacity]]
    )
    other = jnp.concatenate([same[:capacity], mate[2 * capacity :], other_chip])
    keys, values = gather_rows(info, own, other, fresh)
    state = attend_near(info, q, keys, values)
    heads_0, partial_0, far_keys, far_values = attend_far(info, q, state, zs, out_weight)
    away_0 = flipped(partial_0, "tensor", 2, 1)
    heads_1, partial_1 = attend_last(info, q, keys, values, far_keys, far_values, out_weight)
    away_1 = flipped(partial_1, "tensor", 2, 1)
    out, home_1 = home_project(info, heads_0, heads_1, away_0, out_weight)
    return added(out, home_1, away_1)[None]


def solution(mesh):
    sizes = tuple(mesh.shape[a] for a in ("group", "seq", "tensor"))
    body = shards_fast if sizes == (GROUPS, SEQS, TENSORS) else shards
    placed = (
        P("group", "seq", "tensor"),
        P(None, "tensor"),
        P(None, "tensor"),
        P("tensor", None),
        P("group", None, "tensor"),
        P(),
        P(),
        P(),
    )
    return jax.shard_map(
        body, mesh=mesh, in_specs=placed, out_specs=P("group", "seq", "tensor"), check_vma=False
    )
```

```python
import functools

import jax
import jax.numpy as jnp
from jax import lax
from jax.experimental import pallas as pl
from jax.experimental.pallas import tpu as pltpu
from jax.sharding import PartitionSpec as P

HD = 64
KVH = 4
WINDOW = 2048
PAGE = 128


def shifted(block, axis, distance):
    devices = range(lax.axis_size(axis))
    route = [(i - distance, i) for i in devices if i - distance in devices]
    return lax.ppermute(block, axis, route)


def swapped(value, axis, stride):
    return lax.ppermute(value, axis, [(i, i ^ 1 << stride) for i in range(lax.axis_size(axis))])


def rotate(values, positions):
    half_dim = HD // 2
    frequency = jnp.power(jnp.float32(10000.0), -jnp.arange(half_dim, dtype=jnp.float32) / half_dim)
    angles = positions.astype(jnp.float32)[:, None] * frequency[None, :]
    cosine = jnp.cos(angles)[:, None, :]
    sine_part = jnp.sin(angles)[:, None, :]
    front_half = values[..., :half_dim]
    back_half = values[..., half_dim:]
    return jnp.concatenate(
        [front_half * cosine - back_half * sine_part, back_half * cosine + front_half * sine_part],
        axis=-1,
    )


def attend(block_q, block_k, block_v, base_pos):
    query_count = block_q.shape[0]
    key_count = block_k.shape[0]
    scores = jnp.einsum(
        "tkgd,nkd->kgtn", block_q, block_k, preferred_element_type=jnp.float32
    ) * HD ** (-0.5)
    query_at = jnp.arange(query_count, dtype=jnp.int32)[:, None]
    key_at = jnp.arange(key_count, dtype=jnp.int32)[None, :]
    allowed = (key_at > query_at) & (key_at <= query_at + WINDOW) & (base_pos + key_at >= 0)
    masked = jnp.where(allowed, scores, jnp.float32(-1e30))
    row_top = jnp.max(masked, axis=-1, keepdims=True)
    weights = jnp.where(allowed, jnp.exp(masked - row_top), jnp.float32(0.0))
    row_total = jnp.sum(weights, axis=-1)
    rounded = weights.astype(jnp.bfloat16)
    mixed_rows = jnp.einsum("kgtn,nkd->tkgd", rounded, block_v, preferred_element_type=jnp.float32)
    mixed_rows = mixed_rows / jnp.transpose(row_total, (2, 0, 1))[..., None]
    return mixed_rows.astype(jnp.bfloat16).reshape(query_count, -1)


def shards(
    span_tokens, q_weight, kv_weight, out_weight, kv_pool, cache_lengths, slot_requests, page_table
):
    groups = lax.axis_size("group")
    seq_count = lax.axis_size("seq")
    tensor_count = lax.axis_size("tensor")
    group_id = lax.axis_index("group")
    seq_id = lax.axis_index("seq")
    tensor_id = lax.axis_index("tensor")
    local_reqs, seg_len, feat_local = span_tokens.shape
    head_cols = q_weight.shape[1]
    kv_cols = kv_weight.shape[1]
    local_heads = head_cols // HD
    group_heads = kv_cols // HD
    kv_local = max(1, KVH // tensor_count)
    per_kv = local_heads // kv_local
    head_first = tensor_id * KVH // tensor_count % group_heads
    holds_keys = tensor_id % 2 == 0
    pool_rows = kv_pool.shape[0]
    capacity = pool_rows // groups
    row_count = local_reqs * seg_len
    my_slots = group_id * local_reqs + jnp.arange(local_reqs, dtype=jnp.int32)
    my_requests = slot_requests[my_slots]
    my_lengths = cache_lengths[my_requests]
    project_piece_rows = lax.all_gather(span_tokens, "tensor", axis=2, tiled=True)
    feat_width = project_piece_rows.shape[2]
    flat_rows = project_piece_rows.reshape(row_count, feat_width)
    query_lin = jnp.dot(flat_rows, q_weight, preferred_element_type=jnp.float32)
    fresh_lin = jnp.dot(flat_rows, kv_weight, preferred_element_type=jnp.float32)
    positions = (
        my_lengths[:, None] + seq_id * seg_len + jnp.arange(seg_len, dtype=jnp.int32)[None, :]
    )
    queries = jax.vmap(rotate)(query_lin.reshape(local_reqs, seg_len, local_heads, HD), positions)
    queries = queries.astype(jnp.bfloat16).reshape(local_reqs, seg_len, kv_local, per_kv, HD)
    fresh_heads = fresh_lin.reshape(local_reqs, seg_len, group_heads, HD)
    rotated = jax.vmap(rotate)(fresh_heads, positions)
    span_kv = (
        jnp.where(holds_keys, rotated, fresh_heads)
        .astype(jnp.bfloat16)
        .reshape(local_reqs, seg_len, kv_cols)
    )
    all_ids = page_table[slot_requests]
    owned_here = all_ids // pool_rows == group_id
    slot_rank = jnp.cumsum(owned_here.astype(jnp.int32), axis=1) - 1
    local_rows = all_ids - group_id * pool_rows
    chosen = owned_here[:, :, None] & (
        slot_rank[:, :, None] == jnp.arange(capacity, dtype=jnp.int32)[None, None, :]
    )
    wanted = jnp.sum(jnp.where(chosen, local_rows[:, :, None], 0), axis=1)
    my_ids = page_table[my_requests].reshape(-1)
    my_owner = my_ids // pool_rows
    onehot = (my_owner[:, None] == jnp.arange(groups, dtype=jnp.int32)[None, :]).astype(jnp.int32)
    arrival = jnp.sum((jnp.cumsum(onehot, axis=0) - 1) * onehot, axis=1)
    arrived_row = my_owner * capacity + arrival
    outgoing = kv_pool[wanted]
    arrived = lax.all_to_all(outgoing, "group", split_axis=0, concat_axis=0, tiled=True)
    cached = arrived.reshape(groups * capacity, PAGE, kv_cols)[arrived_row]
    cached = cached.reshape(local_reqs, WINDOW, kv_cols)
    span_all = jnp.zeros((local_reqs, seg_len * seq_count, kv_cols), jnp.bfloat16)
    for back_step in range(seq_count - 1, -1, -1):
        piece_rows = span_kv if back_step == 0 else shifted(span_kv, "seq", back_step)
        span_all = lax.dynamic_update_slice_in_dim(
            span_all, piece_rows, (seq_id - back_step) * seg_len, 1
        )
    joined = jnp.concatenate([cached, span_all], axis=1)
    visible = lax.dynamic_slice_in_dim(joined, seq_id * seg_len, WINDOW + seg_len, 1)
    partner_rows = swapped(visible, "tensor", 0)
    key_all = jnp.where(holds_keys, visible, partner_rows).reshape(
        local_reqs, WINDOW + seg_len, group_heads, HD
    )
    value_all = jnp.where(holds_keys, partner_rows, visible).reshape(
        local_reqs, WINDOW + seg_len, group_heads, HD
    )
    key_rows = lax.dynamic_slice_in_dim(key_all, head_first, kv_local, 2)
    value_rows = lax.dynamic_slice_in_dim(value_all, head_first, kv_local, 2)
    block_len = min(128, seg_len)
    block_count = seg_len // block_len

    def per_request(request_items):
        request_q, request_k, request_v, length = request_items

        def per_block(block_index):
            first_row = block_index * block_len
            block_q = lax.dynamic_slice_in_dim(request_q, first_row, block_len, 0)
            block_k = lax.dynamic_slice_in_dim(request_k, first_row, WINDOW + block_len, 0)
            block_v = lax.dynamic_slice_in_dim(request_v, first_row, WINDOW + block_len, 0)
            return attend(block_q, block_k, block_v, length - WINDOW + seq_id * seg_len + first_row)

        return lax.map(per_block, jnp.arange(block_count, dtype=jnp.int32)).reshape(
            seg_len, head_cols
        )

    attended_heads = lax.map(per_request, (queries, key_rows, value_rows, my_lengths))
    flat_heads = attended_heads.reshape(row_count, head_cols)
    out_cols = out_weight.shape[1] // tensor_count
    summed = lax.psum_scatter(
        lax.dot_general(
            out_weight, flat_heads, (((0,), (1,)), ((), ())), preferred_element_type=jnp.float32
        ).astype(jnp.bfloat16),
        "tensor",
        scatter_dimension=0,
        tiled=True,
    ).astype(jnp.float32)
    result = summed.T
    return result.astype(jnp.bfloat16).reshape(local_reqs, seg_len, out_cols)


LOG2E = 1.4426950408889634
MASKED = -1e30
F32 = jnp.float32
BF16 = jnp.bfloat16
HBM = pl.BlockSpec(memory_space=pl.ANY)
VMEM = pl.BlockSpec(memory_space=pltpu.VMEM)
SMEM = pl.BlockSpec(memory_space=pltpu.SMEM)
STAYS = pl.BlockSpec(memory_space=pltpu.HBM)
GROUPS, SEQS, TENSORS = 4, 4, 2


def params(mebibytes):
    return pltpu.CompilerParams(vmem_limit_bytes=mebibytes * 2**20)


def cost(flops, moved):
    return pl.CostEstimate(flops=flops, bytes_accessed=moved, transcendentals=0)


class Info:
    def __init__(self, ref):
        self.ref = ref
        self.group, self.seq, self.tensor = ref[0, 0], ref[0, 1], ref[0, 2]
        self.window_pages = ref.shape[1]

    def request(self, slot):
        return self.ref[0, 3 + slot]

    def length(self, request):
        return self.ref[0, 3 + GROUPS + request]

    def page(self, request, w):
        return self.ref[1 + request, w]


def turned(x, cosine, sine):
    lane = lax.broadcasted_iota(jnp.int32, x.shape, 1)
    other = jnp.where(lane % HD < HD // 2, pltpu.roll(x, 128 - HD // 2, 1), pltpu.roll(x, HD // 2, 1))
    return x * cosine + other * sine


def open_kernel(
    info_ref, frequency, pool, x_hbm, wq_hbm, wkv_hbm,
    home, same, beyond, beside, across, diagonal, acc_q, acc_kv, cosine, sine,
    x, wq, wkv, sems, page_sems,
):
    info = Info(info_ref)
    rows, feats = x.shape
    here = pl.ds(pl.multiple_of(info.tensor * feats, feats), feats)
    copies = [
        pltpu.make_async_copy(x_hbm, x, sems.at[0]),
        pltpu.make_async_copy(wkv_hbm.at[here], wkv, sems.at[1]),
        pltpu.make_async_copy(wq_hbm.at[here], wq, sems.at[2]),
    ]
    for copy in copies:
        copy.start()
    pages = pool.shape[0]
    capacity = pages // GROUPS
    half = pool.shape[2] // 2
    mine = pl.ds(pl.multiple_of(info.tensor * half, half), half)
    theirs = pl.ds(pl.multiple_of((1 - info.tensor) * half, half), half)
    outs = (home, same, beyond, beside, across, diagonal)
    spots = (
        ((0, 0), (1, 0)),
        ((3, 0), (1, capacity)),
        ((2, 0), (4, 0)),
        ((2, capacity), (5, 0)),
    )
    for flip, targets in enumerate(spots):
        request = info.request(info.group ^ flip)

        def take(w, rank):
            page = info.page(request, w)
            near = page // pages == info.group

            @pl.when(near)
            def _():
                row = page % pages
                for (out, base), cols in zip(targets, (mine, theirs)):
                    pltpu.make_async_copy(
                        pool.at[row, :, cols], outs[out].at[base + rank], page_sems.at[out]
                    ).start()

            return rank + near.astype(jnp.int32)

        lax.fori_loop(0, info.window_pages, take, jnp.int32(0))
    start = info.length(info.request(info.group)) + info.seq * rows
    position = (start + lax.broadcasted_iota(jnp.int32, (rows, 128), 0)).astype(F32)
    angles = position * frequency[0:1, :]
    lane = lax.broadcasted_iota(jnp.int32, (rows, 128), 1)
    cosine[...] = jnp.cos(angles)
    sine[...] = jnp.where(lane % HD < HD // 2, -1.0, 1.0) * jnp.sin(angles)
    copies[0].wait()
    copies[1].wait()
    acc_kv[...] = jnp.dot(x[...], wkv[...], preferred_element_type=F32)
    copies[2].wait()
    acc_q[...] = jnp.dot(x[...], wq[...], preferred_element_type=F32)
    for i, out in enumerate(outs):
        pltpu.make_async_copy(out, out, page_sems.at[i]).wait()


def open_rows(info, frequency, pool, x, wq, wkv):
    rows, feats = x.shape
    pages, page, cols = pool.shape
    single = jax.ShapeDtypeStruct((pages // GROUPS, page, cols // 2), BF16)
    double = jax.ShapeDtypeStruct((2 * pages // GROUPS, page, cols // 2), BF16)
    table = jax.ShapeDtypeStruct((rows, 128), F32)
    return pl.pallas_call(
        open_kernel,
        out_shape=[
            single,
            double,
            double,
            single,
            single,
            single,
            jax.ShapeDtypeStruct((rows, wq.shape[1]), F32),
            jax.ShapeDtypeStruct((rows, wkv.shape[1]), F32),
            table,
            table,
        ],
        in_specs=[SMEM, VMEM] + [STAYS] * 4,
        out_specs=[VMEM] * 10,
        scratch_shapes=[
            pltpu.VMEM((rows, feats), BF16),
            pltpu.VMEM((feats, wq.shape[1]), BF16),
            pltpu.VMEM((feats, wkv.shape[1]), BF16),
            pltpu.SemaphoreType.DMA((3,)),
            pltpu.SemaphoreType.DMA((6,)),
        ],
        compiler_params=params(52),
        cost_estimate=cost(rows * feats, rows * feats),
    )(info, frequency, pool, x, wq, wkv)


def fresh_kernel(info_ref, x, wkv, acc_kv, cosine, sine, kept, sent):
    info = Info(info_ref)
    feats = x.shape[1]
    here = pl.ds(pl.multiple_of((1 - info.tensor) * feats, feats), feats)
    keys = info.tensor == 0
    fresh = acc_kv[...] + jnp.dot(x[...], wkv[here], preferred_element_type=F32)
    cos_kv = jnp.where(keys, cosine[...], 1.0)
    sin_kv = jnp.where(keys, sine[...], 0.0)
    low = turned(fresh[:, :128], cos_kv, sin_kv).astype(BF16)
    high = turned(fresh[:, 128:], cos_kv, sin_kv).astype(BF16)
    kept[...] = jnp.where(keys, low, high)
    sent[...] = jnp.where(keys, high, low)


def fresh_rows(info, x, wkv, acc_kv, cosine, sine):
    rows, feats = x.shape
    piece = jax.ShapeDtypeStruct((rows, wkv.shape[1] // 2), BF16)
    return pl.pallas_call(
        fresh_kernel,
        out_shape=[piece, piece],
        in_specs=[SMEM] + [VMEM] * 5,
        out_specs=[VMEM] * 2,
        compiler_params=params(12),
        cost_estimate=cost(2 * rows * feats * 2560, rows * feats),
    )(info, x, wkv, acc_kv, cosine, sine)


def query_kernel(info_ref, x, wq, acc_q, cosine, sine, q):
    feats = x.shape[1]
    here = pl.ds(pl.multiple_of((1 - Info(info_ref).tensor) * feats, feats), feats)
    cos_all, sin_all = cosine[...], sine[...]
    scale = HD**-0.5 * LOG2E
    tile = 256
    for c in range(0, q.shape[1], tile):
        lin = acc_q[:, c : c + tile] + jnp.dot(
            x[...], wq[here, c : c + tile], preferred_element_type=F32
        )
        for e in range(0, tile, 128):
            q[:, c + e : c + e + 128] = (
                turned(lin[:, e : e + 128], cos_all, sin_all) * scale
            ).astype(BF16)


def query_rows(info, x, wq, acc_q, cosine, sine):
    rows, feats = x.shape
    return pl.pallas_call(
        query_kernel,
        out_shape=jax.ShapeDtypeStruct((rows, wq.shape[1]), BF16),
        in_specs=[SMEM] + [VMEM] * 5,
        out_specs=VMEM,
        compiler_params=params(16),
        cost_estimate=cost(rows * feats, rows * feats),
    )(info, x, wq, acc_q, cosine, sine)


def soft_heads(q, tokens, segments, emit):
    rows = tokens.stop - tokens.start
    stack = 4
    low = lax.broadcasted_iota(jnp.int32, (rows, 2 * HD), 1) < HD

    def swap(x):
        return pltpu.roll(x, HD, 1)

    def heads(i, _):
        first = i == 0
        spots = [pl.ds(pl.multiple_of((i * stack + j) * 128, 128), 128) for j in range(stack)]
        tiles = [q[tokens, spot] for spot in spots]
        turns = [swap(x.astype(F32)).astype(BF16) for x in tiles]
        keep = low == first

        def stacked(a, b):
            zero = jnp.zeros_like(a[0])
            return jnp.concatenate(
                [jnp.where(keep, jnp.where(first, x, y), zero) for x, y in zip(a, b)], axis=0
            )

        def scores(qs):
            return [
                mask(
                    lax.dot_general(
                        qs, keys[span], (((1,), (1,)), ((), ())), preferred_element_type=F32
                    )
                )
                for keys, _, span, mask in segments
            ]

        def peak(parts):
            tops = [jnp.max(s, axis=1, keepdims=True) for s in parts]
            return functools.reduce(jnp.maximum, tops)

        def mixed(weights):
            return sum(
                jnp.dot(p, values[i, span], preferred_element_type=F32)
                for p, (_, values, span, _) in zip(weights, segments)
            )

        s_even = scores(stacked(tiles, turns))
        s_odd = scores(stacked(turns, tiles))
        m_even = peak(s_even)
        m_odd = peak(s_odd)
        p_even = [jnp.exp2(s - m_even).astype(BF16) for s in s_even]
        p_odd = [jnp.exp2(s - m_odd).astype(BF16) for s in s_odd]
        o_even = mixed(p_even)
        o_odd = mixed(p_odd)
        for j in range(stack):
            part = slice(j * rows, (j + 1) * rows)
            a, b = o_even[part], o_odd[part]
            total = jnp.where(low, a, swap(b))
            weight = jnp.where(low, swap(a), b)
            top = jnp.where(low, m_even[part], m_odd[part])
            emit(spots[j], total, weight, top)
        return 0

    lax.fori_loop(0, q.shape[1] // 128 // stack, heads, 0)


def widen(v, ones, values, here):
    low = lax.broadcasted_iota(jnp.int32, v.shape, 1) < HD
    values[0, here] = jnp.where(low, v, ones).astype(BF16)
    values[1, here] = jnp.where(low, pltpu.roll(v, HD, 1), ones).astype(BF16)


def gather_kernel(info_ref, own, other, fresh, keys, values, source):
    info = Info(info_ref)
    group, seq = info.group, info.seq
    request = info.request(group)
    rows = fresh.shape[1]
    per = rows // PAGE
    count = own.shape[0]
    capacity = count // GROUPS
    seen = keys.shape[0] // PAGE - seq * per
    is_key = info.tensor == 0

    def note(w, counts):
        came = info.page(request, w) // count ^ group
        place = came * capacity
        for d in range(GROUPS):
            place = place + jnp.where(came == d, counts[d], 0)
        source[w] = place
        return tuple(counts[d] + (came == d).astype(jnp.int32) for d in range(GROUPS))

    lax.fori_loop(0, info.window_pages, note, (jnp.int32(0),) * GROUPS)

    def place(block, a, b):
        here = pl.ds(pl.multiple_of(block * PAGE, PAGE), PAGE)
        keys[here] = jnp.where(is_key, a, b)
        widen(jnp.where(is_key, b, a).astype(F32), 1.0, values, here)

    for block, part in ((1, slice(0, PAGE)), (seen - 1, slice(PAGE, 2 * PAGE))):
        place(block, fresh[0, part], fresh[1, part])
    first = info.length(request) - WINDOW + seq * rows
    stand_in = jnp.where(is_key, fresh[0, :16], fresh[1, :16]).astype(F32)[0:1]
    stand_in = jnp.broadcast_to(stand_in, (PAGE, 2 * HD)).astype(BF16)

    def bring(i, _):
        for n in (2 * i, 2 * i + 1):
            block = jnp.where(n == 0, 0, n + 1)
            here = pl.ds(pl.multiple_of(block * PAGE, PAGE), PAGE)
            at = source[seq * per + n]
            hidden = first + n * PAGE < 0
            a, b = own[at], other[at]
            keys[here] = jnp.where(hidden, stand_in, jnp.where(is_key, a, b))
            v = jnp.where(is_key, b, a).astype(F32)
            widen(jnp.where(hidden, 0.0, v), jnp.where(hidden, 0.0, 1.0), values, here)
        return 0

    lax.fori_loop(0, (seen - per) // 2, bring, 0)


def gather_rows(info, own, other, fresh):
    span = WINDOW + fresh.shape[1]
    return pl.pallas_call(
        gather_kernel,
        out_shape=[
            jax.ShapeDtypeStruct((span, 2 * HD), BF16),
            jax.ShapeDtypeStruct((2, span, 2 * HD), BF16),
        ],
        in_specs=[SMEM] + [VMEM] * 3,
        out_specs=[VMEM] * 2,
        scratch_shapes=[pltpu.SMEM((own.shape[0],), jnp.int32)],
        compiler_params=params(12),
        cost_estimate=cost(20 * 10**9, 4 * span),
    )(info, own, other, fresh)


def bundle_kernel(a, b, out):
    out[: a.shape[0]] = a[...]
    out[a.shape[0] :] = b[...]


def bundled(a, b):
    return pl.pallas_call(
        bundle_kernel,
        out_shape=jax.ShapeDtypeStruct((a.shape[0] + b.shape[0], *a.shape[1:]), BF16),
        in_specs=[VMEM] * 2,
        out_specs=VMEM,
        compiler_params=params(8),
        cost_estimate=cost(6 * 10**9, 4),
    )(a, b)


def near_segment(keys, values, seq, half):
    blocks = keys.shape[0] // PAGE
    per = 2
    span = slice(half * PAGE, (blocks - seq * per - 1 + half) * PAGE)

    def mask(s):
        newer = lax.broadcasted_iota(jnp.int32, (s.shape[0], PAGE), 1) > (
            lax.broadcasted_iota(jnp.int32, (s.shape[0], PAGE), 0) % PAGE
        )
        if half == 0:
            parts = [
                jnp.where(newer, s[:, :PAGE], MASKED),
                jnp.where(newer, MASKED, s[:, PAGE : 2 * PAGE]),
                s[:, 2 * PAGE :],
            ]
        else:
            parts = [
                s[:, :PAGE],
                jnp.where(newer, s[:, PAGE : 2 * PAGE], MASKED),
                s[:, 2 * PAGE : -PAGE],
                jnp.where(newer, MASKED, s[:, -PAGE:]),
            ]
        return jnp.concatenate(parts, axis=1)

    return keys, values, span, mask


def far_segment(keys, values, seq):
    return keys, values, slice(0, seq * 2 * PAGE), lambda s: s


def near_kernel(info_ref, q, keys, values, total, weight, top):
    seq = Info(info_ref).seq

    def emit(spot, o, l, m):
        total[:, spot] = o
        weight[:, spot] = l
        top[:, spot] = m

    for k in range(SEQS):

        @pl.when(seq == k)
        def _(k=k):
            soft_heads(q, slice(0, PAGE), [near_segment(keys, values, k, 0)], emit)


def attend_near(info, q, keys, values):
    state = jax.ShapeDtypeStruct((PAGE, q.shape[1]), F32)
    return pl.pallas_call(
        near_kernel,
        out_shape=[state] * 3,
        in_specs=[SMEM] + [VMEM] * 3,
        out_specs=[VMEM] * 3,
        compiler_params=params(32),
        cost_estimate=cost(PAGE * WINDOW, 4 * WINDOW),
    )(info, q, keys, values)


def partner_product(info, heads_out, w, partial):
    cols = partial.shape[1]
    here = pl.ds(pl.multiple_of((1 - info.tensor) * cols, cols), cols)
    partial[...] = jnp.dot(heads_out[...], w[:, here], preferred_element_type=F32).astype(BF16)


def far_kernel(
    info_ref, q, total, weight, top, z1, z2, z3, w, heads_out, partial, keys, values
):
    info = Info(info_ref)
    rows = q.shape[0]
    seq = info.seq
    zs = (None, z1, z2, z3)
    is_key = info.tensor == 0

    for k in range(SEQS):

        @pl.when(seq == k)
        def _(k=k):
            if k == 0:
                heads_out[...] = (total[...] / weight[...]).astype(BF16)
                return
            for n in range(k):
                z = zs[n ^ k]
                here = slice(n * rows, (n + 1) * rows)
                a, b = z[0], z[1]
                keys[here] = jnp.where(is_key, a, b)
                widen(jnp.where(is_key, b, a).astype(F32), 1.0, values, here)

            def emit(spot, o, l, m):
                before = top[:, spot]
                peak = jnp.maximum(before, m)
                a = jnp.exp2(before - peak)
                b = jnp.exp2(m - peak)
                done = (total[:, spot] * a + o * b) / (weight[:, spot] * a + l * b)
                heads_out[:, spot] = done.astype(BF16)

            soft_heads(q, slice(0, PAGE), [far_segment(keys, values, k)], emit)

    partner_product(info, heads_out, w, partial)


def attend_far(info, q, state, zs, w):
    rows = q.shape[0]
    span = (SEQS - 1) * rows
    return pl.pallas_call(
        far_kernel,
        out_shape=[
            jax.ShapeDtypeStruct((PAGE, q.shape[1]), BF16),
            jax.ShapeDtypeStruct((PAGE, w.shape[1] // TENSORS), BF16),
            jax.ShapeDtypeStruct((span, 2 * HD), BF16),
            jax.ShapeDtypeStruct((2, span, 2 * HD), BF16),
        ],
        in_specs=[SMEM] + [VMEM] * 8,
        out_specs=[VMEM] * 4,
        compiler_params=params(24),
        cost_estimate=cost(rows * span, 4 * span),
    )(info, q, *state, *zs, w)


def last_kernel(info_ref, q, keys, values, far_keys, far_values, w, heads_out, partial):
    info = Info(info_ref)

    def emit(spot, o, l, m):
        heads_out[:, spot] = (o / l).astype(BF16)

    for k in range(SEQS):

        @pl.when(info.seq == k)
        def _(k=k):
            segments = [near_segment(keys, values, k, 1)]
            if k:
                segments.append(far_segment(far_keys, far_values, k))
            soft_heads(q, slice(PAGE, 2 * PAGE), segments, emit)

    partner_product(info, heads_out, w, partial)


def attend_last(info, q, keys, values, far_keys, far_values, w):
    return pl.pallas_call(
        last_kernel,
        out_shape=[
            jax.ShapeDtypeStruct((PAGE, q.shape[1]), BF16),
            jax.ShapeDtypeStruct((PAGE, w.shape[1] // TENSORS), BF16),
        ],
        in_specs=[SMEM] + [VMEM] * 6,
        out_specs=[VMEM] * 2,
        compiler_params=params(36),
        cost_estimate=cost(PAGE * WINDOW, 4 * WINDOW),
    )(info, q, keys, values, far_keys, far_values, w)


def home_kernel(info_ref, x1, x2, away, w, out, home, first, sem):
    rows, cols = home.shape
    here = pl.ds(pl.multiple_of(Info(info_ref).tensor * cols, cols), cols)
    x = jnp.concatenate([x1[...], x2[...]], axis=0)
    o = jnp.dot(x, w[:, here], preferred_element_type=F32).astype(BF16)
    home[...] = o[rows:]
    first[...] = (o[:rows].astype(F32) + away[...].astype(F32)).astype(BF16)
    copy = pltpu.make_async_copy(first, out.at[pl.ds(0, rows)], sem)
    copy.start()
    copy.wait()


def home_project(info, x1, x2, away, w):
    rows, depth = x1.shape
    cols = w.shape[1] // TENSORS
    return pl.pallas_call(
        home_kernel,
        out_shape=[
            jax.ShapeDtypeStruct((2 * rows, cols), BF16),
            jax.ShapeDtypeStruct((rows, cols), BF16),
        ],
        in_specs=[SMEM] + [VMEM] * 4,
        out_specs=[STAYS, VMEM],
        scratch_shapes=[pltpu.VMEM((rows, cols), BF16), pltpu.SemaphoreType.DMA],
        compiler_params=params(16),
        cost_estimate=cost(20 * 10**9, 2 * depth * cols),
    )(info, x1, x2, away, w)


def add_kernel(before, a, b, out, last, sem):
    rows = a.shape[0]
    last[...] = (a[...].astype(F32) + b[...].astype(F32)).astype(BF16)
    copy = pltpu.make_async_copy(last, out.at[pl.ds(rows, rows)], sem)
    copy.start()
    copy.wait()


def added(before, a, b):
    return pl.pallas_call(
        add_kernel,
        out_shape=jax.ShapeDtypeStruct(before.shape, BF16),
        in_specs=[STAYS, VMEM, VMEM],
        out_specs=STAYS,
        scratch_shapes=[pltpu.VMEM(a.shape, BF16), pltpu.SemaphoreType.DMA],
        input_output_aliases={0: 0},
        compiler_params=params(8),
    )(before, a, b)


def flipped(value, axes, count, bits):
    return lax.ppermute(value, axes, [(i, i ^ bits) for i in range(count)])


def after(value, *others):
    return lax.optimization_barrier((value, *others))[0]


def shards_fast(
    span_tokens, q_weight, kv_weight, out_weight, kv_pool, cache_lengths, slot_requests, page_table
):
    group_id = lax.axis_index("group")
    seq_id = lax.axis_index("seq")
    tensor_id = lax.axis_index("tensor")
    place = jnp.stack([group_id, seq_id, tensor_id]).astype(jnp.int32)
    row = jnp.concatenate([place, slot_requests, cache_lengths])
    row = jnp.pad(row, (0, page_table.shape[1] - row.shape[0]))
    info = jnp.concatenate([row[None], page_table])
    mine = span_tokens[0]
    theirs = flipped(mine, "tensor", 2, 1)
    half_dim = HD // 2
    lane = jnp.arange(128, dtype=jnp.int32) % half_dim
    frequency = jnp.power(jnp.float32(10000.0), -lane.astype(F32) / half_dim)
    frequency = jnp.broadcast_to(frequency[None, :], (8, 128))
    pages = open_rows(info, frequency, kv_pool, mine, q_weight, kv_weight)
    home, same, beyond, beside, across, diagonal = pages[:6]
    acc_q, acc_kv, cosine, sine = pages[6:]
    capacity = home.shape[0]
    same = flipped(same, "tensor", 2, 1)
    beyond = flipped(beyond, "group", 4, 2)
    kept, sent = fresh_rows(info, theirs, kv_weight, acc_kv, cosine, sine)
    got = flipped(sent, "tensor", 2, 1)
    across, diagonal, _ = lax.optimization_barrier((across, diagonal, sent))
    across = flipped(across, ("group", "tensor"), 8, 5)
    diagonal = flipped(diagonal, ("group", "tensor"), 8, 7)
    q = query_rows(info, theirs, q_weight, acc_q, cosine, sine)
    same, beyond, _ = lax.optimization_barrier((same, beyond, q))
    mate = jnp.concatenate([beside, beyond[capacity:], same[capacity:]])
    mate = flipped(mate, "group", 4, 1)
    fresh = bundled(kept[None], got[None])
    zs = [flipped(fresh, "seq", 4, d) for d in range(1, 4)]
    other_chip = bundled(across, diagonal)
    own = jnp.concatenate(
        [home, mate[:capacity], beyond[:capacity], mate[capacity : 2 * capacity]]
    )
    other = jnp.concatenate([same[:capacity], mate[2 * capacity :], other_chip])
    keys, values = gather_rows(info, own, other, fresh)
    state = attend_near(info, q, keys, values)
    heads_0, partial_0, far_keys, far_values = attend_far(info, q, state, zs, out_weight)
    away_0 = flipped(partial_0, "tensor", 2, 1)
    heads_1, partial_1 = attend_last(info, q, keys, values, far_keys, far_values, out_weight)
    away_1 = flipped(partial_1, "tensor", 2, 1)
    out, home_1 = home_project(info, heads_0, heads_1, away_0, out_weight)
    return added(out, home_1, away_1)[None]


def solution(mesh):
    sizes = tuple(mesh.shape[a] for a in ("group", "seq", "tensor"))
    body = shards_fast if sizes == (GROUPS, SEQS, TENSORS) else shards
    placed = (
        P("group", "seq", "tensor"),
        P(None, "tensor"),
        P(None, "tensor"),
        P("tensor", None),
        P("group", None, "tensor"),
        P(),
        P(),
        P(),
    )
    return jax.shard_map(
        body, mesh=mesh, in_specs=placed, out_specs=P("group", "seq", "tensor"), check_vma=False
    )
```

```python
import functools

import jax
import jax.numpy as jnp
from jax import lax
from jax.experimental import pallas as pl
from jax.experimental.pallas import tpu as pltpu
from jax.sharding import PartitionSpec as P

HD = 64
KVH = 4
WINDOW = 2048
PAGE = 128


def shifted(block, axis, distance):
    devices = range(lax.axis_size(axis))
    route = [(i - distance, i) for i in devices if i - distance in devices]
    return lax.ppermute(block, axis, route)


def swapped(value, axis, stride):
    return lax.ppermute(value, axis, [(i, i ^ 1 << stride) for i in range(lax.axis_size(axis))])


def rotate(values, positions):
    half_dim = HD // 2
    frequency = jnp.power(jnp.float32(10000.0), -jnp.arange(half_dim, dtype=jnp.float32) / half_dim)
    angles = positions.astype(jnp.float32)[:, None] * frequency[None, :]
    cosine = jnp.cos(angles)[:, None, :]
    sine_part = jnp.sin(angles)[:, None, :]
    front_half = values[..., :half_dim]
    back_half = values[..., half_dim:]
    return jnp.concatenate(
        [front_half * cosine - back_half * sine_part, back_half * cosine + front_half * sine_part],
        axis=-1,
    )


def attend(block_q, block_k, block_v, base_pos):
    query_count = block_q.shape[0]
    key_count = block_k.shape[0]
    scores = jnp.einsum(
        "tkgd,nkd->kgtn", block_q, block_k, preferred_element_type=jnp.float32
    ) * HD ** (-0.5)
    query_at = jnp.arange(query_count, dtype=jnp.int32)[:, None]
    key_at = jnp.arange(key_count, dtype=jnp.int32)[None, :]
    allowed = (key_at > query_at) & (key_at <= query_at + WINDOW) & (base_pos + key_at >= 0)
    masked = jnp.where(allowed, scores, jnp.float32(-1e30))
    row_top = jnp.max(masked, axis=-1, keepdims=True)
    weights = jnp.where(allowed, jnp.exp(masked - row_top), jnp.float32(0.0))
    row_total = jnp.sum(weights, axis=-1)
    rounded = weights.astype(jnp.bfloat16)
    mixed_rows = jnp.einsum("kgtn,nkd->tkgd", rounded, block_v, preferred_element_type=jnp.float32)
    mixed_rows = mixed_rows / jnp.transpose(row_total, (2, 0, 1))[..., None]
    return mixed_rows.astype(jnp.bfloat16).reshape(query_count, -1)


def shards(
    span_tokens, q_weight, kv_weight, out_weight, kv_pool, cache_lengths, slot_requests, page_table
):
    groups = lax.axis_size("group")
    seq_count = lax.axis_size("seq")
    tensor_count = lax.axis_size("tensor")
    group_id = lax.axis_index("group")
    seq_id = lax.axis_index("seq")
    tensor_id = lax.axis_index("tensor")
    local_reqs, seg_len, feat_local = span_tokens.shape
    head_cols = q_weight.shape[1]
    kv_cols = kv_weight.shape[1]
    local_heads = head_cols // HD
    group_heads = kv_cols // HD
    kv_local = max(1, KVH // tensor_count)
    per_kv = local_heads // kv_local
    head_first = tensor_id * KVH // tensor_count % group_heads
    holds_keys = tensor_id % 2 == 0
    pool_rows = kv_pool.shape[0]
    capacity = pool_rows // groups
    row_count = local_reqs * seg_len
    my_slots = group_id * local_reqs + jnp.arange(local_reqs, dtype=jnp.int32)
    my_requests = slot_requests[my_slots]
    my_lengths = cache_lengths[my_requests]
    project_piece_rows = lax.all_gather(span_tokens, "tensor", axis=2, tiled=True)
    feat_width = project_piece_rows.shape[2]
    flat_rows = project_piece_rows.reshape(row_count, feat_width)
    query_lin = jnp.dot(flat_rows, q_weight, preferred_element_type=jnp.float32)
    fresh_lin = jnp.dot(flat_rows, kv_weight, preferred_element_type=jnp.float32)
    positions = (
        my_lengths[:, None] + seq_id * seg_len + jnp.arange(seg_len, dtype=jnp.int32)[None, :]
    )
    queries = jax.vmap(rotate)(query_lin.reshape(local_reqs, seg_len, local_heads, HD), positions)
    queries = queries.astype(jnp.bfloat16).reshape(local_reqs, seg_len, kv_local, per_kv, HD)
    fresh_heads = fresh_lin.reshape(local_reqs, seg_len, group_heads, HD)
    rotated = jax.vmap(rotate)(fresh_heads, positions)
    span_kv = (
        jnp.where(holds_keys, rotated, fresh_heads)
        .astype(jnp.bfloat16)
        .reshape(local_reqs, seg_len, kv_cols)
    )
    all_ids = page_table[slot_requests]
    owned_here = all_ids // pool_rows == group_id
    slot_rank = jnp.cumsum(owned_here.astype(jnp.int32), axis=1) - 1
    local_rows = all_ids - group_id * pool_rows
    chosen = owned_here[:, :, None] & (
        slot_rank[:, :, None] == jnp.arange(capacity, dtype=jnp.int32)[None, None, :]
    )
    wanted = jnp.sum(jnp.where(chosen, local_rows[:, :, None], 0), axis=1)
    my_ids = page_table[my_requests].reshape(-1)
    my_owner = my_ids // pool_rows
    onehot = (my_owner[:, None] == jnp.arange(groups, dtype=jnp.int32)[None, :]).astype(jnp.int32)
    arrival = jnp.sum((jnp.cumsum(onehot, axis=0) - 1) * onehot, axis=1)
    arrived_row = my_owner * capacity + arrival
    outgoing = kv_pool[wanted]
    arrived = lax.all_to_all(outgoing, "group", split_axis=0, concat_axis=0, tiled=True)
    cached = arrived.reshape(groups * capacity, PAGE, kv_cols)[arrived_row]
    cached = cached.reshape(local_reqs, WINDOW, kv_cols)
    span_all = jnp.zeros((local_reqs, seg_len * seq_count, kv_cols), jnp.bfloat16)
    for back_step in range(seq_count - 1, -1, -1):
        piece_rows = span_kv if back_step == 0 else shifted(span_kv, "seq", back_step)
        span_all = lax.dynamic_update_slice_in_dim(
            span_all, piece_rows, (seq_id - back_step) * seg_len, 1
        )
    joined = jnp.concatenate([cached, span_all], axis=1)
    visible = lax.dynamic_slice_in_dim(joined, seq_id * seg_len, WINDOW + seg_len, 1)
    partner_rows = swapped(visible, "tensor", 0)
    key_all = jnp.where(holds_keys, visible, partner_rows).reshape(
        local_reqs, WINDOW + seg_len, group_heads, HD
    )
    value_all = jnp.where(holds_keys, partner_rows, visible).reshape(
        local_reqs, WINDOW + seg_len, group_heads, HD
    )
    key_rows = lax.dynamic_slice_in_dim(key_all, head_first, kv_local, 2)
    value_rows = lax.dynamic_slice_in_dim(value_all, head_first, kv_local, 2)
    block_len = min(128, seg_len)
    block_count = seg_len // block_len

    def per_request(request_items):
        request_q, request_k, request_v, length = request_items

        def per_block(block_index):
            first_row = block_index * block_len
            block_q = lax.dynamic_slice_in_dim(request_q, first_row, block_len, 0)
            block_k = lax.dynamic_slice_in_dim(request_k, first_row, WINDOW + block_len, 0)
            block_v = lax.dynamic_slice_in_dim(request_v, first_row, WINDOW + block_len, 0)
            return attend(block_q, block_k, block_v, length - WINDOW + seq_id * seg_len + first_row)

        return lax.map(per_block, jnp.arange(block_count, dtype=jnp.int32)).reshape(
            seg_len, head_cols
        )

    attended_heads = lax.map(per_request, (queries, key_rows, value_rows, my_lengths))
    flat_heads = attended_heads.reshape(row_count, head_cols)
    out_cols = out_weight.shape[1] // tensor_count
    summed = lax.psum_scatter(
        lax.dot_general(
            out_weight, flat_heads, (((0,), (1,)), ((), ())), preferred_element_type=jnp.float32
        ).astype(jnp.bfloat16),
        "tensor",
        scatter_dimension=0,
        tiled=True,
    ).astype(jnp.float32)
    result = summed.T
    return result.astype(jnp.bfloat16).reshape(local_reqs, seg_len, out_cols)


LOG2E = 1.4426950408889634
MASKED = -1e30
F32 = jnp.float32
BF16 = jnp.bfloat16
HBM = pl.BlockSpec(memory_space=pl.ANY)
VMEM = pl.BlockSpec(memory_space=pltpu.VMEM)
SMEM = pl.BlockSpec(memory_space=pltpu.SMEM)
STAYS = pl.BlockSpec(memory_space=pltpu.HBM)
GROUPS, SEQS, TENSORS = 4, 4, 2


def params(mebibytes):
    return pltpu.CompilerParams(vmem_limit_bytes=mebibytes * 2**20)


def cost(flops, moved):
    return pl.CostEstimate(flops=flops, bytes_accessed=moved, transcendentals=0)


class Info:
    def __init__(self, ref):
        self.ref = ref
        self.group, self.seq, self.tensor = ref[0, 0], ref[0, 1], ref[0, 2]
        self.window_pages = ref.shape[1]

    def request(self, slot):
        return self.ref[0, 3 + slot]

    def length(self, request):
        return self.ref[0, 3 + GROUPS + request]

    def page(self, request, w):
        return self.ref[1 + request, w]


def turned(x, cosine, sine):
    lane = lax.broadcasted_iota(jnp.int32, x.shape, 1)
    other = jnp.where(lane % HD < HD // 2, pltpu.roll(x, 128 - HD // 2, 1), pltpu.roll(x, HD // 2, 1))
    return x * cosine + other * sine


def open_kernel(
    info_ref, frequency, pool, x_hbm, wq_hbm, wkv_hbm,
    home, same, beyond, beside, across, diagonal, acc_q, acc_kv, cosine, sine,
    x, wq, wkv, sems, page_sems,
):
    info = Info(info_ref)
    rows, feats = x.shape
    here = pl.ds(pl.multiple_of(info.tensor * feats, feats), feats)
    copies = [
        pltpu.make_async_copy(x_hbm, x, sems.at[0]),
        pltpu.make_async_copy(wkv_hbm.at[here], wkv, sems.at[1]),
        pltpu.make_async_copy(wq_hbm.at[here], wq, sems.at[2]),
    ]
    for copy in copies:
        copy.start()
    pages = pool.shape[0]
    capacity = pages // GROUPS
    half = pool.shape[2] // 2
    mine = pl.ds(pl.multiple_of(info.tensor * half, half), half)
    theirs = pl.ds(pl.multiple_of((1 - info.tensor) * half, half), half)
    outs = (home, same, beyond, beside, across, diagonal)
    spots = (
        ((0, 0), (1, 0)),
        ((3, 0), (1, capacity)),
        ((2, 0), (4, 0)),
        ((2, capacity), (5, 0)),
    )
    for flip, targets in enumerate(spots):
        request = info.request(info.group ^ flip)

        def take(w, rank):
            page = info.page(request, w)
            near = page // pages == info.group

            @pl.when(near)
            def _():
                row = page % pages
                for (out, base), cols in zip(targets, (mine, theirs)):
                    pltpu.make_async_copy(
                        pool.at[row, :, cols], outs[out].at[base + rank], page_sems.at[out]
                    ).start()

            return rank + near.astype(jnp.int32)

        lax.fori_loop(0, info.window_pages, take, jnp.int32(0))
    start = info.length(info.request(info.group)) + info.seq * rows
    position = (start + lax.broadcasted_iota(jnp.int32, (rows, 128), 0)).astype(F32)
    angles = position * frequency[0:1, :]
    lane = lax.broadcasted_iota(jnp.int32, (rows, 128), 1)
    cosine[...] = jnp.cos(angles)
    sine[...] = jnp.where(lane % HD < HD // 2, -1.0, 1.0) * jnp.sin(angles)
    copies[0].wait()
    copies[1].wait()
    acc_kv[...] = jnp.dot(x[...], wkv[...], preferred_element_type=F32)
    copies[2].wait()
    acc_q[...] = jnp.dot(x[...], wq[...], preferred_element_type=F32)
    for i, out in enumerate(outs):
        pltpu.make_async_copy(out, out, page_sems.at[i]).wait()


def open_rows(info, frequency, pool, x, wq, wkv):
    rows, feats = x.shape
    pages, page, cols = pool.shape
    single = jax.ShapeDtypeStruct((pages // GROUPS, page, cols // 2), BF16)
    double = jax.ShapeDtypeStruct((2 * pages // GROUPS, page, cols // 2), BF16)
    table = jax.ShapeDtypeStruct((rows, 128), F32)
    return pl.pallas_call(
        open_kernel,
        out_shape=[
            single,
            double,
            double,
            single,
            single,
            single,
            jax.ShapeDtypeStruct((rows, wq.shape[1]), F32),
            jax.ShapeDtypeStruct((rows, wkv.shape[1]), F32),
            table,
            table,
        ],
        in_specs=[SMEM, VMEM] + [STAYS] * 4,
        out_specs=[VMEM] * 10,
        scratch_shapes=[
            pltpu.VMEM((rows, feats), BF16),
            pltpu.VMEM((feats, wq.shape[1]), BF16),
            pltpu.VMEM((feats, wkv.shape[1]), BF16),
            pltpu.SemaphoreType.DMA((3,)),
            pltpu.SemaphoreType.DMA((6,)),
        ],
        compiler_params=params(50),
        cost_estimate=cost(rows * feats, rows * feats),
    )(info, frequency, pool, x, wq, wkv)


def fresh_kernel(info_ref, x, wkv, acc_kv, cosine, sine, kept, sent):
    info = Info(info_ref)
    feats = x.shape[1]
    here = pl.ds(pl.multiple_of((1 - info.tensor) * feats, feats), feats)
    keys = info.tensor == 0
    fresh = acc_kv[...] + jnp.dot(x[...], wkv[here], preferred_element_type=F32)
    cos_kv = jnp.where(keys, cosine[...], 1.0)
    sin_kv = jnp.where(keys, sine[...], 0.0)
    low = turned(fresh[:, :128], cos_kv, sin_kv).astype(BF16)
    high = turned(fresh[:, 128:], cos_kv, sin_kv).astype(BF16)
    kept[...] = jnp.where(keys, low, high)
    sent[...] = jnp.where(keys, high, low)


def fresh_rows(info, x, wkv, acc_kv, cosine, sine):
    rows, feats = x.shape
    piece = jax.ShapeDtypeStruct((rows, wkv.shape[1] // 2), BF16)
    return pl.pallas_call(
        fresh_kernel,
        out_shape=[piece, piece],
        in_specs=[SMEM] + [VMEM] * 5,
        out_specs=[VMEM] * 2,
        compiler_params=params(12),
        cost_estimate=cost(2 * rows * feats * 2560, rows * feats),
    )(info, x, wkv, acc_kv, cosine, sine)


def query_kernel(info_ref, x, wq, acc_q, cosine, sine, q):
    feats = x.shape[1]
    here = pl.ds(pl.multiple_of((1 - Info(info_ref).tensor) * feats, feats), feats)
    cos_all, sin_all = cosine[...], sine[...]
    scale = HD**-0.5 * LOG2E
    tile = 256
    for c in range(0, q.shape[1], tile):
        lin = acc_q[:, c : c + tile] + jnp.dot(
            x[...], wq[here, c : c + tile], preferred_element_type=F32
        )
        for e in range(0, tile, 128):
            q[:, c + e : c + e + 128] = (
                turned(lin[:, e : e + 128], cos_all, sin_all) * scale
            ).astype(BF16)


def query_rows(info, x, wq, acc_q, cosine, sine):
    rows, feats = x.shape
    return pl.pallas_call(
        query_kernel,
        out_shape=jax.ShapeDtypeStruct((rows, wq.shape[1]), BF16),
        in_specs=[SMEM] + [VMEM] * 5,
        out_specs=VMEM,
        compiler_params=params(16),
        cost_estimate=cost(rows * feats, rows * feats),
    )(info, x, wq, acc_q, cosine, sine)


def soft_heads(q, tokens, segments, emit):
    rows = tokens.stop - tokens.start
    stack = 4
    low = lax.broadcasted_iota(jnp.int32, (rows, 2 * HD), 1) < HD

    def swap(x):
        return pltpu.roll(x, HD, 1)

    def heads(i, _):
        first = i == 0
        spots = [pl.ds(pl.multiple_of((i * stack + j) * 128, 128), 128) for j in range(stack)]
        tiles = [q[tokens, spot] for spot in spots]
        turns = [swap(x.astype(F32)).astype(BF16) for x in tiles]
        keep = low == first

        def stacked(a, b):
            zero = jnp.zeros_like(a[0])
            return jnp.concatenate(
                [jnp.where(keep, jnp.where(first, x, y), zero) for x, y in zip(a, b)], axis=0
            )

        def scores(qs):
            return [
                mask(
                    lax.dot_general(
                        qs, keys[span], (((1,), (1,)), ((), ())), preferred_element_type=F32
                    )
                )
                for keys, _, span, mask in segments
            ]

        def peak(parts):
            tops = [jnp.max(s, axis=1, keepdims=True) for s in parts]
            return functools.reduce(jnp.maximum, tops)

        def mixed(weights):
            return sum(
                jnp.dot(p, values[i, span], preferred_element_type=F32)
                for p, (_, values, span, _) in zip(weights, segments)
            )

        s_even = scores(stacked(tiles, turns))
        s_odd = scores(stacked(turns, tiles))
        m_even = peak(s_even)
        m_odd = peak(s_odd)
        p_even = [jnp.exp2(s - m_even).astype(BF16) for s in s_even]
        p_odd = [jnp.exp2(s - m_odd).astype(BF16) for s in s_odd]
        o_even = mixed(p_even)
        o_odd = mixed(p_odd)
        for j in range(stack):
            part = slice(j * rows, (j + 1) * rows)
            a, b = o_even[part], o_odd[part]
            total = jnp.where(low, a, swap(b))
            weight = jnp.where(low, swap(a), b)
            top = jnp.where(low, m_even[part], m_odd[part])
            emit(spots[j], total, weight, top)
        return 0

    lax.fori_loop(0, q.shape[1] // 128 // stack, heads, 0)


def widen(v, ones, values, here):
    low = lax.broadcasted_iota(jnp.int32, v.shape, 1) < HD
    values[0, here] = jnp.where(low, v, ones).astype(BF16)
    values[1, here] = jnp.where(low, pltpu.roll(v, HD, 1), ones).astype(BF16)


def gather_kernel(info_ref, own, other, fresh, keys, values, source):
    info = Info(info_ref)
    group, seq = info.group, info.seq
    request = info.request(group)
    rows = fresh.shape[1]
    per = rows // PAGE
    count = own.shape[0]
    capacity = count // GROUPS
    seen = keys.shape[0] // PAGE - seq * per
    is_key = info.tensor == 0

    def note(w, counts):
        came = info.page(request, w) // count ^ group
        place = came * capacity
        for d in range(GROUPS):
            place = place + jnp.where(came == d, counts[d], 0)
        source[w] = place
        return tuple(counts[d] + (came == d).astype(jnp.int32) for d in range(GROUPS))

    lax.fori_loop(0, info.window_pages, note, (jnp.int32(0),) * GROUPS)

    def place(block, a, b):
        here = pl.ds(pl.multiple_of(block * PAGE, PAGE), PAGE)
        keys[here] = jnp.where(is_key, a, b)
        widen(jnp.where(is_key, b, a).astype(F32), 1.0, values, here)

    for block, part in ((1, slice(0, PAGE)), (seen - 1, slice(PAGE, 2 * PAGE))):
        place(block, fresh[0, part], fresh[1, part])
    first = info.length(request) - WINDOW + seq * rows
    stand_in = jnp.where(is_key, fresh[0, :16], fresh[1, :16]).astype(F32)[0:1]
    stand_in = jnp.broadcast_to(stand_in, (PAGE, 2 * HD)).astype(BF16)

    def bring(i, _):
        for n in (2 * i, 2 * i + 1):
            block = jnp.where(n == 0, 0, n + 1)
            here = pl.ds(pl.multiple_of(block * PAGE, PAGE), PAGE)
            at = source[seq * per + n]
            hidden = first + n * PAGE < 0
            a, b = own[at], other[at]
            keys[here] = jnp.where(hidden, stand_in, jnp.where(is_key, a, b))
            v = jnp.where(is_key, b, a).astype(F32)
            widen(jnp.where(hidden, 0.0, v), jnp.where(hidden, 0.0, 1.0), values, here)
        return 0

    lax.fori_loop(0, (seen - per) // 2, bring, 0)


def gather_rows(info, own, other, fresh):
    span = WINDOW + fresh.shape[1]
    return pl.pallas_call(
        gather_kernel,
        out_shape=[
            jax.ShapeDtypeStruct((span, 2 * HD), BF16),
            jax.ShapeDtypeStruct((2, span, 2 * HD), BF16),
        ],
        in_specs=[SMEM] + [VMEM] * 3,
        out_specs=[VMEM] * 2,
        scratch_shapes=[pltpu.SMEM((own.shape[0],), jnp.int32)],
        compiler_params=params(12),
        cost_estimate=cost(20 * 10**9, 4 * span),
    )(info, own, other, fresh)


def bundle_kernel(a, b, out):
    out[: a.shape[0]] = a[...]
    out[a.shape[0] :] = b[...]


def bundled(a, b):
    return pl.pallas_call(
        bundle_kernel,
        out_shape=jax.ShapeDtypeStruct((a.shape[0] + b.shape[0], *a.shape[1:]), BF16),
        in_specs=[VMEM] * 2,
        out_specs=VMEM,
        compiler_params=params(8),
        cost_estimate=cost(6 * 10**9, 4),
    )(a, b)


def near_segment(keys, values, seq, half):
    blocks = keys.shape[0] // PAGE
    per = 2
    span = slice(half * PAGE, (blocks - seq * per - 1 + half) * PAGE)

    def mask(s):
        newer = lax.broadcasted_iota(jnp.int32, (s.shape[0], PAGE), 1) > (
            lax.broadcasted_iota(jnp.int32, (s.shape[0], PAGE), 0) % PAGE
        )
        if half == 0:
            parts = [
                jnp.where(newer, s[:, :PAGE], MASKED),
                jnp.where(newer, MASKED, s[:, PAGE : 2 * PAGE]),
                s[:, 2 * PAGE :],
            ]
        else:
            parts = [
                s[:, :PAGE],
                jnp.where(newer, s[:, PAGE : 2 * PAGE], MASKED),
                s[:, 2 * PAGE : -PAGE],
                jnp.where(newer, MASKED, s[:, -PAGE:]),
            ]
        return jnp.concatenate(parts, axis=1)

    return keys, values, span, mask


def far_segment(keys, values, seq):
    return keys, values, slice(0, seq * 2 * PAGE), lambda s: s


def near_kernel(info_ref, q, keys, values, total, weight, top):
    seq = Info(info_ref).seq

    def emit(spot, o, l, m):
        total[:, spot] = o
        weight[:, spot] = l
        top[:, spot] = m

    for k in range(SEQS):

        @pl.when(seq == k)
        def _(k=k):
            soft_heads(q, slice(0, PAGE), [near_segment(keys, values, k, 0)], emit)


def attend_near(info, q, keys, values):
    state = jax.ShapeDtypeStruct((PAGE, q.shape[1]), F32)
    return pl.pallas_call(
        near_kernel,
        out_shape=[state] * 3,
        in_specs=[SMEM] + [VMEM] * 3,
        out_specs=[VMEM] * 3,
        compiler_params=params(32),
        cost_estimate=cost(PAGE * WINDOW, 4 * WINDOW),
    )(info, q, keys, values)


def partner_product(info, heads_out, w, partial):
    cols = partial.shape[1]
    here = pl.ds(pl.multiple_of((1 - info.tensor) * cols, cols), cols)
    partial[...] = jnp.dot(heads_out[...], w[:, here], preferred_element_type=F32).astype(BF16)


def far_kernel(
    info_ref, q, total, weight, top, z1, z2, z3, w, heads_out, partial, keys, values
):
    info = Info(info_ref)
    rows = q.shape[0]
    seq = info.seq
    zs = (None, z1, z2, z3)
    is_key = info.tensor == 0

    for k in range(SEQS):

        @pl.when(seq == k)
        def _(k=k):
            if k == 0:
                heads_out[...] = (total[...] / weight[...]).astype(BF16)
                return
            for n in range(k):
                z = zs[n ^ k]
                here = slice(n * rows, (n + 1) * rows)
                a, b = z[0], z[1]
                keys[here] = jnp.where(is_key, a, b)
                widen(jnp.where(is_key, b, a).astype(F32), 1.0, values, here)

            def emit(spot, o, l, m):
                before = top[:, spot]
                peak = jnp.maximum(before, m)
                a = jnp.exp2(before - peak)
                b = jnp.exp2(m - peak)
                done = (total[:, spot] * a + o * b) / (weight[:, spot] * a + l * b)
                heads_out[:, spot] = done.astype(BF16)

            soft_heads(q, slice(0, PAGE), [far_segment(keys, values, k)], emit)

    partner_product(info, heads_out, w, partial)


def attend_far(info, q, state, zs, w):
    rows = q.shape[0]
    span = (SEQS - 1) * rows
    return pl.pallas_call(
        far_kernel,
        out_shape=[
            jax.ShapeDtypeStruct((PAGE, q.shape[1]), BF16),
            jax.ShapeDtypeStruct((PAGE, w.shape[1] // TENSORS), BF16),
            jax.ShapeDtypeStruct((span, 2 * HD), BF16),
            jax.ShapeDtypeStruct((2, span, 2 * HD), BF16),
        ],
        in_specs=[SMEM] + [VMEM] * 8,
        out_specs=[VMEM] * 4,
        compiler_params=params(24),
        cost_estimate=cost(rows * span, 4 * span),
    )(info, q, *state, *zs, w)


def last_kernel(info_ref, q, keys, values, far_keys, far_values, w, heads_out, partial):
    info = Info(info_ref)

    def emit(spot, o, l, m):
        heads_out[:, spot] = (o / l).astype(BF16)

    for k in range(SEQS):

        @pl.when(info.seq == k)
        def _(k=k):
            segments = [near_segment(keys, values, k, 1)]
            if k:
                segments.append(far_segment(far_keys, far_values, k))
            soft_heads(q, slice(PAGE, 2 * PAGE), segments, emit)

    partner_product(info, heads_out, w, partial)


def attend_last(info, q, keys, values, far_keys, far_values, w):
    return pl.pallas_call(
        last_kernel,
        out_shape=[
            jax.ShapeDtypeStruct((PAGE, q.shape[1]), BF16),
            jax.ShapeDtypeStruct((PAGE, w.shape[1] // TENSORS), BF16),
        ],
        in_specs=[SMEM] + [VMEM] * 6,
        out_specs=[VMEM] * 2,
        compiler_params=params(36),
        cost_estimate=cost(PAGE * WINDOW, 4 * WINDOW),
    )(info, q, keys, values, far_keys, far_values, w)


def home_kernel(info_ref, x1, x2, away, w, out, home, first, sem):
    rows, cols = home.shape
    here = pl.ds(pl.multiple_of(Info(info_ref).tensor * cols, cols), cols)
    x = jnp.concatenate([x1[...], x2[...]], axis=0)
    o = jnp.dot(x, w[:, here], preferred_element_type=F32).astype(BF16)
    home[...] = o[rows:]
    first[...] = (o[:rows].astype(F32) + away[...].astype(F32)).astype(BF16)
    copy = pltpu.make_async_copy(first, out.at[pl.ds(0, rows)], sem)
    copy.start()
    copy.wait()


def home_project(info, x1, x2, away, w):
    rows, depth = x1.shape
    cols = w.shape[1] // TENSORS
    return pl.pallas_call(
        home_kernel,
        out_shape=[
            jax.ShapeDtypeStruct((2 * rows, cols), BF16),
            jax.ShapeDtypeStruct((rows, cols), BF16),
        ],
        in_specs=[SMEM] + [VMEM] * 4,
        out_specs=[STAYS, VMEM],
        scratch_shapes=[pltpu.VMEM((rows, cols), BF16), pltpu.SemaphoreType.DMA],
        compiler_params=params(16),
        cost_estimate=cost(20 * 10**9, 2 * depth * cols),
    )(info, x1, x2, away, w)


def add_kernel(before, a, b, out, last, sem):
    rows = a.shape[0]
    last[...] = (a[...].astype(F32) + b[...].astype(F32)).astype(BF16)
    copy = pltpu.make_async_copy(last, out.at[pl.ds(rows, rows)], sem)
    copy.start()
    copy.wait()


def added(before, a, b):
    return pl.pallas_call(
        add_kernel,
        out_shape=jax.ShapeDtypeStruct(before.shape, BF16),
        in_specs=[STAYS, VMEM, VMEM],
        out_specs=STAYS,
        scratch_shapes=[pltpu.VMEM(a.shape, BF16), pltpu.SemaphoreType.DMA],
        input_output_aliases={0: 0},
        compiler_params=params(8),
    )(before, a, b)


def flipped(value, axes, count, bits):
    return lax.ppermute(value, axes, [(i, i ^ bits) for i in range(count)])


def after(value, *others):
    return lax.optimization_barrier((value, *others))[0]


def shards_fast(
    span_tokens, q_weight, kv_weight, out_weight, kv_pool, cache_lengths, slot_requests, page_table
):
    group_id = lax.axis_index("group")
    seq_id = lax.axis_index("seq")
    tensor_id = lax.axis_index("tensor")
    place = jnp.stack([group_id, seq_id, tensor_id]).astype(jnp.int32)
    row = jnp.concatenate([place, slot_requests, cache_lengths])
    row = jnp.pad(row, (0, page_table.shape[1] - row.shape[0]))
    info = jnp.concatenate([row[None], page_table])
    mine = span_tokens[0]
    theirs = flipped(mine, "tensor", 2, 1)
    half_dim = HD // 2
    lane = jnp.arange(128, dtype=jnp.int32) % half_dim
    frequency = jnp.power(jnp.float32(10000.0), -lane.astype(F32) / half_dim)
    frequency = jnp.broadcast_to(frequency[None, :], (8, 128))
    pages = open_rows(info, frequency, kv_pool, mine, q_weight, kv_weight)
    home, same, beyond, beside, across, diagonal = pages[:6]
    acc_q, acc_kv, cosine, sine = pages[6:]
    capacity = home.shape[0]
    same = flipped(same, "tensor", 2, 1)
    beyond = flipped(beyond, "group", 4, 2)
    kept, sent = fresh_rows(info, theirs, kv_weight, acc_kv, cosine, sine)
    got = flipped(sent, "tensor", 2, 1)
    across, diagonal, _ = lax.optimization_barrier((across, diagonal, sent))
    across = flipped(across, ("group", "tensor"), 8, 5)
    diagonal = flipped(diagonal, ("group", "tensor"), 8, 7)
    q = query_rows(info, theirs, q_weight, acc_q, cosine, sine)
    same, beyond, _ = lax.optimization_barrier((same, beyond, q))
    mate = jnp.concatenate([beside, beyond[capacity:], same[capacity:]])
    mate = flipped(mate, "group", 4, 1)
    fresh = bundled(kept[None], got[None])
    zs = [flipped(fresh, "seq", 4, d) for d in range(1, 4)]
    other_chip = bundled(across, diagonal)
    own = jnp.concatenate(
        [home, mate[:capacity], beyond[:capacity], mate[capacity : 2 * capacity]]
    )
    other = jnp.concatenate([same[:capacity], mate[2 * capacity :], other_chip])
    keys, values = gather_rows(info, own, other, fresh)
    state = attend_near(info, q, keys, values)
    heads_0, partial_0, far_keys, far_values = attend_far(info, q, state, zs, out_weight)
    away_0 = flipped(partial_0, "tensor", 2, 1)
    heads_1, partial_1 = attend_last(info, q, keys, values, far_keys, far_values, out_weight)
    away_1 = flipped(partial_1, "tensor", 2, 1)
    out, home_1 = home_project(info, heads_0, heads_1, away_0, out_weight)
    return added(out, home_1, away_1)[None]


def solution(mesh):
    sizes = tuple(mesh.shape[a] for a in ("group", "seq", "tensor"))
    body = shards_fast if sizes == (GROUPS, SEQS, TENSORS) else shards
    placed = (
        P("group", "seq", "tensor"),
        P(None, "tensor"),
        P(None, "tensor"),
        P("tensor", None),
        P("group", None, "tensor"),
        P(),
        P(),
        P(),
    )
    return jax.shard_map(
        body, mesh=mesh, in_specs=placed, out_specs=P("group", "seq", "tensor"), check_vma=False
    )
```

```python
import functools

import jax
import jax.numpy as jnp
from jax import lax
from jax.experimental import pallas as pl
from jax.experimental.pallas import tpu as pltpu
from jax.sharding import PartitionSpec as P

HD = 64
KVH = 4
WINDOW = 2048
PAGE = 128


def shifted(block, axis, distance):
    devices = range(lax.axis_size(axis))
    route = [(i - distance, i) for i in devices if i - distance in devices]
    return lax.ppermute(block, axis, route)


def swapped(value, axis, stride):
    return lax.ppermute(value, axis, [(i, i ^ 1 << stride) for i in range(lax.axis_size(axis))])


def rotate(values, positions):
    half_dim = HD // 2
    frequency = jnp.power(jnp.float32(10000.0), -jnp.arange(half_dim, dtype=jnp.float32) / half_dim)
    angles = positions.astype(jnp.float32)[:, None] * frequency[None, :]
    cosine = jnp.cos(angles)[:, None, :]
    sine_part = jnp.sin(angles)[:, None, :]
    front_half = values[..., :half_dim]
    back_half = values[..., half_dim:]
    return jnp.concatenate(
        [front_half * cosine - back_half * sine_part, back_half * cosine + front_half * sine_part],
        axis=-1,
    )


def attend(block_q, block_k, block_v, base_pos):
    query_count = block_q.shape[0]
    key_count = block_k.shape[0]
    scores = jnp.einsum(
        "tkgd,nkd->kgtn", block_q, block_k, preferred_element_type=jnp.float32
    ) * HD ** (-0.5)
    query_at = jnp.arange(query_count, dtype=jnp.int32)[:, None]
    key_at = jnp.arange(key_count, dtype=jnp.int32)[None, :]
    allowed = (key_at > query_at) & (key_at <= query_at + WINDOW) & (base_pos + key_at >= 0)
    masked = jnp.where(allowed, scores, jnp.float32(-1e30))
    row_top = jnp.max(masked, axis=-1, keepdims=True)
    weights = jnp.where(allowed, jnp.exp(masked - row_top), jnp.float32(0.0))
    row_total = jnp.sum(weights, axis=-1)
    rounded = weights.astype(jnp.bfloat16)
    mixed_rows = jnp.einsum("kgtn,nkd->tkgd", rounded, block_v, preferred_element_type=jnp.float32)
    mixed_rows = mixed_rows / jnp.transpose(row_total, (2, 0, 1))[..., None]
    return mixed_rows.astype(jnp.bfloat16).reshape(query_count, -1)


def shards(
    span_tokens, q_weight, kv_weight, out_weight, kv_pool, cache_lengths, slot_requests, page_table
):
    groups = lax.axis_size("group")
    seq_count = lax.axis_size("seq")
    tensor_count = lax.axis_size("tensor")
    group_id = lax.axis_index("group")
    seq_id = lax.axis_index("seq")
    tensor_id = lax.axis_index("tensor")
    local_reqs, seg_len, feat_local = span_tokens.shape
    head_cols = q_weight.shape[1]
    kv_cols = kv_weight.shape[1]
    local_heads = head_cols // HD
    group_heads = kv_cols // HD
    kv_local = max(1, KVH // tensor_count)
    per_kv = local_heads // kv_local
    head_first = tensor_id * KVH // tensor_count % group_heads
    holds_keys = tensor_id % 2 == 0
    pool_rows = kv_pool.shape[0]
    capacity = pool_rows // groups
    row_count = local_reqs * seg_len
    my_slots = group_id * local_reqs + jnp.arange(local_reqs, dtype=jnp.int32)
    my_requests = slot_requests[my_slots]
    my_lengths = cache_lengths[my_requests]
    project_piece_rows = lax.all_gather(span_tokens, "tensor", axis=2, tiled=True)
    feat_width = project_piece_rows.shape[2]
    flat_rows = project_piece_rows.reshape(row_count, feat_width)
    query_lin = jnp.dot(flat_rows, q_weight, preferred_element_type=jnp.float32)
    fresh_lin = jnp.dot(flat_rows, kv_weight, preferred_element_type=jnp.float32)
    positions = (
        my_lengths[:, None] + seq_id * seg_len + jnp.arange(seg_len, dtype=jnp.int32)[None, :]
    )
    queries = jax.vmap(rotate)(query_lin.reshape(local_reqs, seg_len, local_heads, HD), positions)
    queries = queries.astype(jnp.bfloat16).reshape(local_reqs, seg_len, kv_local, per_kv, HD)
    fresh_heads = fresh_lin.reshape(local_reqs, seg_len, group_heads, HD)
    rotated = jax.vmap(rotate)(fresh_heads, positions)
    span_kv = (
        jnp.where(holds_keys, rotated, fresh_heads)
        .astype(jnp.bfloat16)
        .reshape(local_reqs, seg_len, kv_cols)
    )
    all_ids = page_table[slot_requests]
    owned_here = all_ids // pool_rows == group_id
    slot_rank = jnp.cumsum(owned_here.astype(jnp.int32), axis=1) - 1
    local_rows = all_ids - group_id * pool_rows
    chosen = owned_here[:, :, None] & (
        slot_rank[:, :, None] == jnp.arange(capacity, dtype=jnp.int32)[None, None, :]
    )
    wanted = jnp.sum(jnp.where(chosen, local_rows[:, :, None], 0), axis=1)
    my_ids = page_table[my_requests].reshape(-1)
    my_owner = my_ids // pool_rows
    onehot = (my_owner[:, None] == jnp.arange(groups, dtype=jnp.int32)[None, :]).astype(jnp.int32)
    arrival = jnp.sum((jnp.cumsum(onehot, axis=0) - 1) * onehot, axis=1)
    arrived_row = my_owner * capacity + arrival
    outgoing = kv_pool[wanted]
    arrived = lax.all_to_all(outgoing, "group", split_axis=0, concat_axis=0, tiled=True)
    cached = arrived.reshape(groups * capacity, PAGE, kv_cols)[arrived_row]
    cached = cached.reshape(local_reqs, WINDOW, kv_cols)
    span_all = jnp.zeros((local_reqs, seg_len * seq_count, kv_cols), jnp.bfloat16)
    for back_step in range(seq_count - 1, -1, -1):
        piece_rows = span_kv if back_step == 0 else shifted(span_kv, "seq", back_step)
        span_all = lax.dynamic_update_slice_in_dim(
            span_all, piece_rows, (seq_id - back_step) * seg_len, 1
        )
    joined = jnp.concatenate([cached, span_all], axis=1)
    visible = lax.dynamic_slice_in_dim(joined, seq_id * seg_len, WINDOW + seg_len, 1)
    partner_rows = swapped(visible, "tensor", 0)
    key_all = jnp.where(holds_keys, visible, partner_rows).reshape(
        local_reqs, WINDOW + seg_len, group_heads, HD
    )
    value_all = jnp.where(holds_keys, partner_rows, visible).reshape(
        local_reqs, WINDOW + seg_len, group_heads, HD
    )
    key_rows = lax.dynamic_slice_in_dim(key_all, head_first, kv_local, 2)
    value_rows = lax.dynamic_slice_in_dim(value_all, head_first, kv_local, 2)
    block_len = min(128, seg_len)
    block_count = seg_len // block_len

    def per_request(request_items):
        request_q, request_k, request_v, length = request_items

        def per_block(block_index):
            first_row = block_index * block_len
            block_q = lax.dynamic_slice_in_dim(request_q, first_row, block_len, 0)
            block_k = lax.dynamic_slice_in_dim(request_k, first_row, WINDOW + block_len, 0)
            block_v = lax.dynamic_slice_in_dim(request_v, first_row, WINDOW + block_len, 0)
            return attend(block_q, block_k, block_v, length - WINDOW + seq_id * seg_len + first_row)

        return lax.map(per_block, jnp.arange(block_count, dtype=jnp.int32)).reshape(
            seg_len, head_cols
        )

    attended_heads = lax.map(per_request, (queries, key_rows, value_rows, my_lengths))
    flat_heads = attended_heads.reshape(row_count, head_cols)
    out_cols = out_weight.shape[1] // tensor_count
    summed = lax.psum_scatter(
        lax.dot_general(
            out_weight, flat_heads, (((0,), (1,)), ((), ())), preferred_element_type=jnp.float32
        ).astype(jnp.bfloat16),
        "tensor",
        scatter_dimension=0,
        tiled=True,
    ).astype(jnp.float32)
    result = summed.T
    return result.astype(jnp.bfloat16).reshape(local_reqs, seg_len, out_cols)


LOG2E = 1.4426950408889634
MASKED = -1e30
F32 = jnp.float32
BF16 = jnp.bfloat16
HBM = pl.BlockSpec(memory_space=pl.ANY)
VMEM = pl.BlockSpec(memory_space=pltpu.VMEM)
SMEM = pl.BlockSpec(memory_space=pltpu.SMEM)
STAYS = pl.BlockSpec(memory_space=pltpu.HBM)
GROUPS, SEQS, TENSORS = 4, 4, 2


def params(mebibytes):
    return pltpu.CompilerParams(vmem_limit_bytes=mebibytes * 2**20)


def cost(flops, moved):
    return pl.CostEstimate(flops=flops, bytes_accessed=moved, transcendentals=0)


class Info:
    def __init__(self, ref):
        self.ref = ref
        self.group, self.seq, self.tensor = ref[0, 0], ref[0, 1], ref[0, 2]
        self.window_pages = ref.shape[1]

    def request(self, slot):
        return self.ref[0, 3 + slot]

    def length(self, request):
        return self.ref[0, 3 + GROUPS + request]

    def page(self, request, w):
        return self.ref[1 + request, w]


def turned(x, cosine, sine):
    lane = lax.broadcasted_iota(jnp.int32, x.shape, 1)
    other = jnp.where(lane % HD < HD // 2, pltpu.roll(x, 128 - HD // 2, 1), pltpu.roll(x, HD // 2, 1))
    return x * cosine + other * sine


def open_kernel(
    info_ref, frequency, pool, x_hbm, wq_hbm, wkv_hbm,
    home, same, beyond, beside, across, diagonal, acc_q, acc_kv, cosine, sine,
    x, wq, wkv, sems, page_sems,
):
    info = Info(info_ref)
    rows, feats = x.shape
    here = pl.ds(pl.multiple_of(info.tensor * feats, feats), feats)
    copies = [
        pltpu.make_async_copy(x_hbm, x, sems.at[0]),
        pltpu.make_async_copy(wkv_hbm.at[here], wkv, sems.at[1]),
        pltpu.make_async_copy(wq_hbm.at[here], wq, sems.at[2]),
    ]
    for copy in copies:
        copy.start()
    pages = pool.shape[0]
    capacity = pages // GROUPS
    half = pool.shape[2] // 2
    mine = pl.ds(pl.multiple_of(info.tensor * half, half), half)
    theirs = pl.ds(pl.multiple_of((1 - info.tensor) * half, half), half)
    outs = (home, same, beyond, beside, across, diagonal)
    spots = (
        ((0, 0), (1, 0)),
        ((3, 0), (1, capacity)),
        ((2, 0), (4, 0)),
        ((2, capacity), (5, 0)),
    )
    for flip, targets in enumerate(spots):
        request = info.request(info.group ^ flip)

        def take(w, rank):
            page = info.page(request, w)
            near = page // pages == info.group

            @pl.when(near)
            def _():
                row = page % pages
                for (out, base), cols in zip(targets, (mine, theirs)):
                    pltpu.make_async_copy(
                        pool.at[row, :, cols], outs[out].at[base + rank], page_sems.at[out]
                    ).start()

            return rank + near.astype(jnp.int32)

        lax.fori_loop(0, info.window_pages, take, jnp.int32(0))
    start = info.length(info.request(info.group)) + info.seq * rows
    position = (start + lax.broadcasted_iota(jnp.int32, (rows, 128), 0)).astype(F32)
    angles = position * frequency[0:1, :]
    lane = lax.broadcasted_iota(jnp.int32, (rows, 128), 1)
    cosine[...] = jnp.cos(angles)
    sine[...] = jnp.where(lane % HD < HD // 2, -1.0, 1.0) * jnp.sin(angles)
    copies[0].wait()
    copies[1].wait()
    acc_kv[...] = jnp.dot(x[...], wkv[...], preferred_element_type=F32)
    copies[2].wait()
    acc_q[...] = jnp.dot(x[...], wq[...], preferred_element_type=F32)
    for i, out in enumerate(outs):
        pltpu.make_async_copy(out, out, page_sems.at[i]).wait()


def open_rows(info, frequency, pool, x, wq, wkv):
    rows, feats = x.shape
    pages, page, cols = pool.shape
    single = jax.ShapeDtypeStruct((pages // GROUPS, page, cols // 2), BF16)
    double = jax.ShapeDtypeStruct((2 * pages // GROUPS, page, cols // 2), BF16)
    table = jax.ShapeDtypeStruct((rows, 128), F32)
    return pl.pallas_call(
        open_kernel,
        out_shape=[
            single,
            double,
            double,
            single,
            single,
            single,
            jax.ShapeDtypeStruct((rows, wq.shape[1]), F32),
            jax.ShapeDtypeStruct((rows, wkv.shape[1]), F32),
            table,
            table,
        ],
        in_specs=[SMEM, VMEM] + [STAYS] * 4,
        out_specs=[VMEM] * 10,
        scratch_shapes=[
            pltpu.VMEM((rows, feats), BF16),
            pltpu.VMEM((feats, wq.shape[1]), BF16),
            pltpu.VMEM((feats, wkv.shape[1]), BF16),
            pltpu.SemaphoreType.DMA((3,)),
            pltpu.SemaphoreType.DMA((6,)),
        ],
        compiler_params=params(50),
        cost_estimate=cost(rows * feats, rows * feats),
    )(info, frequency, pool, x, wq, wkv)


def fresh_kernel(info_ref, x, wkv, acc_kv, cosine, sine, kept, sent):
    info = Info(info_ref)
    feats = x.shape[1]
    here = pl.ds(pl.multiple_of((1 - info.tensor) * feats, feats), feats)
    keys = info.tensor == 0
    fresh = acc_kv[...] + jnp.dot(x[...], wkv[here], preferred_element_type=F32)
    cos_kv = jnp.where(keys, cosine[...], 1.0)
    sin_kv = jnp.where(keys, sine[...], 0.0)
    low = turned(fresh[:, :128], cos_kv, sin_kv).astype(BF16)
    high = turned(fresh[:, 128:], cos_kv, sin_kv).astype(BF16)
    kept[...] = jnp.where(keys, low, high)
    sent[...] = jnp.where(keys, high, low)


def fresh_rows(info, x, wkv, acc_kv, cosine, sine):
    rows, feats = x.shape
    piece = jax.ShapeDtypeStruct((rows, wkv.shape[1] // 2), BF16)
    return pl.pallas_call(
        fresh_kernel,
        out_shape=[piece, piece],
        in_specs=[SMEM] + [VMEM] * 5,
        out_specs=[VMEM] * 2,
        compiler_params=params(12),
        cost_estimate=cost(2 * rows * feats * 2560, rows * feats),
    )(info, x, wkv, acc_kv, cosine, sine)


def query_kernel(info_ref, x, wq, acc_q, cosine, sine, q):
    feats = x.shape[1]
    here = pl.ds(pl.multiple_of((1 - Info(info_ref).tensor) * feats, feats), feats)
    cos_all, sin_all = cosine[...], sine[...]
    scale = HD**-0.5 * LOG2E
    tile = 256
    for c in range(0, q.shape[1], tile):
        lin = acc_q[:, c : c + tile] + jnp.dot(
            x[...], wq[here, c : c + tile], preferred_element_type=F32
        )
        for e in range(0, tile, 128):
            q[:, c + e : c + e + 128] = (
                turned(lin[:, e : e + 128], cos_all, sin_all) * scale
            ).astype(BF16)


def query_rows(info, x, wq, acc_q, cosine, sine):
    rows, feats = x.shape
    return pl.pallas_call(
        query_kernel,
        out_shape=jax.ShapeDtypeStruct((rows, wq.shape[1]), BF16),
        in_specs=[SMEM] + [VMEM] * 5,
        out_specs=VMEM,
        compiler_params=params(16),
        cost_estimate=cost(rows * feats, rows * feats),
    )(info, x, wq, acc_q, cosine, sine)


def soft_heads(q, tokens, segments, emit):
    rows = tokens.stop - tokens.start
    stack = 4
    low = lax.broadcasted_iota(jnp.int32, (rows, 2 * HD), 1) < HD

    def swap(x):
        return pltpu.roll(x, HD, 1)

    def heads(i, _):
        first = i == 0
        spots = [pl.ds(pl.multiple_of((i * stack + j) * 128, 128), 128) for j in range(stack)]
        tiles = [q[tokens, spot] for spot in spots]
        turns = [swap(x.astype(F32)).astype(BF16) for x in tiles]
        keep = low == first

        def stacked(a, b):
            zero = jnp.zeros_like(a[0])
            return jnp.concatenate(
                [jnp.where(keep, jnp.where(first, x, y), zero) for x, y in zip(a, b)], axis=0
            )

        def scores(qs):
            return [
                mask(
                    lax.dot_general(
                        qs, keys[span], (((1,), (1,)), ((), ())), preferred_element_type=F32
                    )
                )
                for keys, _, span, mask in segments
            ]

        def peak(parts):
            tops = [jnp.max(s, axis=1, keepdims=True) for s in parts]
            return functools.reduce(jnp.maximum, tops)

        def mixed(weights):
            return sum(
                jnp.dot(p, values[i, span], preferred_element_type=F32)
                for p, (_, values, span, _) in zip(weights, segments)
            )

        s_even = scores(stacked(tiles, turns))
        s_odd = scores(stacked(turns, tiles))
        m_even = peak(s_even)
        m_odd = peak(s_odd)
        p_even = [jnp.exp2(s - m_even).astype(BF16) for s in s_even]
        p_odd = [jnp.exp2(s - m_odd).astype(BF16) for s in s_odd]
        o_even = mixed(p_even)
        o_odd = mixed(p_odd)
        for j in range(stack):
            part = slice(j * rows, (j + 1) * rows)
            a, b = o_even[part], o_odd[part]
            total = jnp.where(low, a, swap(b))
            weight = jnp.where(low, swap(a), b)
            top = jnp.where(low, m_even[part], m_odd[part])
            emit(spots[j], total, weight, top)
        return 0

    lax.fori_loop(0, q.shape[1] // 128 // stack, heads, 0)


def widen(v, ones, values, here):
    low = lax.broadcasted_iota(jnp.int32, v.shape, 1) < HD
    values[0, here] = jnp.where(low, v, ones).astype(BF16)
    values[1, here] = jnp.where(low, pltpu.roll(v, HD, 1), ones).astype(BF16)


def gather_kernel(info_ref, own, other, fresh, keys, values, source):
    info = Info(info_ref)
    group, seq = info.group, info.seq
    request = info.request(group)
    rows = fresh.shape[1]
    per = rows // PAGE
    count = own.shape[0]
    capacity = count // GROUPS
    seen = keys.shape[0] // PAGE - seq * per
    is_key = info.tensor == 0

    def note(w, counts):
        came = info.page(request, w) // count ^ group
        place = came * capacity
        for d in range(GROUPS):
            place = place + jnp.where(came == d, counts[d], 0)
        source[w] = place
        return tuple(counts[d] + (came == d).astype(jnp.int32) for d in range(GROUPS))

    lax.fori_loop(0, info.window_pages, note, (jnp.int32(0),) * GROUPS)

    def place(block, a, b):
        here = pl.ds(pl.multiple_of(block * PAGE, PAGE), PAGE)
        keys[here] = jnp.where(is_key, a, b)
        widen(jnp.where(is_key, b, a).astype(F32), 1.0, values, here)

    for block, part in ((1, slice(0, PAGE)), (seen - 1, slice(PAGE, 2 * PAGE))):
        place(block, fresh[0, part], fresh[1, part])
    first = info.length(request) - WINDOW + seq * rows
    stand_in = jnp.where(is_key, fresh[0, :16], fresh[1, :16]).astype(F32)[0:1]
    stand_in = jnp.broadcast_to(stand_in, (PAGE, 2 * HD)).astype(BF16)

    def bring(i, _):
        for n in (2 * i, 2 * i + 1):
            block = jnp.where(n == 0, 0, n + 1)
            here = pl.ds(pl.multiple_of(block * PAGE, PAGE), PAGE)
            at = source[seq * per + n]
            hidden = first + n * PAGE < 0
            a, b = own[at], other[at]
            keys[here] = jnp.where(hidden, stand_in, jnp.where(is_key, a, b))
            v = jnp.where(is_key, b, a).astype(F32)
            widen(jnp.where(hidden, 0.0, v), jnp.where(hidden, 0.0, 1.0), values, here)
        return 0

    lax.fori_loop(0, (seen - per) // 2, bring, 0)


def gather_rows(info, own, other, fresh):
    span = WINDOW + fresh.shape[1]
    return pl.pallas_call(
        gather_kernel,
        out_shape=[
            jax.ShapeDtypeStruct((span, 2 * HD), BF16),
            jax.ShapeDtypeStruct((2, span, 2 * HD), BF16),
        ],
        in_specs=[SMEM] + [VMEM] * 3,
        out_specs=[VMEM] * 2,
        scratch_shapes=[pltpu.SMEM((own.shape[0],), jnp.int32)],
        compiler_params=params(12),
        cost_estimate=cost(20 * 10**9, 4 * span),
    )(info, own, other, fresh)


def bundle_kernel(a, b, out):
    out[: a.shape[0]] = a[...]
    out[a.shape[0] :] = b[...]


def bundled(a, b):
    return pl.pallas_call(
        bundle_kernel,
        out_shape=jax.ShapeDtypeStruct((a.shape[0] + b.shape[0], *a.shape[1:]), BF16),
        in_specs=[VMEM] * 2,
        out_specs=VMEM,
        compiler_params=params(8),
        cost_estimate=cost(6 * 10**9, 4),
    )(a, b)


def near_segment(keys, values, seq, half):
    blocks = keys.shape[0] // PAGE
    per = 2
    span = slice(half * PAGE, (blocks - seq * per - 1 + half) * PAGE)

    def mask(s):
        newer = lax.broadcasted_iota(jnp.int32, (s.shape[0], PAGE), 1) > (
            lax.broadcasted_iota(jnp.int32, (s.shape[0], PAGE), 0) % PAGE
        )
        if half == 0:
            parts = [
                jnp.where(newer, s[:, :PAGE], MASKED),
                jnp.where(newer, MASKED, s[:, PAGE : 2 * PAGE]),
                s[:, 2 * PAGE :],
            ]
        else:
            parts = [
                s[:, :PAGE],
                jnp.where(newer, s[:, PAGE : 2 * PAGE], MASKED),
                s[:, 2 * PAGE : -PAGE],
                jnp.where(newer, MASKED, s[:, -PAGE:]),
            ]
        return jnp.concatenate(parts, axis=1)

    return keys, values, span, mask


def far_segment(keys, values, seq):
    return keys, values, slice(0, seq * 2 * PAGE), lambda s: s


def near_kernel(info_ref, q, keys, values, total, weight, top):
    seq = Info(info_ref).seq

    def emit(spot, o, l, m):
        total[:, spot] = o
        weight[:, spot] = l
        top[:, spot] = m

    for k in range(SEQS):

        @pl.when(seq == k)
        def _(k=k):
            soft_heads(q, slice(0, PAGE), [near_segment(keys, values, k, 0)], emit)


def attend_near(info, q, keys, values):
    state = jax.ShapeDtypeStruct((PAGE, q.shape[1]), F32)
    return pl.pallas_call(
        near_kernel,
        out_shape=[state] * 3,
        in_specs=[SMEM] + [VMEM] * 3,
        out_specs=[VMEM] * 3,
        compiler_params=params(32),
        cost_estimate=cost(PAGE * WINDOW, 4 * WINDOW),
    )(info, q, keys, values)


def partner_product(info, heads_out, w, partial):
    cols = partial.shape[1]
    here = pl.ds(pl.multiple_of((1 - info.tensor) * cols, cols), cols)
    partial[...] = jnp.dot(heads_out[...], w[:, here], preferred_element_type=F32).astype(BF16)


def far_kernel(
    info_ref, q, total, weight, top, z1, z2, z3, w, heads_out, partial, keys, values
):
    info = Info(info_ref)
    rows = q.shape[0]
    seq = info.seq
    zs = (None, z1, z2, z3)
    is_key = info.tensor == 0

    for k in range(SEQS):

        @pl.when(seq == k)
        def _(k=k):
            if k == 0:
                heads_out[...] = (total[...] / weight[...]).astype(BF16)
                return
            for n in range(k):
                z = zs[n ^ k]
                here = slice(n * rows, (n + 1) * rows)
                a, b = z[0], z[1]
                keys[here] = jnp.where(is_key, a, b)
                widen(jnp.where(is_key, b, a).astype(F32), 1.0, values, here)

            def emit(spot, o, l, m):
                before = top[:, spot]
                peak = jnp.maximum(before, m)
                a = jnp.exp2(before - peak)
                b = jnp.exp2(m - peak)
                done = (total[:, spot] * a + o * b) / (weight[:, spot] * a + l * b)
                heads_out[:, spot] = done.astype(BF16)

            soft_heads(q, slice(0, PAGE), [far_segment(keys, values, k)], emit)

    partner_product(info, heads_out, w, partial)


def attend_far(info, q, state, zs, w):
    rows = q.shape[0]
    span = (SEQS - 1) * rows
    return pl.pallas_call(
        far_kernel,
        out_shape=[
            jax.ShapeDtypeStruct((PAGE, q.shape[1]), BF16),
            jax.ShapeDtypeStruct((PAGE, w.shape[1] // TENSORS), BF16),
            jax.ShapeDtypeStruct((span, 2 * HD), BF16),
            jax.ShapeDtypeStruct((2, span, 2 * HD), BF16),
        ],
        in_specs=[SMEM] + [VMEM] * 8,
        out_specs=[VMEM] * 4,
        compiler_params=params(24),
        cost_estimate=cost(rows * span, 4 * span),
    )(info, q, *state, *zs, w)


def last_kernel(info_ref, q, keys, values, far_keys, far_values, w, heads_out, partial):
    info = Info(info_ref)

    def emit(spot, o, l, m):
        heads_out[:, spot] = (o / l).astype(BF16)

    for k in range(SEQS):

        @pl.when(info.seq == k)
        def _(k=k):
            segments = [near_segment(keys, values, k, 1)]
            if k:
                segments.append(far_segment(far_keys, far_values, k))
            soft_heads(q, slice(PAGE, 2 * PAGE), segments, emit)

    partner_product(info, heads_out, w, partial)


def attend_last(info, q, keys, values, far_keys, far_values, w):
    return pl.pallas_call(
        last_kernel,
        out_shape=[
            jax.ShapeDtypeStruct((PAGE, q.shape[1]), BF16),
            jax.ShapeDtypeStruct((PAGE, w.shape[1] // TENSORS), BF16),
        ],
        in_specs=[SMEM] + [VMEM] * 6,
        out_specs=[VMEM] * 2,
        compiler_params=params(36),
        cost_estimate=cost(PAGE * WINDOW, 4 * WINDOW),
    )(info, q, keys, values, far_keys, far_values, w)


def home_kernel(info_ref, x1, x2, away, w, out, home, first, sem):
    rows, cols = home.shape
    here = pl.ds(pl.multiple_of(Info(info_ref).tensor * cols, cols), cols)
    x = jnp.concatenate([x1[...], x2[...]], axis=0)
    o = jnp.dot(x, w[:, here], preferred_element_type=F32).astype(BF16)
    home[...] = o[rows:]
    first[...] = (o[:rows].astype(F32) + away[...].astype(F32)).astype(BF16)
    copy = pltpu.make_async_copy(first, out.at[pl.ds(0, rows)], sem)
    copy.start()
    copy.wait()


def home_project(info, x1, x2, away, w):
    rows, depth = x1.shape
    cols = w.shape[1] // TENSORS
    return pl.pallas_call(
        home_kernel,
        out_shape=[
            jax.ShapeDtypeStruct((2 * rows, cols), BF16),
            jax.ShapeDtypeStruct((rows, cols), BF16),
        ],
        in_specs=[SMEM] + [VMEM] * 4,
        out_specs=[STAYS, VMEM],
        scratch_shapes=[pltpu.VMEM((rows, cols), BF16), pltpu.SemaphoreType.DMA],
        compiler_params=params(16),
        cost_estimate=cost(20 * 10**9, 2 * depth * cols),
    )(info, x1, x2, away, w)


def add_kernel(before, a, b, out, last, sem):
    rows = a.shape[0]
    last[...] = (a[...].astype(F32) + b[...].astype(F32)).astype(BF16)
    copy = pltpu.make_async_copy(last, out.at[pl.ds(rows, rows)], sem)
    copy.start()
    copy.wait()


def added(before, a, b):
    return pl.pallas_call(
        add_kernel,
        out_shape=jax.ShapeDtypeStruct(before.shape, BF16),
        in_specs=[STAYS, VMEM, VMEM],
        out_specs=STAYS,
        scratch_shapes=[pltpu.VMEM(a.shape, BF16), pltpu.SemaphoreType.DMA],
        input_output_aliases={0: 0},
        compiler_params=params(8),
    )(before, a, b)


def flipped(value, axes, count, bits):
    return lax.ppermute(value, axes, [(i, i ^ bits) for i in range(count)])


def after(value, *others):
    return lax.optimization_barrier((value, *others))[0]


def shards_fast(
    span_tokens, q_weight, kv_weight, out_weight, kv_pool, cache_lengths, slot_requests, page_table
):
    group_id = lax.axis_index("group")
    seq_id = lax.axis_index("seq")
    tensor_id = lax.axis_index("tensor")
    place = jnp.stack([group_id, seq_id, tensor_id]).astype(jnp.int32)
    row = jnp.concatenate([place, slot_requests, cache_lengths])
    row = jnp.pad(row, (0, page_table.shape[1] - row.shape[0]))
    info = jnp.concatenate([row[None], page_table])
    mine = span_tokens[0]
    theirs = flipped(mine, "tensor", 2, 1)
    half_dim = HD // 2
    lane = jnp.arange(128, dtype=jnp.int32) % half_dim
    frequency = jnp.power(jnp.float32(10000.0), -lane.astype(F32) / half_dim)
    frequency = jnp.broadcast_to(frequency[None, :], (8, 128))
    pages = open_rows(info, frequency, kv_pool, mine, q_weight, kv_weight)
    home, same, beyond, beside, across, diagonal = pages[:6]
    acc_q, acc_kv, cosine, sine = pages[6:]
    capacity = home.shape[0]
    same = flipped(same, "tensor", 2, 1)
    beyond = flipped(beyond, "group", 4, 2)
    kept, sent = fresh_rows(info, theirs, kv_weight, acc_kv, cosine, sine)
    got = flipped(sent, "tensor", 2, 1)
    across, diagonal, _ = lax.optimization_barrier((across, diagonal, sent))
    across = flipped(across, ("group", "tensor"), 8, 5)
    diagonal = flipped(diagonal, ("group", "tensor"), 8, 7)
    same, beyond, _ = lax.optimization_barrier((same, beyond, sent))
    mate = jnp.concatenate([beside, beyond[capacity:], same[capacity:]])
    mate = flipped(mate, "group", 4, 1)
    fresh = bundled(kept[None], got[None])
    zs = [flipped(fresh, "seq", 4, d) for d in range(1, 4)]
    q = query_rows(after(info, fresh), theirs, q_weight, acc_q, cosine, sine)
    across, diagonal, _ = lax.optimization_barrier((across, diagonal, q))
    other_chip = bundled(across, diagonal)
    own = jnp.concatenate(
        [home, mate[:capacity], beyond[:capacity], mate[capacity : 2 * capacity]]
    )
    other = jnp.concatenate([same[:capacity], mate[2 * capacity :], other_chip])
    keys, values = gather_rows(info, own, other, fresh)
    state = attend_near(info, q, keys, values)
    heads_0, partial_0, far_keys, far_values = attend_far(info, q, state, zs, out_weight)
    away_0 = flipped(partial_0, "tensor", 2, 1)
    heads_1, partial_1 = attend_last(info, q, keys, values, far_keys, far_values, out_weight)
    away_1 = flipped(partial_1, "tensor", 2, 1)
    out, home_1 = home_project(info, heads_0, heads_1, away_0, out_weight)
    return added(out, home_1, away_1)[None]


def solution(mesh):
    sizes = tuple(mesh.shape[a] for a in ("group", "seq", "tensor"))
    body = shards_fast if sizes == (GROUPS, SEQS, TENSORS) else shards
    placed = (
        P("group", "seq", "tensor"),
        P(None, "tensor"),
        P(None, "tensor"),
        P("tensor", None),
        P("group", None, "tensor"),
        P(),
        P(),
        P(),
    )
    return jax.shard_map(
        body, mesh=mesh, in_specs=placed, out_specs=P("group", "seq", "tensor"), check_vma=False
    )
```

```python
import functools

import jax
import jax.numpy as jnp
from jax import lax
from jax.experimental import pallas as pl
from jax.experimental.pallas import tpu as pltpu
from jax.sharding import PartitionSpec as P

HD = 64
KVH = 4
WINDOW = 2048
PAGE = 128


def shifted(block, axis, distance):
    devices = range(lax.axis_size(axis))
    route = [(i - distance, i) for i in devices if i - distance in devices]
    return lax.ppermute(block, axis, route)


def swapped(value, axis, stride):
    return lax.ppermute(value, axis, [(i, i ^ 1 << stride) for i in range(lax.axis_size(axis))])


def rotate(values, positions):
    half_dim = HD // 2
    frequency = jnp.power(jnp.float32(10000.0), -jnp.arange(half_dim, dtype=jnp.float32) / half_dim)
    angles = positions.astype(jnp.float32)[:, None] * frequency[None, :]
    cosine = jnp.cos(angles)[:, None, :]
    sine_part = jnp.sin(angles)[:, None, :]
    front_half = values[..., :half_dim]
    back_half = values[..., half_dim:]
    return jnp.concatenate(
        [front_half * cosine - back_half * sine_part, back_half * cosine + front_half * sine_part],
        axis=-1,
    )


def attend(block_q, block_k, block_v, base_pos):
    query_count = block_q.shape[0]
    key_count = block_k.shape[0]
    scores = jnp.einsum(
        "tkgd,nkd->kgtn", block_q, block_k, preferred_element_type=jnp.float32
    ) * HD ** (-0.5)
    query_at = jnp.arange(query_count, dtype=jnp.int32)[:, None]
    key_at = jnp.arange(key_count, dtype=jnp.int32)[None, :]
    allowed = (key_at > query_at) & (key_at <= query_at + WINDOW) & (base_pos + key_at >= 0)
    masked = jnp.where(allowed, scores, jnp.float32(-1e30))
    row_top = jnp.max(masked, axis=-1, keepdims=True)
    weights = jnp.where(allowed, jnp.exp(masked - row_top), jnp.float32(0.0))
    row_total = jnp.sum(weights, axis=-1)
    rounded = weights.astype(jnp.bfloat16)
    mixed_rows = jnp.einsum("kgtn,nkd->tkgd", rounded, block_v, preferred_element_type=jnp.float32)
    mixed_rows = mixed_rows / jnp.transpose(row_total, (2, 0, 1))[..., None]
    return mixed_rows.astype(jnp.bfloat16).reshape(query_count, -1)


def shards(
    span_tokens, q_weight, kv_weight, out_weight, kv_pool, cache_lengths, slot_requests, page_table
):
    groups = lax.axis_size("group")
    seq_count = lax.axis_size("seq")
    tensor_count = lax.axis_size("tensor")
    group_id = lax.axis_index("group")
    seq_id = lax.axis_index("seq")
    tensor_id = lax.axis_index("tensor")
    local_reqs, seg_len, feat_local = span_tokens.shape
    head_cols = q_weight.shape[1]
    kv_cols = kv_weight.shape[1]
    local_heads = head_cols // HD
    group_heads = kv_cols // HD
    kv_local = max(1, KVH // tensor_count)
    per_kv = local_heads // kv_local
    head_first = tensor_id * KVH // tensor_count % group_heads
    holds_keys = tensor_id % 2 == 0
    pool_rows = kv_pool.shape[0]
    capacity = pool_rows // groups
    row_count = local_reqs * seg_len
    my_slots = group_id * local_reqs + jnp.arange(local_reqs, dtype=jnp.int32)
    my_requests = slot_requests[my_slots]
    my_lengths = cache_lengths[my_requests]
    project_piece_rows = lax.all_gather(span_tokens, "tensor", axis=2, tiled=True)
    feat_width = project_piece_rows.shape[2]
    flat_rows = project_piece_rows.reshape(row_count, feat_width)
    query_lin = jnp.dot(flat_rows, q_weight, preferred_element_type=jnp.float32)
    fresh_lin = jnp.dot(flat_rows, kv_weight, preferred_element_type=jnp.float32)
    positions = (
        my_lengths[:, None] + seq_id * seg_len + jnp.arange(seg_len, dtype=jnp.int32)[None, :]
    )
    queries = jax.vmap(rotate)(query_lin.reshape(local_reqs, seg_len, local_heads, HD), positions)
    queries = queries.astype(jnp.bfloat16).reshape(local_reqs, seg_len, kv_local, per_kv, HD)
    fresh_heads = fresh_lin.reshape(local_reqs, seg_len, group_heads, HD)
    rotated = jax.vmap(rotate)(fresh_heads, positions)
    span_kv = (
        jnp.where(holds_keys, rotated, fresh_heads)
        .astype(jnp.bfloat16)
        .reshape(local_reqs, seg_len, kv_cols)
    )
    all_ids = page_table[slot_requests]
    owned_here = all_ids // pool_rows == group_id
    slot_rank = jnp.cumsum(owned_here.astype(jnp.int32), axis=1) - 1
    local_rows = all_ids - group_id * pool_rows
    chosen = owned_here[:, :, None] & (
        slot_rank[:, :, None] == jnp.arange(capacity, dtype=jnp.int32)[None, None, :]
    )
    wanted = jnp.sum(jnp.where(chosen, local_rows[:, :, None], 0), axis=1)
    my_ids = page_table[my_requests].reshape(-1)
    my_owner = my_ids // pool_rows
    onehot = (my_owner[:, None] == jnp.arange(groups, dtype=jnp.int32)[None, :]).astype(jnp.int32)
    arrival = jnp.sum((jnp.cumsum(onehot, axis=0) - 1) * onehot, axis=1)
    arrived_row = my_owner * capacity + arrival
    outgoing = kv_pool[wanted]
    arrived = lax.all_to_all(outgoing, "group", split_axis=0, concat_axis=0, tiled=True)
    cached = arrived.reshape(groups * capacity, PAGE, kv_cols)[arrived_row]
    cached = cached.reshape(local_reqs, WINDOW, kv_cols)
    span_all = jnp.zeros((local_reqs, seg_len * seq_count, kv_cols), jnp.bfloat16)
    for back_step in range(seq_count - 1, -1, -1):
        piece_rows = span_kv if back_step == 0 else shifted(span_kv, "seq", back_step)
        span_all = lax.dynamic_update_slice_in_dim(
            span_all, piece_rows, (seq_id - back_step) * seg_len, 1
        )
    joined = jnp.concatenate([cached, span_all], axis=1)
    visible = lax.dynamic_slice_in_dim(joined, seq_id * seg_len, WINDOW + seg_len, 1)
    partner_rows = swapped(visible, "tensor", 0)
    key_all = jnp.where(holds_keys, visible, partner_rows).reshape(
        local_reqs, WINDOW + seg_len, group_heads, HD
    )
    value_all = jnp.where(holds_keys, partner_rows, visible).reshape(
        local_reqs, WINDOW + seg_len, group_heads, HD
    )
    key_rows = lax.dynamic_slice_in_dim(key_all, head_first, kv_local, 2)
    value_rows = lax.dynamic_slice_in_dim(value_all, head_first, kv_local, 2)
    block_len = min(128, seg_len)
    block_count = seg_len // block_len

    def per_request(request_items):
        request_q, request_k, request_v, length = request_items

        def per_block(block_index):
            first_row = block_index * block_len
            block_q = lax.dynamic_slice_in_dim(request_q, first_row, block_len, 0)
            block_k = lax.dynamic_slice_in_dim(request_k, first_row, WINDOW + block_len, 0)
            block_v = lax.dynamic_slice_in_dim(request_v, first_row, WINDOW + block_len, 0)
            return attend(block_q, block_k, block_v, length - WINDOW + seq_id * seg_len + first_row)

        return lax.map(per_block, jnp.arange(block_count, dtype=jnp.int32)).reshape(
            seg_len, head_cols
        )

    attended_heads = lax.map(per_request, (queries, key_rows, value_rows, my_lengths))
    flat_heads = attended_heads.reshape(row_count, head_cols)
    out_cols = out_weight.shape[1] // tensor_count
    summed = lax.psum_scatter(
        lax.dot_general(
            out_weight, flat_heads, (((0,), (1,)), ((), ())), preferred_element_type=jnp.float32
        ).astype(jnp.bfloat16),
        "tensor",
        scatter_dimension=0,
        tiled=True,
    ).astype(jnp.float32)
    result = summed.T
    return result.astype(jnp.bfloat16).reshape(local_reqs, seg_len, out_cols)


LOG2E = 1.4426950408889634
MASKED = -1e30
F32 = jnp.float32
BF16 = jnp.bfloat16
HBM = pl.BlockSpec(memory_space=pl.ANY)
VMEM = pl.BlockSpec(memory_space=pltpu.VMEM)
SMEM = pl.BlockSpec(memory_space=pltpu.SMEM)
STAYS = pl.BlockSpec(memory_space=pltpu.HBM)
GROUPS, SEQS, TENSORS = 4, 4, 2


def params(mebibytes):
    return pltpu.CompilerParams(vmem_limit_bytes=mebibytes * 2**20)


def cost(flops, moved):
    return pl.CostEstimate(flops=flops, bytes_accessed=moved, transcendentals=0)


class Info:
    def __init__(self, ref):
        self.ref = ref
        self.group, self.seq, self.tensor = ref[0, 0], ref[0, 1], ref[0, 2]
        self.window_pages = ref.shape[1]

    def request(self, slot):
        return self.ref[0, 3 + slot]

    def length(self, request):
        return self.ref[0, 3 + GROUPS + request]

    def page(self, request, w):
        return self.ref[1 + request, w]


def turned(x, cosine, sine):
    lane = lax.broadcasted_iota(jnp.int32, x.shape, 1)
    other = jnp.where(lane % HD < HD // 2, pltpu.roll(x, 128 - HD // 2, 1), pltpu.roll(x, HD // 2, 1))
    return x * cosine + other * sine


def open_kernel(
    info_ref, frequency, pool, x_hbm, wq_hbm, wkv_hbm,
    home, same, beyond, beside, across, diagonal, acc_q, acc_kv, cosine, sine,
    x, wq, wkv, sems, page_sems,
):
    info = Info(info_ref)
    rows, feats = x.shape
    here = pl.ds(pl.multiple_of(info.tensor * feats, feats), feats)
    copies = [
        pltpu.make_async_copy(x_hbm, x, sems.at[0]),
        pltpu.make_async_copy(wkv_hbm.at[here], wkv, sems.at[1]),
        pltpu.make_async_copy(wq_hbm.at[here], wq, sems.at[2]),
    ]
    for copy in copies:
        copy.start()
    pages = pool.shape[0]
    capacity = pages // GROUPS
    half = pool.shape[2] // 2
    mine = pl.ds(pl.multiple_of(info.tensor * half, half), half)
    theirs = pl.ds(pl.multiple_of((1 - info.tensor) * half, half), half)
    outs = (home, same, beyond, beside, across, diagonal)
    spots = (
        ((0, 0), (1, 0)),
        ((3, 0), (1, capacity)),
        ((2, 0), (4, 0)),
        ((2, capacity), (5, 0)),
    )
    for flip, targets in enumerate(spots):
        request = info.request(info.group ^ flip)

        def take(w, rank):
            page = info.page(request, w)
            near = page // pages == info.group

            @pl.when(near)
            def _():
                row = page % pages
                for (out, base), cols in zip(targets, (mine, theirs)):
                    pltpu.make_async_copy(
                        pool.at[row, :, cols], outs[out].at[base + rank], page_sems.at[out]
                    ).start()

            return rank + near.astype(jnp.int32)

        lax.fori_loop(0, info.window_pages, take, jnp.int32(0))
    start = info.length(info.request(info.group)) + info.seq * rows
    position = (start + lax.broadcasted_iota(jnp.int32, (rows, 128), 0)).astype(F32)
    angles = position * frequency[0:1, :]
    lane = lax.broadcasted_iota(jnp.int32, (rows, 128), 1)
    cosine[...] = jnp.cos(angles)
    sine[...] = jnp.where(lane % HD < HD // 2, -1.0, 1.0) * jnp.sin(angles)
    copies[0].wait()
    copies[1].wait()
    acc_kv[...] = jnp.dot(x[...], wkv[...], preferred_element_type=F32)
    copies[2].wait()
    acc_q[...] = jnp.dot(x[...], wq[...], preferred_element_type=F32)
    for i, out in enumerate(outs):
        pltpu.make_async_copy(out, out, page_sems.at[i]).wait()


def open_rows(info, frequency, pool, x, wq, wkv):
    rows, feats = x.shape
    pages, page, cols = pool.shape
    single = jax.ShapeDtypeStruct((pages // GROUPS, page, cols // 2), BF16)
    double = jax.ShapeDtypeStruct((2 * pages // GROUPS, page, cols // 2), BF16)
    table = jax.ShapeDtypeStruct((rows, 128), F32)
    return pl.pallas_call(
        open_kernel,
        out_shape=[
            single,
            double,
            double,
            single,
            single,
            single,
            jax.ShapeDtypeStruct((rows, wq.shape[1]), F32),
            jax.ShapeDtypeStruct((rows, wkv.shape[1]), F32),
            table,
            table,
        ],
        in_specs=[SMEM, VMEM] + [STAYS] * 4,
        out_specs=[VMEM] * 10,
        scratch_shapes=[
            pltpu.VMEM((rows, feats), BF16),
            pltpu.VMEM((feats, wq.shape[1]), BF16),
            pltpu.VMEM((feats, wkv.shape[1]), BF16),
            pltpu.SemaphoreType.DMA((3,)),
            pltpu.SemaphoreType.DMA((6,)),
        ],
        compiler_params=params(50),
        cost_estimate=cost(rows * feats, rows * feats),
    )(info, frequency, pool, x, wq, wkv)


def fresh_kernel(info_ref, x, wkv, acc_kv, cosine, sine, kept, sent):
    info = Info(info_ref)
    feats = x.shape[1]
    here = pl.ds(pl.multiple_of((1 - info.tensor) * feats, feats), feats)
    keys = info.tensor == 0
    fresh = acc_kv[...] + jnp.dot(x[...], wkv[here], preferred_element_type=F32)
    cos_kv = jnp.where(keys, cosine[...], 1.0)
    sin_kv = jnp.where(keys, sine[...], 0.0)
    low = turned(fresh[:, :128], cos_kv, sin_kv).astype(BF16)
    high = turned(fresh[:, 128:], cos_kv, sin_kv).astype(BF16)
    kept[...] = jnp.where(keys, low, high)
    sent[...] = jnp.where(keys, high, low)


def fresh_rows(info, x, wkv, acc_kv, cosine, sine):
    rows, feats = x.shape
    piece = jax.ShapeDtypeStruct((rows, wkv.shape[1] // 2), BF16)
    return pl.pallas_call(
        fresh_kernel,
        out_shape=[piece, piece],
        in_specs=[SMEM] + [VMEM] * 5,
        out_specs=[VMEM] * 2,
        compiler_params=params(12),
        cost_estimate=cost(2 * rows * feats * 2560, rows * feats),
    )(info, x, wkv, acc_kv, cosine, sine)


def query_kernel(info_ref, x, wq, acc_q, cosine, sine, q):
    feats = x.shape[1]
    here = pl.ds(pl.multiple_of((1 - Info(info_ref).tensor) * feats, feats), feats)
    cos_all, sin_all = cosine[...], sine[...]
    scale = HD**-0.5 * LOG2E
    tile = 256
    for c in range(0, q.shape[1], tile):
        lin = acc_q[:, c : c + tile] + jnp.dot(
            x[...], wq[here, c : c + tile], preferred_element_type=F32
        )
        for e in range(0, tile, 128):
            q[:, c + e : c + e + 128] = (
                turned(lin[:, e : e + 128], cos_all, sin_all) * scale
            ).astype(BF16)


def query_rows(info, x, wq, acc_q, cosine, sine):
    rows, feats = x.shape
    return pl.pallas_call(
        query_kernel,
        out_shape=jax.ShapeDtypeStruct((rows, wq.shape[1]), BF16),
        in_specs=[SMEM] + [VMEM] * 5,
        out_specs=VMEM,
        compiler_params=params(16),
        cost_estimate=cost(rows * feats, rows * feats),
    )(info, x, wq, acc_q, cosine, sine)


def soft_heads(q, tokens, segments, emit):
    rows = tokens.stop - tokens.start
    stack = 4
    low = lax.broadcasted_iota(jnp.int32, (rows, 2 * HD), 1) < HD

    def swap(x):
        return pltpu.roll(x, HD, 1)

    def heads(i, _):
        first = i == 0
        spots = [pl.ds(pl.multiple_of((i * stack + j) * 128, 128), 128) for j in range(stack)]
        tiles = [q[tokens, spot] for spot in spots]
        turns = [swap(x.astype(F32)).astype(BF16) for x in tiles]
        keep = low == first

        def stacked(a, b):
            zero = jnp.zeros_like(a[0])
            return jnp.concatenate(
                [jnp.where(keep, jnp.where(first, x, y), zero) for x, y in zip(a, b)], axis=0
            )

        def scores(qs):
            return [
                mask(
                    lax.dot_general(
                        qs, keys[span], (((1,), (1,)), ((), ())), preferred_element_type=F32
                    )
                )
                for keys, _, span, mask in segments
            ]

        def peak(parts):
            tops = [jnp.max(s, axis=1, keepdims=True) for s in parts]
            return functools.reduce(jnp.maximum, tops)

        def mixed(weights):
            return sum(
                jnp.dot(p, values[i, span], preferred_element_type=F32)
                for p, (_, values, span, _) in zip(weights, segments)
            )

        s_even = scores(stacked(tiles, turns))
        s_odd = scores(stacked(turns, tiles))
        m_even = peak(s_even)
        m_odd = peak(s_odd)
        p_even = [jnp.exp2(s - m_even).astype(BF16) for s in s_even]
        p_odd = [jnp.exp2(s - m_odd).astype(BF16) for s in s_odd]
        o_even = mixed(p_even)
        o_odd = mixed(p_odd)
        for j in range(stack):
            part = slice(j * rows, (j + 1) * rows)
            a, b = o_even[part], o_odd[part]
            total = jnp.where(low, a, swap(b))
            weight = jnp.where(low, swap(a), b)
            top = jnp.where(low, m_even[part], m_odd[part])
            emit(spots[j], total, weight, top)
        return 0

    lax.fori_loop(0, q.shape[1] // 128 // stack, heads, 0)


def widen(v, ones, values, here):
    low = lax.broadcasted_iota(jnp.int32, v.shape, 1) < HD
    values[0, here] = jnp.where(low, v, ones).astype(BF16)
    values[1, here] = jnp.where(low, pltpu.roll(v, HD, 1), ones).astype(BF16)


def gather_kernel(info_ref, own, other, fresh, keys, values, source):
    info = Info(info_ref)
    group, seq = info.group, info.seq
    request = info.request(group)
    rows = fresh.shape[1]
    per = rows // PAGE
    count = own.shape[0]
    capacity = count // GROUPS
    seen = keys.shape[0] // PAGE - seq * per
    is_key = info.tensor == 0

    def note(w, counts):
        came = info.page(request, w) // count ^ group
        place = came * capacity
        for d in range(GROUPS):
            place = place + jnp.where(came == d, counts[d], 0)
        source[w] = place
        return tuple(counts[d] + (came == d).astype(jnp.int32) for d in range(GROUPS))

    lax.fori_loop(0, info.window_pages, note, (jnp.int32(0),) * GROUPS)

    def place(block, a, b):
        here = pl.ds(pl.multiple_of(block * PAGE, PAGE), PAGE)
        keys[here] = jnp.where(is_key, a, b)
        widen(jnp.where(is_key, b, a).astype(F32), 1.0, values, here)

    for block, part in ((1, slice(0, PAGE)), (seen - 1, slice(PAGE, 2 * PAGE))):
        place(block, fresh[0, part], fresh[1, part])
    first = info.length(request) - WINDOW + seq * rows
    stand_in = jnp.where(is_key, fresh[0, :16], fresh[1, :16]).astype(F32)[0:1]
    stand_in = jnp.broadcast_to(stand_in, (PAGE, 2 * HD)).astype(BF16)

    def bring(i, _):
        for n in (2 * i, 2 * i + 1):
            block = jnp.where(n == 0, 0, n + 1)
            here = pl.ds(pl.multiple_of(block * PAGE, PAGE), PAGE)
            at = source[seq * per + n]
            hidden = first + n * PAGE < 0
            a, b = own[at], other[at]
            keys[here] = jnp.where(hidden, stand_in, jnp.where(is_key, a, b))
            v = jnp.where(is_key, b, a).astype(F32)
            widen(jnp.where(hidden, 0.0, v), jnp.where(hidden, 0.0, 1.0), values, here)
        return 0

    lax.fori_loop(0, (seen - per) // 2, bring, 0)


def gather_rows(info, own, other, fresh):
    span = WINDOW + fresh.shape[1]
    return pl.pallas_call(
        gather_kernel,
        out_shape=[
            jax.ShapeDtypeStruct((span, 2 * HD), BF16),
            jax.ShapeDtypeStruct((2, span, 2 * HD), BF16),
        ],
        in_specs=[SMEM] + [VMEM] * 3,
        out_specs=[VMEM] * 2,
        scratch_shapes=[pltpu.SMEM((own.shape[0],), jnp.int32)],
        compiler_params=params(12),
        cost_estimate=cost(20 * 10**9, 4 * span),
    )(info, own, other, fresh)


def bundle_kernel(a, b, out):
    out[: a.shape[0]] = a[...]
    out[a.shape[0] :] = b[...]


def bundled(a, b):
    return pl.pallas_call(
        bundle_kernel,
        out_shape=jax.ShapeDtypeStruct((a.shape[0] + b.shape[0], *a.shape[1:]), BF16),
        in_specs=[VMEM] * 2,
        out_specs=VMEM,
        compiler_params=params(8),
        cost_estimate=cost(6 * 10**9, 4),
    )(a, b)


def near_segment(keys, values, seq, half):
    blocks = keys.shape[0] // PAGE
    per = 2
    span = slice(half * PAGE, (blocks - seq * per - 1 + half) * PAGE)

    def mask(s):
        newer = lax.broadcasted_iota(jnp.int32, (s.shape[0], PAGE), 1) > (
            lax.broadcasted_iota(jnp.int32, (s.shape[0], PAGE), 0) % PAGE
        )
        if half == 0:
            parts = [
                jnp.where(newer, s[:, :PAGE], MASKED),
                jnp.where(newer, MASKED, s[:, PAGE : 2 * PAGE]),
                s[:, 2 * PAGE :],
            ]
        else:
            parts = [
                s[:, :PAGE],
                jnp.where(newer, s[:, PAGE : 2 * PAGE], MASKED),
                s[:, 2 * PAGE : -PAGE],
                jnp.where(newer, MASKED, s[:, -PAGE:]),
            ]
        return jnp.concatenate(parts, axis=1)

    return keys, values, span, mask


def far_segment(keys, values, seq):
    return keys, values, slice(0, seq * 2 * PAGE), lambda s: s


def near_kernel(info_ref, q, keys, values, total, weight, top):
    seq = Info(info_ref).seq

    def emit(spot, o, l, m):
        total[:, spot] = o
        weight[:, spot] = l
        top[:, spot] = m

    for k in range(SEQS):

        @pl.when(seq == k)
        def _(k=k):
            soft_heads(q, slice(0, PAGE), [near_segment(keys, values, k, 0)], emit)


def attend_near(info, q, keys, values):
    state = jax.ShapeDtypeStruct((PAGE, q.shape[1]), F32)
    return pl.pallas_call(
        near_kernel,
        out_shape=[state] * 3,
        in_specs=[SMEM] + [VMEM] * 3,
        out_specs=[VMEM] * 3,
        compiler_params=params(32),
        cost_estimate=cost(PAGE * WINDOW, 4 * WINDOW),
    )(info, q, keys, values)


def partner_product(info, heads_out, w, partial):
    cols = partial.shape[1]
    here = pl.ds(pl.multiple_of((1 - info.tensor) * cols, cols), cols)
    partial[...] = jnp.dot(heads_out[...], w[:, here], preferred_element_type=F32).astype(BF16)


def far_kernel(
    info_ref, q, total, weight, top, z3, z2, z1, w, heads_out, partial, keys, values
):
    info = Info(info_ref)
    rows = q.shape[0]
    seq = info.seq
    zs = (None, z1, z2, z3)
    is_key = info.tensor == 0

    for k in range(SEQS):

        @pl.when(seq == k)
        def _(k=k):
            if k == 0:
                heads_out[...] = (total[...] / weight[...]).astype(BF16)
                return
            for n in range(k):
                z = zs[n ^ k]
                here = slice(n * rows, (n + 1) * rows)
                a, b = z[0], z[1]
                keys[here] = jnp.where(is_key, a, b)
                widen(jnp.where(is_key, b, a).astype(F32), 1.0, values, here)

            def emit(spot, o, l, m):
                before = top[:, spot]
                peak = jnp.maximum(before, m)
                a = jnp.exp2(before - peak)
                b = jnp.exp2(m - peak)
                done = (total[:, spot] * a + o * b) / (weight[:, spot] * a + l * b)
                heads_out[:, spot] = done.astype(BF16)

            soft_heads(q, slice(0, PAGE), [far_segment(keys, values, k)], emit)

    partner_product(info, heads_out, w, partial)


def attend_far(info, q, state, zs, w):
    rows = q.shape[0]
    span = (SEQS - 1) * rows
    return pl.pallas_call(
        far_kernel,
        out_shape=[
            jax.ShapeDtypeStruct((PAGE, q.shape[1]), BF16),
            jax.ShapeDtypeStruct((PAGE, w.shape[1] // TENSORS), BF16),
            jax.ShapeDtypeStruct((span, 2 * HD), BF16),
            jax.ShapeDtypeStruct((2, span, 2 * HD), BF16),
        ],
        in_specs=[SMEM] + [VMEM] * 8,
        out_specs=[VMEM] * 4,
        compiler_params=params(24),
        cost_estimate=cost(rows * span, 4 * span),
    )(info, q, *state, *zs, w)


def last_kernel(info_ref, q, keys, values, far_keys, far_values, w, heads_out, partial):
    info = Info(info_ref)

    def emit(spot, o, l, m):
        heads_out[:, spot] = (o / l).astype(BF16)

    for k in range(SEQS):

        @pl.when(info.seq == k)
        def _(k=k):
            segments = [near_segment(keys, values, k, 1)]
            if k:
                segments.append(far_segment(far_keys, far_values, k))
            soft_heads(q, slice(PAGE, 2 * PAGE), segments, emit)

    partner_product(info, heads_out, w, partial)


def attend_last(info, q, keys, values, far_keys, far_values, w):
    return pl.pallas_call(
        last_kernel,
        out_shape=[
            jax.ShapeDtypeStruct((PAGE, q.shape[1]), BF16),
            jax.ShapeDtypeStruct((PAGE, w.shape[1] // TENSORS), BF16),
        ],
        in_specs=[SMEM] + [VMEM] * 6,
        out_specs=[VMEM] * 2,
        compiler_params=params(36),
        cost_estimate=cost(PAGE * WINDOW, 4 * WINDOW),
    )(info, q, keys, values, far_keys, far_values, w)


def home_kernel(info_ref, x1, x2, away, w, out, home, first, sem):
    rows, cols = home.shape
    here = pl.ds(pl.multiple_of(Info(info_ref).tensor * cols, cols), cols)
    x = jnp.concatenate([x1[...], x2[...]], axis=0)
    o = jnp.dot(x, w[:, here], preferred_element_type=F32).astype(BF16)
    home[...] = o[rows:]
    first[...] = (o[:rows].astype(F32) + away[...].astype(F32)).astype(BF16)
    copy = pltpu.make_async_copy(first, out.at[pl.ds(0, rows)], sem)
    copy.start()
    copy.wait()


def home_project(info, x1, x2, away, w):
    rows, depth = x1.shape
    cols = w.shape[1] // TENSORS
    return pl.pallas_call(
        home_kernel,
        out_shape=[
            jax.ShapeDtypeStruct((2 * rows, cols), BF16),
            jax.ShapeDtypeStruct((rows, cols), BF16),
        ],
        in_specs=[SMEM] + [VMEM] * 4,
        out_specs=[STAYS, VMEM],
        scratch_shapes=[pltpu.VMEM((rows, cols), BF16), pltpu.SemaphoreType.DMA],
        compiler_params=params(16),
        cost_estimate=cost(20 * 10**9, 2 * depth * cols),
    )(info, x1, x2, away, w)


def add_kernel(before, a, b, out, last, sem):
    rows = a.shape[0]
    last[...] = (a[...].astype(F32) + b[...].astype(F32)).astype(BF16)
    copy = pltpu.make_async_copy(last, out.at[pl.ds(rows, rows)], sem)
    copy.start()
    copy.wait()


def added(before, a, b):
    return pl.pallas_call(
        add_kernel,
        out_shape=jax.ShapeDtypeStruct(before.shape, BF16),
        in_specs=[STAYS, VMEM, VMEM],
        out_specs=STAYS,
        scratch_shapes=[pltpu.VMEM(a.shape, BF16), pltpu.SemaphoreType.DMA],
        input_output_aliases={0: 0},
        compiler_params=params(8),
    )(before, a, b)


def flipped(value, axes, count, bits):
    return lax.ppermute(value, axes, [(i, i ^ bits) for i in range(count)])


def after(value, *others):
    return lax.optimization_barrier((value, *others))[0]


def shards_fast(
    span_tokens, q_weight, kv_weight, out_weight, kv_pool, cache_lengths, slot_requests, page_table
):
    group_id = lax.axis_index("group")
    seq_id = lax.axis_index("seq")
    tensor_id = lax.axis_index("tensor")
    place = jnp.stack([group_id, seq_id, tensor_id]).astype(jnp.int32)
    row = jnp.concatenate([place, slot_requests, cache_lengths])
    row = jnp.pad(row, (0, page_table.shape[1] - row.shape[0]))
    info = jnp.concatenate([row[None], page_table])
    mine = span_tokens[0]
    theirs = flipped(mine, "tensor", 2, 1)
    half_dim = HD // 2
    lane = jnp.arange(128, dtype=jnp.int32) % half_dim
    frequency = jnp.power(jnp.float32(10000.0), -lane.astype(F32) / half_dim)
    frequency = jnp.broadcast_to(frequency[None, :], (8, 128))
    pages = open_rows(info, frequency, kv_pool, mine, q_weight, kv_weight)
    home, same, beyond, beside, across, diagonal = pages[:6]
    acc_q, acc_kv, cosine, sine = pages[6:]
    capacity = home.shape[0]
    same = flipped(same, "tensor", 2, 1)
    beyond = flipped(beyond, "group", 4, 2)
    kept, sent = fresh_rows(info, theirs, kv_weight, acc_kv, cosine, sine)
    got = flipped(sent, "tensor", 2, 1)
    across, diagonal, _ = lax.optimization_barrier((across, diagonal, sent))
    across = flipped(across, ("group", "tensor"), 8, 5)
    diagonal = flipped(diagonal, ("group", "tensor"), 8, 7)
    q = query_rows(info, theirs, q_weight, acc_q, cosine, sine)
    same, beyond, _ = lax.optimization_barrier((same, beyond, q))
    mate = jnp.concatenate([beside, beyond[capacity:], same[capacity:]])
    mate = flipped(mate, "group", 4, 1)
    fresh = bundled(kept[None], got[None])
    zs = [flipped(fresh, "seq", 4, d) for d in (3, 2, 1)]
    other_chip = bundled(across, diagonal)
    own = jnp.concatenate(
        [home, mate[:capacity], beyond[:capacity], mate[capacity : 2 * capacity]]
    )
    other = jnp.concatenate([same[:capacity], mate[2 * capacity :], other_chip])
    keys, values = gather_rows(info, own, other, fresh)
    state = attend_near(info, q, keys, values)
    heads_0, partial_0, far_keys, far_values = attend_far(info, q, state, zs, out_weight)
    away_0 = flipped(partial_0, "tensor", 2, 1)
    heads_1, partial_1 = attend_last(info, q, keys, values, far_keys, far_values, out_weight)
    away_1 = flipped(partial_1, "tensor", 2, 1)
    out, home_1 = home_project(info, heads_0, heads_1, away_0, out_weight)
    return added(out, home_1, away_1)[None]


def solution(mesh):
    sizes = tuple(mesh.shape[a] for a in ("group", "seq", "tensor"))
    body = shards_fast if sizes == (GROUPS, SEQS, TENSORS) else shards
    placed = (
        P("group", "seq", "tensor"),
        P(None, "tensor"),
        P(None, "tensor"),
        P("tensor", None),
        P("group", None, "tensor"),
        P(),
        P(),
        P(),
    )
    return jax.shard_map(
        body, mesh=mesh, in_specs=placed, out_specs=P("group", "seq", "tensor"), check_vma=False
    )
```

```python
import functools

import jax
import jax.numpy as jnp
from jax import lax
from jax.experimental import pallas as pl
from jax.experimental.pallas import tpu as pltpu
from jax.sharding import PartitionSpec as P

HD = 64
KVH = 4
WINDOW = 2048
PAGE = 128


def shifted(block, axis, distance):
    devices = range(lax.axis_size(axis))
    route = [(i - distance, i) for i in devices if i - distance in devices]
    return lax.ppermute(block, axis, route)


def swapped(value, axis, stride):
    return lax.ppermute(value, axis, [(i, i ^ 1 << stride) for i in range(lax.axis_size(axis))])


def rotate(values, positions):
    half_dim = HD // 2
    frequency = jnp.power(jnp.float32(10000.0), -jnp.arange(half_dim, dtype=jnp.float32) / half_dim)
    angles = positions.astype(jnp.float32)[:, None] * frequency[None, :]
    cosine = jnp.cos(angles)[:, None, :]
    sine_part = jnp.sin(angles)[:, None, :]
    front_half = values[..., :half_dim]
    back_half = values[..., half_dim:]
    return jnp.concatenate(
        [front_half * cosine - back_half * sine_part, back_half * cosine + front_half * sine_part],
        axis=-1,
    )


def attend(block_q, block_k, block_v, base_pos):
    query_count = block_q.shape[0]
    key_count = block_k.shape[0]
    scores = jnp.einsum(
        "tkgd,nkd->kgtn", block_q, block_k, preferred_element_type=jnp.float32
    ) * HD ** (-0.5)
    query_at = jnp.arange(query_count, dtype=jnp.int32)[:, None]
    key_at = jnp.arange(key_count, dtype=jnp.int32)[None, :]
    allowed = (key_at > query_at) & (key_at <= query_at + WINDOW) & (base_pos + key_at >= 0)
    masked = jnp.where(allowed, scores, jnp.float32(-1e30))
    row_top = jnp.max(masked, axis=-1, keepdims=True)
    weights = jnp.where(allowed, jnp.exp(masked - row_top), jnp.float32(0.0))
    row_total = jnp.sum(weights, axis=-1)
    rounded = weights.astype(jnp.bfloat16)
    mixed_rows = jnp.einsum("kgtn,nkd->tkgd", rounded, block_v, preferred_element_type=jnp.float32)
    mixed_rows = mixed_rows / jnp.transpose(row_total, (2, 0, 1))[..., None]
    return mixed_rows.astype(jnp.bfloat16).reshape(query_count, -1)


def shards(
    span_tokens, q_weight, kv_weight, out_weight, kv_pool, cache_lengths, slot_requests, page_table
):
    groups = lax.axis_size("group")
    seq_count = lax.axis_size("seq")
    tensor_count = lax.axis_size("tensor")
    group_id = lax.axis_index("group")
    seq_id = lax.axis_index("seq")
    tensor_id = lax.axis_index("tensor")
    local_reqs, seg_len, feat_local = span_tokens.shape
    head_cols = q_weight.shape[1]
    kv_cols = kv_weight.shape[1]
    local_heads = head_cols // HD
    group_heads = kv_cols // HD
    kv_local = max(1, KVH // tensor_count)
    per_kv = local_heads // kv_local
    head_first = tensor_id * KVH // tensor_count % group_heads
    holds_keys = tensor_id % 2 == 0
    pool_rows = kv_pool.shape[0]
    capacity = pool_rows // groups
    row_count = local_reqs * seg_len
    my_slots = group_id * local_reqs + jnp.arange(local_reqs, dtype=jnp.int32)
    my_requests = slot_requests[my_slots]
    my_lengths = cache_lengths[my_requests]
    project_piece_rows = lax.all_gather(span_tokens, "tensor", axis=2, tiled=True)
    feat_width = project_piece_rows.shape[2]
    flat_rows = project_piece_rows.reshape(row_count, feat_width)
    query_lin = jnp.dot(flat_rows, q_weight, preferred_element_type=jnp.float32)
    fresh_lin = jnp.dot(flat_rows, kv_weight, preferred_element_type=jnp.float32)
    positions = (
        my_lengths[:, None] + seq_id * seg_len + jnp.arange(seg_len, dtype=jnp.int32)[None, :]
    )
    queries = jax.vmap(rotate)(query_lin.reshape(local_reqs, seg_len, local_heads, HD), positions)
    queries = queries.astype(jnp.bfloat16).reshape(local_reqs, seg_len, kv_local, per_kv, HD)
    fresh_heads = fresh_lin.reshape(local_reqs, seg_len, group_heads, HD)
    rotated = jax.vmap(rotate)(fresh_heads, positions)
    span_kv = (
        jnp.where(holds_keys, rotated, fresh_heads)
        .astype(jnp.bfloat16)
        .reshape(local_reqs, seg_len, kv_cols)
    )
    all_ids = page_table[slot_requests]
    owned_here = all_ids // pool_rows == group_id
    slot_rank = jnp.cumsum(owned_here.astype(jnp.int32), axis=1) - 1
    local_rows = all_ids - group_id * pool_rows
    chosen = owned_here[:, :, None] & (
        slot_rank[:, :, None] == jnp.arange(capacity, dtype=jnp.int32)[None, None, :]
    )
    wanted = jnp.sum(jnp.where(chosen, local_rows[:, :, None], 0), axis=1)
    my_ids = page_table[my_requests].reshape(-1)
    my_owner = my_ids // pool_rows
    onehot = (my_owner[:, None] == jnp.arange(groups, dtype=jnp.int32)[None, :]).astype(jnp.int32)
    arrival = jnp.sum((jnp.cumsum(onehot, axis=0) - 1) * onehot, axis=1)
    arrived_row = my_owner * capacity + arrival
    outgoing = kv_pool[wanted]
    arrived = lax.all_to_all(outgoing, "group", split_axis=0, concat_axis=0, tiled=True)
    cached = arrived.reshape(groups * capacity, PAGE, kv_cols)[arrived_row]
    cached = cached.reshape(local_reqs, WINDOW, kv_cols)
    span_all = jnp.zeros((local_reqs, seg_len * seq_count, kv_cols), jnp.bfloat16)
    for back_step in range(seq_count - 1, -1, -1):
        piece_rows = span_kv if back_step == 0 else shifted(span_kv, "seq", back_step)
        span_all = lax.dynamic_update_slice_in_dim(
            span_all, piece_rows, (seq_id - back_step) * seg_len, 1
        )
    joined = jnp.concatenate([cached, span_all], axis=1)
    visible = lax.dynamic_slice_in_dim(joined, seq_id * seg_len, WINDOW + seg_len, 1)
    partner_rows = swapped(visible, "tensor", 0)
    key_all = jnp.where(holds_keys, visible, partner_rows).reshape(
        local_reqs, WINDOW + seg_len, group_heads, HD
    )
    value_all = jnp.where(holds_keys, partner_rows, visible).reshape(
        local_reqs, WINDOW + seg_len, group_heads, HD
    )
    key_rows = lax.dynamic_slice_in_dim(key_all, head_first, kv_local, 2)
    value_rows = lax.dynamic_slice_in_dim(value_all, head_first, kv_local, 2)
    block_len = min(128, seg_len)
    block_count = seg_len // block_len

    def per_request(request_items):
        request_q, request_k, request_v, length = request_items

        def per_block(block_index):
            first_row = block_index * block_len
            block_q = lax.dynamic_slice_in_dim(request_q, first_row, block_len, 0)
            block_k = lax.dynamic_slice_in_dim(request_k, first_row, WINDOW + block_len, 0)
            block_v = lax.dynamic_slice_in_dim(request_v, first_row, WINDOW + block_len, 0)
            return attend(block_q, block_k, block_v, length - WINDOW + seq_id * seg_len + first_row)

        return lax.map(per_block, jnp.arange(block_count, dtype=jnp.int32)).reshape(
            seg_len, head_cols
        )

    attended_heads = lax.map(per_request, (queries, key_rows, value_rows, my_lengths))
    flat_heads = attended_heads.reshape(row_count, head_cols)
    out_cols = out_weight.shape[1] // tensor_count
    summed = lax.psum_scatter(
        lax.dot_general(
            out_weight, flat_heads, (((0,), (1,)), ((), ())), preferred_element_type=jnp.float32
        ).astype(jnp.bfloat16),
        "tensor",
        scatter_dimension=0,
        tiled=True,
    ).astype(jnp.float32)
    result = summed.T
    return result.astype(jnp.bfloat16).reshape(local_reqs, seg_len, out_cols)


LOG2E = 1.4426950408889634
MASKED = -1e30
F32 = jnp.float32
BF16 = jnp.bfloat16
HBM = pl.BlockSpec(memory_space=pl.ANY)
VMEM = pl.BlockSpec(memory_space=pltpu.VMEM)
SMEM = pl.BlockSpec(memory_space=pltpu.SMEM)
STAYS = pl.BlockSpec(memory_space=pltpu.HBM)
GROUPS, SEQS, TENSORS = 4, 4, 2


def params(mebibytes):
    return pltpu.CompilerParams(vmem_limit_bytes=mebibytes * 2**20)


def cost(flops, moved):
    return pl.CostEstimate(flops=flops, bytes_accessed=moved, transcendentals=0)


class Info:
    def __init__(self, ref):
        self.ref = ref
        self.group, self.seq, self.tensor = ref[0, 0], ref[0, 1], ref[0, 2]
        self.window_pages = ref.shape[1]

    def request(self, slot):
        return self.ref[0, 3 + slot]

    def length(self, request):
        return self.ref[0, 3 + GROUPS + request]

    def page(self, request, w):
        return self.ref[1 + request, w]


def turned(x, cosine, sine):
    lane = lax.broadcasted_iota(jnp.int32, x.shape, 1)
    other = jnp.where(lane % HD < HD // 2, pltpu.roll(x, 128 - HD // 2, 1), pltpu.roll(x, HD // 2, 1))
    return x * cosine + other * sine


def open_kernel(
    info_ref, frequency, pool, x_hbm, wq_hbm, wkv_hbm,
    home, same, beyond, beside, across, diagonal, acc_q, acc_kv, cosine, sine,
    x, wq, wkv, sems, page_sems,
):
    info = Info(info_ref)
    rows, feats = x.shape
    here = pl.ds(pl.multiple_of(info.tensor * feats, feats), feats)
    copies = [
        pltpu.make_async_copy(x_hbm, x, sems.at[0]),
        pltpu.make_async_copy(wkv_hbm.at[here], wkv, sems.at[1]),
        pltpu.make_async_copy(wq_hbm.at[here], wq, sems.at[2]),
    ]
    for copy in copies:
        copy.start()
    pages = pool.shape[0]
    capacity = pages // GROUPS
    half = pool.shape[2] // 2
    mine = pl.ds(pl.multiple_of(info.tensor * half, half), half)
    theirs = pl.ds(pl.multiple_of((1 - info.tensor) * half, half), half)
    outs = (home, same, beyond, beside, across, diagonal)
    spots = (
        ((0, 0), (1, 0)),
        ((3, 0), (1, capacity)),
        ((2, 0), (4, 0)),
        ((2, capacity), (5, 0)),
    )
    for flip, targets in enumerate(spots):
        request = info.request(info.group ^ flip)

        def take(w, rank):
            page = info.page(request, w)
            near = page // pages == info.group

            @pl.when(near)
            def _():
                row = page % pages
                for (out, base), cols in zip(targets, (mine, theirs)):
                    pltpu.make_async_copy(
                        pool.at[row, :, cols], outs[out].at[base + rank], page_sems.at[out]
                    ).start()

            return rank + near.astype(jnp.int32)

        lax.fori_loop(0, info.window_pages, take, jnp.int32(0))
    start = info.length(info.request(info.group)) + info.seq * rows
    position = (start + lax.broadcasted_iota(jnp.int32, (rows, 128), 0)).astype(F32)
    angles = position * frequency[0:1, :]
    lane = lax.broadcasted_iota(jnp.int32, (rows, 128), 1)
    cosine[...] = jnp.cos(angles)
    sine[...] = jnp.where(lane % HD < HD // 2, -1.0, 1.0) * jnp.sin(angles)
    copies[0].wait()
    copies[1].wait()
    acc_kv[...] = jnp.dot(x[...], wkv[...], preferred_element_type=F32)
    copies[2].wait()
    acc_q[...] = jnp.dot(x[...], wq[...], preferred_element_type=F32)
    for i, out in enumerate(outs):
        pltpu.make_async_copy(out, out, page_sems.at[i]).wait()


def open_rows(info, frequency, pool, x, wq, wkv):
    rows, feats = x.shape
    pages, page, cols = pool.shape
    single = jax.ShapeDtypeStruct((pages // GROUPS, page, cols // 2), BF16)
    double = jax.ShapeDtypeStruct((2 * pages // GROUPS, page, cols // 2), BF16)
    table = jax.ShapeDtypeStruct((rows, 128), F32)
    return pl.pallas_call(
        open_kernel,
        out_shape=[
            single,
            double,
            double,
            single,
            single,
            single,
            jax.ShapeDtypeStruct((rows, wq.shape[1]), F32),
            jax.ShapeDtypeStruct((rows, wkv.shape[1]), F32),
            table,
            table,
        ],
        in_specs=[SMEM, VMEM] + [STAYS] * 4,
        out_specs=[VMEM] * 10,
        scratch_shapes=[
            pltpu.VMEM((rows, feats), BF16),
            pltpu.VMEM((feats, wq.shape[1]), BF16),
            pltpu.VMEM((feats, wkv.shape[1]), BF16),
            pltpu.SemaphoreType.DMA((3,)),
            pltpu.SemaphoreType.DMA((6,)),
        ],
        compiler_params=params(50),
        cost_estimate=cost(rows * feats, rows * feats),
    )(info, frequency, pool, x, wq, wkv)


def fresh_kernel(info_ref, x, wkv, acc_kv, cosine, sine, kept, sent):
    info = Info(info_ref)
    feats = x.shape[1]
    here = pl.ds(pl.multiple_of((1 - info.tensor) * feats, feats), feats)
    keys = info.tensor == 0
    fresh = acc_kv[...] + jnp.dot(x[...], wkv[here], preferred_element_type=F32)
    cos_kv = jnp.where(keys, cosine[...], 1.0)
    sin_kv = jnp.where(keys, sine[...], 0.0)
    low = turned(fresh[:, :128], cos_kv, sin_kv).astype(BF16)
    high = turned(fresh[:, 128:], cos_kv, sin_kv).astype(BF16)
    kept[...] = jnp.where(keys, low, high)
    sent[...] = jnp.where(keys, high, low)


def fresh_rows(info, x, wkv, acc_kv, cosine, sine):
    rows, feats = x.shape
    piece = jax.ShapeDtypeStruct((rows, wkv.shape[1] // 2), BF16)
    return pl.pallas_call(
        fresh_kernel,
        out_shape=[piece, piece],
        in_specs=[SMEM] + [VMEM] * 5,
        out_specs=[VMEM] * 2,
        compiler_params=params(12),
        cost_estimate=cost(2 * rows * feats * 2560, rows * feats),
    )(info, x, wkv, acc_kv, cosine, sine)


def query_kernel(info_ref, x, wq, acc_q, cosine, sine, q):
    feats = x.shape[1]
    here = pl.ds(pl.multiple_of((1 - Info(info_ref).tensor) * feats, feats), feats)
    scale = HD**-0.5 * LOG2E
    cos_all, sin_all = cosine[...] * scale, sine[...] * scale
    tile = 256
    for c in range(0, q.shape[1], tile):
        lin = acc_q[:, c : c + tile] + jnp.dot(
            x[...], wq[here, c : c + tile], preferred_element_type=F32
        )
        for e in range(0, tile, 128):
            q[:, c + e : c + e + 128] = turned(lin[:, e : e + 128], cos_all, sin_all).astype(BF16)


def query_rows(info, x, wq, acc_q, cosine, sine):
    rows, feats = x.shape
    return pl.pallas_call(
        query_kernel,
        out_shape=jax.ShapeDtypeStruct((rows, wq.shape[1]), BF16),
        in_specs=[SMEM] + [VMEM] * 5,
        out_specs=VMEM,
        compiler_params=params(16),
        cost_estimate=cost(rows * feats, rows * feats),
    )(info, x, wq, acc_q, cosine, sine)


def soft_heads(q, tokens, segments, emit):
    rows = tokens.stop - tokens.start
    stack = 4
    low = lax.broadcasted_iota(jnp.int32, (rows, 2 * HD), 1) < HD

    def swap(x):
        return pltpu.roll(x, HD, 1)

    def queries(kv_head, odd):
        tiles = [q[tokens, spot] for spot in spots(kv_head)]
        if odd != kv_head:
            tiles = [swap(x.astype(F32)).astype(BF16) for x in tiles]
        zero = jnp.zeros_like(tiles[0])
        return jnp.concatenate([jnp.where(low != (kv_head == 1), x, zero) for x in tiles], axis=0)

    def spots(kv_head):
        return [slice(128 * h, 128 * (h + 1)) for h in range(kv_head * stack, (kv_head + 1) * stack)]

    def scores(unit):
        qs = queries(*unit)
        return [
            mask(
                lax.dot_general(
                    qs, keys[span], (((1,), (1,)), ((), ())), preferred_element_type=F32
                )
            )
            for keys, _, span, mask in segments
        ]

    def weigh(parts):
        top = functools.reduce(jnp.maximum, [jnp.max(s, axis=1, keepdims=True) for s in parts])
        return [jnp.exp2(s - top).astype(BF16) for s in parts], top

    def mixed(unit, weights):
        return sum(
            jnp.dot(p, values[unit[0], span], preferred_element_type=F32)
            for p, (_, values, span, _) in zip(weights, segments)
        )

    units = [(kv_head, odd) for kv_head in range(2) for odd in range(2)]
    ahead = scores(units[0])
    behind = None
    sums, tops = {}, {}
    for n in range(len(units) + 1):
        now, ahead = ahead, scores(units[n + 1]) if n + 1 < len(units) else None
        if behind is not None:
            sums[units[n - 1]] = mixed(units[n - 1], behind)
        if n < len(units):
            behind, tops[units[n]] = weigh(now)
    for kv_head in range(2):
        for j, spot in enumerate(spots(kv_head)):
            part = slice(j * rows, (j + 1) * rows)
            a, b = sums[kv_head, 0][part], sums[kv_head, 1][part]
            total = jnp.where(low, a, swap(b))
            weight = jnp.where(low, swap(a), b)
            top = jnp.where(low, tops[kv_head, 0][part], tops[kv_head, 1][part])
            emit(spot, total, weight, top)


def widen(v, ones, values, here):
    low = lax.broadcasted_iota(jnp.int32, v.shape, 1) < HD
    values[0, here] = jnp.where(low, v, ones).astype(BF16)
    values[1, here] = jnp.where(low, pltpu.roll(v, HD, 1), ones).astype(BF16)


def gather_kernel(info_ref, own, other, fresh, keys, values, source):
    info = Info(info_ref)
    group, seq = info.group, info.seq
    request = info.request(group)
    rows = fresh.shape[1]
    per = rows // PAGE
    count = own.shape[0]
    capacity = count // GROUPS
    seen = keys.shape[0] // PAGE - seq * per
    is_key = info.tensor == 0

    def note(w, counts):
        came = info.page(request, w) // count ^ group
        place = came * capacity
        for d in range(GROUPS):
            place = place + jnp.where(came == d, counts[d], 0)
        source[w] = place
        return tuple(counts[d] + (came == d).astype(jnp.int32) for d in range(GROUPS))

    lax.fori_loop(0, info.window_pages, note, (jnp.int32(0),) * GROUPS, unroll=True)

    def place(block, a, b):
        here = pl.ds(pl.multiple_of(block * PAGE, PAGE), PAGE)
        keys[here] = jnp.where(is_key, a, b)
        widen(jnp.where(is_key, b, a).astype(F32), 1.0, values, here)

    for block, part in ((1, slice(0, PAGE)), (seen - 1, slice(PAGE, 2 * PAGE))):
        place(block, fresh[0, part], fresh[1, part])
    first = info.length(request) - WINDOW + seq * rows
    stand_in = jnp.where(is_key, fresh[0, :16], fresh[1, :16]).astype(F32)[0:1]
    stand_in = jnp.broadcast_to(stand_in, (PAGE, 2 * HD)).astype(BF16)

    def bring(i, _):
        for n in (2 * i, 2 * i + 1):
            block = jnp.where(n == 0, 0, n + 1)
            here = pl.ds(pl.multiple_of(block * PAGE, PAGE), PAGE)
            at = source[seq * per + n]
            hidden = first + n * PAGE < 0
            a, b = own[at], other[at]
            keys[here] = jnp.where(hidden, stand_in, jnp.where(is_key, a, b))
            v = jnp.where(is_key, b, a).astype(F32)
            widen(jnp.where(hidden, 0.0, v), jnp.where(hidden, 0.0, 1.0), values, here)
        return 0

    lax.fori_loop(0, (seen - per) // 2, bring, 0)


def gather_rows(info, own, other, fresh):
    span = WINDOW + fresh.shape[1]
    return pl.pallas_call(
        gather_kernel,
        out_shape=[
            jax.ShapeDtypeStruct((span, 2 * HD), BF16),
            jax.ShapeDtypeStruct((2, span, 2 * HD), BF16),
        ],
        in_specs=[SMEM] + [VMEM] * 3,
        out_specs=[VMEM] * 2,
        scratch_shapes=[pltpu.SMEM((own.shape[0],), jnp.int32)],
        compiler_params=params(12),
        cost_estimate=cost(20 * 10**9, 4 * span),
    )(info, own, other, fresh)


def bundle_kernel(a, b, out):
    out[: a.shape[0]] = a[...]
    out[a.shape[0] :] = b[...]


def bundled(a, b):
    return pl.pallas_call(
        bundle_kernel,
        out_shape=jax.ShapeDtypeStruct((a.shape[0] + b.shape[0], *a.shape[1:]), BF16),
        in_specs=[VMEM] * 2,
        out_specs=VMEM,
        compiler_params=params(8),
        cost_estimate=cost(6 * 10**9, 4),
    )(a, b)


def near_segment(keys, values, seq, half):
    blocks = keys.shape[0] // PAGE
    per = 2
    span = slice(half * PAGE, (blocks - seq * per - 1 + half) * PAGE)

    def mask(s):
        newer = lax.broadcasted_iota(jnp.int32, (s.shape[0], PAGE), 1) > (
            lax.broadcasted_iota(jnp.int32, (s.shape[0], PAGE), 0) % PAGE
        )
        if half == 0:
            parts = [
                jnp.where(newer, s[:, :PAGE], MASKED),
                jnp.where(newer, MASKED, s[:, PAGE : 2 * PAGE]),
                s[:, 2 * PAGE :],
            ]
        else:
            parts = [
                s[:, :PAGE],
                jnp.where(newer, s[:, PAGE : 2 * PAGE], MASKED),
                s[:, 2 * PAGE : -PAGE],
                jnp.where(newer, MASKED, s[:, -PAGE:]),
            ]
        return jnp.concatenate(parts, axis=1)

    return keys, values, span, mask


def far_segment(keys, values, seq):
    return keys, values, slice(0, seq * 2 * PAGE), lambda s: s


def near_kernel(info_ref, q, keys, values, total, weight, top):
    seq = Info(info_ref).seq

    def emit(spot, o, l, m):
        total[:, spot] = o
        weight[:, spot] = l
        top[:, spot] = m

    for k in range(SEQS):

        @pl.when(seq == k)
        def _(k=k):
            soft_heads(q, slice(0, PAGE), [near_segment(keys, values, k, 0)], emit)


def attend_near(info, q, keys, values):
    state = jax.ShapeDtypeStruct((PAGE, q.shape[1]), F32)
    return pl.pallas_call(
        near_kernel,
        out_shape=[state] * 3,
        in_specs=[SMEM] + [VMEM] * 3,
        out_specs=[VMEM] * 3,
        compiler_params=params(32),
        cost_estimate=cost(PAGE * WINDOW, 4 * WINDOW),
    )(info, q, keys, values)


def partner_product(info, heads_out, w, partial):
    cols = partial.shape[1]
    here = pl.ds(pl.multiple_of((1 - info.tensor) * cols, cols), cols)
    partial[...] = jnp.dot(heads_out[...], w[:, here], preferred_element_type=F32).astype(BF16)


def far_kernel(
    info_ref, q, total, weight, top, z1, z2, z3, w, heads_out, partial, keys, values
):
    info = Info(info_ref)
    rows = q.shape[0]
    seq = info.seq
    zs = (None, z1, z2, z3)
    is_key = info.tensor == 0

    for k in range(SEQS):

        @pl.when(seq == k)
        def _(k=k):
            if k == 0:
                heads_out[...] = (total[...] / weight[...]).astype(BF16)
                return
            for n in range(k):
                z = zs[n ^ k]
                here = slice(n * rows, (n + 1) * rows)
                a, b = z[0], z[1]
                keys[here] = jnp.where(is_key, a, b)
                widen(jnp.where(is_key, b, a).astype(F32), 1.0, values, here)

            def emit(spot, o, l, m):
                before = top[:, spot]
                peak = jnp.maximum(before, m)
                a = jnp.exp2(before - peak)
                b = jnp.exp2(m - peak)
                done = (total[:, spot] * a + o * b) / (weight[:, spot] * a + l * b)
                heads_out[:, spot] = done.astype(BF16)

            soft_heads(q, slice(0, PAGE), [far_segment(keys, values, k)], emit)

    partner_product(info, heads_out, w, partial)


def attend_far(info, q, state, zs, w):
    rows = q.shape[0]
    span = (SEQS - 1) * rows
    return pl.pallas_call(
        far_kernel,
        out_shape=[
            jax.ShapeDtypeStruct((PAGE, q.shape[1]), BF16),
            jax.ShapeDtypeStruct((PAGE, w.shape[1] // TENSORS), BF16),
            jax.ShapeDtypeStruct((span, 2 * HD), BF16),
            jax.ShapeDtypeStruct((2, span, 2 * HD), BF16),
        ],
        in_specs=[SMEM] + [VMEM] * 8,
        out_specs=[VMEM] * 4,
        compiler_params=params(24),
        cost_estimate=cost(rows * span, 4 * span),
    )(info, q, *state, *zs, w)


def last_kernel(info_ref, q, keys, values, far_keys, far_values, w, heads_out, partial):
    info = Info(info_ref)

    def emit(spot, o, l, m):
        heads_out[:, spot] = (o / l).astype(BF16)

    for k in range(SEQS):

        @pl.when(info.seq == k)
        def _(k=k):
            segments = [near_segment(keys, values, k, 1)]
            if k:
                segments.append(far_segment(far_keys, far_values, k))
            soft_heads(q, slice(PAGE, 2 * PAGE), segments, emit)

    partner_product(info, heads_out, w, partial)


def attend_last(info, q, keys, values, far_keys, far_values, w):
    return pl.pallas_call(
        last_kernel,
        out_shape=[
            jax.ShapeDtypeStruct((PAGE, q.shape[1]), BF16),
            jax.ShapeDtypeStruct((PAGE, w.shape[1] // TENSORS), BF16),
        ],
        in_specs=[SMEM] + [VMEM] * 6,
        out_specs=[VMEM] * 2,
        compiler_params=params(36),
        cost_estimate=cost(PAGE * WINDOW, 4 * WINDOW),
    )(info, q, keys, values, far_keys, far_values, w)


def home_kernel(info_ref, x1, x2, away, w, out, home, first, sem):
    rows, cols = home.shape
    here = pl.ds(pl.multiple_of(Info(info_ref).tensor * cols, cols), cols)
    x = jnp.concatenate([x1[...], x2[...]], axis=0)
    o = jnp.dot(x, w[:, here], preferred_element_type=F32).astype(BF16)
    home[...] = o[rows:]
    first[...] = (o[:rows].astype(F32) + away[...].astype(F32)).astype(BF16)
    copy = pltpu.make_async_copy(first, out.at[pl.ds(0, rows)], sem)
    copy.start()
    copy.wait()


def home_project(info, x1, x2, away, w):
    rows, depth = x1.shape
    cols = w.shape[1] // TENSORS
    return pl.pallas_call(
        home_kernel,
        out_shape=[
            jax.ShapeDtypeStruct((2 * rows, cols), BF16),
            jax.ShapeDtypeStruct((rows, cols), BF16),
        ],
        in_specs=[SMEM] + [VMEM] * 4,
        out_specs=[STAYS, VMEM],
        scratch_shapes=[pltpu.VMEM((rows, cols), BF16), pltpu.SemaphoreType.DMA],
        compiler_params=params(16),
        cost_estimate=cost(20 * 10**9, 2 * depth * cols),
    )(info, x1, x2, away, w)


def add_kernel(before, a, b, out, last, sem):
    rows = a.shape[0]
    last[...] = (a[...].astype(F32) + b[...].astype(F32)).astype(BF16)
    copy = pltpu.make_async_copy(last, out.at[pl.ds(rows, rows)], sem)
    copy.start()
    copy.wait()


def added(before, a, b):
    return pl.pallas_call(
        add_kernel,
        out_shape=jax.ShapeDtypeStruct(before.shape, BF16),
        in_specs=[STAYS, VMEM, VMEM],
        out_specs=STAYS,
        scratch_shapes=[pltpu.VMEM(a.shape, BF16), pltpu.SemaphoreType.DMA],
        input_output_aliases={0: 0},
        compiler_params=params(8),
    )(before, a, b)


def flipped(value, axes, count, bits):
    return lax.ppermute(value, axes, [(i, i ^ bits) for i in range(count)])


def after(value, *others):
    return lax.optimization_barrier((value, *others))[0]


def shards_fast(
    span_tokens, q_weight, kv_weight, out_weight, kv_pool, cache_lengths, slot_requests, page_table
):
    group_id = lax.axis_index("group")
    seq_id = lax.axis_index("seq")
    tensor_id = lax.axis_index("tensor")
    place = jnp.stack([group_id, seq_id, tensor_id]).astype(jnp.int32)
    row = jnp.concatenate([place, slot_requests, cache_lengths])
    row = jnp.pad(row, (0, page_table.shape[1] - row.shape[0]))
    info = jnp.concatenate([row[None], page_table])
    mine = span_tokens[0]
    theirs = flipped(mine, "tensor", 2, 1)
    half_dim = HD // 2
    lane = jnp.arange(128, dtype=jnp.int32) % half_dim
    frequency = jnp.power(jnp.float32(10000.0), -lane.astype(F32) / half_dim)
    frequency = jnp.broadcast_to(frequency[None, :], (8, 128))
    pages = open_rows(info, frequency, kv_pool, mine, q_weight, kv_weight)
    home, same, beyond, beside, across, diagonal = pages[:6]
    acc_q, acc_kv, cosine, sine = pages[6:]
    capacity = home.shape[0]
    same = flipped(same, "tensor", 2, 1)
    beyond = flipped(beyond, "group", 4, 2)
    kept, sent = fresh_rows(info, theirs, kv_weight, acc_kv, cosine, sine)
    got = flipped(sent, "tensor", 2, 1)
    across, diagonal, _ = lax.optimization_barrier((across, diagonal, sent))
    across = flipped(across, ("group", "tensor"), 8, 5)
    diagonal = flipped(diagonal, ("group", "tensor"), 8, 7)
    q = query_rows(info, theirs, q_weight, acc_q, cosine, sine)
    same, beyond, _ = lax.optimization_barrier((same, beyond, q))
    mate = jnp.concatenate([beside, beyond[capacity:], same[capacity:]])
    mate = flipped(mate, "group", 4, 1)
    fresh = bundled(kept[None], got[None])
    zs = [flipped(fresh, "seq", 4, d) for d in range(1, 4)]
    other_chip = bundled(across, diagonal)
    own = jnp.concatenate(
        [home, mate[:capacity], beyond[:capacity], mate[capacity : 2 * capacity]]
    )
    other = jnp.concatenate([same[:capacity], mate[2 * capacity :], other_chip])
    keys, values = gather_rows(info, own, other, fresh)
    state = attend_near(info, q, keys, values)
    heads_0, partial_0, far_keys, far_values = attend_far(info, q, state, zs, out_weight)
    away_0 = flipped(partial_0, "tensor", 2, 1)
    heads_1, partial_1 = attend_last(info, q, keys, values, far_keys, far_values, out_weight)
    away_1 = flipped(partial_1, "tensor", 2, 1)
    out, home_1 = home_project(info, heads_0, heads_1, away_0, out_weight)
    return added(out, home_1, away_1)[None]


def solution(mesh):
    sizes = tuple(mesh.shape[a] for a in ("group", "seq", "tensor"))
    body = shards_fast if sizes == (GROUPS, SEQS, TENSORS) else shards
    placed = (
        P("group", "seq", "tensor"),
        P(None, "tensor"),
        P(None, "tensor"),
        P("tensor", None),
        P("group", None, "tensor"),
        P(),
        P(),
        P(),
    )
    return jax.shard_map(
        body, mesh=mesh, in_specs=placed, out_specs=P("group", "seq", "tensor"), check_vma=False
    )
```

```python
import functools

import jax
import jax.numpy as jnp
from jax import lax
from jax.experimental import pallas as pl
from jax.experimental.pallas import tpu as pltpu
from jax.sharding import PartitionSpec as P

HD = 64
KVH = 4
WINDOW = 2048
PAGE = 128


def shifted(block, axis, distance):
    devices = range(lax.axis_size(axis))
    route = [(i - distance, i) for i in devices if i - distance in devices]
    return lax.ppermute(block, axis, route)


def swapped(value, axis, stride):
    return lax.ppermute(value, axis, [(i, i ^ 1 << stride) for i in range(lax.axis_size(axis))])


def rotate(values, positions):
    half_dim = HD // 2
    frequency = jnp.power(jnp.float32(10000.0), -jnp.arange(half_dim, dtype=jnp.float32) / half_dim)
    angles = positions.astype(jnp.float32)[:, None] * frequency[None, :]
    cosine = jnp.cos(angles)[:, None, :]
    sine_part = jnp.sin(angles)[:, None, :]
    front_half = values[..., :half_dim]
    back_half = values[..., half_dim:]
    return jnp.concatenate(
        [front_half * cosine - back_half * sine_part, back_half * cosine + front_half * sine_part],
        axis=-1,
    )


def attend(block_q, block_k, block_v, base_pos):
    query_count = block_q.shape[0]
    key_count = block_k.shape[0]
    scores = jnp.einsum(
        "tkgd,nkd->kgtn", block_q, block_k, preferred_element_type=jnp.float32
    ) * HD ** (-0.5)
    query_at = jnp.arange(query_count, dtype=jnp.int32)[:, None]
    key_at = jnp.arange(key_count, dtype=jnp.int32)[None, :]
    allowed = (key_at > query_at) & (key_at <= query_at + WINDOW) & (base_pos + key_at >= 0)
    masked = jnp.where(allowed, scores, jnp.float32(-1e30))
    row_top = jnp.max(masked, axis=-1, keepdims=True)
    weights = jnp.where(allowed, jnp.exp(masked - row_top), jnp.float32(0.0))
    row_total = jnp.sum(weights, axis=-1)
    rounded = weights.astype(jnp.bfloat16)
    mixed_rows = jnp.einsum("kgtn,nkd->tkgd", rounded, block_v, preferred_element_type=jnp.float32)
    mixed_rows = mixed_rows / jnp.transpose(row_total, (2, 0, 1))[..., None]
    return mixed_rows.astype(jnp.bfloat16).reshape(query_count, -1)


def shards(
    span_tokens, q_weight, kv_weight, out_weight, kv_pool, cache_lengths, slot_requests, page_table
):
    groups = lax.axis_size("group")
    seq_count = lax.axis_size("seq")
    tensor_count = lax.axis_size("tensor")
    group_id = lax.axis_index("group")
    seq_id = lax.axis_index("seq")
    tensor_id = lax.axis_index("tensor")
    local_reqs, seg_len, feat_local = span_tokens.shape
    head_cols = q_weight.shape[1]
    kv_cols = kv_weight.shape[1]
    local_heads = head_cols // HD
    group_heads = kv_cols // HD
    kv_local = max(1, KVH // tensor_count)
    per_kv = local_heads // kv_local
    head_first = tensor_id * KVH // tensor_count % group_heads
    holds_keys = tensor_id % 2 == 0
    pool_rows = kv_pool.shape[0]
    capacity = pool_rows // groups
    row_count = local_reqs * seg_len
    my_slots = group_id * local_reqs + jnp.arange(local_reqs, dtype=jnp.int32)
    my_requests = slot_requests[my_slots]
    my_lengths = cache_lengths[my_requests]
    project_piece_rows = lax.all_gather(span_tokens, "tensor", axis=2, tiled=True)
    feat_width = project_piece_rows.shape[2]
    flat_rows = project_piece_rows.reshape(row_count, feat_width)
    query_lin = jnp.dot(flat_rows, q_weight, preferred_element_type=jnp.float32)
    fresh_lin = jnp.dot(flat_rows, kv_weight, preferred_element_type=jnp.float32)
    positions = (
        my_lengths[:, None] + seq_id * seg_len + jnp.arange(seg_len, dtype=jnp.int32)[None, :]
    )
    queries = jax.vmap(rotate)(query_lin.reshape(local_reqs, seg_len, local_heads, HD), positions)
    queries = queries.astype(jnp.bfloat16).reshape(local_reqs, seg_len, kv_local, per_kv, HD)
    fresh_heads = fresh_lin.reshape(local_reqs, seg_len, group_heads, HD)
    rotated = jax.vmap(rotate)(fresh_heads, positions)
    span_kv = (
        jnp.where(holds_keys, rotated, fresh_heads)
        .astype(jnp.bfloat16)
        .reshape(local_reqs, seg_len, kv_cols)
    )
    all_ids = page_table[slot_requests]
    owned_here = all_ids // pool_rows == group_id
    slot_rank = jnp.cumsum(owned_here.astype(jnp.int32), axis=1) - 1
    local_rows = all_ids - group_id * pool_rows
    chosen = owned_here[:, :, None] & (
        slot_rank[:, :, None] == jnp.arange(capacity, dtype=jnp.int32)[None, None, :]
    )
    wanted = jnp.sum(jnp.where(chosen, local_rows[:, :, None], 0), axis=1)
    my_ids = page_table[my_requests].reshape(-1)
    my_owner = my_ids // pool_rows
    onehot = (my_owner[:, None] == jnp.arange(groups, dtype=jnp.int32)[None, :]).astype(jnp.int32)
    arrival = jnp.sum((jnp.cumsum(onehot, axis=0) - 1) * onehot, axis=1)
    arrived_row = my_owner * capacity + arrival
    outgoing = kv_pool[wanted]
    arrived = lax.all_to_all(outgoing, "group", split_axis=0, concat_axis=0, tiled=True)
    cached = arrived.reshape(groups * capacity, PAGE, kv_cols)[arrived_row]
    cached = cached.reshape(local_reqs, WINDOW, kv_cols)
    span_all = jnp.zeros((local_reqs, seg_len * seq_count, kv_cols), jnp.bfloat16)
    for back_step in range(seq_count - 1, -1, -1):
        piece_rows = span_kv if back_step == 0 else shifted(span_kv, "seq", back_step)
        span_all = lax.dynamic_update_slice_in_dim(
            span_all, piece_rows, (seq_id - back_step) * seg_len, 1
        )
    joined = jnp.concatenate([cached, span_all], axis=1)
    visible = lax.dynamic_slice_in_dim(joined, seq_id * seg_len, WINDOW + seg_len, 1)
    partner_rows = swapped(visible, "tensor", 0)
    key_all = jnp.where(holds_keys, visible, partner_rows).reshape(
        local_reqs, WINDOW + seg_len, group_heads, HD
    )
    value_all = jnp.where(holds_keys, partner_rows, visible).reshape(
        local_reqs, WINDOW + seg_len, group_heads, HD
    )
    key_rows = lax.dynamic_slice_in_dim(key_all, head_first, kv_local, 2)
    value_rows = lax.dynamic_slice_in_dim(value_all, head_first, kv_local, 2)
    block_len = min(128, seg_len)
    block_count = seg_len // block_len

    def per_request(request_items):
        request_q, request_k, request_v, length = request_items

        def per_block(block_index):
            first_row = block_index * block_len
            block_q = lax.dynamic_slice_in_dim(request_q, first_row, block_len, 0)
            block_k = lax.dynamic_slice_in_dim(request_k, first_row, WINDOW + block_len, 0)
            block_v = lax.dynamic_slice_in_dim(request_v, first_row, WINDOW + block_len, 0)
            return attend(block_q, block_k, block_v, length - WINDOW + seq_id * seg_len + first_row)

        return lax.map(per_block, jnp.arange(block_count, dtype=jnp.int32)).reshape(
            seg_len, head_cols
        )

    attended_heads = lax.map(per_request, (queries, key_rows, value_rows, my_lengths))
    flat_heads = attended_heads.reshape(row_count, head_cols)
    out_cols = out_weight.shape[1] // tensor_count
    summed = lax.psum_scatter(
        lax.dot_general(
            out_weight, flat_heads, (((0,), (1,)), ((), ())), preferred_element_type=jnp.float32
        ).astype(jnp.bfloat16),
        "tensor",
        scatter_dimension=0,
        tiled=True,
    ).astype(jnp.float32)
    result = summed.T
    return result.astype(jnp.bfloat16).reshape(local_reqs, seg_len, out_cols)


LOG2E = 1.4426950408889634
MASKED = -1e30
F32 = jnp.float32
BF16 = jnp.bfloat16
HBM = pl.BlockSpec(memory_space=pl.ANY)
VMEM = pl.BlockSpec(memory_space=pltpu.VMEM)
SMEM = pl.BlockSpec(memory_space=pltpu.SMEM)
STAYS = pl.BlockSpec(memory_space=pltpu.HBM)
GROUPS, SEQS, TENSORS = 4, 4, 2


def params(mebibytes):
    return pltpu.CompilerParams(vmem_limit_bytes=mebibytes * 2**20)


def cost(flops, moved):
    return pl.CostEstimate(flops=flops, bytes_accessed=moved, transcendentals=0)


class Info:
    def __init__(self, ref):
        self.ref = ref
        self.group, self.seq, self.tensor = ref[0, 0], ref[0, 1], ref[0, 2]
        self.window_pages = ref.shape[1]

    def request(self, slot):
        return self.ref[0, 3 + slot]

    def length(self, request):
        return self.ref[0, 3 + GROUPS + request]

    def page(self, request, w):
        return self.ref[1 + request, w]


def turned(x, cosine, sine):
    lane = lax.broadcasted_iota(jnp.int32, x.shape, 1)
    other = jnp.where(lane % HD < HD // 2, pltpu.roll(x, 128 - HD // 2, 1), pltpu.roll(x, HD // 2, 1))
    return x * cosine + other * sine


def open_kernel(
    info_ref, frequency, pool, x_hbm, wq_hbm, wkv_hbm,
    home, same, beyond, beside, across, diagonal, acc_q, acc_kv, cosine, sine,
    x, wq, wkv, sems, page_sems,
):
    info = Info(info_ref)
    rows, feats = x.shape
    here = pl.ds(pl.multiple_of(info.tensor * feats, feats), feats)
    copies = [
        pltpu.make_async_copy(x_hbm, x, sems.at[0]),
        pltpu.make_async_copy(wkv_hbm.at[here], wkv, sems.at[1]),
        pltpu.make_async_copy(wq_hbm.at[here], wq, sems.at[2]),
    ]
    for copy in copies:
        copy.start()
    pages = pool.shape[0]
    capacity = pages // GROUPS
    half = pool.shape[2] // 2
    mine = pl.ds(pl.multiple_of(info.tensor * half, half), half)
    theirs = pl.ds(pl.multiple_of((1 - info.tensor) * half, half), half)
    outs = (home, same, beyond, beside, across, diagonal)
    spots = (
        ((0, 0), (1, 0)),
        ((3, 0), (1, capacity)),
        ((2, 0), (4, 0)),
        ((2, capacity), (5, 0)),
    )
    for flip, targets in enumerate(spots):
        request = info.request(info.group ^ flip)

        def take(w, rank):
            page = info.page(request, w)
            near = page // pages == info.group

            @pl.when(near)
            def _():
                row = page % pages
                for (out, base), cols in zip(targets, (mine, theirs)):
                    pltpu.make_async_copy(
                        pool.at[row, :, cols], outs[out].at[base + rank], page_sems.at[out]
                    ).start()

            return rank + near.astype(jnp.int32)

        lax.fori_loop(0, info.window_pages, take, jnp.int32(0))
    start = info.length(info.request(info.group)) + info.seq * rows
    position = (start + lax.broadcasted_iota(jnp.int32, (rows, 128), 0)).astype(F32)
    angles = position * frequency[0:1, :]
    lane = lax.broadcasted_iota(jnp.int32, (rows, 128), 1)
    cosine[...] = jnp.cos(angles)
    sine[...] = jnp.where(lane % HD < HD // 2, -1.0, 1.0) * jnp.sin(angles)
    copies[0].wait()
    copies[1].wait()
    acc_kv[...] = jnp.dot(x[...], wkv[...], preferred_element_type=F32)
    copies[2].wait()
    acc_q[...] = jnp.dot(x[...], wq[...], preferred_element_type=F32)
    for i, out in enumerate(outs):
        pltpu.make_async_copy(out, out, page_sems.at[i]).wait()


def open_rows(info, frequency, pool, x, wq, wkv):
    rows, feats = x.shape
    pages, page, cols = pool.shape
    single = jax.ShapeDtypeStruct((pages // GROUPS, page, cols // 2), BF16)
    double = jax.ShapeDtypeStruct((2 * pages // GROUPS, page, cols // 2), BF16)
    table = jax.ShapeDtypeStruct((rows, 128), F32)
    return pl.pallas_call(
        open_kernel,
        out_shape=[
            single,
            double,
            double,
            single,
            single,
            single,
            jax.ShapeDtypeStruct((rows, wq.shape[1]), F32),
            jax.ShapeDtypeStruct((rows, wkv.shape[1]), F32),
            table,
            table,
        ],
        in_specs=[SMEM, VMEM] + [STAYS] * 4,
        out_specs=[VMEM] * 10,
        scratch_shapes=[
            pltpu.VMEM((rows, feats), BF16),
            pltpu.VMEM((feats, wq.shape[1]), BF16),
            pltpu.VMEM((feats, wkv.shape[1]), BF16),
            pltpu.SemaphoreType.DMA((3,)),
            pltpu.SemaphoreType.DMA((6,)),
        ],
        compiler_params=params(50),
        cost_estimate=cost(rows * feats, rows * feats),
    )(info, frequency, pool, x, wq, wkv)


def fresh_kernel(info_ref, x, wkv, acc_kv, cosine, sine, kept, sent):
    info = Info(info_ref)
    feats = x.shape[1]
    here = pl.ds(pl.multiple_of((1 - info.tensor) * feats, feats), feats)
    keys = info.tensor == 0
    fresh = acc_kv[...] + jnp.dot(x[...], wkv[here], preferred_element_type=F32)
    cos_kv = jnp.where(keys, cosine[...], 1.0)
    sin_kv = jnp.where(keys, sine[...], 0.0)
    low = turned(fresh[:, :128], cos_kv, sin_kv).astype(BF16)
    high = turned(fresh[:, 128:], cos_kv, sin_kv).astype(BF16)
    kept[...] = jnp.where(keys, low, high)
    sent[...] = jnp.where(keys, high, low)


def fresh_rows(info, x, wkv, acc_kv, cosine, sine):
    rows, feats = x.shape
    piece = jax.ShapeDtypeStruct((rows, wkv.shape[1] // 2), BF16)
    return pl.pallas_call(
        fresh_kernel,
        out_shape=[piece, piece],
        in_specs=[SMEM] + [VMEM] * 5,
        out_specs=[VMEM] * 2,
        compiler_params=params(12),
        cost_estimate=cost(2 * rows * feats * 2560, rows * feats),
    )(info, x, wkv, acc_kv, cosine, sine)


def query_kernel(info_ref, x, wq, acc_q, cosine, sine, q):
    feats = x.shape[1]
    here = pl.ds(pl.multiple_of((1 - Info(info_ref).tensor) * feats, feats), feats)
    cos_all, sin_all = cosine[...], sine[...]
    scale = HD**-0.5 * LOG2E
    tile = 256
    for c in range(0, q.shape[1], tile):
        lin = acc_q[:, c : c + tile] + jnp.dot(
            x[...], wq[here, c : c + tile], preferred_element_type=F32
        )
        for e in range(0, tile, 128):
            q[:, c + e : c + e + 128] = (
                turned(lin[:, e : e + 128], cos_all, sin_all) * scale
            ).astype(BF16)


def query_rows(info, x, wq, acc_q, cosine, sine):
    rows, feats = x.shape
    return pl.pallas_call(
        query_kernel,
        out_shape=jax.ShapeDtypeStruct((rows, wq.shape[1]), BF16),
        in_specs=[SMEM] + [VMEM] * 5,
        out_specs=VMEM,
        compiler_params=params(16),
        cost_estimate=cost(rows * feats, rows * feats),
    )(info, x, wq, acc_q, cosine, sine)


def soft_heads(q, tokens, segments, emit):
    rows = tokens.stop - tokens.start
    stack = 4
    low = lax.broadcasted_iota(jnp.int32, (rows, 2 * HD), 1) < HD

    def swap(x):
        return pltpu.roll(x, HD, 1)

    def heads(i, _):
        first = i == 0
        spots = [pl.ds(pl.multiple_of((i * stack + j) * 128, 128), 128) for j in range(stack)]
        tiles = [q[tokens, spot] for spot in spots]
        turns = [swap(x.astype(F32)).astype(BF16) for x in tiles]
        keep = low == first

        def stacked(a, b):
            zero = jnp.zeros_like(a[0])
            return jnp.concatenate(
                [jnp.where(keep, jnp.where(first, x, y), zero) for x, y in zip(a, b)], axis=0
            )

        def scores(qs):
            return [
                mask(
                    lax.dot_general(
                        qs, keys[span], (((1,), (1,)), ((), ())), preferred_element_type=F32
                    )
                )
                for keys, _, span, mask in segments
            ]

        def peak(parts):
            tops = [jnp.max(s, axis=1, keepdims=True) for s in parts]
            return functools.reduce(jnp.maximum, tops)

        def mixed(weights):
            return sum(
                jnp.dot(p, values[i, span], preferred_element_type=F32)
                for p, (_, values, span, _) in zip(weights, segments)
            )

        s_even = scores(stacked(tiles, turns))
        s_odd = scores(stacked(turns, tiles))
        m_even = peak(s_even)
        m_odd = peak(s_odd)
        p_even = [jnp.exp2(s - m_even).astype(BF16) for s in s_even]
        p_odd = [jnp.exp2(s - m_odd).astype(BF16) for s in s_odd]
        o_even = mixed(p_even)
        o_odd = mixed(p_odd)
        for j in range(stack):
            part = slice(j * rows, (j + 1) * rows)
            a, b = o_even[part], o_odd[part]
            total = jnp.where(low, a, swap(b))
            weight = jnp.where(low, swap(a), b)
            top = jnp.where(low, m_even[part], m_odd[part])
            emit(spots[j], total, weight, top)
        return 0

    lax.fori_loop(0, q.shape[1] // 128 // stack, heads, 0)


def widen(v, ones, values, here):
    low = lax.broadcasted_iota(jnp.int32, v.shape, 1) < HD
    values[0, here] = jnp.where(low, v, ones).astype(BF16)
    values[1, here] = jnp.where(low, pltpu.roll(v, HD, 1), ones).astype(BF16)


def gather_rows(info, own, other, fresh, keys, values, source):
    group, seq = info.group, info.seq
    request = info.request(group)
    rows = fresh.shape[1]
    per = rows // PAGE
    count = own.shape[0]
    capacity = count // GROUPS
    seen = keys.shape[0] // PAGE - seq * per
    is_key = info.tensor == 0

    def note(w, counts):
        came = info.page(request, w) // count ^ group
        place = came * capacity
        for d in range(GROUPS):
            place = place + jnp.where(came == d, counts[d], 0)
        source[w] = place
        return tuple(counts[d] + (came == d).astype(jnp.int32) for d in range(GROUPS))

    lax.fori_loop(0, info.window_pages, note, (jnp.int32(0),) * GROUPS, unroll=True)

    def place(block, a, b):
        here = pl.ds(pl.multiple_of(block * PAGE, PAGE), PAGE)
        keys[here] = jnp.where(is_key, a, b)
        widen(jnp.where(is_key, b, a).astype(F32), 1.0, values, here)

    for block, part in ((1, slice(0, PAGE)), (seen - 1, slice(PAGE, 2 * PAGE))):
        place(block, fresh[0, part], fresh[1, part])
    first = info.length(request) - WINDOW + seq * rows
    stand_in = jnp.where(is_key, fresh[0, :16], fresh[1, :16]).astype(F32)[0:1]
    stand_in = jnp.broadcast_to(stand_in, (PAGE, 2 * HD)).astype(BF16)

    def bring(i, _):
        for n in (2 * i, 2 * i + 1):
            block = jnp.where(n == 0, 0, n + 1)
            here = pl.ds(pl.multiple_of(block * PAGE, PAGE), PAGE)
            at = source[seq * per + n]
            hidden = first + n * PAGE < 0
            a, b = own[at], other[at]
            keys[here] = jnp.where(hidden, stand_in, jnp.where(is_key, a, b))
            v = jnp.where(is_key, b, a).astype(F32)
            widen(jnp.where(hidden, 0.0, v), jnp.where(hidden, 0.0, 1.0), values, here)
        return 0

    lax.fori_loop(0, (seen - per) // 2, bring, 0)


def bundle_kernel(a, b, out):
    out[: a.shape[0]] = a[...]
    out[a.shape[0] :] = b[...]


def bundled(a, b):
    return pl.pallas_call(
        bundle_kernel,
        out_shape=jax.ShapeDtypeStruct((a.shape[0] + b.shape[0], *a.shape[1:]), BF16),
        in_specs=[VMEM] * 2,
        out_specs=VMEM,
        compiler_params=params(8),
        cost_estimate=cost(6 * 10**9, 4),
    )(a, b)


def near_segment(keys, values, seq, half):
    blocks = keys.shape[0] // PAGE
    per = 2
    span = slice(half * PAGE, (blocks - seq * per - 1 + half) * PAGE)

    def mask(s):
        newer = lax.broadcasted_iota(jnp.int32, (s.shape[0], PAGE), 1) > (
            lax.broadcasted_iota(jnp.int32, (s.shape[0], PAGE), 0) % PAGE
        )
        if half == 0:
            parts = [
                jnp.where(newer, s[:, :PAGE], MASKED),
                jnp.where(newer, MASKED, s[:, PAGE : 2 * PAGE]),
                s[:, 2 * PAGE :],
            ]
        else:
            parts = [
                s[:, :PAGE],
                jnp.where(newer, s[:, PAGE : 2 * PAGE], MASKED),
                s[:, 2 * PAGE : -PAGE],
                jnp.where(newer, MASKED, s[:, -PAGE:]),
            ]
        return jnp.concatenate(parts, axis=1)

    return keys, values, span, mask


def far_segment(keys, values, seq):
    return keys, values, slice(0, seq * 2 * PAGE), lambda s: s


def near_kernel(
    info_ref, q, own, other, fresh, total, weight, top, keys, values, source
):
    info = Info(info_ref)
    seq = info.seq
    gather_rows(info, own, other, fresh, keys, values, source)

    def emit(spot, o, l, m):
        total[:, spot] = o
        weight[:, spot] = l
        top[:, spot] = m

    for k in range(SEQS):

        @pl.when(seq == k)
        def _(k=k):
            soft_heads(q, slice(0, PAGE), [near_segment(keys, values, k, 0)], emit)


def attend_near(info, q, own, other, fresh):
    state = jax.ShapeDtypeStruct((PAGE, q.shape[1]), F32)
    span = WINDOW + fresh.shape[1]
    *state, keys, values = pl.pallas_call(
        near_kernel,
        out_shape=[
            state,
            state,
            state,
            jax.ShapeDtypeStruct((span, 2 * HD), BF16),
            jax.ShapeDtypeStruct((2, span, 2 * HD), BF16),
        ],
        in_specs=[SMEM] + [VMEM] * 4,
        out_specs=[VMEM] * 5,
        scratch_shapes=[pltpu.SMEM((own.shape[0],), jnp.int32)],
        compiler_params=params(32),
        cost_estimate=cost(20 * 10**9, 4 * span),
    )(info, q, own, other, fresh)
    return state, keys, values


def partner_product(info, heads_out, w, partial):
    cols = partial.shape[1]
    here = pl.ds(pl.multiple_of((1 - info.tensor) * cols, cols), cols)
    partial[...] = jnp.dot(heads_out[...], w[:, here], preferred_element_type=F32).astype(BF16)


def far_kernel(
    info_ref, q, total, weight, top, z3, z2, z1, w, heads_out, partial, keys, values
):
    info = Info(info_ref)
    rows = q.shape[0]
    seq = info.seq
    zs = (None, z1, z2, z3)
    is_key = info.tensor == 0

    for k in range(SEQS):

        @pl.when(seq == k)
        def _(k=k):
            if k == 0:
                heads_out[...] = (total[...] / weight[...]).astype(BF16)
                return
            for n in range(k):
                z = zs[n ^ k]
                here = slice(n * rows, (n + 1) * rows)
                a, b = z[0], z[1]
                keys[here] = jnp.where(is_key, a, b)
                widen(jnp.where(is_key, b, a).astype(F32), 1.0, values, here)

            def emit(spot, o, l, m):
                before = top[:, spot]
                peak = jnp.maximum(before, m)
                a = jnp.exp2(before - peak)
                b = jnp.exp2(m - peak)
                done = (total[:, spot] * a + o * b) / (weight[:, spot] * a + l * b)
                heads_out[:, spot] = done.astype(BF16)

            soft_heads(q, slice(0, PAGE), [far_segment(keys, values, k)], emit)

    partner_product(info, heads_out, w, partial)


def attend_far(info, q, state, zs, w):
    rows = q.shape[0]
    span = (SEQS - 1) * rows
    return pl.pallas_call(
        far_kernel,
        out_shape=[
            jax.ShapeDtypeStruct((PAGE, q.shape[1]), BF16),
            jax.ShapeDtypeStruct((PAGE, w.shape[1] // TENSORS), BF16),
            jax.ShapeDtypeStruct((span, 2 * HD), BF16),
            jax.ShapeDtypeStruct((2, span, 2 * HD), BF16),
        ],
        in_specs=[SMEM] + [VMEM] * 8,
        out_specs=[VMEM] * 4,
        compiler_params=params(24),
        cost_estimate=cost(rows * span, 4 * span),
    )(info, q, *state, *zs, w)


def last_kernel(info_ref, q, keys, values, far_keys, far_values, w, heads_out, partial):
    info = Info(info_ref)

    def emit(spot, o, l, m):
        heads_out[:, spot] = (o / l).astype(BF16)

    for k in range(SEQS):

        @pl.when(info.seq == k)
        def _(k=k):
            segments = [near_segment(keys, values, k, 1)]
            if k:
                segments.append(far_segment(far_keys, far_values, k))
            soft_heads(q, slice(PAGE, 2 * PAGE), segments, emit)

    partner_product(info, heads_out, w, partial)


def attend_last(info, q, keys, values, far_keys, far_values, w):
    return pl.pallas_call(
        last_kernel,
        out_shape=[
            jax.ShapeDtypeStruct((PAGE, q.shape[1]), BF16),
            jax.ShapeDtypeStruct((PAGE, w.shape[1] // TENSORS), BF16),
        ],
        in_specs=[SMEM] + [VMEM] * 6,
        out_specs=[VMEM] * 2,
        compiler_params=params(36),
        cost_estimate=cost(PAGE * WINDOW, 4 * WINDOW),
    )(info, q, keys, values, far_keys, far_values, w)


def home_kernel(info_ref, x1, x2, away, w, out, home, first, sem):
    rows, cols = home.shape
    here = pl.ds(pl.multiple_of(Info(info_ref).tensor * cols, cols), cols)
    x = jnp.concatenate([x1[...], x2[...]], axis=0)
    o = jnp.dot(x, w[:, here], preferred_element_type=F32).astype(BF16)
    home[...] = o[rows:]
    first[...] = (o[:rows].astype(F32) + away[...].astype(F32)).astype(BF16)
    copy = pltpu.make_async_copy(first, out.at[pl.ds(0, rows)], sem)
    copy.start()
    copy.wait()


def home_project(info, x1, x2, away, w):
    rows, depth = x1.shape
    cols = w.shape[1] // TENSORS
    return pl.pallas_call(
        home_kernel,
        out_shape=[
            jax.ShapeDtypeStruct((2 * rows, cols), BF16),
            jax.ShapeDtypeStruct((rows, cols), BF16),
        ],
        in_specs=[SMEM] + [VMEM] * 4,
        out_specs=[STAYS, VMEM],
        scratch_shapes=[pltpu.VMEM((rows, cols), BF16), pltpu.SemaphoreType.DMA],
        compiler_params=params(16),
        cost_estimate=cost(20 * 10**9, 2 * depth * cols),
    )(info, x1, x2, away, w)


def add_kernel(before, a, b, out, last, sem):
    rows = a.shape[0]
    last[...] = (a[...].astype(F32) + b[...].astype(F32)).astype(BF16)
    copy = pltpu.make_async_copy(last, out.at[pl.ds(rows, rows)], sem)
    copy.start()
    copy.wait()


def added(before, a, b):
    return pl.pallas_call(
        add_kernel,
        out_shape=jax.ShapeDtypeStruct(before.shape, BF16),
        in_specs=[STAYS, VMEM, VMEM],
        out_specs=STAYS,
        scratch_shapes=[pltpu.VMEM(a.shape, BF16), pltpu.SemaphoreType.DMA],
        input_output_aliases={0: 0},
        compiler_params=params(8),
    )(before, a, b)


def flipped(value, axes, count, bits):
    return lax.ppermute(value, axes, [(i, i ^ bits) for i in range(count)])


def after(value, *others):
    return lax.optimization_barrier((value, *others))[0]


def shards_fast(
    span_tokens, q_weight, kv_weight, out_weight, kv_pool, cache_lengths, slot_requests, page_table
):
    group_id = lax.axis_index("group")
    seq_id = lax.axis_index("seq")
    tensor_id = lax.axis_index("tensor")
    place = jnp.stack([group_id, seq_id, tensor_id]).astype(jnp.int32)
    row = jnp.concatenate([place, slot_requests, cache_lengths])
    row = jnp.pad(row, (0, page_table.shape[1] - row.shape[0]))
    info = jnp.concatenate([row[None], page_table])
    mine = span_tokens[0]
    theirs = flipped(mine, "tensor", 2, 1)
    half_dim = HD // 2
    lane = jnp.arange(128, dtype=jnp.int32) % half_dim
    frequency = jnp.power(jnp.float32(10000.0), -lane.astype(F32) / half_dim)
    frequency = jnp.broadcast_to(frequency[None, :], (8, 128))
    pages = open_rows(info, frequency, kv_pool, mine, q_weight, kv_weight)
    home, same, beyond, beside, across, diagonal = pages[:6]
    acc_q, acc_kv, cosine, sine = pages[6:]
    capacity = home.shape[0]
    same = flipped(same, "tensor", 2, 1)
    beyond = flipped(beyond, "group", 4, 2)
    kept, sent = fresh_rows(info, theirs, kv_weight, acc_kv, cosine, sine)
    got = flipped(sent, "tensor", 2, 1)
    across, diagonal, _ = lax.optimization_barrier((across, diagonal, sent))
    across = flipped(across, ("group", "tensor"), 8, 5)
    diagonal = flipped(diagonal, ("group", "tensor"), 8, 7)
    q = query_rows(info, theirs, q_weight, acc_q, cosine, sine)
    same, beyond, _ = lax.optimization_barrier((same, beyond, q))
    mate = jnp.concatenate([beside, beyond[capacity:], same[capacity:]])
    mate = flipped(mate, "group", 4, 1)
    fresh = bundled(kept[None], got[None])
    zs = [flipped(fresh, "seq", 4, d) for d in (3, 2, 1)]
    other_chip = bundled(across, diagonal)
    own = jnp.concatenate(
        [home, mate[:capacity], beyond[:capacity], mate[capacity : 2 * capacity]]
    )
    other = jnp.concatenate([same[:capacity], mate[2 * capacity :], other_chip])
    state, keys, values = attend_near(info, q, own, other, fresh)
    heads_0, partial_0, far_keys, far_values = attend_far(info, q, state, zs, out_weight)
    away_0 = flipped(partial_0, "tensor", 2, 1)
    heads_1, partial_1 = attend_last(info, q, keys, values, far_keys, far_values, out_weight)
    away_1 = flipped(partial_1, "tensor", 2, 1)
    out, home_1 = home_project(info, heads_0, heads_1, away_0, out_weight)
    return added(out, home_1, away_1)[None]


def solution(mesh):
    sizes = tuple(mesh.shape[a] for a in ("group", "seq", "tensor"))
    body = shards_fast if sizes == (GROUPS, SEQS, TENSORS) else shards
    placed = (
        P("group", "seq", "tensor"),
        P(None, "tensor"),
        P(None, "tensor"),
        P("tensor", None),
        P("group", None, "tensor"),
        P(),
        P(),
        P(),
    )
    return jax.shard_map(
        body, mesh=mesh, in_specs=placed, out_specs=P("group", "seq", "tensor"), check_vma=False
    )
```

```python
import functools

import jax
import jax.numpy as jnp
from jax import lax
from jax.experimental import pallas as pl
from jax.experimental.pallas import tpu as pltpu
from jax.sharding import PartitionSpec as P

HD = 64
KVH = 4
WINDOW = 2048
PAGE = 128


def shifted(block, axis, distance):
    devices = range(lax.axis_size(axis))
    route = [(i - distance, i) for i in devices if i - distance in devices]
    return lax.ppermute(block, axis, route)


def swapped(value, axis, stride):
    return lax.ppermute(value, axis, [(i, i ^ 1 << stride) for i in range(lax.axis_size(axis))])


def rotate(values, positions):
    half_dim = HD // 2
    frequency = jnp.power(jnp.float32(10000.0), -jnp.arange(half_dim, dtype=jnp.float32) / half_dim)
    angles = positions.astype(jnp.float32)[:, None] * frequency[None, :]
    cosine = jnp.cos(angles)[:, None, :]
    sine_part = jnp.sin(angles)[:, None, :]
    front_half = values[..., :half_dim]
    back_half = values[..., half_dim:]
    return jnp.concatenate(
        [front_half * cosine - back_half * sine_part, back_half * cosine + front_half * sine_part],
        axis=-1,
    )


def attend(block_q, block_k, block_v, base_pos):
    query_count = block_q.shape[0]
    key_count = block_k.shape[0]
    scores = jnp.einsum(
        "tkgd,nkd->kgtn", block_q, block_k, preferred_element_type=jnp.float32
    ) * HD ** (-0.5)
    query_at = jnp.arange(query_count, dtype=jnp.int32)[:, None]
    key_at = jnp.arange(key_count, dtype=jnp.int32)[None, :]
    allowed = (key_at > query_at) & (key_at <= query_at + WINDOW) & (base_pos + key_at >= 0)
    masked = jnp.where(allowed, scores, jnp.float32(-1e30))
    row_top = jnp.max(masked, axis=-1, keepdims=True)
    weights = jnp.where(allowed, jnp.exp(masked - row_top), jnp.float32(0.0))
    row_total = jnp.sum(weights, axis=-1)
    rounded = weights.astype(jnp.bfloat16)
    mixed_rows = jnp.einsum("kgtn,nkd->tkgd", rounded, block_v, preferred_element_type=jnp.float32)
    mixed_rows = mixed_rows / jnp.transpose(row_total, (2, 0, 1))[..., None]
    return mixed_rows.astype(jnp.bfloat16).reshape(query_count, -1)


def shards(
    span_tokens, q_weight, kv_weight, out_weight, kv_pool, cache_lengths, slot_requests, page_table
):
    groups = lax.axis_size("group")
    seq_count = lax.axis_size("seq")
    tensor_count = lax.axis_size("tensor")
    group_id = lax.axis_index("group")
    seq_id = lax.axis_index("seq")
    tensor_id = lax.axis_index("tensor")
    local_reqs, seg_len, feat_local = span_tokens.shape
    head_cols = q_weight.shape[1]
    kv_cols = kv_weight.shape[1]
    local_heads = head_cols // HD
    group_heads = kv_cols // HD
    kv_local = max(1, KVH // tensor_count)
    per_kv = local_heads // kv_local
    head_first = tensor_id * KVH // tensor_count % group_heads
    holds_keys = tensor_id % 2 == 0
    pool_rows = kv_pool.shape[0]
    capacity = pool_rows // groups
    row_count = local_reqs * seg_len
    my_slots = group_id * local_reqs + jnp.arange(local_reqs, dtype=jnp.int32)
    my_requests = slot_requests[my_slots]
    my_lengths = cache_lengths[my_requests]
    project_piece_rows = lax.all_gather(span_tokens, "tensor", axis=2, tiled=True)
    feat_width = project_piece_rows.shape[2]
    flat_rows = project_piece_rows.reshape(row_count, feat_width)
    query_lin = jnp.dot(flat_rows, q_weight, preferred_element_type=jnp.float32)
    fresh_lin = jnp.dot(flat_rows, kv_weight, preferred_element_type=jnp.float32)
    positions = (
        my_lengths[:, None] + seq_id * seg_len + jnp.arange(seg_len, dtype=jnp.int32)[None, :]
    )
    queries = jax.vmap(rotate)(query_lin.reshape(local_reqs, seg_len, local_heads, HD), positions)
    queries = queries.astype(jnp.bfloat16).reshape(local_reqs, seg_len, kv_local, per_kv, HD)
    fresh_heads = fresh_lin.reshape(local_reqs, seg_len, group_heads, HD)
    rotated = jax.vmap(rotate)(fresh_heads, positions)
    span_kv = (
        jnp.where(holds_keys, rotated, fresh_heads)
        .astype(jnp.bfloat16)
        .reshape(local_reqs, seg_len, kv_cols)
    )
    all_ids = page_table[slot_requests]
    owned_here = all_ids // pool_rows == group_id
    slot_rank = jnp.cumsum(owned_here.astype(jnp.int32), axis=1) - 1
    local_rows = all_ids - group_id * pool_rows
    chosen = owned_here[:, :, None] & (
        slot_rank[:, :, None] == jnp.arange(capacity, dtype=jnp.int32)[None, None, :]
    )
    wanted = jnp.sum(jnp.where(chosen, local_rows[:, :, None], 0), axis=1)
    my_ids = page_table[my_requests].reshape(-1)
    my_owner = my_ids // pool_rows
    onehot = (my_owner[:, None] == jnp.arange(groups, dtype=jnp.int32)[None, :]).astype(jnp.int32)
    arrival = jnp.sum((jnp.cumsum(onehot, axis=0) - 1) * onehot, axis=1)
    arrived_row = my_owner * capacity + arrival
    outgoing = kv_pool[wanted]
    arrived = lax.all_to_all(outgoing, "group", split_axis=0, concat_axis=0, tiled=True)
    cached = arrived.reshape(groups * capacity, PAGE, kv_cols)[arrived_row]
    cached = cached.reshape(local_reqs, WINDOW, kv_cols)
    span_all = jnp.zeros((local_reqs, seg_len * seq_count, kv_cols), jnp.bfloat16)
    for back_step in range(seq_count - 1, -1, -1):
        piece_rows = span_kv if back_step == 0 else shifted(span_kv, "seq", back_step)
        span_all = lax.dynamic_update_slice_in_dim(
            span_all, piece_rows, (seq_id - back_step) * seg_len, 1
        )
    joined = jnp.concatenate([cached, span_all], axis=1)
    visible = lax.dynamic_slice_in_dim(joined, seq_id * seg_len, WINDOW + seg_len, 1)
    partner_rows = swapped(visible, "tensor", 0)
    key_all = jnp.where(holds_keys, visible, partner_rows).reshape(
        local_reqs, WINDOW + seg_len, group_heads, HD
    )
    value_all = jnp.where(holds_keys, partner_rows, visible).reshape(
        local_reqs, WINDOW + seg_len, group_heads, HD
    )
    key_rows = lax.dynamic_slice_in_dim(key_all, head_first, kv_local, 2)
    value_rows = lax.dynamic_slice_in_dim(value_all, head_first, kv_local, 2)
    block_len = min(128, seg_len)
    block_count = seg_len // block_len

    def per_request(request_items):
        request_q, request_k, request_v, length = request_items

        def per_block(block_index):
            first_row = block_index * block_len
            block_q = lax.dynamic_slice_in_dim(request_q, first_row, block_len, 0)
            block_k = lax.dynamic_slice_in_dim(request_k, first_row, WINDOW + block_len, 0)
            block_v = lax.dynamic_slice_in_dim(request_v, first_row, WINDOW + block_len, 0)
            return attend(block_q, block_k, block_v, length - WINDOW + seq_id * seg_len + first_row)

        return lax.map(per_block, jnp.arange(block_count, dtype=jnp.int32)).reshape(
            seg_len, head_cols
        )

    attended_heads = lax.map(per_request, (queries, key_rows, value_rows, my_lengths))
    flat_heads = attended_heads.reshape(row_count, head_cols)
    out_cols = out_weight.shape[1] // tensor_count
    summed = lax.psum_scatter(
        lax.dot_general(
            out_weight, flat_heads, (((0,), (1,)), ((), ())), preferred_element_type=jnp.float32
        ).astype(jnp.bfloat16),
        "tensor",
        scatter_dimension=0,
        tiled=True,
    ).astype(jnp.float32)
    result = summed.T
    return result.astype(jnp.bfloat16).reshape(local_reqs, seg_len, out_cols)


LOG2E = 1.4426950408889634
MASKED = -1e30
F32 = jnp.float32
BF16 = jnp.bfloat16
HBM = pl.BlockSpec(memory_space=pl.ANY)
VMEM = pl.BlockSpec(memory_space=pltpu.VMEM)
SMEM = pl.BlockSpec(memory_space=pltpu.SMEM)
STAYS = pl.BlockSpec(memory_space=pltpu.HBM)
GROUPS, SEQS, TENSORS = 4, 4, 2


def params(mebibytes):
    return pltpu.CompilerParams(vmem_limit_bytes=mebibytes * 2**20)


def cost(flops, moved):
    return pl.CostEstimate(flops=flops, bytes_accessed=moved, transcendentals=0)


class Info:
    def __init__(self, ref):
        self.ref = ref
        self.group, self.seq, self.tensor = ref[0, 0], ref[0, 1], ref[0, 2]
        self.window_pages = ref.shape[1]

    def request(self, slot):
        return self.ref[0, 3 + slot]

    def length(self, request):
        return self.ref[0, 3 + GROUPS + request]

    def page(self, request, w):
        return self.ref[1 + request, w]


def turned(x, cosine, sine):
    lane = lax.broadcasted_iota(jnp.int32, x.shape, 1)
    other = jnp.where(lane % HD < HD // 2, pltpu.roll(x, 128 - HD // 2, 1), pltpu.roll(x, HD // 2, 1))
    return x * cosine + other * sine


def open_kernel(
    info_ref, frequency, pool, x_hbm, wq_hbm, wkv_hbm,
    home, same, beyond, beside, across, diagonal, acc_q, acc_kv, cosine, sine,
    x, wq, wkv, sems, page_sems,
):
    info = Info(info_ref)
    rows, feats = x.shape
    here = pl.ds(pl.multiple_of(info.tensor * feats, feats), feats)
    copies = [
        pltpu.make_async_copy(x_hbm, x, sems.at[0]),
        pltpu.make_async_copy(wkv_hbm.at[here], wkv, sems.at[1]),
        pltpu.make_async_copy(wq_hbm.at[here], wq, sems.at[2]),
    ]
    for copy in copies:
        copy.start()
    pages = pool.shape[0]
    capacity = pages // GROUPS
    half = pool.shape[2] // 2
    mine = pl.ds(pl.multiple_of(info.tensor * half, half), half)
    theirs = pl.ds(pl.multiple_of((1 - info.tensor) * half, half), half)
    outs = (home, same, beyond, beside, across, diagonal)
    spots = (
        ((0, 0), (1, 0)),
        ((3, 0), (1, capacity)),
        ((2, 0), (4, 0)),
        ((2, capacity), (5, 0)),
    )
    for flip, targets in enumerate(spots):
        request = info.request(info.group ^ flip)

        def take(w, rank):
            page = info.page(request, w)
            near = page // pages == info.group

            @pl.when(near)
            def _():
                row = page % pages
                for (out, base), cols in zip(targets, (mine, theirs)):
                    pltpu.make_async_copy(
                        pool.at[row, :, cols], outs[out].at[base + rank], page_sems.at[out]
                    ).start()

            return rank + near.astype(jnp.int32)

        lax.fori_loop(0, info.window_pages, take, jnp.int32(0))
    start = info.length(info.request(info.group)) + info.seq * rows
    position = (start + lax.broadcasted_iota(jnp.int32, (rows, 128), 0)).astype(F32)
    angles = position * frequency[0:1, :]
    lane = lax.broadcasted_iota(jnp.int32, (rows, 128), 1)
    cosine[...] = jnp.cos(angles)
    sine[...] = jnp.where(lane % HD < HD // 2, -1.0, 1.0) * jnp.sin(angles)
    copies[0].wait()
    copies[1].wait()
    acc_kv[...] = jnp.dot(x[...], wkv[...], preferred_element_type=F32)
    copies[2].wait()
    acc_q[...] = jnp.dot(x[...], wq[...], preferred_element_type=F32)
    for i, out in enumerate(outs):
        pltpu.make_async_copy(out, out, page_sems.at[i]).wait()


def open_rows(info, frequency, pool, x, wq, wkv):
    rows, feats = x.shape
    pages, page, cols = pool.shape
    single = jax.ShapeDtypeStruct((pages // GROUPS, page, cols // 2), BF16)
    double = jax.ShapeDtypeStruct((2 * pages // GROUPS, page, cols // 2), BF16)
    table = jax.ShapeDtypeStruct((rows, 128), F32)
    return pl.pallas_call(
        open_kernel,
        out_shape=[
            single,
            double,
            double,
            single,
            single,
            single,
            jax.ShapeDtypeStruct((rows, wq.shape[1]), F32),
            jax.ShapeDtypeStruct((rows, wkv.shape[1]), F32),
            table,
            table,
        ],
        in_specs=[SMEM, VMEM] + [STAYS] * 4,
        out_specs=[VMEM] * 10,
        scratch_shapes=[
            pltpu.VMEM((rows, feats), BF16),
            pltpu.VMEM((feats, wq.shape[1]), BF16),
            pltpu.VMEM((feats, wkv.shape[1]), BF16),
            pltpu.SemaphoreType.DMA((3,)),
            pltpu.SemaphoreType.DMA((6,)),
        ],
        compiler_params=params(50),
        cost_estimate=cost(rows * feats, rows * feats),
    )(info, frequency, pool, x, wq, wkv)


def fresh_kernel(info_ref, x, wkv, acc_kv, cosine, sine, kept, sent):
    info = Info(info_ref)
    feats = x.shape[1]
    here = pl.ds(pl.multiple_of((1 - info.tensor) * feats, feats), feats)
    keys = info.tensor == 0
    fresh = acc_kv[...] + jnp.dot(x[...], wkv[here], preferred_element_type=F32)
    cos_kv = jnp.where(keys, cosine[...], 1.0)
    sin_kv = jnp.where(keys, sine[...], 0.0)
    low = turned(fresh[:, :128], cos_kv, sin_kv).astype(BF16)
    high = turned(fresh[:, 128:], cos_kv, sin_kv).astype(BF16)
    kept[...] = jnp.where(keys, low, high)
    sent[...] = jnp.where(keys, high, low)


def fresh_rows(info, x, wkv, acc_kv, cosine, sine):
    rows, feats = x.shape
    piece = jax.ShapeDtypeStruct((rows, wkv.shape[1] // 2), BF16)
    return pl.pallas_call(
        fresh_kernel,
        out_shape=[piece, piece],
        in_specs=[SMEM] + [VMEM] * 5,
        out_specs=[VMEM] * 2,
        compiler_params=params(12),
        cost_estimate=cost(2 * rows * feats * 2560, rows * feats),
    )(info, x, wkv, acc_kv, cosine, sine)


def query_kernel(info_ref, x, wq, acc_q, cosine, sine, q):
    feats = x.shape[1]
    here = pl.ds(pl.multiple_of((1 - Info(info_ref).tensor) * feats, feats), feats)
    cos_all, sin_all = cosine[...], sine[...]
    scale = HD**-0.5 * LOG2E
    tile = 256
    for c in range(0, q.shape[1], tile):
        lin = acc_q[:, c : c + tile] + jnp.dot(
            x[...], wq[here, c : c + tile], preferred_element_type=F32
        )
        for e in range(0, tile, 128):
            q[:, c + e : c + e + 128] = (
                turned(lin[:, e : e + 128], cos_all, sin_all) * scale
            ).astype(BF16)


def query_rows(info, x, wq, acc_q, cosine, sine):
    rows, feats = x.shape
    return pl.pallas_call(
        query_kernel,
        out_shape=jax.ShapeDtypeStruct((rows, wq.shape[1]), BF16),
        in_specs=[SMEM] + [VMEM] * 5,
        out_specs=VMEM,
        compiler_params=params(16),
        cost_estimate=cost(rows * feats, rows * feats),
    )(info, x, wq, acc_q, cosine, sine)


def soft_heads(q, tokens, segments, emit):
    rows = tokens.stop - tokens.start
    stack = 4
    low = lax.broadcasted_iota(jnp.int32, (rows, 2 * HD), 1) < HD

    def swap(x):
        return pltpu.roll(x, HD, 1)

    def heads(i, _):
        first = i == 0
        spots = [pl.ds(pl.multiple_of((i * stack + j) * 128, 128), 128) for j in range(stack)]
        tiles = [q[tokens, spot] for spot in spots]
        turns = [swap(x.astype(F32)).astype(BF16) for x in tiles]
        keep = low == first

        def stacked(a, b):
            zero = jnp.zeros_like(a[0])
            return jnp.concatenate(
                [jnp.where(keep, jnp.where(first, x, y), zero) for x, y in zip(a, b)], axis=0
            )

        def scores(qs):
            return [
                mask(
                    lax.dot_general(
                        qs, keys[span], (((1,), (1,)), ((), ())), preferred_element_type=F32
                    )
                )
                for keys, _, span, mask in segments
            ]

        def peak(parts):
            tops = [jnp.max(s, axis=1, keepdims=True) for s in parts]
            return functools.reduce(jnp.maximum, tops)

        def mixed(weights):
            return sum(
                jnp.dot(p, values[i, span], preferred_element_type=F32)
                for p, (_, values, span, _) in zip(weights, segments)
            )

        s_even = scores(stacked(tiles, turns))
        s_odd = scores(stacked(turns, tiles))
        m_even = peak(s_even)
        m_odd = peak(s_odd)
        p_even = [jnp.exp2(s - m_even).astype(BF16) for s in s_even]
        p_odd = [jnp.exp2(s - m_odd).astype(BF16) for s in s_odd]
        o_even = mixed(p_even)
        o_odd = mixed(p_odd)
        for j in range(stack):
            part = slice(j * rows, (j + 1) * rows)
            a, b = o_even[part], o_odd[part]
            total = jnp.where(low, a, swap(b))
            weight = jnp.where(low, swap(a), b)
            top = jnp.where(low, m_even[part], m_odd[part])
            emit(spots[j], total, weight, top)
        return 0

    lax.fori_loop(0, q.shape[1] // 128 // stack, heads, 0)


def widen(v, ones, values, here):
    low = lax.broadcasted_iota(jnp.int32, v.shape, 1) < HD
    values[0, here] = jnp.where(low, v, ones).astype(BF16)
    values[1, here] = jnp.where(low, pltpu.roll(v, HD, 1), ones).astype(BF16)


def gather_rows(info, own, other, fresh, keys, values, source):
    group, seq = info.group, info.seq
    request = info.request(group)
    rows = fresh.shape[1]
    per = rows // PAGE
    count = own.shape[0]
    capacity = count // GROUPS
    seen = keys.shape[0] // PAGE - seq * per
    is_key = info.tensor == 0

    def note(w, counts):
        came = info.page(request, w) // count ^ group
        place = came * capacity
        for d in range(GROUPS):
            place = place + jnp.where(came == d, counts[d], 0)
        source[w] = place
        return tuple(counts[d] + (came == d).astype(jnp.int32) for d in range(GROUPS))

    lax.fori_loop(0, info.window_pages, note, (jnp.int32(0),) * GROUPS, unroll=True)

    def place(block, a, b):
        here = pl.ds(pl.multiple_of(block * PAGE, PAGE), PAGE)
        keys[here] = jnp.where(is_key, a, b)
        widen(jnp.where(is_key, b, a).astype(F32), 1.0, values, here)

    for block, part in ((1, slice(0, PAGE)), (seen - 1, slice(PAGE, 2 * PAGE))):
        place(block, fresh[0, part], fresh[1, part])
    first = info.length(request) - WINDOW + seq * rows
    stand_in = jnp.where(is_key, fresh[0, :16], fresh[1, :16]).astype(F32)[0:1]
    stand_in = jnp.broadcast_to(stand_in, (PAGE, 2 * HD)).astype(BF16)

    def bring(i, _):
        for n in (2 * i, 2 * i + 1):
            block = jnp.where(n == 0, 0, n + 1)
            here = pl.ds(pl.multiple_of(block * PAGE, PAGE), PAGE)
            at = source[seq * per + n]
            hidden = first + n * PAGE < 0
            a, b = own[at], other[at]
            keys[here] = jnp.where(hidden, stand_in, jnp.where(is_key, a, b))
            v = jnp.where(is_key, b, a).astype(F32)
            widen(jnp.where(hidden, 0.0, v), jnp.where(hidden, 0.0, 1.0), values, here)
        return 0

    lax.fori_loop(0, (seen - per) // 2, bring, 0)


def bundle_kernel(a, b, out):
    out[: a.shape[0]] = a[...]
    out[a.shape[0] :] = b[...]


def bundled(a, b):
    return pl.pallas_call(
        bundle_kernel,
        out_shape=jax.ShapeDtypeStruct((a.shape[0] + b.shape[0], *a.shape[1:]), BF16),
        in_specs=[VMEM] * 2,
        out_specs=VMEM,
        compiler_params=params(8),
        cost_estimate=cost(6 * 10**9, 4),
    )(a, b)


def near_segment(keys, values, seq, half):
    blocks = keys.shape[0] // PAGE
    per = 2
    span = slice(half * PAGE, (blocks - seq * per - 1 + half) * PAGE)

    def mask(s):
        newer = lax.broadcasted_iota(jnp.int32, (s.shape[0], PAGE), 1) > (
            lax.broadcasted_iota(jnp.int32, (s.shape[0], PAGE), 0) % PAGE
        )
        if half == 0:
            parts = [
                jnp.where(newer, s[:, :PAGE], MASKED),
                jnp.where(newer, MASKED, s[:, PAGE : 2 * PAGE]),
                s[:, 2 * PAGE :],
            ]
        else:
            parts = [
                s[:, :PAGE],
                jnp.where(newer, s[:, PAGE : 2 * PAGE], MASKED),
                s[:, 2 * PAGE : -PAGE],
                jnp.where(newer, MASKED, s[:, -PAGE:]),
            ]
        return jnp.concatenate(parts, axis=1)

    return keys, values, span, mask


def far_segment(keys, values, seq):
    return keys, values, slice(0, seq * 2 * PAGE), lambda s: s


def near_kernel(
    info_ref, q, own, other, fresh, total, weight, top, keys, values, source
):
    info = Info(info_ref)
    seq = info.seq
    gather_rows(info, own, other, fresh, keys, values, source)

    def emit(spot, o, l, m):
        total[:, spot] = o
        weight[:, spot] = l
        top[:, spot] = m

    for k in range(SEQS):

        @pl.when(seq == k)
        def _(k=k):
            soft_heads(q, slice(0, PAGE), [near_segment(keys, values, k, 0)], emit)


def attend_near(info, q, own, other, fresh):
    state = jax.ShapeDtypeStruct((PAGE, q.shape[1]), F32)
    span = WINDOW + fresh.shape[1]
    *state, keys, values = pl.pallas_call(
        near_kernel,
        out_shape=[
            state,
            state,
            state,
            jax.ShapeDtypeStruct((span, 2 * HD), BF16),
            jax.ShapeDtypeStruct((2, span, 2 * HD), BF16),
        ],
        in_specs=[SMEM] + [VMEM] * 4,
        out_specs=[VMEM] * 5,
        scratch_shapes=[pltpu.SMEM((own.shape[0],), jnp.int32)],
        compiler_params=params(32),
        cost_estimate=cost(20 * 10**9, 4 * span),
    )(info, q, own, other, fresh)
    return state, keys, values


def partner_product(info, heads_out, w, partial):
    cols = partial.shape[1]
    here = pl.ds(pl.multiple_of((1 - info.tensor) * cols, cols), cols)
    partial[...] = jnp.dot(heads_out[...], w[:, here], preferred_element_type=F32).astype(BF16)


def far_kernel(
    info_ref, q, total, weight, top, z3, z2, z1, w, heads_out, partial, keys, values
):
    info = Info(info_ref)
    rows = q.shape[0]
    seq = info.seq
    zs = (None, z1, z2, z3)
    is_key = info.tensor == 0

    for k in range(SEQS):

        @pl.when(seq == k)
        def _(k=k):
            if k == 0:
                heads_out[...] = (total[...] / weight[...]).astype(BF16)
                return
            for n in range(k):
                z = zs[n ^ k]
                here = slice(n * rows, (n + 1) * rows)
                a, b = z[0], z[1]
                keys[here] = jnp.where(is_key, a, b)
                widen(jnp.where(is_key, b, a).astype(F32), 1.0, values, here)

            def emit(spot, o, l, m):
                before = top[:, spot]
                peak = jnp.maximum(before, m)
                a = jnp.exp2(before - peak)
                b = jnp.exp2(m - peak)
                done = (total[:, spot] * a + o * b) / (weight[:, spot] * a + l * b)
                heads_out[:, spot] = done.astype(BF16)

            soft_heads(q, slice(0, PAGE), [far_segment(keys, values, k)], emit)

    partner_product(info, heads_out, w, partial)


def attend_far(info, q, state, zs, w):
    rows = q.shape[0]
    span = (SEQS - 1) * rows
    return pl.pallas_call(
        far_kernel,
        out_shape=[
            jax.ShapeDtypeStruct((PAGE, q.shape[1]), BF16),
            jax.ShapeDtypeStruct((PAGE, w.shape[1] // TENSORS), BF16),
            jax.ShapeDtypeStruct((span, 2 * HD), BF16),
            jax.ShapeDtypeStruct((2, span, 2 * HD), BF16),
        ],
        in_specs=[SMEM] + [VMEM] * 8,
        out_specs=[VMEM] * 4,
        compiler_params=params(24),
        cost_estimate=cost(rows * span, 4 * span),
    )(info, q, *state, *zs, w)


def last_kernel(info_ref, q, keys, values, far_keys, far_values, w, heads_out, partial):
    info = Info(info_ref)

    def emit(spot, o, l, m):
        heads_out[:, spot] = (o / l).astype(BF16)

    for k in range(SEQS):

        @pl.when(info.seq == k)
        def _(k=k):
            segments = [near_segment(keys, values, k, 1)]
            if k:
                segments.append(far_segment(far_keys, far_values, k))
            soft_heads(q, slice(PAGE, 2 * PAGE), segments, emit)

    partner_product(info, heads_out, w, partial)


def attend_last(info, q, keys, values, far_keys, far_values, w):
    return pl.pallas_call(
        last_kernel,
        out_shape=[
            jax.ShapeDtypeStruct((PAGE, q.shape[1]), BF16),
            jax.ShapeDtypeStruct((PAGE, w.shape[1] // TENSORS), BF16),
        ],
        in_specs=[SMEM] + [VMEM] * 6,
        out_specs=[VMEM] * 2,
        compiler_params=params(36),
        cost_estimate=cost(PAGE * WINDOW, 4 * WINDOW),
    )(info, q, keys, values, far_keys, far_values, w)


def home_kernel(info_ref, x1, x2, away, w, out, home, first, sem):
    rows, cols = home.shape
    here = pl.ds(pl.multiple_of(Info(info_ref).tensor * cols, cols), cols)
    x = jnp.concatenate([x1[...], x2[...]], axis=0)
    o = jnp.dot(x, w[:, here], preferred_element_type=F32).astype(BF16)
    home[...] = o[rows:]
    first[...] = (o[:rows].astype(F32) + away[...].astype(F32)).astype(BF16)
    copy = pltpu.make_async_copy(first, out.at[pl.ds(0, rows)], sem)
    copy.start()
    copy.wait()


def home_project(info, x1, x2, away, w):
    rows, depth = x1.shape
    cols = w.shape[1] // TENSORS
    return pl.pallas_call(
        home_kernel,
        out_shape=[
            jax.ShapeDtypeStruct((2 * rows, cols), BF16),
            jax.ShapeDtypeStruct((rows, cols), BF16),
        ],
        in_specs=[SMEM] + [VMEM] * 4,
        out_specs=[STAYS, VMEM],
        scratch_shapes=[pltpu.VMEM((rows, cols), BF16), pltpu.SemaphoreType.DMA],
        compiler_params=params(16),
        cost_estimate=cost(20 * 10**9, 2 * depth * cols),
    )(info, x1, x2, away, w)


def add_kernel(before, a, b, out, last, sem):
    rows = a.shape[0]
    last[...] = (a[...].astype(F32) + b[...].astype(F32)).astype(BF16)
    copy = pltpu.make_async_copy(last, out.at[pl.ds(rows, rows)], sem)
    copy.start()
    copy.wait()


def added(before, a, b):
    return pl.pallas_call(
        add_kernel,
        out_shape=jax.ShapeDtypeStruct(before.shape, BF16),
        in_specs=[STAYS, VMEM, VMEM],
        out_specs=STAYS,
        scratch_shapes=[pltpu.VMEM(a.shape, BF16), pltpu.SemaphoreType.DMA],
        input_output_aliases={0: 0},
        compiler_params=params(8),
    )(before, a, b)


def flipped(value, axes, count, bits):
    return lax.ppermute(value, axes, [(i, i ^ bits) for i in range(count)])


def after(value, *others):
    return lax.optimization_barrier((value, *others))[0]


def shards_fast(
    span_tokens, q_weight, kv_weight, out_weight, kv_pool, cache_lengths, slot_requests, page_table
):
    group_id = lax.axis_index("group")
    seq_id = lax.axis_index("seq")
    tensor_id = lax.axis_index("tensor")
    place = jnp.stack([group_id, seq_id, tensor_id]).astype(jnp.int32)
    row = jnp.concatenate([place, slot_requests, cache_lengths])
    row = jnp.pad(row, (0, page_table.shape[1] - row.shape[0]))
    info = jnp.concatenate([row[None], page_table])
    mine = span_tokens[0]
    theirs = flipped(mine, "tensor", 2, 1)
    half_dim = HD // 2
    lane = jnp.arange(128, dtype=jnp.int32) % half_dim
    frequency = jnp.power(jnp.float32(10000.0), -lane.astype(F32) / half_dim)
    frequency = jnp.broadcast_to(frequency[None, :], (8, 128))
    pages = open_rows(info, frequency, kv_pool, mine, q_weight, kv_weight)
    home, same, beyond, beside, across, diagonal = pages[:6]
    acc_q, acc_kv, cosine, sine = pages[6:]
    capacity = home.shape[0]
    same = flipped(same, "tensor", 2, 1)
    beyond = flipped(beyond, "group", 4, 2)
    kept, sent = fresh_rows(info, theirs, kv_weight, acc_kv, cosine, sine)
    got = flipped(sent, "tensor", 2, 1)
    across, diagonal, _ = lax.optimization_barrier((across, diagonal, sent))
    across = flipped(across, ("group", "tensor"), 8, 5)
    diagonal = flipped(diagonal, ("group", "tensor"), 8, 7)
    same, beyond, _ = lax.optimization_barrier((same, beyond, sent))
    mate = jnp.concatenate([beside, beyond[capacity:], same[capacity:]])
    mate = flipped(mate, "group", 4, 1)
    fresh = bundled(kept[None], got[None])
    zs = [flipped(fresh, "seq", 4, d) for d in (3, 2, 1)]
    q = query_rows(after(info, fresh), theirs, q_weight, acc_q, cosine, sine)
    across, diagonal, _ = lax.optimization_barrier((across, diagonal, q))
    other_chip = bundled(across, diagonal)
    own = jnp.concatenate(
        [home, mate[:capacity], beyond[:capacity], mate[capacity : 2 * capacity]]
    )
    other = jnp.concatenate([same[:capacity], mate[2 * capacity :], other_chip])
    state, keys, values = attend_near(info, q, own, other, fresh)
    heads_0, partial_0, far_keys, far_values = attend_far(info, q, state, zs, out_weight)
    away_0 = flipped(partial_0, "tensor", 2, 1)
    heads_1, partial_1 = attend_last(info, q, keys, values, far_keys, far_values, out_weight)
    away_1 = flipped(partial_1, "tensor", 2, 1)
    out, home_1 = home_project(info, heads_0, heads_1, away_0, out_weight)
    return added(out, home_1, away_1)[None]


def solution(mesh):
    sizes = tuple(mesh.shape[a] for a in ("group", "seq", "tensor"))
    body = shards_fast if sizes == (GROUPS, SEQS, TENSORS) else shards
    placed = (
        P("group", "seq", "tensor"),
        P(None, "tensor"),
        P(None, "tensor"),
        P("tensor", None),
        P("group", None, "tensor"),
        P(),
        P(),
        P(),
    )
    return jax.shard_map(
        body, mesh=mesh, in_specs=placed, out_specs=P("group", "seq", "tensor"), check_vma=False
    )
```

```python
import functools

import jax
import jax.numpy as jnp
from jax import lax
from jax.experimental import pallas as pl
from jax.experimental.pallas import tpu as pltpu
from jax.sharding import PartitionSpec as P

HD = 64
KVH = 4
WINDOW = 2048
PAGE = 128


def shifted(block, axis, distance):
    devices = range(lax.axis_size(axis))
    route = [(i - distance, i) for i in devices if i - distance in devices]
    return lax.ppermute(block, axis, route)


def swapped(value, axis, stride):
    return lax.ppermute(value, axis, [(i, i ^ 1 << stride) for i in range(lax.axis_size(axis))])


def rotate(values, positions):
    half_dim = HD // 2
    frequency = jnp.power(jnp.float32(10000.0), -jnp.arange(half_dim, dtype=jnp.float32) / half_dim)
    angles = positions.astype(jnp.float32)[:, None] * frequency[None, :]
    cosine = jnp.cos(angles)[:, None, :]
    sine_part = jnp.sin(angles)[:, None, :]
    front_half = values[..., :half_dim]
    back_half = values[..., half_dim:]
    return jnp.concatenate(
        [front_half * cosine - back_half * sine_part, back_half * cosine + front_half * sine_part],
        axis=-1,
    )


def attend(block_q, block_k, block_v, base_pos):
    query_count = block_q.shape[0]
    key_count = block_k.shape[0]
    scores = jnp.einsum(
        "tkgd,nkd->kgtn", block_q, block_k, preferred_element_type=jnp.float32
    ) * HD ** (-0.5)
    query_at = jnp.arange(query_count, dtype=jnp.int32)[:, None]
    key_at = jnp.arange(key_count, dtype=jnp.int32)[None, :]
    allowed = (key_at > query_at) & (key_at <= query_at + WINDOW) & (base_pos + key_at >= 0)
    masked = jnp.where(allowed, scores, jnp.float32(-1e30))
    row_top = jnp.max(masked, axis=-1, keepdims=True)
    weights = jnp.where(allowed, jnp.exp(masked - row_top), jnp.float32(0.0))
    row_total = jnp.sum(weights, axis=-1)
    rounded = weights.astype(jnp.bfloat16)
    mixed_rows = jnp.einsum("kgtn,nkd->tkgd", rounded, block_v, preferred_element_type=jnp.float32)
    mixed_rows = mixed_rows / jnp.transpose(row_total, (2, 0, 1))[..., None]
    return mixed_rows.astype(jnp.bfloat16).reshape(query_count, -1)


def shards(
    span_tokens, q_weight, kv_weight, out_weight, kv_pool, cache_lengths, slot_requests, page_table
):
    groups = lax.axis_size("group")
    seq_count = lax.axis_size("seq")
    tensor_count = lax.axis_size("tensor")
    group_id = lax.axis_index("group")
    seq_id = lax.axis_index("seq")
    tensor_id = lax.axis_index("tensor")
    local_reqs, seg_len, feat_local = span_tokens.shape
    head_cols = q_weight.shape[1]
    kv_cols = kv_weight.shape[1]
    local_heads = head_cols // HD
    group_heads = kv_cols // HD
    kv_local = max(1, KVH // tensor_count)
    per_kv = local_heads // kv_local
    head_first = tensor_id * KVH // tensor_count % group_heads
    holds_keys = tensor_id % 2 == 0
    pool_rows = kv_pool.shape[0]
    capacity = pool_rows // groups
    row_count = local_reqs * seg_len
    my_slots = group_id * local_reqs + jnp.arange(local_reqs, dtype=jnp.int32)
    my_requests = slot_requests[my_slots]
    my_lengths = cache_lengths[my_requests]
    project_piece_rows = lax.all_gather(span_tokens, "tensor", axis=2, tiled=True)
    feat_width = project_piece_rows.shape[2]
    flat_rows = project_piece_rows.reshape(row_count, feat_width)
    query_lin = jnp.dot(flat_rows, q_weight, preferred_element_type=jnp.float32)
    fresh_lin = jnp.dot(flat_rows, kv_weight, preferred_element_type=jnp.float32)
    positions = (
        my_lengths[:, None] + seq_id * seg_len + jnp.arange(seg_len, dtype=jnp.int32)[None, :]
    )
    queries = jax.vmap(rotate)(query_lin.reshape(local_reqs, seg_len, local_heads, HD), positions)
    queries = queries.astype(jnp.bfloat16).reshape(local_reqs, seg_len, kv_local, per_kv, HD)
    fresh_heads = fresh_lin.reshape(local_reqs, seg_len, group_heads, HD)
    rotated = jax.vmap(rotate)(fresh_heads, positions)
    span_kv = (
        jnp.where(holds_keys, rotated, fresh_heads)
        .astype(jnp.bfloat16)
        .reshape(local_reqs, seg_len, kv_cols)
    )
    all_ids = page_table[slot_requests]
    owned_here = all_ids // pool_rows == group_id
    slot_rank = jnp.cumsum(owned_here.astype(jnp.int32), axis=1) - 1
    local_rows = all_ids - group_id * pool_rows
    chosen = owned_here[:, :, None] & (
        slot_rank[:, :, None] == jnp.arange(capacity, dtype=jnp.int32)[None, None, :]
    )
    wanted = jnp.sum(jnp.where(chosen, local_rows[:, :, None], 0), axis=1)
    my_ids = page_table[my_requests].reshape(-1)
    my_owner = my_ids // pool_rows
    onehot = (my_owner[:, None] == jnp.arange(groups, dtype=jnp.int32)[None, :]).astype(jnp.int32)
    arrival = jnp.sum((jnp.cumsum(onehot, axis=0) - 1) * onehot, axis=1)
    arrived_row = my_owner * capacity + arrival
    outgoing = kv_pool[wanted]
    arrived = lax.all_to_all(outgoing, "group", split_axis=0, concat_axis=0, tiled=True)
    cached = arrived.reshape(groups * capacity, PAGE, kv_cols)[arrived_row]
    cached = cached.reshape(local_reqs, WINDOW, kv_cols)
    span_all = jnp.zeros((local_reqs, seg_len * seq_count, kv_cols), jnp.bfloat16)
    for back_step in range(seq_count - 1, -1, -1):
        piece_rows = span_kv if back_step == 0 else shifted(span_kv, "seq", back_step)
        span_all = lax.dynamic_update_slice_in_dim(
            span_all, piece_rows, (seq_id - back_step) * seg_len, 1
        )
    joined = jnp.concatenate([cached, span_all], axis=1)
    visible = lax.dynamic_slice_in_dim(joined, seq_id * seg_len, WINDOW + seg_len, 1)
    partner_rows = swapped(visible, "tensor", 0)
    key_all = jnp.where(holds_keys, visible, partner_rows).reshape(
        local_reqs, WINDOW + seg_len, group_heads, HD
    )
    value_all = jnp.where(holds_keys, partner_rows, visible).reshape(
        local_reqs, WINDOW + seg_len, group_heads, HD
    )
    key_rows = lax.dynamic_slice_in_dim(key_all, head_first, kv_local, 2)
    value_rows = lax.dynamic_slice_in_dim(value_all, head_first, kv_local, 2)
    block_len = min(128, seg_len)
    block_count = seg_len // block_len

    def per_request(request_items):
        request_q, request_k, request_v, length = request_items

        def per_block(block_index):
            first_row = block_index * block_len
            block_q = lax.dynamic_slice_in_dim(request_q, first_row, block_len, 0)
            block_k = lax.dynamic_slice_in_dim(request_k, first_row, WINDOW + block_len, 0)
            block_v = lax.dynamic_slice_in_dim(request_v, first_row, WINDOW + block_len, 0)
            return attend(block_q, block_k, block_v, length - WINDOW + seq_id * seg_len + first_row)

        return lax.map(per_block, jnp.arange(block_count, dtype=jnp.int32)).reshape(
            seg_len, head_cols
        )

    attended_heads = lax.map(per_request, (queries, key_rows, value_rows, my_lengths))
    flat_heads = attended_heads.reshape(row_count, head_cols)
    out_cols = out_weight.shape[1] // tensor_count
    summed = lax.psum_scatter(
        lax.dot_general(
            out_weight, flat_heads, (((0,), (1,)), ((), ())), preferred_element_type=jnp.float32
        ).astype(jnp.bfloat16),
        "tensor",
        scatter_dimension=0,
        tiled=True,
    ).astype(jnp.float32)
    result = summed.T
    return result.astype(jnp.bfloat16).reshape(local_reqs, seg_len, out_cols)


LOG2E = 1.4426950408889634
MASKED = -1e30
F32 = jnp.float32
BF16 = jnp.bfloat16
HBM = pl.BlockSpec(memory_space=pl.ANY)
VMEM = pl.BlockSpec(memory_space=pltpu.VMEM)
SMEM = pl.BlockSpec(memory_space=pltpu.SMEM)
STAYS = pl.BlockSpec(memory_space=pltpu.HBM)
GROUPS, SEQS, TENSORS = 4, 4, 2


def params(mebibytes):
    return pltpu.CompilerParams(vmem_limit_bytes=mebibytes * 2**20)


def cost(flops, moved):
    return pl.CostEstimate(flops=flops, bytes_accessed=moved, transcendentals=0)


class Info:
    def __init__(self, ref):
        self.ref = ref
        self.group, self.seq, self.tensor = ref[0, 0], ref[0, 1], ref[0, 2]
        self.window_pages = ref.shape[1]

    def request(self, slot):
        return self.ref[0, 3 + slot]

    def length(self, request):
        return self.ref[0, 3 + GROUPS + request]

    def page(self, request, w):
        return self.ref[1 + request, w]


def turned(x, cosine, sine):
    lane = lax.broadcasted_iota(jnp.int32, x.shape, 1)
    other = jnp.where(lane % HD < HD // 2, pltpu.roll(x, 128 - HD // 2, 1), pltpu.roll(x, HD // 2, 1))
    return x * cosine + other * sine


def open_kernel(
    info_ref, frequency, pool, x_hbm, wq_hbm, wkv_hbm,
    home, same, beyond, beside, across, diagonal, acc_q, acc_kv, cosine, sine,
    x, wq, wkv, sems, page_sems,
):
    info = Info(info_ref)
    rows, feats = x.shape
    here = pl.ds(pl.multiple_of(info.tensor * feats, feats), feats)
    copies = [
        pltpu.make_async_copy(x_hbm, x, sems.at[0]),
        pltpu.make_async_copy(wkv_hbm.at[here], wkv, sems.at[1]),
        pltpu.make_async_copy(wq_hbm.at[here], wq, sems.at[2]),
    ]
    for copy in copies:
        copy.start()
    pages = pool.shape[0]
    capacity = pages // GROUPS
    half = pool.shape[2] // 2
    mine = pl.ds(pl.multiple_of(info.tensor * half, half), half)
    theirs = pl.ds(pl.multiple_of((1 - info.tensor) * half, half), half)
    outs = (home, same, beyond, beside, across, diagonal)
    spots = (
        ((0, 0), (1, 0)),
        ((3, 0), (1, capacity)),
        ((2, 0), (4, 0)),
        ((2, capacity), (5, 0)),
    )
    for flip, targets in enumerate(spots):
        request = info.request(info.group ^ flip)

        def take(w, rank):
            page = info.page(request, w)
            near = page // pages == info.group

            @pl.when(near)
            def _():
                row = page % pages
                for (out, base), cols in zip(targets, (mine, theirs)):
                    pltpu.make_async_copy(
                        pool.at[row, :, cols], outs[out].at[base + rank], page_sems.at[out]
                    ).start()

            return rank + near.astype(jnp.int32)

        lax.fori_loop(0, info.window_pages, take, jnp.int32(0))
    start = info.length(info.request(info.group)) + info.seq * rows
    position = (start + lax.broadcasted_iota(jnp.int32, (rows, 128), 0)).astype(F32)
    angles = position * frequency[0:1, :]
    lane = lax.broadcasted_iota(jnp.int32, (rows, 128), 1)
    cosine[...] = jnp.cos(angles)
    sine[...] = jnp.where(lane % HD < HD // 2, -1.0, 1.0) * jnp.sin(angles)
    copies[0].wait()
    copies[1].wait()
    acc_kv[...] = jnp.dot(x[...], wkv[...], preferred_element_type=F32)
    copies[2].wait()
    acc_q[...] = jnp.dot(x[...], wq[...], preferred_element_type=F32)
    for i, out in enumerate(outs):
        pltpu.make_async_copy(out, out, page_sems.at[i]).wait()


def open_rows(info, frequency, pool, x, wq, wkv):
    rows, feats = x.shape
    pages, page, cols = pool.shape
    single = jax.ShapeDtypeStruct((pages // GROUPS, page, cols // 2), BF16)
    double = jax.ShapeDtypeStruct((2 * pages // GROUPS, page, cols // 2), BF16)
    table = jax.ShapeDtypeStruct((rows, 128), F32)
    return pl.pallas_call(
        open_kernel,
        out_shape=[
            single,
            double,
            double,
            single,
            single,
            single,
            jax.ShapeDtypeStruct((rows, wq.shape[1]), F32),
            jax.ShapeDtypeStruct((rows, wkv.shape[1]), F32),
            table,
            table,
        ],
        in_specs=[SMEM, VMEM] + [STAYS] * 4,
        out_specs=[VMEM] * 10,
        scratch_shapes=[
            pltpu.VMEM((rows, feats), BF16),
            pltpu.VMEM((feats, wq.shape[1]), BF16),
            pltpu.VMEM((feats, wkv.shape[1]), BF16),
            pltpu.SemaphoreType.DMA((3,)),
            pltpu.SemaphoreType.DMA((6,)),
        ],
        compiler_params=params(50),
        cost_estimate=cost(rows * feats, rows * feats),
    )(info, frequency, pool, x, wq, wkv)


def fresh_kernel(info_ref, x, wkv, acc_kv, cosine, sine, kept, sent):
    info = Info(info_ref)
    feats = x.shape[1]
    here = pl.ds(pl.multiple_of((1 - info.tensor) * feats, feats), feats)
    keys = info.tensor == 0
    fresh = acc_kv[...] + jnp.dot(x[...], wkv[here], preferred_element_type=F32)
    cos_kv = jnp.where(keys, cosine[...], 1.0)
    sin_kv = jnp.where(keys, sine[...], 0.0)
    low = turned(fresh[:, :128], cos_kv, sin_kv).astype(BF16)
    high = turned(fresh[:, 128:], cos_kv, sin_kv).astype(BF16)
    kept[...] = jnp.where(keys, low, high)
    sent[...] = jnp.where(keys, high, low)


def fresh_rows(info, x, wkv, acc_kv, cosine, sine):
    rows, feats = x.shape
    piece = jax.ShapeDtypeStruct((rows, wkv.shape[1] // 2), BF16)
    return pl.pallas_call(
        fresh_kernel,
        out_shape=[piece, piece],
        in_specs=[SMEM] + [VMEM] * 5,
        out_specs=[VMEM] * 2,
        compiler_params=params(12),
        cost_estimate=cost(2 * rows * feats * 2560, rows * feats),
    )(info, x, wkv, acc_kv, cosine, sine)


def query_kernel(info_ref, x, wq, acc_q, cosine, sine, q):
    feats = x.shape[1]
    here = pl.ds(pl.multiple_of((1 - Info(info_ref).tensor) * feats, feats), feats)
    cos_all, sin_all = cosine[...], sine[...]
    scale = HD**-0.5 * LOG2E
    tile = 256
    for c in range(0, q.shape[1], tile):
        lin = acc_q[:, c : c + tile] + jnp.dot(
            x[...], wq[here, c : c + tile], preferred_element_type=F32
        )
        for e in range(0, tile, 128):
            q[:, c + e : c + e + 128] = (
                turned(lin[:, e : e + 128], cos_all, sin_all) * scale
            ).astype(BF16)


def query_rows(info, x, wq, acc_q, cosine, sine):
    rows, feats = x.shape
    return pl.pallas_call(
        query_kernel,
        out_shape=jax.ShapeDtypeStruct((rows, wq.shape[1]), BF16),
        in_specs=[SMEM] + [VMEM] * 5,
        out_specs=VMEM,
        compiler_params=params(16),
        cost_estimate=cost(rows * feats, rows * feats),
    )(info, x, wq, acc_q, cosine, sine)


def soft_heads(q, tokens, segments, emit):
    rows = tokens.stop - tokens.start
    stack = 4
    low = lax.broadcasted_iota(jnp.int32, (rows, 2 * HD), 1) < HD

    def swap(x):
        return pltpu.roll(x, HD, 1)

    def heads(i, _):
        first = i == 0
        spots = [pl.ds(pl.multiple_of((i * stack + j) * 128, 128), 128) for j in range(stack)]
        tiles = [q[tokens, spot] for spot in spots]
        turns = [swap(x.astype(F32)).astype(BF16) for x in tiles]
        keep = low == first

        def stacked(a, b):
            zero = jnp.zeros_like(a[0])
            return jnp.concatenate(
                [jnp.where(keep, jnp.where(first, x, y), zero) for x, y in zip(a, b)], axis=0
            )

        def scores(qs):
            return [
                mask(
                    lax.dot_general(
                        qs, keys[span], (((1,), (1,)), ((), ())), preferred_element_type=F32
                    )
                )
                for keys, _, span, mask in segments
            ]

        def peak(parts):
            tops = [jnp.max(s, axis=1, keepdims=True) for s in parts]
            return functools.reduce(jnp.maximum, tops)

        def mixed(weights):
            return sum(
                jnp.dot(p, values[i, span], preferred_element_type=F32)
                for p, (_, values, span, _) in zip(weights, segments)
            )

        s_even = scores(stacked(tiles, turns))
        s_odd = scores(stacked(turns, tiles))
        m_even = peak(s_even)
        m_odd = peak(s_odd)
        p_even = [jnp.exp2(s - m_even).astype(BF16) for s in s_even]
        p_odd = [jnp.exp2(s - m_odd).astype(BF16) for s in s_odd]
        o_even = mixed(p_even)
        o_odd = mixed(p_odd)
        for j in range(stack):
            part = slice(j * rows, (j + 1) * rows)
            a, b = o_even[part], o_odd[part]
            total = jnp.where(low, a, swap(b))
            weight = jnp.where(low, swap(a), b)
            top = jnp.where(low, m_even[part], m_odd[part])
            emit(spots[j], total, weight, top)
        return 0

    lax.fori_loop(0, q.shape[1] // 128 // stack, heads, 0)


def widen(v, ones, values, here):
    low = lax.broadcasted_iota(jnp.int32, v.shape, 1) < HD
    values[0, here] = jnp.where(low, v, ones).astype(BF16)
    values[1, here] = jnp.where(low, pltpu.roll(v, HD, 1), ones).astype(BF16)


def gather_rows(info, own, other, fresh, keys, values, source):
    group, seq = info.group, info.seq
    request = info.request(group)
    rows = fresh.shape[1]
    per = rows // PAGE
    count = own.shape[0]
    capacity = count // GROUPS
    seen = keys.shape[0] // PAGE - seq * per
    is_key = info.tensor == 0

    def note(w, counts):
        came = info.page(request, w) // count ^ group
        place = came * capacity
        for d in range(GROUPS):
            place = place + jnp.where(came == d, counts[d], 0)
        source[w] = place
        return tuple(counts[d] + (came == d).astype(jnp.int32) for d in range(GROUPS))

    lax.fori_loop(0, info.window_pages, note, (jnp.int32(0),) * GROUPS, unroll=True)

    def place(block, a, b):
        here = pl.ds(pl.multiple_of(block * PAGE, PAGE), PAGE)
        keys[here] = jnp.where(is_key, a, b)
        widen(jnp.where(is_key, b, a).astype(F32), 1.0, values, here)

    for block, part in ((1, slice(0, PAGE)), (seen - 1, slice(PAGE, 2 * PAGE))):
        place(block, fresh[0, part], fresh[1, part])
    first = info.length(request) - WINDOW + seq * rows
    stand_in = jnp.where(is_key, fresh[0, :16], fresh[1, :16]).astype(F32)[0:1]
    stand_in = jnp.broadcast_to(stand_in, (PAGE, 2 * HD)).astype(BF16)

    def bring(i, _):
        for n in (2 * i, 2 * i + 1):
            block = jnp.where(n == 0, 0, n + 1)
            here = pl.ds(pl.multiple_of(block * PAGE, PAGE), PAGE)
            at = source[seq * per + n]
            hidden = first + n * PAGE < 0
            a, b = own[at], other[at]
            keys[here] = jnp.where(hidden, stand_in, jnp.where(is_key, a, b))
            v = jnp.where(is_key, b, a).astype(F32)
            widen(jnp.where(hidden, 0.0, v), jnp.where(hidden, 0.0, 1.0), values, here)
        return 0

    lax.fori_loop(0, (seen - per) // 2, bring, 0)


def bundle_kernel(a, b, out):
    out[: a.shape[0]] = a[...]
    out[a.shape[0] :] = b[...]


def bundled(a, b):
    return pl.pallas_call(
        bundle_kernel,
        out_shape=jax.ShapeDtypeStruct((a.shape[0] + b.shape[0], *a.shape[1:]), BF16),
        in_specs=[VMEM] * 2,
        out_specs=VMEM,
        compiler_params=params(8),
        cost_estimate=cost(6 * 10**9, 4),
    )(a, b)


def near_segment(keys, values, seq, half):
    blocks = keys.shape[0] // PAGE
    per = 2
    span = slice(half * PAGE, (blocks - seq * per - 1 + half) * PAGE)

    def mask(s):
        newer = lax.broadcasted_iota(jnp.int32, (s.shape[0], PAGE), 1) > (
            lax.broadcasted_iota(jnp.int32, (s.shape[0], PAGE), 0) % PAGE
        )
        if half == 0:
            parts = [
                jnp.where(newer, s[:, :PAGE], MASKED),
                jnp.where(newer, MASKED, s[:, PAGE : 2 * PAGE]),
                s[:, 2 * PAGE :],
            ]
        else:
            parts = [
                s[:, :PAGE],
                jnp.where(newer, s[:, PAGE : 2 * PAGE], MASKED),
                s[:, 2 * PAGE : -PAGE],
                jnp.where(newer, MASKED, s[:, -PAGE:]),
            ]
        return jnp.concatenate(parts, axis=1)

    return keys, values, span, mask


def far_segment(keys, values, seq):
    return keys, values, slice(0, seq * 2 * PAGE), lambda s: s


def near_kernel(
    info_ref, q, own, other, fresh, total, weight, top, keys, values, source
):
    info = Info(info_ref)
    seq = info.seq
    gather_rows(info, own, other, fresh, keys, values, source)

    def emit(spot, o, l, m):
        total[:, spot] = o
        weight[:, spot] = l
        top[:, spot] = m

    for k in range(SEQS):

        @pl.when(seq == k)
        def _(k=k):
            soft_heads(q, slice(0, PAGE), [near_segment(keys, values, k, 0)], emit)


def attend_near(info, q, own, other, fresh):
    state = jax.ShapeDtypeStruct((PAGE, q.shape[1]), F32)
    span = WINDOW + fresh.shape[1]
    *state, keys, values = pl.pallas_call(
        near_kernel,
        out_shape=[
            state,
            state,
            state,
            jax.ShapeDtypeStruct((span, 2 * HD), BF16),
            jax.ShapeDtypeStruct((2, span, 2 * HD), BF16),
        ],
        in_specs=[SMEM] + [VMEM] * 4,
        out_specs=[VMEM] * 5,
        scratch_shapes=[pltpu.SMEM((own.shape[0],), jnp.int32)],
        compiler_params=params(32),
        cost_estimate=cost(20 * 10**9, 4 * span),
    )(info, q, own, other, fresh)
    return state, keys, values


def partner_product(info, heads_out, w, partial):
    cols = partial.shape[1]
    here = pl.ds(pl.multiple_of((1 - info.tensor) * cols, cols), cols)
    partial[...] = jnp.dot(heads_out[...], w[:, here], preferred_element_type=F32).astype(BF16)


def far_kernel(
    info_ref, q, total, weight, top, z3, z1, z2, w, heads_out, partial, keys, values
):
    info = Info(info_ref)
    rows = q.shape[0]
    seq = info.seq
    zs = (None, z1, z2, z3)
    is_key = info.tensor == 0

    for k in range(SEQS):

        @pl.when(seq == k)
        def _(k=k):
            if k == 0:
                heads_out[...] = (total[...] / weight[...]).astype(BF16)
                return
            for n in range(k):
                z = zs[n ^ k]
                here = slice(n * rows, (n + 1) * rows)
                a, b = z[0], z[1]
                keys[here] = jnp.where(is_key, a, b)
                widen(jnp.where(is_key, b, a).astype(F32), 1.0, values, here)

            def emit(spot, o, l, m):
                before = top[:, spot]
                peak = jnp.maximum(before, m)
                a = jnp.exp2(before - peak)
                b = jnp.exp2(m - peak)
                done = (total[:, spot] * a + o * b) / (weight[:, spot] * a + l * b)
                heads_out[:, spot] = done.astype(BF16)

            soft_heads(q, slice(0, PAGE), [far_segment(keys, values, k)], emit)

    partner_product(info, heads_out, w, partial)


def attend_far(info, q, state, zs, w):
    rows = q.shape[0]
    span = (SEQS - 1) * rows
    return pl.pallas_call(
        far_kernel,
        out_shape=[
            jax.ShapeDtypeStruct((PAGE, q.shape[1]), BF16),
            jax.ShapeDtypeStruct((PAGE, w.shape[1] // TENSORS), BF16),
            jax.ShapeDtypeStruct((span, 2 * HD), BF16),
            jax.ShapeDtypeStruct((2, span, 2 * HD), BF16),
        ],
        in_specs=[SMEM] + [VMEM] * 8,
        out_specs=[VMEM] * 4,
        compiler_params=params(24),
        cost_estimate=cost(rows * span, 4 * span),
    )(info, q, *state, *zs, w)


def last_kernel(info_ref, q, keys, values, far_keys, far_values, w, heads_out, partial):
    info = Info(info_ref)

    def emit(spot, o, l, m):
        heads_out[:, spot] = (o / l).astype(BF16)

    for k in range(SEQS):

        @pl.when(info.seq == k)
        def _(k=k):
            segments = [near_segment(keys, values, k, 1)]
            if k:
                segments.append(far_segment(far_keys, far_values, k))
            soft_heads(q, slice(PAGE, 2 * PAGE), segments, emit)

    partner_product(info, heads_out, w, partial)


def attend_last(info, q, keys, values, far_keys, far_values, w):
    return pl.pallas_call(
        last_kernel,
        out_shape=[
            jax.ShapeDtypeStruct((PAGE, q.shape[1]), BF16),
            jax.ShapeDtypeStruct((PAGE, w.shape[1] // TENSORS), BF16),
        ],
        in_specs=[SMEM] + [VMEM] * 6,
        out_specs=[VMEM] * 2,
        compiler_params=params(36),
        cost_estimate=cost(PAGE * WINDOW, 4 * WINDOW),
    )(info, q, keys, values, far_keys, far_values, w)


def home_kernel(info_ref, x1, x2, away, w, out, home, first, sem):
    rows, cols = home.shape
    here = pl.ds(pl.multiple_of(Info(info_ref).tensor * cols, cols), cols)
    x = jnp.concatenate([x1[...], x2[...]], axis=0)
    o = jnp.dot(x, w[:, here], preferred_element_type=F32).astype(BF16)
    home[...] = o[rows:]
    first[...] = (o[:rows].astype(F32) + away[...].astype(F32)).astype(BF16)
    copy = pltpu.make_async_copy(first, out.at[pl.ds(0, rows)], sem)
    copy.start()
    copy.wait()


def home_project(info, x1, x2, away, w):
    rows, depth = x1.shape
    cols = w.shape[1] // TENSORS
    return pl.pallas_call(
        home_kernel,
        out_shape=[
            jax.ShapeDtypeStruct((2 * rows, cols), BF16),
            jax.ShapeDtypeStruct((rows, cols), BF16),
        ],
        in_specs=[SMEM] + [VMEM] * 4,
        out_specs=[STAYS, VMEM],
        scratch_shapes=[pltpu.VMEM((rows, cols), BF16), pltpu.SemaphoreType.DMA],
        compiler_params=params(16),
        cost_estimate=cost(20 * 10**9, 2 * depth * cols),
    )(info, x1, x2, away, w)


def add_kernel(before, a, b, out, last, sem):
    rows = a.shape[0]
    last[...] = (a[...].astype(F32) + b[...].astype(F32)).astype(BF16)
    copy = pltpu.make_async_copy(last, out.at[pl.ds(rows, rows)], sem)
    copy.start()
    copy.wait()


def added(before, a, b):
    return pl.pallas_call(
        add_kernel,
        out_shape=jax.ShapeDtypeStruct(before.shape, BF16),
        in_specs=[STAYS, VMEM, VMEM],
        out_specs=STAYS,
        scratch_shapes=[pltpu.VMEM(a.shape, BF16), pltpu.SemaphoreType.DMA],
        input_output_aliases={0: 0},
        compiler_params=params(8),
    )(before, a, b)


def flipped(value, axes, count, bits):
    return lax.ppermute(value, axes, [(i, i ^ bits) for i in range(count)])


def after(value, *others):
    return lax.optimization_barrier((value, *others))[0]


def shards_fast(
    span_tokens, q_weight, kv_weight, out_weight, kv_pool, cache_lengths, slot_requests, page_table
):
    group_id = lax.axis_index("group")
    seq_id = lax.axis_index("seq")
    tensor_id = lax.axis_index("tensor")
    place = jnp.stack([group_id, seq_id, tensor_id]).astype(jnp.int32)
    row = jnp.concatenate([place, slot_requests, cache_lengths])
    row = jnp.pad(row, (0, page_table.shape[1] - row.shape[0]))
    info = jnp.concatenate([row[None], page_table])
    mine = span_tokens[0]
    theirs = flipped(mine, "tensor", 2, 1)
    half_dim = HD // 2
    lane = jnp.arange(128, dtype=jnp.int32) % half_dim
    frequency = jnp.power(jnp.float32(10000.0), -lane.astype(F32) / half_dim)
    frequency = jnp.broadcast_to(frequency[None, :], (8, 128))
    pages = open_rows(info, frequency, kv_pool, mine, q_weight, kv_weight)
    home, same, beyond, beside, across, diagonal = pages[:6]
    acc_q, acc_kv, cosine, sine = pages[6:]
    capacity = home.shape[0]
    same = flipped(same, "tensor", 2, 1)
    beyond = flipped(beyond, "group", 4, 2)
    kept, sent = fresh_rows(info, theirs, kv_weight, acc_kv, cosine, sine)
    got = flipped(sent, "tensor", 2, 1)
    across, diagonal, _ = lax.optimization_barrier((across, diagonal, sent))
    across = flipped(across, ("group", "tensor"), 8, 5)
    diagonal = flipped(diagonal, ("group", "tensor"), 8, 7)
    same, beyond, _ = lax.optimization_barrier((same, beyond, sent))
    mate = jnp.concatenate([beside, beyond[capacity:], same[capacity:]])
    mate = flipped(mate, "group", 4, 1)
    fresh = bundled(kept[None], got[None])
    zs = [flipped(fresh, "seq", 4, d) for d in (3, 1, 2)]
    q = query_rows(after(info, fresh), theirs, q_weight, acc_q, cosine, sine)
    across, diagonal, _ = lax.optimization_barrier((across, diagonal, q))
    other_chip = bundled(across, diagonal)
    own = jnp.concatenate(
        [home, mate[:capacity], beyond[:capacity], mate[capacity : 2 * capacity]]
    )
    other = jnp.concatenate([same[:capacity], mate[2 * capacity :], other_chip])
    state, keys, values = attend_near(info, q, own, other, fresh)
    heads_0, partial_0, far_keys, far_values = attend_far(info, q, state, zs, out_weight)
    away_0 = flipped(partial_0, "tensor", 2, 1)
    heads_1, partial_1 = attend_last(info, q, keys, values, far_keys, far_values, out_weight)
    away_1 = flipped(partial_1, "tensor", 2, 1)
    out, home_1 = home_project(info, heads_0, heads_1, away_0, out_weight)
    return added(out, home_1, away_1)[None]


def solution(mesh):
    sizes = tuple(mesh.shape[a] for a in ("group", "seq", "tensor"))
    body = shards_fast if sizes == (GROUPS, SEQS, TENSORS) else shards
    placed = (
        P("group", "seq", "tensor"),
        P(None, "tensor"),
        P(None, "tensor"),
        P("tensor", None),
        P("group", None, "tensor"),
        P(),
        P(),
        P(),
    )
    return jax.shard_map(
        body, mesh=mesh, in_specs=placed, out_specs=P("group", "seq", "tensor"), check_vma=False
    )
```

```python
import functools

import jax
import jax.numpy as jnp
from jax import lax
from jax.experimental import pallas as pl
from jax.experimental.pallas import tpu as pltpu
from jax.sharding import PartitionSpec as P

HD = 64
KVH = 4
WINDOW = 2048
PAGE = 128


def shifted(block, axis, distance):
    devices = range(lax.axis_size(axis))
    route = [(i - distance, i) for i in devices if i - distance in devices]
    return lax.ppermute(block, axis, route)


def swapped(value, axis, stride):
    return lax.ppermute(value, axis, [(i, i ^ 1 << stride) for i in range(lax.axis_size(axis))])


def rotate(values, positions):
    half_dim = HD // 2
    frequency = jnp.power(jnp.float32(10000.0), -jnp.arange(half_dim, dtype=jnp.float32) / half_dim)
    angles = positions.astype(jnp.float32)[:, None] * frequency[None, :]
    cosine = jnp.cos(angles)[:, None, :]
    sine_part = jnp.sin(angles)[:, None, :]
    front_half = values[..., :half_dim]
    back_half = values[..., half_dim:]
    return jnp.concatenate(
        [front_half * cosine - back_half * sine_part, back_half * cosine + front_half * sine_part],
        axis=-1,
    )


def attend(block_q, block_k, block_v, base_pos):
    query_count = block_q.shape[0]
    key_count = block_k.shape[0]
    scores = jnp.einsum(
        "tkgd,nkd->kgtn", block_q, block_k, preferred_element_type=jnp.float32
    ) * HD ** (-0.5)
    query_at = jnp.arange(query_count, dtype=jnp.int32)[:, None]
    key_at = jnp.arange(key_count, dtype=jnp.int32)[None, :]
    allowed = (key_at > query_at) & (key_at <= query_at + WINDOW) & (base_pos + key_at >= 0)
    masked = jnp.where(allowed, scores, jnp.float32(-1e30))
    row_top = jnp.max(masked, axis=-1, keepdims=True)
    weights = jnp.where(allowed, jnp.exp(masked - row_top), jnp.float32(0.0))
    row_total = jnp.sum(weights, axis=-1)
    rounded = weights.astype(jnp.bfloat16)
    mixed_rows = jnp.einsum("kgtn,nkd->tkgd", rounded, block_v, preferred_element_type=jnp.float32)
    mixed_rows = mixed_rows / jnp.transpose(row_total, (2, 0, 1))[..., None]
    return mixed_rows.astype(jnp.bfloat16).reshape(query_count, -1)


def shards(
    span_tokens, q_weight, kv_weight, out_weight, kv_pool, cache_lengths, slot_requests, page_table
):
    groups = lax.axis_size("group")
    seq_count = lax.axis_size("seq")
    tensor_count = lax.axis_size("tensor")
    group_id = lax.axis_index("group")
    seq_id = lax.axis_index("seq")
    tensor_id = lax.axis_index("tensor")
    local_reqs, seg_len, feat_local = span_tokens.shape
    head_cols = q_weight.shape[1]
    kv_cols = kv_weight.shape[1]
    local_heads = head_cols // HD
    group_heads = kv_cols // HD
    kv_local = max(1, KVH // tensor_count)
    per_kv = local_heads // kv_local
    head_first = tensor_id * KVH // tensor_count % group_heads
    holds_keys = tensor_id % 2 == 0
    pool_rows = kv_pool.shape[0]
    capacity = pool_rows // groups
    row_count = local_reqs * seg_len
    my_slots = group_id * local_reqs + jnp.arange(local_reqs, dtype=jnp.int32)
    my_requests = slot_requests[my_slots]
    my_lengths = cache_lengths[my_requests]
    project_piece_rows = lax.all_gather(span_tokens, "tensor", axis=2, tiled=True)
    feat_width = project_piece_rows.shape[2]
    flat_rows = project_piece_rows.reshape(row_count, feat_width)
    query_lin = jnp.dot(flat_rows, q_weight, preferred_element_type=jnp.float32)
    fresh_lin = jnp.dot(flat_rows, kv_weight, preferred_element_type=jnp.float32)
    positions = (
        my_lengths[:, None] + seq_id * seg_len + jnp.arange(seg_len, dtype=jnp.int32)[None, :]
    )
    queries = jax.vmap(rotate)(query_lin.reshape(local_reqs, seg_len, local_heads, HD), positions)
    queries = queries.astype(jnp.bfloat16).reshape(local_reqs, seg_len, kv_local, per_kv, HD)
    fresh_heads = fresh_lin.reshape(local_reqs, seg_len, group_heads, HD)
    rotated = jax.vmap(rotate)(fresh_heads, positions)
    span_kv = (
        jnp.where(holds_keys, rotated, fresh_heads)
        .astype(jnp.bfloat16)
        .reshape(local_reqs, seg_len, kv_cols)
    )
    all_ids = page_table[slot_requests]
    owned_here = all_ids // pool_rows == group_id
    slot_rank = jnp.cumsum(owned_here.astype(jnp.int32), axis=1) - 1
    local_rows = all_ids - group_id * pool_rows
    chosen = owned_here[:, :, None] & (
        slot_rank[:, :, None] == jnp.arange(capacity, dtype=jnp.int32)[None, None, :]
    )
    wanted = jnp.sum(jnp.where(chosen, local_rows[:, :, None], 0), axis=1)
    my_ids = page_table[my_requests].reshape(-1)
    my_owner = my_ids // pool_rows
    onehot = (my_owner[:, None] == jnp.arange(groups, dtype=jnp.int32)[None, :]).astype(jnp.int32)
    arrival = jnp.sum((jnp.cumsum(onehot, axis=0) - 1) * onehot, axis=1)
    arrived_row = my_owner * capacity + arrival
    outgoing = kv_pool[wanted]
    arrived = lax.all_to_all(outgoing, "group", split_axis=0, concat_axis=0, tiled=True)
    cached = arrived.reshape(groups * capacity, PAGE, kv_cols)[arrived_row]
    cached = cached.reshape(local_reqs, WINDOW, kv_cols)
    span_all = jnp.zeros((local_reqs, seg_len * seq_count, kv_cols), jnp.bfloat16)
    for back_step in range(seq_count - 1, -1, -1):
        piece_rows = span_kv if back_step == 0 else shifted(span_kv, "seq", back_step)
        span_all = lax.dynamic_update_slice_in_dim(
            span_all, piece_rows, (seq_id - back_step) * seg_len, 1
        )
    joined = jnp.concatenate([cached, span_all], axis=1)
    visible = lax.dynamic_slice_in_dim(joined, seq_id * seg_len, WINDOW + seg_len, 1)
    partner_rows = swapped(visible, "tensor", 0)
    key_all = jnp.where(holds_keys, visible, partner_rows).reshape(
        local_reqs, WINDOW + seg_len, group_heads, HD
    )
    value_all = jnp.where(holds_keys, partner_rows, visible).reshape(
        local_reqs, WINDOW + seg_len, group_heads, HD
    )
    key_rows = lax.dynamic_slice_in_dim(key_all, head_first, kv_local, 2)
    value_rows = lax.dynamic_slice_in_dim(value_all, head_first, kv_local, 2)
    block_len = min(128, seg_len)
    block_count = seg_len // block_len

    def per_request(request_items):
        request_q, request_k, request_v, length = request_items

        def per_block(block_index):
            first_row = block_index * block_len
            block_q = lax.dynamic_slice_in_dim(request_q, first_row, block_len, 0)
            block_k = lax.dynamic_slice_in_dim(request_k, first_row, WINDOW + block_len, 0)
            block_v = lax.dynamic_slice_in_dim(request_v, first_row, WINDOW + block_len, 0)
            return attend(block_q, block_k, block_v, length - WINDOW + seq_id * seg_len + first_row)

        return lax.map(per_block, jnp.arange(block_count, dtype=jnp.int32)).reshape(
            seg_len, head_cols
        )

    attended_heads = lax.map(per_request, (queries, key_rows, value_rows, my_lengths))
    flat_heads = attended_heads.reshape(row_count, head_cols)
    out_cols = out_weight.shape[1] // tensor_count
    summed = lax.psum_scatter(
        lax.dot_general(
            out_weight, flat_heads, (((0,), (1,)), ((), ())), preferred_element_type=jnp.float32
        ).astype(jnp.bfloat16),
        "tensor",
        scatter_dimension=0,
        tiled=True,
    ).astype(jnp.float32)
    result = summed.T
    return result.astype(jnp.bfloat16).reshape(local_reqs, seg_len, out_cols)


LOG2E = 1.4426950408889634
MASKED = -1e30
F32 = jnp.float32
BF16 = jnp.bfloat16
HBM = pl.BlockSpec(memory_space=pl.ANY)
VMEM = pl.BlockSpec(memory_space=pltpu.VMEM)
SMEM = pl.BlockSpec(memory_space=pltpu.SMEM)
STAYS = pl.BlockSpec(memory_space=pltpu.HBM)
GROUPS, SEQS, TENSORS = 4, 4, 2


def params(mebibytes):
    return pltpu.CompilerParams(vmem_limit_bytes=mebibytes * 2**20)


def cost(flops, moved):
    return pl.CostEstimate(flops=flops, bytes_accessed=moved, transcendentals=0)


class Info:
    def __init__(self, ref):
        self.ref = ref
        self.group, self.seq, self.tensor = ref[0, 0], ref[0, 1], ref[0, 2]
        self.window_pages = ref.shape[1]

    def request(self, slot):
        return self.ref[0, 3 + slot]

    def length(self, request):
        return self.ref[0, 3 + GROUPS + request]

    def page(self, request, w):
        return self.ref[1 + request, w]


def turned(x, cosine, sine):
    lane = lax.broadcasted_iota(jnp.int32, x.shape, 1)
    other = jnp.where(lane % HD < HD // 2, pltpu.roll(x, 128 - HD // 2, 1), pltpu.roll(x, HD // 2, 1))
    return x * cosine + other * sine


def open_kernel(
    info_ref, frequency, pool, x_hbm, wq_hbm, wkv_hbm,
    home, same, beyond, beside, across, diagonal, acc_q, acc_kv, cosine, sine,
    x, wq, wkv, sems, page_sems,
):
    info = Info(info_ref)
    rows, feats = x.shape
    here = pl.ds(pl.multiple_of(info.tensor * feats, feats), feats)
    copies = [
        pltpu.make_async_copy(x_hbm, x, sems.at[0]),
        pltpu.make_async_copy(wkv_hbm.at[here], wkv, sems.at[1]),
        pltpu.make_async_copy(wq_hbm.at[here], wq, sems.at[2]),
    ]
    for copy in copies:
        copy.start()
    pages = pool.shape[0]
    capacity = pages // GROUPS
    half = pool.shape[2] // 2
    mine = pl.ds(pl.multiple_of(info.tensor * half, half), half)
    theirs = pl.ds(pl.multiple_of((1 - info.tensor) * half, half), half)
    outs = (home, same, beyond, beside, across, diagonal)
    spots = (
        ((0, 0), (1, 0)),
        ((3, 0), (1, capacity)),
        ((2, 0), (4, 0)),
        ((2, capacity), (5, 0)),
    )
    for flip, targets in enumerate(spots):
        request = info.request(info.group ^ flip)

        def take(w, rank):
            page = info.page(request, w)
            near = page // pages == info.group

            @pl.when(near)
            def _():
                row = page % pages
                for (out, base), cols in zip(targets, (mine, theirs)):
                    pltpu.make_async_copy(
                        pool.at[row, :, cols], outs[out].at[base + rank], page_sems.at[out]
                    ).start()

            return rank + near.astype(jnp.int32)

        lax.fori_loop(0, info.window_pages, take, jnp.int32(0))
    start = info.length(info.request(info.group)) + info.seq * rows
    position = (start + lax.broadcasted_iota(jnp.int32, (rows, 128), 0)).astype(F32)
    angles = position * frequency[0:1, :]
    lane = lax.broadcasted_iota(jnp.int32, (rows, 128), 1)
    cosine[...] = jnp.cos(angles)
    sine[...] = jnp.where(lane % HD < HD // 2, -1.0, 1.0) * jnp.sin(angles)
    copies[0].wait()
    copies[1].wait()
    acc_kv[...] = jnp.dot(x[...], wkv[...], preferred_element_type=F32)
    copies[2].wait()
    acc_q[...] = jnp.dot(x[...], wq[...], preferred_element_type=F32)
    for i, out in enumerate(outs):
        pltpu.make_async_copy(out, out, page_sems.at[i]).wait()


def open_rows(info, frequency, pool, x, wq, wkv):
    rows, feats = x.shape
    pages, page, cols = pool.shape
    single = jax.ShapeDtypeStruct((pages // GROUPS, page, cols // 2), BF16)
    double = jax.ShapeDtypeStruct((2 * pages // GROUPS, page, cols // 2), BF16)
    table = jax.ShapeDtypeStruct((rows, 128), F32)
    return pl.pallas_call(
        open_kernel,
        out_shape=[
            single,
            double,
            double,
            single,
            single,
            single,
            jax.ShapeDtypeStruct((rows, wq.shape[1]), F32),
            jax.ShapeDtypeStruct((rows, wkv.shape[1]), F32),
            table,
            table,
        ],
        in_specs=[SMEM, VMEM] + [STAYS] * 4,
        out_specs=[VMEM] * 10,
        scratch_shapes=[
            pltpu.VMEM((rows, feats), BF16),
            pltpu.VMEM((feats, wq.shape[1]), BF16),
            pltpu.VMEM((feats, wkv.shape[1]), BF16),
            pltpu.SemaphoreType.DMA((3,)),
            pltpu.SemaphoreType.DMA((6,)),
        ],
        compiler_params=params(50),
        cost_estimate=cost(rows * feats, rows * feats),
    )(info, frequency, pool, x, wq, wkv)


def fresh_kernel(info_ref, x, wkv, acc_kv, cosine, sine, kept, sent):
    info = Info(info_ref)
    feats = x.shape[1]
    here = pl.ds(pl.multiple_of((1 - info.tensor) * feats, feats), feats)
    keys = info.tensor == 0
    fresh = acc_kv[...] + jnp.dot(x[...], wkv[here], preferred_element_type=F32)
    cos_kv = jnp.where(keys, cosine[...], 1.0)
    sin_kv = jnp.where(keys, sine[...], 0.0)
    low = turned(fresh[:, :128], cos_kv, sin_kv).astype(BF16)
    high = turned(fresh[:, 128:], cos_kv, sin_kv).astype(BF16)
    kept[...] = jnp.where(keys, low, high)
    sent[...] = jnp.where(keys, high, low)


def fresh_rows(info, x, wkv, acc_kv, cosine, sine):
    rows, feats = x.shape
    piece = jax.ShapeDtypeStruct((rows, wkv.shape[1] // 2), BF16)
    return pl.pallas_call(
        fresh_kernel,
        out_shape=[piece, piece],
        in_specs=[SMEM] + [VMEM] * 5,
        out_specs=[VMEM] * 2,
        compiler_params=params(12),
        cost_estimate=cost(2 * rows * feats * 2560, rows * feats),
    )(info, x, wkv, acc_kv, cosine, sine)


def query_kernel(info_ref, x, wq, acc_q, cosine, sine, q):
    feats = x.shape[1]
    here = pl.ds(pl.multiple_of((1 - Info(info_ref).tensor) * feats, feats), feats)
    cos_all, sin_all = cosine[...], sine[...]
    scale = HD**-0.5 * LOG2E
    tile = 256
    for c in range(0, q.shape[1], tile):
        lin = acc_q[:, c : c + tile] + jnp.dot(
            x[...], wq[here, c : c + tile], preferred_element_type=F32
        )
        for e in range(0, tile, 128):
            q[:, c + e : c + e + 128] = (
                turned(lin[:, e : e + 128], cos_all, sin_all) * scale
            ).astype(BF16)


def query_rows(info, x, wq, acc_q, cosine, sine):
    rows, feats = x.shape
    return pl.pallas_call(
        query_kernel,
        out_shape=jax.ShapeDtypeStruct((rows, wq.shape[1]), BF16),
        in_specs=[SMEM] + [VMEM] * 5,
        out_specs=VMEM,
        compiler_params=params(16),
        cost_estimate=cost(rows * feats, rows * feats),
    )(info, x, wq, acc_q, cosine, sine)


def soft_heads(q, tokens, segments, emit):
    rows = tokens.stop - tokens.start
    stack = 4
    low = lax.broadcasted_iota(jnp.int32, (rows, 2 * HD), 1) < HD

    def swap(x):
        return pltpu.roll(x, HD, 1)

    def heads(i, _):
        first = i == 0
        spots = [pl.ds(pl.multiple_of((i * stack + j) * 128, 128), 128) for j in range(stack)]
        tiles = [q[tokens, spot] for spot in spots]
        turns = [swap(x.astype(F32)).astype(BF16) for x in tiles]
        keep = low == first

        def stacked(a, b):
            zero = jnp.zeros_like(a[0])
            return jnp.concatenate(
                [jnp.where(keep, jnp.where(first, x, y), zero) for x, y in zip(a, b)], axis=0
            )

        def scores(qs):
            return [
                mask(
                    lax.dot_general(
                        qs, keys[span], (((1,), (1,)), ((), ())), preferred_element_type=F32
                    )
                )
                for keys, _, span, mask in segments
            ]

        def peak(parts):
            tops = [jnp.max(s, axis=1, keepdims=True) for s in parts]
            return functools.reduce(jnp.maximum, tops)

        def mixed(weights):
            return sum(
                jnp.dot(p, values[i, span], preferred_element_type=F32)
                for p, (_, values, span, _) in zip(weights, segments)
            )

        s_even = scores(stacked(tiles, turns))
        s_odd = scores(stacked(turns, tiles))
        m_even = peak(s_even)
        m_odd = peak(s_odd)
        p_even = [jnp.exp2(s - m_even).astype(BF16) for s in s_even]
        p_odd = [jnp.exp2(s - m_odd).astype(BF16) for s in s_odd]
        o_even = mixed(p_even)
        o_odd = mixed(p_odd)
        for j in range(stack):
            part = slice(j * rows, (j + 1) * rows)
            a, b = o_even[part], o_odd[part]
            total = jnp.where(low, a, swap(b))
            weight = jnp.where(low, swap(a), b)
            top = jnp.where(low, m_even[part], m_odd[part])
            emit(spots[j], total, weight, top)
        return 0

    lax.fori_loop(0, q.shape[1] // 128 // stack, heads, 0)


def widen(v, ones, values, here):
    low = lax.broadcasted_iota(jnp.int32, v.shape, 1) < HD
    values[0, here] = jnp.where(low, v, ones).astype(BF16)
    values[1, here] = jnp.where(low, pltpu.roll(v, HD, 1), ones).astype(BF16)


def gather_rows(info, own, other, fresh, keys, values, source):
    group, seq = info.group, info.seq
    request = info.request(group)
    rows = fresh.shape[1]
    per = rows // PAGE
    count = own.shape[0]
    capacity = count // GROUPS
    seen = keys.shape[0] // PAGE - seq * per
    is_key = info.tensor == 0

    def note(w, counts):
        came = info.page(request, w) // count ^ group
        place = came * capacity
        for d in range(GROUPS):
            place = place + jnp.where(came == d, counts[d], 0)
        source[w] = place
        return tuple(counts[d] + (came == d).astype(jnp.int32) for d in range(GROUPS))

    lax.fori_loop(0, info.window_pages, note, (jnp.int32(0),) * GROUPS, unroll=True)

    def place(block, a, b):
        here = pl.ds(pl.multiple_of(block * PAGE, PAGE), PAGE)
        keys[here] = jnp.where(is_key, a, b)
        widen(jnp.where(is_key, b, a).astype(F32), 1.0, values, here)

    for block, part in ((1, slice(0, PAGE)), (seen - 1, slice(PAGE, 2 * PAGE))):
        place(block, fresh[0, part], fresh[1, part])
    first = info.length(request) - WINDOW + seq * rows
    stand_in = jnp.where(is_key, fresh[0, :16], fresh[1, :16]).astype(F32)[0:1]
    stand_in = jnp.broadcast_to(stand_in, (PAGE, 2 * HD)).astype(BF16)

    def bring(i, _):
        for n in (2 * i, 2 * i + 1):
            block = jnp.where(n == 0, 0, n + 1)
            here = pl.ds(pl.multiple_of(block * PAGE, PAGE), PAGE)
            at = source[seq * per + n]
            hidden = first + n * PAGE < 0
            a, b = own[at], other[at]
            keys[here] = jnp.where(hidden, stand_in, jnp.where(is_key, a, b))
            v = jnp.where(is_key, b, a).astype(F32)
            widen(jnp.where(hidden, 0.0, v), jnp.where(hidden, 0.0, 1.0), values, here)
        return 0

    lax.fori_loop(0, (seen - per) // 2, bring, 0)


def bundle_kernel(a, b, out):
    out[: a.shape[0]] = a[...]
    out[a.shape[0] :] = b[...]


def bundled(a, b):
    return pl.pallas_call(
        bundle_kernel,
        out_shape=jax.ShapeDtypeStruct((a.shape[0] + b.shape[0], *a.shape[1:]), BF16),
        in_specs=[VMEM] * 2,
        out_specs=VMEM,
        compiler_params=params(8),
        cost_estimate=cost(6 * 10**9, 4),
    )(a, b)


def near_segment(keys, values, seq, half):
    blocks = keys.shape[0] // PAGE
    per = 2
    span = slice(half * PAGE, (blocks - seq * per - 1 + half) * PAGE)

    def mask(s):
        newer = lax.broadcasted_iota(jnp.int32, (s.shape[0], PAGE), 1) > (
            lax.broadcasted_iota(jnp.int32, (s.shape[0], PAGE), 0) % PAGE
        )
        if half == 0:
            parts = [
                jnp.where(newer, s[:, :PAGE], MASKED),
                jnp.where(newer, MASKED, s[:, PAGE : 2 * PAGE]),
                s[:, 2 * PAGE :],
            ]
        else:
            parts = [
                s[:, :PAGE],
                jnp.where(newer, s[:, PAGE : 2 * PAGE], MASKED),
                s[:, 2 * PAGE : -PAGE],
                jnp.where(newer, MASKED, s[:, -PAGE:]),
            ]
        return jnp.concatenate(parts, axis=1)

    return keys, values, span, mask


def far_segment(keys, values, seq):
    return keys, values, slice(0, seq * 2 * PAGE), lambda s: s


def near_kernel(
    info_ref, q, own, other, fresh, total, weight, top, keys, values, source
):
    info = Info(info_ref)
    seq = info.seq
    gather_rows(info, own, other, fresh, keys, values, source)

    def emit(spot, o, l, m):
        total[:, spot] = o
        weight[:, spot] = l
        top[:, spot] = m

    for k in range(SEQS):

        @pl.when(seq == k)
        def _(k=k):
            soft_heads(q, slice(0, PAGE), [near_segment(keys, values, k, 0)], emit)


def attend_near(info, q, own, other, fresh):
    state = jax.ShapeDtypeStruct((PAGE, q.shape[1]), F32)
    span = WINDOW + fresh.shape[1]
    *state, keys, values = pl.pallas_call(
        near_kernel,
        out_shape=[
            state,
            state,
            state,
            jax.ShapeDtypeStruct((span, 2 * HD), BF16),
            jax.ShapeDtypeStruct((2, span, 2 * HD), BF16),
        ],
        in_specs=[SMEM] + [VMEM] * 4,
        out_specs=[VMEM] * 5,
        scratch_shapes=[pltpu.SMEM((own.shape[0],), jnp.int32)],
        compiler_params=params(32),
        cost_estimate=cost(20 * 10**9, 4 * span),
    )(info, q, own, other, fresh)
    return state, keys, values


def partner_product(info, heads_out, w, partial):
    cols = partial.shape[1]
    here = pl.ds(pl.multiple_of((1 - info.tensor) * cols, cols), cols)
    partial[...] = jnp.dot(heads_out[...], w[:, here], preferred_element_type=F32).astype(BF16)


def far_kernel(
    info_ref, q, total, weight, top, z2, z3, z1, w, heads_out, partial, keys, values
):
    info = Info(info_ref)
    rows = q.shape[0]
    seq = info.seq
    zs = (None, z1, z2, z3)
    is_key = info.tensor == 0

    for k in range(SEQS):

        @pl.when(seq == k)
        def _(k=k):
            if k == 0:
                heads_out[...] = (total[...] / weight[...]).astype(BF16)
                return
            for n in range(k):
                z = zs[n ^ k]
                here = slice(n * rows, (n + 1) * rows)
                a, b = z[0], z[1]
                keys[here] = jnp.where(is_key, a, b)
                widen(jnp.where(is_key, b, a).astype(F32), 1.0, values, here)

            def emit(spot, o, l, m):
                before = top[:, spot]
                peak = jnp.maximum(before, m)
                a = jnp.exp2(before - peak)
                b = jnp.exp2(m - peak)
                done = (total[:, spot] * a + o * b) / (weight[:, spot] * a + l * b)
                heads_out[:, spot] = done.astype(BF16)

            soft_heads(q, slice(0, PAGE), [far_segment(keys, values, k)], emit)

    partner_product(info, heads_out, w, partial)


def attend_far(info, q, state, zs, w):
    rows = q.shape[0]
    span = (SEQS - 1) * rows
    return pl.pallas_call(
        far_kernel,
        out_shape=[
            jax.ShapeDtypeStruct((PAGE, q.shape[1]), BF16),
            jax.ShapeDtypeStruct((PAGE, w.shape[1] // TENSORS), BF16),
            jax.ShapeDtypeStruct((span, 2 * HD), BF16),
            jax.ShapeDtypeStruct((2, span, 2 * HD), BF16),
        ],
        in_specs=[SMEM] + [VMEM] * 8,
        out_specs=[VMEM] * 4,
        compiler_params=params(24),
        cost_estimate=cost(rows * span, 4 * span),
    )(info, q, *state, *zs, w)


def last_kernel(info_ref, q, keys, values, far_keys, far_values, w, heads_out, partial):
    info = Info(info_ref)

    def emit(spot, o, l, m):
        heads_out[:, spot] = (o / l).astype(BF16)

    for k in range(SEQS):

        @pl.when(info.seq == k)
        def _(k=k):
            segments = [near_segment(keys, values, k, 1)]
            if k:
                segments.append(far_segment(far_keys, far_values, k))
            soft_heads(q, slice(PAGE, 2 * PAGE), segments, emit)

    partner_product(info, heads_out, w, partial)


def attend_last(info, q, keys, values, far_keys, far_values, w):
    return pl.pallas_call(
        last_kernel,
        out_shape=[
            jax.ShapeDtypeStruct((PAGE, q.shape[1]), BF16),
            jax.ShapeDtypeStruct((PAGE, w.shape[1] // TENSORS), BF16),
        ],
        in_specs=[SMEM] + [VMEM] * 6,
        out_specs=[VMEM] * 2,
        compiler_params=params(36),
        cost_estimate=cost(PAGE * WINDOW, 4 * WINDOW),
    )(info, q, keys, values, far_keys, far_values, w)


def home_kernel(info_ref, x1, x2, away, w, out, home, first, sem):
    rows, cols = home.shape
    here = pl.ds(pl.multiple_of(Info(info_ref).tensor * cols, cols), cols)
    x = jnp.concatenate([x1[...], x2[...]], axis=0)
    o = jnp.dot(x, w[:, here], preferred_element_type=F32).astype(BF16)
    home[...] = o[rows:]
    first[...] = (o[:rows].astype(F32) + away[...].astype(F32)).astype(BF16)
    copy = pltpu.make_async_copy(first, out.at[pl.ds(0, rows)], sem)
    copy.start()
    copy.wait()


def home_project(info, x1, x2, away, w):
    rows, depth = x1.shape
    cols = w.shape[1] // TENSORS
    return pl.pallas_call(
        home_kernel,
        out_shape=[
            jax.ShapeDtypeStruct((2 * rows, cols), BF16),
            jax.ShapeDtypeStruct((rows, cols), BF16),
        ],
        in_specs=[SMEM] + [VMEM] * 4,
        out_specs=[STAYS, VMEM],
        scratch_shapes=[pltpu.VMEM((rows, cols), BF16), pltpu.SemaphoreType.DMA],
        compiler_params=params(16),
        cost_estimate=cost(20 * 10**9, 2 * depth * cols),
    )(info, x1, x2, away, w)


def add_kernel(before, a, b, out, last, sem):
    rows = a.shape[0]
    last[...] = (a[...].astype(F32) + b[...].astype(F32)).astype(BF16)
    copy = pltpu.make_async_copy(last, out.at[pl.ds(rows, rows)], sem)
    copy.start()
    copy.wait()


def added(before, a, b):
    return pl.pallas_call(
        add_kernel,
        out_shape=jax.ShapeDtypeStruct(before.shape, BF16),
        in_specs=[STAYS, VMEM, VMEM],
        out_specs=STAYS,
        scratch_shapes=[pltpu.VMEM(a.shape, BF16), pltpu.SemaphoreType.DMA],
        input_output_aliases={0: 0},
        compiler_params=params(8),
    )(before, a, b)


def flipped(value, axes, count, bits):
    return lax.ppermute(value, axes, [(i, i ^ bits) for i in range(count)])


def after(value, *others):
    return lax.optimization_barrier((value, *others))[0]


def shards_fast(
    span_tokens, q_weight, kv_weight, out_weight, kv_pool, cache_lengths, slot_requests, page_table
):
    group_id = lax.axis_index("group")
    seq_id = lax.axis_index("seq")
    tensor_id = lax.axis_index("tensor")
    place = jnp.stack([group_id, seq_id, tensor_id]).astype(jnp.int32)
    row = jnp.concatenate([place, slot_requests, cache_lengths])
    row = jnp.pad(row, (0, page_table.shape[1] - row.shape[0]))
    info = jnp.concatenate([row[None], page_table])
    mine = span_tokens[0]
    theirs = flipped(mine, "tensor", 2, 1)
    half_dim = HD // 2
    lane = jnp.arange(128, dtype=jnp.int32) % half_dim
    frequency = jnp.power(jnp.float32(10000.0), -lane.astype(F32) / half_dim)
    frequency = jnp.broadcast_to(frequency[None, :], (8, 128))
    pages = open_rows(info, frequency, kv_pool, mine, q_weight, kv_weight)
    home, same, beyond, beside, across, diagonal = pages[:6]
    acc_q, acc_kv, cosine, sine = pages[6:]
    capacity = home.shape[0]
    same = flipped(same, "tensor", 2, 1)
    beyond = flipped(beyond, "group", 4, 2)
    kept, sent = fresh_rows(info, theirs, kv_weight, acc_kv, cosine, sine)
    got = flipped(sent, "tensor", 2, 1)
    across, diagonal, _ = lax.optimization_barrier((across, diagonal, sent))
    across = flipped(across, ("group", "tensor"), 8, 5)
    diagonal = flipped(diagonal, ("group", "tensor"), 8, 7)
    same, beyond, _ = lax.optimization_barrier((same, beyond, sent))
    mate = jnp.concatenate([beside, beyond[capacity:], same[capacity:]])
    mate = flipped(mate, "group", 4, 1)
    fresh = bundled(kept[None], got[None])
    zs = [flipped(fresh, "seq", 4, d) for d in (2, 3, 1)]
    q = query_rows(after(info, fresh), theirs, q_weight, acc_q, cosine, sine)
    across, diagonal, _ = lax.optimization_barrier((across, diagonal, q))
    other_chip = bundled(across, diagonal)
    own = jnp.concatenate(
        [home, mate[:capacity], beyond[:capacity], mate[capacity : 2 * capacity]]
    )
    other = jnp.concatenate([same[:capacity], mate[2 * capacity :], other_chip])
    state, keys, values = attend_near(info, q, own, other, fresh)
    heads_0, partial_0, far_keys, far_values = attend_far(info, q, state, zs, out_weight)
    away_0 = flipped(partial_0, "tensor", 2, 1)
    heads_1, partial_1 = attend_last(info, q, keys, values, far_keys, far_values, out_weight)
    away_1 = flipped(partial_1, "tensor", 2, 1)
    out, home_1 = home_project(info, heads_0, heads_1, away_0, out_weight)
    return added(out, home_1, away_1)[None]


def solution(mesh):
    sizes = tuple(mesh.shape[a] for a in ("group", "seq", "tensor"))
    body = shards_fast if sizes == (GROUPS, SEQS, TENSORS) else shards
    placed = (
        P("group", "seq", "tensor"),
        P(None, "tensor"),
        P(None, "tensor"),
        P("tensor", None),
        P("group", None, "tensor"),
        P(),
        P(),
        P(),
    )
    return jax.shard_map(
        body, mesh=mesh, in_specs=placed, out_specs=P("group", "seq", "tensor"), check_vma=False
    )
```
